32 devices in a mesh: expert: 8 (over y, x, core), tensor: 4 (over z).
Axes of the slice: x: 2, y: 2, z: 4, core: 2. Of those that a mesh axis runs over, the one named last changes fastest.
Arguments:
- inputs: bfloat16 [3072, 1024], P('expert'), may hold values from -6 to 6
- attention_gain: float32 [1024], replicated, may hold values from 0.5 to 1.5
- query_weight: bfloat16 [1024, 1024], P(None, 'tensor'), may hold values from -0.1875 to 0.1875
- key_weight: bfloat16 [1024, 512], P(None, 'tensor'), may hold values from -0.1875 to 0.1875
- value_weight: bfloat16 [1024, 512], P(None, 'tensor'), may hold values from -0.1875 to 0.1875
- out_weight: bfloat16 [1024, 1024], P('tensor'), may hold values from -1.5 to 1.5
- expert_gain: float32 [1024], replicated, may hold values from 0.5 to 1.5
- router_weight: bfloat16 [1024, 32], replicated, may hold values from -0.09375 to 0.09375
- gate_weight: bfloat16 [32, 1024, 512], P('expert', None, 'tensor'), may hold values from -0.1875 to 0.1875
- up_weight: bfloat16 [32, 1024, 512], P('expert', None, 'tensor'), may hold values from -0.1875 to 0.1875
- down_weight: bfloat16 [32, 512, 1024], P('expert', 'tensor'), may hold values from -1 to 1
- routes: int32 [3072, 8], P('expert'), may hold values from 0 to 31, all different within a row; in each aligned block of 384 rows (0 to 383, 384 to 767, ...) at most 192 rows name the same one
- seq_lens: int32 [2], replicated, may hold values from 384 to 1536, as said below
- cotangent: float32 [3072, 1024], P('expert'), may hold values from -6 to 6
Outputs:
- output: float32 [3072, 1024], P('expert')
- input_grad: float32 [3072, 1024], P('expert')
- balance_loss: float32 [], replicated
- expert_load: float32 [32], replicated
- attention_gain_grad: float32 [1024], replicated
- query_grad: float32 [1024, 1024], P(None, 'tensor')
- key_grad: float32 [1024, 512], P(None, 'tensor')
- value_grad: float32 [1024, 512], P(None, 'tensor')
- out_weight_grad: float32 [1024, 1024], P('tensor')
- expert_gain_grad: float32 [1024], replicated
- router_grad: float32 [1024, 32], replicated
- gate_grad: float32 [32, 1024, 512], P('expert', None, 'tensor')
- up_grad: float32 [32, 1024, 512], P('expert', None, 'tensor')
- down_grad: float32 [32, 512, 1024], P('expert', 'tensor')
The draws below stay inside these ranges and needn't reach their ends.
Inputs may be any that keep to these rules, and one draw needn't show every extreme that they name: `routes`: in each aligned block of 384 rows (the rows of one device) no expert is named by more than 192 rows, a bound that some block reaches. `seq_lens`: one sequence has exactly 1536 valid tokens.
All inputs are finite; a program needn't handle non-finite values.
Results may differ from the reference program's by a relative error of at most 0.018.
Values may be sent and summed in bfloat16 or wider, within the bound.
A program may use at most 192 MiB of HBM per device.

```python
import math
import jax
import jax.numpy as jnp
import numpy as np
from jax import lax

D = 1024
QH = 16
KVH = 8
HD = 64
EXPERTS = 32
FF = 512
TOP = 8
TOK_DEV = 384
SEQS = 2
CAP = 192
TOKENS = 3072
SEQ_LEN = 1536
N_EXPERT = 8


def draw_seq_lens(key, part):
    lengths = jax.random.randint(key, (SEQS,), SEQ_LEN // 4, SEQ_LEN + 1)
    longest = jax.random.randint(jax.random.fold_in(key, 7), (), 0, SEQS)
    return jnp.where(jnp.arange(SEQS) == longest, SEQ_LEN, lengths).astype(jnp.int32)


def block_levels(stream_key, extent, cuts, low, largest):
    level = 1.0
    for dim, blocks in cuts:
        steps = jax.random.uniform(jax.random.fold_in(jax.random.fold_in(stream_key, 6), dim), (blocks,), jnp.float32, low / len(cuts), largest / len(cuts))
        level = level * jnp.repeat(jnp.exp(steps), extent[dim] // blocks).reshape((-1,) + (1,) * (len(extent) - 1 - dim))
    return level


def deal_out(own_key, own, number, rows, number_of, top, most, slope):
    sequence = jax.random.permutation(own_key, number_of)
    packed, ordinary = shares(number_of, rows * top, most, slope, True), shares(number_of, rows * top, most, slope, False)
    places = jnp.arange(number_of)

    def named(sizes, turn):
        used = int((sizes > 0).sum())
        fixed = max(1, used // 4)
        passed = fixed + (places - fixed + turn * (used - fixed)) % max(1, number_of - fixed)
        return jnp.zeros((number_of,), jnp.int32).at[sequence[jnp.where(places < fixed, places, passed)]].set(jnp.asarray(sizes, jnp.int32))

    sizes = jnp.where(number % 4 == 0, named(packed, number // 4), named(ordinary, number - number // 4 - 1))
    mixed = jax.random.permutation(jax.random.fold_in(own, 3), number_of)
    donor, taker = mixed[0:number_of // 2 * 2:2], mixed[1:number_of // 2 * 2:2]
    margin = jnp.minimum(sizes[donor] - 1, most - sizes[taker]) // 2
    margin = jnp.where((donor == sequence[0]) | (taker == sequence[0]) | (sizes[taker] == 0), 0, jnp.maximum(margin, 0))
    passed = jax.random.randint(jax.random.fold_in(own, 4), (number_of // 2,), 0, 1 << 20) % (margin + 1)
    sizes = sizes.at[donor].add(-passed).at[taker].add(passed)
    members = jnp.searchsorted(jnp.cumsum(sizes), jnp.arange(rows * top), side="right").astype(jnp.int32)
    grid = members.reshape(top, rows).T
    grid = grid[jax.random.permutation(jax.random.fold_in(own, 1), rows)]
    turn = jax.random.randint(jax.random.fold_in(own, 2), (rows, 1), 0, top)
    return jnp.take_along_axis(grid, (jnp.arange(top)[None, :] + turn) % top, axis=1)


def shares(amount, total, bound, lean, full):
    portions = [(1 << 20) // math.isqrt(standing ** lean) + 1 for standing in range(1, amount + 1)]
    largest = bound if full else min(bound, max(-(-total // amount), total * portions[0] // sum(portions)))
    least = 1 if total - largest >= amount - 1 else 0
    holding, surplus = [largest] + [least] * (amount - 1), total - largest - least * (amount - 1)
    while surplus > 0:
        free = [i for i in range(1, amount) if holding[i] < largest] or [i for i in range(1, amount) if holding[i] < bound]
        mass, left = sum([portions[i] for i in free]), surplus
        for i in free:
            extra = min(bound - holding[i], max(1, left * portions[i] // mass), surplus)
            holding[i] = holding[i] + extra
            surplus = surplus - extra
    return np.array(holding)


def noise(rng, extent, scale, most, split=(), kind=jnp.bfloat16):
    array = scale * jax.random.normal(rng, extent, jnp.float32)
    if split:
        array = array * block_levels(rng, extent, split, -0.22, 0.18)
    return jnp.clip(array, -most, most).astype(kind)


def setup_inputs(seed: int = 0) -> dict:
    key_of = jax.random.split(jax.random.key(seed), 15)
    inputs = noise(key_of[0], (TOKENS, D), 1.0, 6.0, ((0, 8),))
    attention_gain = jnp.clip(1.0 + 0.1 * jax.random.normal(key_of[1], (D,), jnp.float32), 0.5, 1.5)
    query_weight = noise(key_of[2], (D, QH * HD), D ** -0.5, 0.1875, ((1, 4),))
    key_weight = noise(key_of[3], (D, KVH * HD), D ** -0.5, 0.1875, ((1, 4),))
    value_weight = noise(key_of[4], (D, KVH * HD), D ** -0.5, 0.1875, ((1, 4),))
    out_weight = noise(key_of[5], (QH * HD, D), 16 ** -0.5, 1.5, ((0, 4),))
    expert_gain = jnp.clip(1.0 + 0.1 * jax.random.normal(key_of[6], (D,), jnp.float32), 0.5, 1.5)
    router_weight = noise(key_of[7], (D, EXPERTS), (4 * D) ** -0.5, 0.09375)
    gate_weight = noise(key_of[8], (EXPERTS, D, FF), D ** -0.5, 0.1875, ((0, 8), (2, 4)))
    up_weight = noise(key_of[9], (EXPERTS, D, FF), D ** -0.5, 0.1875, ((0, 8), (2, 4)))
    down_weight = noise(key_of[10], (EXPERTS, FF, D), (FF // 16) ** -0.5, 1.0, ((0, 8), (1, 4)))
    routes_keys = jax.random.split(jax.random.fold_in(key_of[11], 1), TOKENS // TOK_DEV)
    routes_turns = jax.random.permutation(jax.random.fold_in(key_of[11], 3), TOKENS // TOK_DEV)
    routes = jax.vmap(lambda own, number: deal_out(jax.random.fold_in(key_of[11], 2), own, number, TOK_DEV, EXPERTS, TOP, CAP, 1))(routes_keys, routes_turns).reshape((TOKENS, TOP))
    seq_lens = draw_seq_lens(jax.random.fold_in(key_of[14], 71), 0)
    cotangent = noise(key_of[13], (TOKENS, D), 1.0, 6.0, ((0, 8),), jnp.float32)
    return {"inputs": inputs, "attention_gain": attention_gain, "query_weight": query_weight, "key_weight": key_weight, "value_weight": value_weight, "out_weight": out_weight, "expert_gain": expert_gain, "router_weight": router_weight, "gate_weight": gate_weight, "up_weight": up_weight, "down_weight": down_weight, "routes": routes, "seq_lens": seq_lens, "cotangent": cotangent}


EPS = 1e-06
THETA = 10000.0
highest = lax.Precision.HIGHEST

@jax.custom_vjp
def low(v):
    return lax.optimization_barrier(v.astype(jnp.bfloat16)).astype(jnp.float32)

@jax.custom_vjp
def low_back(v):
    return v

def low_keep(v):
    return (low(v), None)

def low_pass(kept, grad):
    return (grad,)

def back_keep(v):
    return (v, None)

def back_low(kept, grad):
    return (low(grad),)
low.defvjp(low_keep, low_pass)
low_back.defvjp(back_keep, back_low)

def matmul(left, right):
    return jnp.dot(left, right, precision=highest, preferred_element_type=jnp.float32)

def rms_norm(values, gain):
    return values * lax.rsqrt(lax.optimization_barrier(jnp.mean(values * values, -1, keepdims=True)) + EPS) * gain

def rotate(values, positions):
    half_size = HD // 2
    frequency = THETA ** (-2.0 * jnp.arange(half_size, dtype=jnp.float32) / HD)
    angles = positions.astype(jnp.float32)[:, None] * frequency[None, :]
    cosines = jnp.concatenate([jnp.cos(angles), jnp.cos(angles)], -1)[:, None, :]
    sine_table = jnp.concatenate([jnp.sin(angles), jnp.sin(angles)], -1)[:, None, :]
    turned = jnp.concatenate([-values[..., half_size:], values[..., :half_size]], -1)
    return values * cosines + turned * sine_table

def to_sequences(values):
    span = TOK_DEV // SEQS
    rest = values.shape[1:]
    return values.reshape((N_EXPERT, SEQS, span) + rest).swapaxes(0, 1).reshape((SEQS, SEQ_LEN) + rest)

def attend(items):
    queries, keys, values, length = items
    groups = QH // KVH
    keys_wide = jnp.repeat(keys, groups, axis=1)
    values_wide = jnp.repeat(values, groups, axis=1)
    query_block = math.gcd(SEQ_LEN, 512)
    key_pos = jnp.arange(SEQ_LEN, dtype=jnp.int32)

    def one_block(index):
        start = (index * query_block).astype(jnp.int32)
        block_rows = lax.dynamic_slice_in_dim(queries, start, query_block, 0)
        query_pos = start + jnp.arange(query_block, dtype=jnp.int32)
        scores = jnp.einsum('qhd,khd->hqk', block_rows, keys_wide, precision=highest) * HD ** (-0.5)
        scores = low_back(scores)
        allowed = (key_pos[None, :] <= query_pos[:, None]) & (key_pos[None, :] < length)
        scores = jnp.where(allowed[None], scores, -1e+30)
        probs_low = low(jax.nn.softmax(scores, -1))
        return jnp.einsum('hqk,khd->qhd', probs_low, values_wide, precision=highest)
    blocks = lax.map(jax.checkpoint(one_block), jnp.arange(SEQ_LEN // query_block, dtype=jnp.int32))
    return blocks.reshape(SEQ_LEN, QH, HD)

def forward(inputs, attention_gain, query_weight, key_weight, value_weight, out_weight, expert_gain, router_weight, gate_weight, up_weight, down_weight, routes, seq_lens):
    span = TOK_DEV // SEQS
    normed = low(rms_norm(inputs, attention_gain))
    rows = jnp.arange(TOKENS, dtype=jnp.int32)
    positions = rows // TOK_DEV * span + rows % TOK_DEV % span
    queries = low(rotate(low_back(matmul(normed, query_weight)).reshape(TOKENS, QH, HD), positions))
    keys = low(rotate(low_back(matmul(normed, key_weight)).reshape(TOKENS, KVH, HD), positions))
    values = low(low_back(matmul(normed, value_weight))).reshape(TOKENS, KVH, HD)
    attended = lax.map(attend, (to_sequences(queries), to_sequences(keys), to_sequences(values), seq_lens))
    attended = attended.reshape(SEQS, N_EXPERT, span, QH * HD).swapaxes(0, 1).reshape(TOKENS, QH * HD)
    attended = low(low_back(attended))
    mid = inputs + low_back(matmul(attended, out_weight))
    normed2 = low(rms_norm(mid, expert_gain))
    logits = low_back(matmul(normed2, router_weight))
    router_probs = jax.nn.softmax(logits, -1)
    onehot = (routes[:, :, None] == jnp.arange(EXPERTS, dtype=jnp.int32)[None, None, :]).astype(jnp.float32)
    chosen = jnp.einsum('tke,te->tk', onehot, logits, precision=highest)
    gates = jax.nn.softmax(chosen, -1)
    combine = jnp.einsum('tke,tk->te', onehot, gates, precision=highest)
    share = lax.optimization_barrier(jnp.sum(onehot, (0, 1))) / (TOKENS * TOP)
    expert_load = EXPERTS * EXPERTS * share * lax.optimization_barrier(jnp.mean(router_probs, 0))
    balance_loss = jnp.mean(expert_load)

    def one_expert(total, item):
        gate_one, up_one, down_one, weight_col = item
        rows_in = low_back(normed2)
        gate_val = low_back(matmul(rows_in, gate_one))
        up_val = low_back(matmul(rows_in, up_one))
        inner = low(jax.nn.silu(gate_val) * up_val)
        result = low(low_back(matmul(inner, down_one)))
        return (total + weight_col[:, None] * result, None)
    mixed, _ = lax.scan(jax.checkpoint(one_expert), jnp.zeros((TOKENS, D), jnp.float32), (gate_weight, up_weight, down_weight, combine.T))
    return (mid + mixed, balance_loss, expert_load)

def reference(inputs, attention_gain, query_weight, key_weight, value_weight, out_weight, expert_gain, router_weight, gate_weight, up_weight, down_weight, routes, seq_lens, cotangent):
    floats = tuple((item.astype(jnp.float32) for item in (inputs, attention_gain, query_weight, key_weight, value_weight, out_weight, expert_gain, router_weight, gate_weight, up_weight, down_weight)))

    def wrapped(*params):
        return forward(*params, routes, seq_lens)
    (output, balance_loss, expert_load), pullback = jax.vjp(wrapped, *floats)
    grads = pullback((cotangent.astype(jnp.float32), jnp.ones((), jnp.float32), jnp.zeros((EXPERTS,), jnp.float32)))
    return (output, grads[0], balance_loss, expert_load, grads[1], grads[2], grads[3], grads[4], grads[5], grads[6], grads[7], grads[8], grads[9], grads[10])
```

```python
import math

import jax
import jax.numpy as jnp
from jax import lax
from jax.sharding import PartitionSpec as P

HD = 64

EPS = 1e-06
THETA = 10000.0


def rope_tables(positions, head_size):
    half_size = head_size // 2
    frequency = THETA ** (-2.0 * jnp.arange(half_size, dtype=jnp.float32) / head_size)
    angles = positions.astype(jnp.float32)[:, None] * frequency[None, :]
    cosines = jnp.cos(angles)
    sine_table = jnp.sin(angles)
    return (jnp.concatenate([cosines, cosines], -1), jnp.concatenate([sine_table, sine_table], -1))


def rotate(values, cosines, sine_table, forward):
    half_size = values.shape[-1] // 2
    if forward:
        turned = jnp.concatenate([-values[..., half_size:], values[..., :half_size]], -1)
        return values * cosines[:, None, :] + turned * sine_table[:, None, :]
    scaled = values * sine_table[:, None, :]
    turned = jnp.concatenate([scaled[..., half_size:], -scaled[..., :half_size]], -1)
    return values * cosines[:, None, :] + turned


def head_total(partial_value):
    return lax.psum(partial_value, "tensor")


def shards(
    inputs,
    attention_gain,
    query_weight,
    key_weight,
    value_weight,
    out_weight,
    expert_gain,
    router_weight,
    gate_weight,
    up_weight,
    down_weight,
    routes,
    seq_lens,
    cotangent,
):
    f32 = jnp.float32
    bf16 = jnp.bfloat16
    tok_rows, model_width = inputs.shape
    expert_ranks = lax.axis_size("expert")
    expert_rank = lax.axis_index("expert")
    total_rows = tok_rows * expert_ranks
    seq_count = seq_lens.shape[0]
    seq_length = total_rows // seq_count
    span_rows = tok_rows // seq_count
    query_width = query_weight.shape[1]
    key_width = key_weight.shape[1]
    query_heads = query_width // HD
    key_heads = key_width // HD
    groups = query_heads // key_heads
    experts = router_weight.shape[1]
    chosen_count = routes.shape[1]
    local_experts = gate_weight.shape[0]
    hidden_units = gate_weight.shape[2]
    score_scale = HD ** (-0.5)
    local_pos = expert_rank * span_rows + jnp.arange(span_rows, dtype=jnp.int32)
    row_pos = jnp.tile(local_pos, seq_count)
    key_block = math.gcd(seq_length, 2048)
    last_pos = expert_rank * span_rows + span_rows - 1
    used_blocks = last_pos // key_block + 1
    residual = inputs.astype(f32)
    norm_scale = lax.rsqrt(jnp.mean(residual * residual, -1, keepdims=True) + EPS)
    normed = (residual * norm_scale * attention_gain).astype(bf16)
    cosines, sine_table = rope_tables(row_pos, HD)
    query_lin = jnp.dot(normed, query_weight, preferred_element_type=f32)
    key_lin = jnp.dot(normed, key_weight, preferred_element_type=f32)
    value_lin = jnp.dot(normed, value_weight, preferred_element_type=f32)
    queries = rotate(
        query_lin.reshape(tok_rows, query_heads, HD), cosines, sine_table, True
    ).astype(bf16)
    keys_rot = rotate(key_lin.reshape(tok_rows, key_heads, HD), cosines, sine_table, True).astype(
        bf16
    )
    pair_local = jnp.concatenate(
        [keys_rot.reshape(tok_rows, key_width), value_lin.astype(bf16)], -1
    )
    flat = lax.all_gather(pair_local, "expert", axis=0, tiled=True)
    width_now = flat.shape[-1]
    shaped = flat.reshape(expert_ranks, seq_count, span_rows, width_now).transpose(1, 0, 2, 3)
    pairs_seq = shaped.reshape(seq_count, seq_length, width_now)
    query_groups = queries.reshape(seq_count, span_rows, key_heads, groups, HD)

    def block_scores(pairs_here, index):
        start = index * key_block
        pair_block = lax.dynamic_slice_in_dim(pairs_here, start, key_block, 1)
        pos_block = start + jnp.arange(key_block, dtype=jnp.int32)
        key_part = pair_block[..., :key_width].reshape(seq_count, key_block, key_heads, HD)
        value_part = pair_block[..., key_width:].reshape(seq_count, key_block, key_heads, HD)
        scores = (
            jnp.einsum("sqhgd,skhd->shgqk", query_groups, key_part, preferred_element_type=f32)
            * score_scale
        )
        allowed = (pos_block[None, None, :] <= local_pos[None, :, None]) & (
            pos_block[None, None, :] < seq_lens[:, None, None]
        )
        return (scores, allowed[:, None, None], key_part, value_part)

    def score_maxima(index, carry):
        running_max, running_sum = carry
        scores, allowed, _, _ = block_scores(pairs_seq, index)
        scores = jnp.where(allowed, scores, -1e30)
        new_max = jnp.maximum(running_max, jnp.max(scores, -1))
        weights_now = jnp.where(allowed, jnp.exp(scores - new_max[..., None]), 0.0)
        running_sum = running_sum * jnp.exp(running_max - new_max) + jnp.sum(weights_now, -1)
        return (new_max, running_sum)

    start_max = jnp.full((seq_count, key_heads, groups, span_rows), -1e30, f32)
    row_max, row_sum = lax.fori_loop(
        0, used_blocks, score_maxima, (start_max, jnp.zeros_like(start_max))
    )
    log_total = row_max + jnp.log(row_sum)

    def value_sums(index, totals):
        scores, allowed, _, value_part = block_scores(pairs_seq, index)
        probs_low = jnp.where(allowed, jnp.exp(scores - log_total[..., None]), 0.0).astype(bf16)
        return totals + jnp.einsum(
            "shgqk,skhd->shgqd", probs_low, value_part, preferred_element_type=f32
        )

    attended_raw = lax.fori_loop(
        0, used_blocks, value_sums, jnp.zeros((seq_count, key_heads, groups, span_rows, HD), f32)
    )
    attended = attended_raw.transpose(0, 3, 1, 2, 4).reshape(tok_rows, query_width).astype(bf16)
    middle = residual + head_total(jnp.dot(attended, out_weight, preferred_element_type=f32))
    norm_scale2 = lax.rsqrt(jnp.mean(middle * middle, -1, keepdims=True) + EPS)
    normed2 = (middle * norm_scale2 * expert_gain).astype(bf16)
    logits = jnp.dot(normed2, router_weight, preferred_element_type=f32)
    router_probs = jax.nn.softmax(logits, -1)
    onehot = (routes[:, :, None] == jnp.arange(experts, dtype=jnp.int32)[None, None, :]).astype(f32)
    chosen = jnp.einsum("tke,te->tk", onehot, logits)
    gates = jax.nn.softmax(chosen, -1)
    counts = jnp.sum(onehot, (0, 1))
    prob_sums = jnp.sum(router_probs, 0)
    counts_all, prob_all = lax.psum((counts, prob_sums), "expert")
    share = counts_all / (total_rows * chosen_count)
    expert_load = experts * experts * share * (prob_all / total_rows)
    balance_loss = jnp.mean(expert_load)
    combine = jnp.einsum("tke,tk->te", onehot, gates)

    rows_all = lax.all_gather(normed2, "expert", axis=0, tiled=True)
    cot_all = lax.all_gather(cotangent.astype(bf16), "expert", axis=0, tiled=True)
    combine_own = lax.all_to_all(
        combine.reshape(tok_rows, expert_ranks, local_experts),
        "expert",
        split_axis=1,
        concat_axis=0,
        tiled=True,
    ).reshape(total_rows, local_experts)
    width = local_experts * hidden_units
    gate_flat = gate_weight.transpose(1, 0, 2).reshape(model_width, width)
    up_flat = up_weight.transpose(1, 0, 2).reshape(model_width, width)
    down_flat = down_weight.reshape(width, model_width)
    gate_val = jnp.dot(rows_all, gate_flat, preferred_element_type=f32)
    up_val = jnp.dot(rows_all, up_flat, preferred_element_type=f32)
    sigmoid_gate = jax.nn.sigmoid(gate_val)
    silu_gate = gate_val * sigmoid_gate
    inner = silu_gate * up_val
    weight_wide = jnp.repeat(combine_own, hidden_units, axis=1)
    inner_low = (inner * weight_wide).astype(bf16)
    cot_down = jnp.dot(cot_all, down_flat.T, preferred_element_type=f32)
    gate_sums = jnp.sum((inner * cot_down).reshape(total_rows, local_experts, hidden_units), -1)
    grad_inner = cot_down * weight_wide
    grad_gate_val = (
        grad_inner * up_val * sigmoid_gate * (1.0 + gate_val * (1.0 - sigmoid_gate))
    ).astype(bf16)
    grad_up_val = (grad_inner * silu_gate).astype(bf16)

    def collect(partial_value):
        parts = lax.all_to_all(
            partial_value.astype(bf16).reshape(expert_ranks, tok_rows, model_width),
            "expert",
            split_axis=0,
            concat_axis=0,
            tiled=True,
        )
        return lax.psum(jnp.sum(parts.astype(f32), 0), "tensor")

    mixed = collect(jnp.dot(inner_low, down_flat, preferred_element_type=f32))
    output = middle + mixed
    grad_normed2 = collect(
        jnp.dot(grad_gate_val, gate_flat.T, preferred_element_type=f32)
        + jnp.dot(grad_up_val, up_flat.T, preferred_element_type=f32)
    )
    grad_gates = lax.psum(
        lax.all_to_all(
            gate_sums.reshape(expert_ranks, tok_rows, local_experts),
            "expert",
            split_axis=0,
            concat_axis=2,
            tiled=True,
        ).reshape(tok_rows, experts),
        "tensor",
    )
    gate_grad = (
        jnp.dot(rows_all.T, grad_gate_val, preferred_element_type=f32)
        .reshape(model_width, local_experts, hidden_units)
        .transpose(1, 0, 2)
    )
    up_grad = (
        jnp.dot(rows_all.T, grad_up_val, preferred_element_type=f32)
        .reshape(model_width, local_experts, hidden_units)
        .transpose(1, 0, 2)
    )
    down_term = jnp.dot(inner_low.T, cot_all, preferred_element_type=f32).reshape(
        local_experts, hidden_units, model_width
    )
    grad_logits = combine * (grad_gates - jnp.sum(grad_gates * combine, -1, keepdims=True))
    loss_weight = (experts * share / total_rows)[None, :]
    grad_logits = grad_logits + router_probs * (
        loss_weight - jnp.sum(loss_weight * router_probs, -1, keepdims=True)
    )
    grad_logit_low = grad_logits.astype(bf16)
    router_grad = jnp.dot(normed2.T, grad_logit_low, preferred_element_type=f32)
    grad_normed2 = grad_normed2 + jnp.dot(
        grad_logit_low, router_weight.T, preferred_element_type=f32
    )
    gained2 = grad_normed2 * expert_gain
    expert_gain_grad = jnp.sum(grad_normed2 * middle * norm_scale2, 0)
    grad_middle = (
        cotangent
        + norm_scale2 * gained2
        - middle * norm_scale2**3 * jnp.mean(gained2 * middle, -1, keepdims=True)
    )
    grad_attn = grad_middle.astype(bf16)
    out_weight_grad = jnp.dot(attended.T, grad_attn, preferred_element_type=f32)
    grad_attended = jnp.dot(grad_attn, out_weight.T, preferred_element_type=f32).astype(bf16)
    grad_og = grad_attended.reshape(seq_count, span_rows, key_heads, groups, HD)
    delta = jnp.einsum("sqhgd,shgqd->shgq", grad_og.astype(f32), attended_raw)

    def score_grads(index, carry):
        query_acc, pair_buffer = carry
        scores, allowed, key_part, value_part = block_scores(pairs_seq, index)
        soft = jnp.where(allowed, jnp.exp(scores - log_total[..., None]), 0.0)
        grad_probs = jnp.einsum(
            "sqhgd,skhd->shgqk", grad_og, value_part, preferred_element_type=f32
        )
        grad_scores = (soft * (grad_probs - delta[..., None])).astype(bf16)
        query_acc = query_acc + jnp.einsum(
            "shgqk,skhd->sqhgd", grad_scores, key_part, preferred_element_type=f32
        )
        key_term = (
            jnp.einsum("shgqk,sqhgd->skhd", grad_scores, query_groups, preferred_element_type=f32)
            * score_scale
        )
        value_term = jnp.einsum(
            "shgqk,sqhgd->skhd", soft.astype(bf16), grad_og, preferred_element_type=f32
        )
        block_terms = jnp.concatenate(
            [
                key_term.reshape(seq_count, -1, key_width),
                value_term.reshape(seq_count, -1, key_width),
            ],
            -1,
        )
        pair_buffer = lax.dynamic_update_slice_in_dim(
            pair_buffer, block_terms, index * key_block, 1
        )
        return (query_acc, pair_buffer)

    grad_query_rot, seq_terms = lax.fori_loop(
        0,
        used_blocks,
        score_grads,
        (
            jnp.zeros((seq_count, span_rows, key_heads, groups, HD), f32),
            jnp.zeros((seq_count, seq_length, 2 * key_width), f32),
        ),
    )
    all_terms = seq_terms.reshape(seq_count, expert_ranks, span_rows, 2 * key_width).transpose(
        1, 0, 2, 3
    )
    all_terms = all_terms.reshape(total_rows, 2 * key_width)
    pair_grad = lax.psum_scatter(all_terms, "expert", scatter_dimension=0, tiled=True)
    grad_query_rot = grad_query_rot.reshape(tok_rows, query_heads, HD) * score_scale
    grad_query_lin = (
        rotate(grad_query_rot, cosines, sine_table, False)
        .reshape(tok_rows, query_width)
        .astype(bf16)
    )
    grad_key_lin = (
        rotate(
            pair_grad[:, :key_width].reshape(tok_rows, key_heads, HD), cosines, sine_table, False
        )
        .reshape(tok_rows, key_width)
        .astype(bf16)
    )
    grad_value_lin = pair_grad[:, key_width:].astype(bf16)
    query_grad = jnp.dot(normed.T, grad_query_lin, preferred_element_type=f32)
    key_grad = jnp.dot(normed.T, grad_key_lin, preferred_element_type=f32)
    value_grad = jnp.dot(normed.T, grad_value_lin, preferred_element_type=f32)
    grad_normed = head_total(
        jnp.dot(grad_query_lin, query_weight.T, preferred_element_type=f32)
        + jnp.dot(grad_key_lin, key_weight.T, preferred_element_type=f32)
        + jnp.dot(grad_value_lin, value_weight.T, preferred_element_type=f32)
    )
    gained1 = grad_normed * attention_gain
    attention_gain_grad = jnp.sum(grad_normed * residual * norm_scale, 0)
    input_grad = (
        grad_middle
        + norm_scale * gained1
        - residual * norm_scale**3 * jnp.mean(gained1 * residual, -1, keepdims=True)
    )
    (
        attention_gain_grad,
        query_grad,
        key_grad,
        value_grad,
        out_weight_grad,
        expert_gain_grad,
        router_grad,
    ) = lax.psum(
        (
            attention_gain_grad,
            query_grad,
            key_grad,
            value_grad,
            out_weight_grad,
            expert_gain_grad,
            router_grad,
        ),
        "expert",
    )
    return (
        output,
        input_grad,
        balance_loss,
        expert_load,
        attention_gain_grad,
        query_grad,
        key_grad,
        value_grad,
        out_weight_grad,
        expert_gain_grad,
        router_grad,
        gate_grad,
        up_grad,
        down_term,
    )


def solution(mesh):
    placed = (
        P("expert", None),
        P(),
        P(None, "tensor"),
        P(None, "tensor"),
        P(None, "tensor"),
        P("tensor", None),
        P(),
        P(),
        P("expert", None, "tensor"),
        P("expert", None, "tensor"),
        P("expert", "tensor", None),
        P("expert", None),
        P(),
        P("expert", None),
    )
    return jax.shard_map(
        shards,
        mesh=mesh,
        in_specs=placed,
        out_specs=(
            P("expert", None),
            P("expert", None),
            P(),
            P(),
            P(),
            P(None, "tensor"),
            P(None, "tensor"),
            P(None, "tensor"),
            P("tensor", None),
            P(),
            P(),
            P("expert", None, "tensor"),
            P("expert", None, "tensor"),
            P("expert", "tensor", None),
        ),
        check_vma=False,
    )
```

```python
import functools
import math

import jax
import jax.numpy as jnp
from jax import lax
from jax.experimental import pallas as pl
from jax.experimental.pallas import tpu as pltpu
from jax.sharding import PartitionSpec as P

HD = 64
EPS = 1e-06
THETA = 10000.0
MESH = pl.DeviceIdType.MESH
f32 = jnp.float32
bf16 = jnp.bfloat16


def dot_nn(left, right):
    return lax.dot_general(left, right, (((1,), (0,)), ((), ())), preferred_element_type=f32)


def dot_nt(left, right):
    return lax.dot_general(left, right, (((1,), (1,)), ((), ())), preferred_element_type=f32)


def dot_tn(left, right):
    return lax.dot_general(left, right, (((0,), (0,)), ((), ())), preferred_element_type=f32)


def remote(src, dst, send_sem, recv_sem, device):
    return pltpu.make_async_remote_copy(
        src_ref=src,
        dst_ref=dst,
        send_sem=send_sem,
        recv_sem=recv_sem,
        device_id=device,
        device_id_type=MESH,
    )


def expert_kernel(
    n,
    nz,
    big,
    mid_ref,
    gain_ref,
    router_ref,
    routes_ref,
    gate_ref,
    up_ref,
    down_ref,
    cot_ref,
    cot_all,
    *rest,
):
    outs, rest = rest[:8], rest[8:]
    out_ref, gmid_ref, rgrad_ref, ggrad_ref, load_ref, dgate, dup, ddown = outs
    if big:
        xbuf, rest = rest[0], rest[1:]
        xstage, rest = rest[0], rest[1:]
    else:
        xbuf, rest = rest[0], rest[1:]
        xstage = None
    (
        wbuf,
        xn_s,
        wg,
        wu,
        cbuf,
        dg_s,
        du_s,
        wi_s,
        hold,
        osend,
        sin,
        fbuf,
        fin,
        acc,
        zsend,
        zin,
        zs,
        zr,
        zws,
        zwr,
        xs,
        xr,
        ws,
        wr,
        fs,
        fr,
        wfs,
        wfr,
        csem,
        os_,
        or_,
        fsem,
        frem,
        zgs,
        zgr,
        lsem,
    ) = rest
    e = lax.axis_index("expert")
    z = lax.axis_index("tensor")
    sib = e + 1 - 2 * lax.rem(e, 2)
    half = n // 2
    rows, width = mid_ref.shape
    tok = rows * nz
    experts = router_ref.shape[1]
    local_experts, _, hid = gate_ref.shape
    inner_w = local_experts * hid
    fc = min(inner_w, 256)
    slots = fbuf.shape[0]

    barrier = pltpu.get_barrier_semaphore()
    pl.semaphore_signal(barrier, inc=1, device_id=(sib, z), device_id_type=MESH)
    for s in range(1, half):
        pl.semaphore_signal(
            barrier, inc=1, device_id=(lax.rem(e + 2 * s, n), z), device_id_type=MESH
        )
    for k in range(1, nz):
        pl.semaphore_signal(barrier, inc=1, device_id=(e, lax.rem(z + k, nz)), device_id_type=MESH)

    own_rows = pl.ds(pl.multiple_of(z * rows, 16), rows)
    mid = mid_ref[...]
    scale2 = lax.rsqrt(jnp.mean(mid * mid, -1, keepdims=True) + EPS)
    xn = (mid * scale2 * gain_ref[...]).astype(bf16)
    xn_s[...] = xn
    logits = dot_nn(xn, router_ref[...])
    picks = routes_ref[own_rows, :]
    lanes = lax.broadcasted_iota(jnp.int32, (rows, experts), 1)
    chosen = jnp.zeros((rows, experts), f32)
    for k in range(picks.shape[1]):
        chosen = jnp.where(picks[:, k : k + 1] == lanes, 1.0, chosen)
    top = jnp.max(logits, -1, keepdims=True)
    powers = jnp.exp(logits - top)
    probs = powers / jnp.sum(powers, -1, keepdims=True)
    low_logits = jnp.where(chosen > 0.0, logits, -1e30)
    ctop = jnp.max(low_logits, -1, keepdims=True)
    cpow = jnp.exp(low_logits - ctop)
    comb = cpow / jnp.sum(cpow, -1, keepdims=True)
    padded = jnp.concatenate([comb, jnp.zeros((rows, 128 - experts), f32)], 1)
    if rows < 128:
        padded = jnp.concatenate([padded, jnp.zeros((128 - rows, 128), f32)], 0)
    piece = padded.T[:experts]
    lane_pad = jnp.zeros((1, 128 - experts), f32)
    cnt = jnp.concatenate([jnp.sum(chosen, 0, keepdims=True), lane_pad], 1)
    psum = jnp.concatenate([jnp.sum(probs, 0, keepdims=True), lane_pad], 1)
    psum_hi = psum.astype(bf16).astype(f32)
    stats = jnp.concatenate([cnt, psum_hi, psum - psum_hi, jnp.zeros((13, 128), f32)], 0)
    wbuf[e, z] = jnp.concatenate([piece, stats], 0).astype(bf16)
    if big:
        copy = pltpu.make_async_copy(xn_s, xbuf.at[e, own_rows], lsem)
        copy.start()
        copy.wait()
    else:
        xbuf[e, own_rows] = xn
    pl.semaphore_wait(barrier, half + nz - 1)

    for k in range(1, nz):
        to = (e, lax.rem(z + k, nz))
        piece_ref = xbuf.at[e, own_rows]
        remote(piece_ref, piece_ref, zs.at[k - 1], zr.at[k - 1], to).start()
        remote(wbuf.at[e, z], wbuf.at[e, z], zws.at[k - 1], zwr.at[k - 1], to).start()

    def push_piece(zz):
        piece_ref = xbuf.at[e, pl.ds(pl.multiple_of(zz * rows, 16), rows)]
        small = wbuf.at[e, zz]
        for s in range(1, half):
            to = (lax.rem(e + 2 * s, n), z)
            remote(piece_ref, piece_ref, xs.at[s], xr.at[s], to).start()
            remote(small, small, ws.at[s], wr.at[s], to).start()
        remote(piece_ref, piece_ref, fs.at[0], fr.at[0], (sib, z)).start()
        remote(small, small, wfs.at[0], wfr.at[0], (sib, z)).start()

    push_piece(z)

    def cot_copy(index, slot):
        start = pl.ds(pl.multiple_of(index * tok, 16), tok)
        return pltpu.make_async_copy(cot_all.at[start], cbuf.at[slot], csem.at[slot])

    cot_copy(e, 0).start()
    for el in range(local_experts):
        cols = slice(el * hid, (el + 1) * hid)
        wg[:, cols] = gate_ref[el]
        wu[:, cols] = up_ref[el]
    dgate[...] = jnp.zeros_like(dgate)
    dup[...] = jnp.zeros_like(dup)
    ddown[...] = jnp.zeros_like(ddown)

    for k in range(1, nz):
        zz = lax.rem(z + nz - k, nz)
        piece_ref = xbuf.at[e, pl.ds(pl.multiple_of(zz * rows, 16), rows)]
        peer = (e, zz)
        remote(piece_ref, piece_ref, zs.at[k - 1], zr.at[k - 1], peer).wait_recv()
        remote(wbuf.at[e, zz], wbuf.at[e, zz], zws.at[k - 1], zwr.at[k - 1], peer).wait_recv()
        push_piece(zz)

    sel_row = lax.broadcasted_iota(jnp.int32, (experts, fc), 0)
    sel_col = lax.broadcasted_iota(jnp.int32, (experts, fc), 1)

    def block(index, slot, dst, dslot):
        if big:
            copy = pltpu.make_async_copy(xbuf.at[index], xstage, lsem)
            copy.start()
            copy.wait()
            x_ref = xstage
        else:
            x_ref = xbuf.at[index]
        c_ref = cbuf.at[slot]
        sums = [jnp.zeros((experts, rows), f32) for _ in range(nz)]
        for q in range(inner_w // fc):
            cols = slice(q * fc, (q + 1) * fc)
            x = x_ref[...]
            gate_val = dot_nn(x, wg[:, cols])
            up_val = dot_nn(x, wu[:, cols])
            back = dot_nt(c_ref[...], down_ref[cols, :])
            select = jnp.where(
                sel_row == e * local_experts + (q * fc + sel_col) // hid, 1.0, 0.0
            ).astype(bf16)
            wide = jnp.concatenate(
                [dot_tn(wbuf[index, zz, :experts, :], select)[:rows] for zz in range(nz)], 0
            )
            sig = 1.0 / (1.0 + jnp.exp(-gate_val))
            silu = gate_val * sig
            inner = silu * up_val
            wi_s[:, cols] = (inner * wide).astype(bf16)
            scaled = back * wide
            dg_s[:, cols] = (scaled * up_val * (sig * (1.0 + gate_val * (1.0 - sig)))).astype(bf16)
            du_s[:, cols] = (scaled * silu).astype(bf16)
            both = (inner * back).astype(bf16)
            for zz in range(nz):
                sums[zz] = sums[zz] + dot_nt(select, both[zz * rows : (zz + 1) * rows])
        for zz in range(nz):
            gap = jnp.zeros((experts, 128 - rows), f32)
            dst[dslot, tok : tok + experts, zz * 128 : (zz + 1) * 128] = jnp.concatenate(
                [sums[zz], gap], 1
            ).astype(bf16)
        for h in range(width // 256):
            cols = slice(h * 256, (h + 1) * 256)
            dst[dslot, 0:tok, cols] = (
                dot_nt(dg_s[...], wg[cols, :]) + dot_nt(du_s[...], wu[cols, :])
            ).astype(bf16)
            dst[dslot, tok + experts :, cols] = dot_nn(wi_s[...], down_ref[:, cols]).astype(bf16)
        for h in range(width // 256):
            cols = slice(h * 256, (h + 1) * 256)
            x_part = x_ref[:, cols]
            gate_part = dot_tn(x_part, dg_s[...])
            up_part = dot_tn(x_part, du_s[...])
            for el in range(local_experts):
                dgate[el, cols, :] += gate_part[:, el * hid : (el + 1) * hid]
                dup[el, cols, :] += up_part[:, el * hid : (el + 1) * hid]
            ddown[:, cols] += dot_tn(wi_s[...], c_ref[:, cols])

    def finish(s):
        slot = lax.rem(s, 2)
        remote(osend.at[slot], sin.at[slot], os_.at[slot], or_.at[slot], (sib, z)).wait_recv()

        @pl.when(s == 0)
        def _():
            acc[...] = hold[slot].astype(f32) + sin[slot].astype(f32)

        @pl.when(s > 0)
        def _():
            fslot = lax.rem(s - 1, slots)
            to = (lax.rem(e - 2 * s + n, n), z)
            out = remote(fbuf.at[fslot], fin.at[s - 1], fsem.at[fslot], frem.at[s - 1], to)
            if half - 1 > slots:

                @pl.when(s - 1 >= slots)
                def _():
                    out.wait_send()

            fbuf[fslot] = (hold[slot].astype(f32) + sin[slot].astype(f32)).astype(bf16)
            out.start()

    def step(s, carry):
        own = lax.rem(e - 2 * s + n, n)
        oth = lax.rem(sib - 2 * s + n, n)
        slot = lax.rem(s, 2)

        @pl.when(s > 0)
        def _():
            remote(xbuf.at[own], xbuf.at[own], xs.at[s], xr.at[s], (own, z)).wait_recv()
            remote(wbuf.at[own], wbuf.at[own], ws.at[s], wr.at[s], (own, z)).wait_recv()
            remote(xbuf.at[own], xbuf.at[own], fs.at[s], fr.at[s], (sib, z)).start()
            remote(wbuf.at[own], wbuf.at[own], wfs.at[s], wfr.at[s], (sib, z)).start()

        cot_copy(oth, 1).start()
        cot_copy(own, 0).wait()
        block(own, 0, hold, slot)

        @pl.when(s < half - 1)
        def _():
            cot_copy(lax.rem(e - 2 * s - 2 + n, n), 0).start()

        @pl.when(s > 0)
        def _():
            finish(s - 1)

        remote(xbuf.at[oth], xbuf.at[oth], fs.at[s], fr.at[s], (sib, z)).wait_recv()
        remote(wbuf.at[oth], wbuf.at[oth], wfs.at[s], wfr.at[s], (sib, z)).wait_recv()
        cot_copy(oth, 1).wait()
        give = remote(osend.at[slot], sin.at[slot], os_.at[slot], or_.at[slot], (sib, z))

        @pl.when(s >= 2)
        def _():
            give.wait_send()

        block(oth, 1, osend, slot)
        give.start()
        return carry

    lax.fori_loop(0, half, step, 0)
    finish(jnp.int32(half - 1))

    def total_stats(j, carry):
        for zz in range(nz):
            carry = carry + wbuf[j, zz, experts:, :].astype(f32)
        return carry

    stats = lax.fori_loop(0, n, total_stats, jnp.zeros((16, 128), f32))
    for s in range(1, half):
        src = lax.rem(e + 2 * s, n)
        fslot = (s - 1) % slots
        remote(fbuf.at[fslot], fin.at[s - 1], fsem.at[fslot], frem.at[s - 1], (src, z)).wait_recv()
        acc[...] += fin[s - 1].astype(f32)

    def take(zz):
        part = pl.ds(pl.multiple_of(zz * rows, 16), rows)
        lane = pl.ds(pl.multiple_of(zz * 128, 128), 128)
        low = pl.ds(pl.multiple_of(tok + experts + zz * rows, 16), rows)
        return acc[part, :], acc[tok : tok + experts, lane], acc[low, :]

    for k in range(1, nz):
        zz = lax.rem(z + k, nz)
        first, second, third = take(zz)
        zsend[k - 1, 0:rows, :] = first.astype(bf16)
        zsend[k - 1, rows : rows + experts, 0:128] = second.astype(bf16)
        zsend[k - 1, rows + experts :, :] = third.astype(bf16)
        remote(zsend.at[k - 1], zin.at[k - 1], zgs.at[k - 1], zgr.at[k - 1], (e, zz)).start()

    grad_rows, gate_sums, mixed = take(z)
    for k in range(1, nz):
        remote(zsend.at[k - 1], zin.at[k - 1], zgs.at[k - 1], zgr.at[k - 1], (e, z)).wait_recv()
        grad_rows = grad_rows + zin[k - 1, 0:rows, :].astype(f32)
        gate_sums = gate_sums + zin[k - 1, rows : rows + experts, 0:128].astype(f32)
        mixed = mixed + zin[k - 1, rows + experts :, :].astype(f32)

    out_ref[...] = mid_ref[...] + mixed
    total_rows = n * tok
    share = stats[0:1, :experts] / (total_rows * routes_ref.shape[1])
    load_ref[...] = experts * experts * share * ((stats[1:2, :experts] + stats[2:3, :experts]) / total_rows)
    loss_w = experts * share / total_rows
    grow = jnp.concatenate([gate_sums, jnp.zeros((128 - experts, 128), f32)], 0).T
    grad_gates = grow[:rows, :experts]
    grad_logits = comb * (grad_gates - jnp.sum(grad_gates * comb, -1, keepdims=True))
    grad_logits = grad_logits + probs * (loss_w - jnp.sum(loss_w * probs, -1, keepdims=True))
    low_grad = grad_logits.astype(bf16)
    rgrad_ref[...] = dot_tn(low_grad, xn_s[...])
    grad_rows = grad_rows + dot_nt(low_grad, router_ref[...])
    mid = mid_ref[...]
    ggrad_ref[...] = jnp.sum(grad_rows * mid * scale2, 0, keepdims=True)
    gained = grad_rows * gain_ref[...]
    gmid_ref[...] = (
        cot_ref[own_rows, :]
        + scale2 * gained
        - mid * (scale2 * scale2 * scale2) * jnp.mean(gained * mid, -1, keepdims=True)
    )

    for k in range(1, nz):
        piece_ref = xbuf.at[e, own_rows]
        peer = (e, lax.rem(z + k, nz))
        remote(piece_ref, piece_ref, zs.at[k - 1], zr.at[k - 1], peer).wait_send()
        remote(wbuf.at[e, z], wbuf.at[e, z], zws.at[k - 1], zwr.at[k - 1], peer).wait_send()
        remote(zsend.at[k - 1], zin.at[k - 1], zgs.at[k - 1], zgr.at[k - 1], peer).wait_send()
    for s in range(half):
        peer = (lax.rem(e + 2 * s, n), z) if s else (sib, z)
        if s:
            remote(xbuf.at[e], xbuf.at[e], xs.at[s], xr.at[s], peer).wait_send()
            remote(wbuf.at[e], wbuf.at[e], ws.at[s], wr.at[s], peer).wait_send()
        remote(xbuf.at[e], xbuf.at[e], fs.at[s], fr.at[s], (sib, z)).wait_send()
        remote(wbuf.at[e], wbuf.at[e], wfs.at[s], wfr.at[s], (sib, z)).wait_send()
    for s in range(max(0, half - 2), half):
        slot = s % 2
        remote(osend.at[slot], sin.at[slot], os_.at[slot], or_.at[slot], (sib, z)).wait_send()
    for s in range(max(1, half - slots), half):
        fslot = (s - 1) % slots
        remote(fbuf.at[fslot], fin.at[s - 1], fsem.at[fslot], frem.at[s - 1], (sib, z)).wait_send()


def expert_layer(n, nz, mid, gain, router, routes, gate, up, down, cot, cot_all):
    rows, width = mid.shape
    tok = rows * nz
    experts = router.shape[1]
    local_experts, _, hid = gate.shape
    inner_w = local_experts * hid
    half = n // 2
    big = n > 8
    slots = min(half - 1, 3)
    pay = 2 * tok + experts
    dma = pltpu.SemaphoreType.DMA
    vmem = pl.BlockSpec(memory_space=pltpu.VMEM)
    hbm = pl.BlockSpec(memory_space=pl.ANY)
    sds = jax.ShapeDtypeStruct
    out_shape = [
        sds((rows, width), f32),
        sds((rows, width), f32),
        sds((experts, width), f32),
        sds((1, width), f32),
        sds((1, experts), f32),
        sds((local_experts, width, hid), f32),
        sds((local_experts, width, hid), f32),
        sds((inner_w, width), f32),
    ]
    out_specs = [vmem] * 8
    scratch = []
    if big:
        out_shape.append(sds((n, tok, width), bf16))
        out_specs.append(hbm)
        scratch.append(pltpu.VMEM((tok, width), bf16))
    else:
        scratch.append(pltpu.VMEM((n, tok, width), bf16))
    scratch += [
        pltpu.VMEM((n, nz, experts + 16, 128), bf16),
        pltpu.VMEM((rows, width), bf16),
        pltpu.VMEM((width, inner_w), bf16),
        pltpu.VMEM((width, inner_w), bf16),
        pltpu.VMEM((2, tok, width), bf16),
        pltpu.VMEM((tok, inner_w), bf16),
        pltpu.VMEM((tok, inner_w), bf16),
        pltpu.VMEM((tok, inner_w), bf16),
        pltpu.VMEM((2, pay, width), bf16),
        pltpu.VMEM((2, pay, width), bf16),
        pltpu.VMEM((2, pay, width), bf16),
        pltpu.VMEM((slots, pay, width), bf16),
        pltpu.VMEM((half - 1, pay, width), bf16),
        pltpu.VMEM((pay, width), f32),
        pltpu.VMEM((nz - 1, 2 * rows + experts, width), bf16),
        pltpu.VMEM((nz - 1, 2 * rows + experts, width), bf16),
    ]
    scratch += [dma((nz - 1,))] * 4
    scratch += [dma((half,))] * 8
    scratch += [dma((2,))] * 3
    scratch += [dma((slots,)), dma((half - 1,)), dma((nz - 1,)), dma((nz - 1,)), dma]
    return pl.pallas_call(
        functools.partial(expert_kernel, n, nz, big),
        out_shape=out_shape,
        in_specs=[vmem] * 8 + [hbm],
        out_specs=out_specs,
        scratch_shapes=scratch,
        compiler_params=pltpu.CompilerParams(
            collective_id=1, has_side_effects=True, vmem_limit_bytes=62 << 20
        ),
        name="experts",
    )(mid, gain[None], router, routes, gate, up, down.reshape(inner_w, width), cot, cot_all)[:8]


def rope_tables(positions, head_size):
    half_size = head_size // 2
    frequency = THETA ** (-2.0 * jnp.arange(half_size, dtype=jnp.float32) / head_size)
    angles = positions.astype(jnp.float32)[:, None] * frequency[None, :]
    cosines = jnp.cos(angles)
    sine_table = jnp.sin(angles)
    return (jnp.concatenate([cosines, cosines], -1), jnp.concatenate([sine_table, sine_table], -1))


def rotate(values, cosines, sine_table, forward):
    half_size = values.shape[-1] // 2
    if forward:
        turned = jnp.concatenate([-values[..., half_size:], values[..., :half_size]], -1)
        return values * cosines[:, None, :] + turned * sine_table[:, None, :]
    scaled = values * sine_table[:, None, :]
    turned = jnp.concatenate([scaled[..., half_size:], -scaled[..., :half_size]], -1)
    return values * cosines[:, None, :] + turned


def shards(
    inputs,
    attention_gain,
    query_weight,
    key_weight,
    value_weight,
    out_weight,
    expert_gain,
    router_weight,
    gate_weight,
    up_weight,
    down_weight,
    routes,
    seq_lens,
    cotangent,
):
    tok_rows, model_width = inputs.shape
    expert_ranks = lax.axis_size("expert")
    expert_rank = lax.axis_index("expert")
    total_rows = tok_rows * expert_ranks
    seq_count = seq_lens.shape[0]
    seq_length = total_rows // seq_count
    span_rows = tok_rows // seq_count
    query_width = query_weight.shape[1]
    key_width = key_weight.shape[1]
    query_heads = query_width // HD
    key_heads = key_width // HD
    groups = query_heads // key_heads
    score_scale = HD ** (-0.5)
    local_pos = expert_rank * span_rows + jnp.arange(span_rows, dtype=jnp.int32)
    row_pos = jnp.tile(local_pos, seq_count)
    key_block = math.gcd(seq_length, 2048)
    last_pos = expert_rank * span_rows + span_rows - 1
    used_blocks = last_pos // key_block + 1
    residual = inputs.astype(f32)
    norm_scale = lax.rsqrt(jnp.mean(residual * residual, -1, keepdims=True) + EPS)
    normed = (residual * norm_scale * attention_gain).astype(bf16)
    cosines, sine_table = rope_tables(row_pos, HD)
    query_lin = jnp.dot(normed, query_weight, preferred_element_type=f32)
    key_lin = jnp.dot(normed, key_weight, preferred_element_type=f32)
    value_lin = jnp.dot(normed, value_weight, preferred_element_type=f32)
    queries = rotate(
        query_lin.reshape(tok_rows, query_heads, HD), cosines, sine_table, True
    ).astype(bf16)
    keys_rot = rotate(key_lin.reshape(tok_rows, key_heads, HD), cosines, sine_table, True).astype(
        bf16
    )
    pair_local = jnp.concatenate(
        [keys_rot.reshape(tok_rows, key_width), value_lin.astype(bf16)], -1
    )
    flat = lax.all_gather(pair_local, "expert", axis=0, tiled=True)
    width_now = flat.shape[-1]
    shaped = flat.reshape(expert_ranks, seq_count, span_rows, width_now).transpose(1, 0, 2, 3)
    pairs_seq = shaped.reshape(seq_count, seq_length, width_now)
    query_groups = queries.reshape(seq_count, span_rows, key_heads, groups, HD)

    def block_scores(pairs_here, index):
        start = index * key_block
        pair_block = lax.dynamic_slice_in_dim(pairs_here, start, key_block, 1)
        pos_block = start + jnp.arange(key_block, dtype=jnp.int32)
        key_part = pair_block[..., :key_width].reshape(seq_count, key_block, key_heads, HD)
        value_part = pair_block[..., key_width:].reshape(seq_count, key_block, key_heads, HD)
        scores = (
            jnp.einsum("sqhgd,skhd->shgqk", query_groups, key_part, preferred_element_type=f32)
            * score_scale
        )
        allowed = (pos_block[None, None, :] <= local_pos[None, :, None]) & (
            pos_block[None, None, :] < seq_lens[:, None, None]
        )
        return (scores, allowed[:, None, None], key_part, value_part)

    def score_maxima(index, carry):
        running_max, running_sum = carry
        scores, allowed, _, _ = block_scores(pairs_seq, index)
        scores = jnp.where(allowed, scores, -1e30)
        new_max = jnp.maximum(running_max, jnp.max(scores, -1))
        weights_now = jnp.where(allowed, jnp.exp(scores - new_max[..., None]), 0.0)
        running_sum = running_sum * jnp.exp(running_max - new_max) + jnp.sum(weights_now, -1)
        return (new_max, running_sum)

    start_max = jnp.full((seq_count, key_heads, groups, span_rows), -1e30, f32)
    row_max, row_sum = lax.fori_loop(
        0, used_blocks, score_maxima, (start_max, jnp.zeros_like(start_max))
    )
    log_total = row_max + jnp.log(row_sum)

    def value_sums(index, totals):
        scores, allowed, _, value_part = block_scores(pairs_seq, index)
        probs_low = jnp.where(allowed, jnp.exp(scores - log_total[..., None]), 0.0).astype(bf16)
        return totals + jnp.einsum(
            "shgqk,skhd->shgqd", probs_low, value_part, preferred_element_type=f32
        )

    attended_raw = lax.fori_loop(
        0, used_blocks, value_sums, jnp.zeros((seq_count, key_heads, groups, span_rows, HD), f32)
    )
    attended = attended_raw.transpose(0, 3, 1, 2, 4).reshape(tok_rows, query_width).astype(bf16)
    tensor_ranks = lax.axis_size("tensor")
    tensor_rank = lax.axis_index("tensor")
    own_count = tok_rows // tensor_ranks

    def own_part(values):
        return lax.dynamic_slice_in_dim(values, tensor_rank * own_count, own_count, 0)

    cot_all = lax.all_gather(cotangent.astype(bf16), "expert", axis=0, tiled=True)
    middle = own_part(residual) + lax.psum_scatter(
        jnp.dot(attended, out_weight, preferred_element_type=f32),
        "tensor",
        scatter_dimension=0,
        tiled=True,
    )
    (
        out_part,
        grad_middle,
        router_part,
        expert_gain_part,
        expert_load,
        gate_grad,
        up_grad,
        down_term,
    ) = expert_layer(
        expert_ranks,
        tensor_ranks,
        middle,
        expert_gain,
        router_weight,
        routes,
        gate_weight,
        up_weight,
        down_weight,
        cotangent,
        cot_all,
    )
    expert_load = expert_load[0]
    balance_loss = jnp.mean(expert_load)
    down_term = down_term.reshape(down_weight.shape)
    output = lax.all_gather(out_part.astype(bf16), "tensor", axis=0, tiled=True).astype(f32)
    grad_attn = lax.all_gather(grad_middle.astype(bf16), "tensor", axis=0, tiled=True)
    out_weight_grad = jnp.dot(attended.T, grad_attn, preferred_element_type=f32)
    grad_attended = jnp.dot(grad_attn, out_weight.T, preferred_element_type=f32).astype(bf16)
    grad_og = grad_attended.reshape(seq_count, span_rows, key_heads, groups, HD)
    delta = jnp.einsum("sqhgd,shgqd->shgq", grad_og.astype(f32), attended_raw)

    def score_grads(index, carry):
        query_acc, pair_buffer = carry
        scores, allowed, key_part, value_part = block_scores(pairs_seq, index)
        soft = jnp.where(allowed, jnp.exp(scores - log_total[..., None]), 0.0)
        grad_probs = jnp.einsum(
            "sqhgd,skhd->shgqk", grad_og, value_part, preferred_element_type=f32
        )
        grad_scores = (soft * (grad_probs - delta[..., None])).astype(bf16)
        query_acc = query_acc + jnp.einsum(
            "shgqk,skhd->sqhgd", grad_scores, key_part, preferred_element_type=f32
        )
        key_term = (
            jnp.einsum("shgqk,sqhgd->skhd", grad_scores, query_groups, preferred_element_type=f32)
            * score_scale
        )
        value_term = jnp.einsum(
            "shgqk,sqhgd->skhd", soft.astype(bf16), grad_og, preferred_element_type=f32
        )
        block_terms = jnp.concatenate(
            [
                key_term.reshape(seq_count, -1, key_width),
                value_term.reshape(seq_count, -1, key_width),
            ],
            -1,
        )
        pair_buffer = lax.dynamic_update_slice_in_dim(
            pair_buffer, block_terms, index * key_block, 1
        )
        return (query_acc, pair_buffer)

    grad_query_rot, seq_terms = lax.fori_loop(
        0,
        used_blocks,
        score_grads,
        (
            jnp.zeros((seq_count, span_rows, key_heads, groups, HD), f32),
            jnp.zeros((seq_count, seq_length, 2 * key_width), f32),
        ),
    )
    all_terms = seq_terms.reshape(seq_count, expert_ranks, span_rows, 2 * key_width).transpose(
        1, 0, 2, 3
    )
    all_terms = all_terms.reshape(total_rows, 2 * key_width)
    pair_grad = lax.psum_scatter(all_terms, "expert", scatter_dimension=0, tiled=True)
    grad_query_rot = grad_query_rot.reshape(tok_rows, query_heads, HD) * score_scale
    grad_query_lin = (
        rotate(grad_query_rot, cosines, sine_table, False)
        .reshape(tok_rows, query_width)
        .astype(bf16)
    )
    grad_key_lin = (
        rotate(
            pair_grad[:, :key_width].reshape(tok_rows, key_heads, HD), cosines, sine_table, False
        )
        .reshape(tok_rows, key_width)
        .astype(bf16)
    )
    grad_value_lin = pair_grad[:, key_width:].astype(bf16)
    query_grad = jnp.dot(normed.T, grad_query_lin, preferred_element_type=f32)
    key_grad = jnp.dot(normed.T, grad_key_lin, preferred_element_type=f32)
    value_grad = jnp.dot(normed.T, grad_value_lin, preferred_element_type=f32)
    grad_normed = lax.psum_scatter(
        jnp.dot(grad_query_lin, query_weight.T, preferred_element_type=f32)
        + jnp.dot(grad_key_lin, key_weight.T, preferred_element_type=f32)
        + jnp.dot(grad_value_lin, value_weight.T, preferred_element_type=f32),
        "tensor",
        scatter_dimension=0,
        tiled=True,
    )
    own_res = own_part(residual)
    own_scale = own_part(norm_scale)
    gained1 = grad_normed * attention_gain
    attention_gain_part = jnp.sum(grad_normed * own_res * own_scale, 0)
    input_part = (
        grad_middle
        + own_scale * gained1
        - own_res * own_scale**3 * jnp.mean(gained1 * own_res, -1, keepdims=True)
    )
    input_grad = lax.all_gather(input_part.astype(bf16), "tensor", axis=0, tiled=True).astype(f32)
    query_grad, key_grad, value_grad, out_weight_grad = lax.psum(
        (query_grad, key_grad, value_grad, out_weight_grad), "expert"
    )
    attention_gain_grad, expert_gain_grad, router_grad = lax.psum(
        (attention_gain_part, expert_gain_part[0], router_part), ("expert", "tensor")
    )
    router_grad = router_grad.T
    return (
        output,
        input_grad,
        balance_loss,
        expert_load,
        attention_gain_grad,
        query_grad,
        key_grad,
        value_grad,
        out_weight_grad,
        expert_gain_grad,
        router_grad,
        gate_grad,
        up_grad,
        down_term,
    )


def solution(mesh):
    placed = (
        P("expert", None),
        P(),
        P(None, "tensor"),
        P(None, "tensor"),
        P(None, "tensor"),
        P("tensor", None),
        P(),
        P(),
        P("expert", None, "tensor"),
        P("expert", None, "tensor"),
        P("expert", "tensor", None),
        P("expert", None),
        P(),
        P("expert", None),
    )
    return jax.shard_map(
        shards,
        mesh=mesh,
        in_specs=placed,
        out_specs=(
            P("expert", None),
            P("expert", None),
            P(),
            P(),
            P(),
            P(None, "tensor"),
            P(None, "tensor"),
            P(None, "tensor"),
            P("tensor", None),
            P(),
            P(),
            P("expert", None, "tensor"),
            P("expert", None, "tensor"),
            P("expert", "tensor", None),
        ),
        check_vma=False,
    )
```

```python
import functools

import jax
import jax.numpy as jnp
from jax import lax
from jax.experimental import pallas as pl
from jax.experimental.pallas import tpu as pltpu
from jax.sharding import PartitionSpec as P

HD = 64
EPS = 1e-06
THETA = 10000.0
MESH = pl.DeviceIdType.MESH
f32 = jnp.float32
bf16 = jnp.bfloat16


def dot_nn(left, right):
    return lax.dot_general(left, right, (((1,), (0,)), ((), ())), preferred_element_type=f32)


def dot_nt(left, right):
    return lax.dot_general(left, right, (((1,), (1,)), ((), ())), preferred_element_type=f32)


def dot_tn(left, right):
    return lax.dot_general(left, right, (((0,), (0,)), ((), ())), preferred_element_type=f32)


def remote(src, dst, send_sem, recv_sem, device):
    return pltpu.make_async_remote_copy(
        src_ref=src,
        dst_ref=dst,
        send_sem=send_sem,
        recv_sem=recv_sem,
        device_id=device,
        device_id_type=MESH,
    )


def expert_kernel(
    n,
    nz,
    big,
    mid_ref,
    gain_ref,
    router_ref,
    routes_ref,
    gate_ref,
    up_ref,
    down_ref,
    cot_ref,
    cot_all,
    *rest,
):
    outs, rest = rest[:8], rest[8:]
    out_ref, gmid_ref, rgrad_ref, ggrad_ref, load_ref, dgate, dup, ddown = outs
    if big:
        xbuf, rest = rest[0], rest[1:]
        xstage, rest = rest[0], rest[1:]
    else:
        xbuf, rest = rest[0], rest[1:]
        xstage = None
    (
        wbuf,
        xn_s,
        wg,
        wu,
        cbuf,
        dg_s,
        du_s,
        wi_s,
        hold,
        osend,
        sin,
        fbuf,
        fin,
        acc,
        zsend,
        zin,
        zs,
        zr,
        zws,
        zwr,
        xs,
        xr,
        ws,
        wr,
        fs,
        fr,
        wfs,
        wfr,
        csem,
        os_,
        or_,
        fsem,
        frem,
        zgs,
        zgr,
        lsem,
    ) = rest
    e = lax.axis_index("expert")
    z = lax.axis_index("tensor")
    sib = e + 1 - 2 * lax.rem(e, 2)
    half = n // 2
    rows, width = mid_ref.shape
    tok = rows * nz
    experts = router_ref.shape[1]
    local_experts, _, hid = gate_ref.shape
    inner_w = local_experts * hid
    fc = min(inner_w, 256)
    slots = fbuf.shape[0]

    barrier = pltpu.get_barrier_semaphore()
    pl.semaphore_signal(barrier, inc=1, device_id=(sib, z), device_id_type=MESH)
    for s in range(1, half):
        pl.semaphore_signal(
            barrier, inc=1, device_id=(lax.rem(e + 2 * s, n), z), device_id_type=MESH
        )
    for k in range(1, nz):
        pl.semaphore_signal(barrier, inc=1, device_id=(e, lax.rem(z + k, nz)), device_id_type=MESH)

    own_rows = pl.ds(pl.multiple_of(z * rows, 16), rows)
    mid = mid_ref[...]
    scale2 = lax.rsqrt(jnp.mean(mid * mid, -1, keepdims=True) + EPS)
    xn = (mid * scale2 * gain_ref[...]).astype(bf16)
    xn_s[...] = xn
    logits = dot_nn(xn, router_ref[...])
    picks = routes_ref[own_rows, :]
    lanes = lax.broadcasted_iota(jnp.int32, (rows, experts), 1)
    chosen = jnp.zeros((rows, experts), f32)
    for k in range(picks.shape[1]):
        chosen = jnp.where(picks[:, k : k + 1] == lanes, 1.0, chosen)
    top = jnp.max(logits, -1, keepdims=True)
    powers = jnp.exp(logits - top)
    probs = powers / jnp.sum(powers, -1, keepdims=True)
    low_logits = jnp.where(chosen > 0.0, logits, -1e30)
    ctop = jnp.max(low_logits, -1, keepdims=True)
    cpow = jnp.exp(low_logits - ctop)
    comb = cpow / jnp.sum(cpow, -1, keepdims=True)
    padded = jnp.concatenate([comb, jnp.zeros((rows, 128 - experts), f32)], 1)
    if rows < 128:
        padded = jnp.concatenate([padded, jnp.zeros((128 - rows, 128), f32)], 0)
    piece = padded.T[:experts]
    lane_pad = jnp.zeros((1, 128 - experts), f32)
    cnt = jnp.concatenate([jnp.sum(chosen, 0, keepdims=True), lane_pad], 1)
    psum = jnp.concatenate([jnp.sum(probs, 0, keepdims=True), lane_pad], 1)
    psum_hi = psum.astype(bf16).astype(f32)
    stats = jnp.concatenate([cnt, psum_hi, psum - psum_hi, jnp.zeros((13, 128), f32)], 0)
    wbuf[e, z] = jnp.concatenate([piece, stats], 0).astype(bf16)
    if big:
        copy = pltpu.make_async_copy(xn_s, xbuf.at[e, own_rows], lsem)
        copy.start()
        copy.wait()
    else:
        xbuf[e, own_rows] = xn
    pl.semaphore_wait(barrier, half + nz - 1)

    for k in range(1, nz):
        to = (e, lax.rem(z + k, nz))
        piece_ref = xbuf.at[e, own_rows]
        remote(piece_ref, piece_ref, zs.at[k - 1], zr.at[k - 1], to).start()
        remote(wbuf.at[e, z], wbuf.at[e, z], zws.at[k - 1], zwr.at[k - 1], to).start()

    def push_piece(zz):
        piece_ref = xbuf.at[e, pl.ds(pl.multiple_of(zz * rows, 16), rows)]
        small = wbuf.at[e, zz]
        for s in range(1, half):
            to = (lax.rem(e + 2 * s, n), z)
            remote(piece_ref, piece_ref, xs.at[s], xr.at[s], to).start()
            remote(small, small, ws.at[s], wr.at[s], to).start()
        remote(piece_ref, piece_ref, fs.at[0], fr.at[0], (sib, z)).start()
        remote(small, small, wfs.at[0], wfr.at[0], (sib, z)).start()

    push_piece(z)

    def cot_copy(index, slot):
        start = pl.ds(pl.multiple_of(index * tok, 16), tok)
        return pltpu.make_async_copy(cot_all.at[start], cbuf.at[slot], csem.at[slot])

    cot_copy(e, 0).start()
    for el in range(local_experts):
        cols = slice(el * hid, (el + 1) * hid)
        wg[:, cols] = gate_ref[el]
        wu[:, cols] = up_ref[el]
    dgate[...] = jnp.zeros_like(dgate)
    dup[...] = jnp.zeros_like(dup)
    ddown[...] = jnp.zeros_like(ddown)

    for k in range(1, nz):
        zz = lax.rem(z + nz - k, nz)
        piece_ref = xbuf.at[e, pl.ds(pl.multiple_of(zz * rows, 16), rows)]
        peer = (e, zz)
        remote(piece_ref, piece_ref, zs.at[k - 1], zr.at[k - 1], peer).wait_recv()
        remote(wbuf.at[e, zz], wbuf.at[e, zz], zws.at[k - 1], zwr.at[k - 1], peer).wait_recv()
        push_piece(zz)

    sel_row = lax.broadcasted_iota(jnp.int32, (experts, fc), 0)
    sel_col = lax.broadcasted_iota(jnp.int32, (experts, fc), 1)

    def block(index, slot, dst, dslot):
        if big:
            copy = pltpu.make_async_copy(xbuf.at[index], xstage, lsem)
            copy.start()
            copy.wait()
            x_ref = xstage
        else:
            x_ref = xbuf.at[index]
        c_ref = cbuf.at[slot]
        sums = [jnp.zeros((experts, rows), f32) for _ in range(nz)]
        for q in range(inner_w // fc):
            cols = slice(q * fc, (q + 1) * fc)
            x = x_ref[...]
            gate_val = dot_nn(x, wg[:, cols])
            up_val = dot_nn(x, wu[:, cols])
            back = dot_nt(c_ref[...], down_ref[cols, :])
            select = jnp.where(
                sel_row == e * local_experts + (q * fc + sel_col) // hid, 1.0, 0.0
            ).astype(bf16)
            wide = jnp.concatenate(
                [dot_tn(wbuf[index, zz, :experts, :], select)[:rows] for zz in range(nz)], 0
            )
            sig = 1.0 / (1.0 + jnp.exp(-gate_val))
            silu = gate_val * sig
            inner = silu * up_val
            wi_s[:, cols] = (inner * wide).astype(bf16)
            scaled = back * wide
            dg_s[:, cols] = (scaled * up_val * (sig * (1.0 + gate_val * (1.0 - sig)))).astype(bf16)
            du_s[:, cols] = (scaled * silu).astype(bf16)
            both = (inner * back).astype(bf16)
            for zz in range(nz):
                sums[zz] = sums[zz] + dot_nt(select, both[zz * rows : (zz + 1) * rows])
        for zz in range(nz):
            gap = jnp.zeros((experts, 128 - rows), f32)
            dst[dslot, tok : tok + experts, zz * 128 : (zz + 1) * 128] = jnp.concatenate(
                [sums[zz], gap], 1
            ).astype(bf16)
        for h in range(width // 256):
            cols = slice(h * 256, (h + 1) * 256)
            dst[dslot, 0:tok, cols] = (
                dot_nt(dg_s[...], wg[cols, :]) + dot_nt(du_s[...], wu[cols, :])
            ).astype(bf16)
            dst[dslot, tok + experts :, cols] = dot_nn(wi_s[...], down_ref[:, cols]).astype(bf16)
        for h in range(width // 256):
            cols = slice(h * 256, (h + 1) * 256)
            x_part = x_ref[:, cols]
            gate_part = dot_tn(x_part, dg_s[...])
            up_part = dot_tn(x_part, du_s[...])
            for el in range(local_experts):
                dgate[el, cols, :] += gate_part[:, el * hid : (el + 1) * hid]
                dup[el, cols, :] += up_part[:, el * hid : (el + 1) * hid]
            ddown[:, cols] += dot_tn(wi_s[...], c_ref[:, cols])

    def finish(s):
        slot = lax.rem(s, 2)
        remote(osend.at[slot], sin.at[slot], os_.at[slot], or_.at[slot], (sib, z)).wait_recv()

        @pl.when(s == 0)
        def _():
            acc[...] = hold[slot].astype(f32) + sin[slot].astype(f32)

        @pl.when(s > 0)
        def _():
            fslot = lax.rem(s - 1, slots)
            to = (lax.rem(e - 2 * s + n, n), z)
            out = remote(fbuf.at[fslot], fin.at[s - 1], fsem.at[fslot], frem.at[s - 1], to)
            if half - 1 > slots:

                @pl.when(s - 1 >= slots)
                def _():
                    out.wait_send()

            fbuf[fslot] = (hold[slot].astype(f32) + sin[slot].astype(f32)).astype(bf16)
            out.start()

    def step(s, carry):
        own = lax.rem(e - 2 * s + n, n)
        oth = lax.rem(sib - 2 * s + n, n)
        slot = lax.rem(s, 2)

        @pl.when(s > 0)
        def _():
            remote(xbuf.at[own], xbuf.at[own], xs.at[s], xr.at[s], (own, z)).wait_recv()
            remote(wbuf.at[own], wbuf.at[own], ws.at[s], wr.at[s], (own, z)).wait_recv()
            remote(xbuf.at[own], xbuf.at[own], fs.at[s], fr.at[s], (sib, z)).start()
            remote(wbuf.at[own], wbuf.at[own], wfs.at[s], wfr.at[s], (sib, z)).start()

        cot_copy(oth, 1).start()
        cot_copy(own, 0).wait()
        block(own, 0, hold, slot)

        @pl.when(s < half - 1)
        def _():
            cot_copy(lax.rem(e - 2 * s - 2 + n, n), 0).start()

        @pl.when(s > 0)
        def _():
            finish(s - 1)

        remote(xbuf.at[oth], xbuf.at[oth], fs.at[s], fr.at[s], (sib, z)).wait_recv()
        remote(wbuf.at[oth], wbuf.at[oth], wfs.at[s], wfr.at[s], (sib, z)).wait_recv()
        cot_copy(oth, 1).wait()
        give = remote(osend.at[slot], sin.at[slot], os_.at[slot], or_.at[slot], (sib, z))

        @pl.when(s >= 2)
        def _():
            give.wait_send()

        block(oth, 1, osend, slot)
        give.start()
        return carry

    lax.fori_loop(0, half, step, 0)
    finish(jnp.int32(half - 1))

    def total_stats(j, carry):
        for zz in range(nz):
            carry = carry + wbuf[j, zz, experts:, :].astype(f32)
        return carry

    stats = lax.fori_loop(0, n, total_stats, jnp.zeros((16, 128), f32))
    for s in range(1, half):
        src = lax.rem(e + 2 * s, n)
        fslot = (s - 1) % slots
        remote(fbuf.at[fslot], fin.at[s - 1], fsem.at[fslot], frem.at[s - 1], (src, z)).wait_recv()
        acc[...] += fin[s - 1].astype(f32)

    def take(zz):
        part = pl.ds(pl.multiple_of(zz * rows, 16), rows)
        lane = pl.ds(pl.multiple_of(zz * 128, 128), 128)
        low = pl.ds(pl.multiple_of(tok + experts + zz * rows, 16), rows)
        return acc[part, :], acc[tok : tok + experts, lane], acc[low, :]

    for k in range(1, nz):
        zz = lax.rem(z + k, nz)
        first, second, third = take(zz)
        zsend[k - 1, 0:rows, :] = first.astype(bf16)
        zsend[k - 1, rows : rows + experts, 0:128] = second.astype(bf16)
        zsend[k - 1, rows + experts :, :] = third.astype(bf16)
        remote(zsend.at[k - 1], zin.at[k - 1], zgs.at[k - 1], zgr.at[k - 1], (e, zz)).start()

    grad_rows, gate_sums, mixed = take(z)
    for k in range(1, nz):
        remote(zsend.at[k - 1], zin.at[k - 1], zgs.at[k - 1], zgr.at[k - 1], (e, z)).wait_recv()
        grad_rows = grad_rows + zin[k - 1, 0:rows, :].astype(f32)
        gate_sums = gate_sums + zin[k - 1, rows : rows + experts, 0:128].astype(f32)
        mixed = mixed + zin[k - 1, rows + experts :, :].astype(f32)

    out_ref[...] = mid_ref[...] + mixed
    total_rows = n * tok
    share = stats[0:1, :experts] / (total_rows * routes_ref.shape[1])
    load_ref[...] = experts * experts * share * ((stats[1:2, :experts] + stats[2:3, :experts]) / total_rows)
    loss_w = experts * share / total_rows
    grow = jnp.concatenate([gate_sums, jnp.zeros((128 - experts, 128), f32)], 0).T
    grad_gates = grow[:rows, :experts]
    grad_logits = comb * (grad_gates - jnp.sum(grad_gates * comb, -1, keepdims=True))
    grad_logits = grad_logits + probs * (loss_w - jnp.sum(loss_w * probs, -1, keepdims=True))
    low_grad = grad_logits.astype(bf16)
    rgrad_ref[...] = dot_tn(low_grad, xn_s[...])
    grad_rows = grad_rows + dot_nt(low_grad, router_ref[...])
    mid = mid_ref[...]
    ggrad_ref[...] = jnp.sum(grad_rows * mid * scale2, 0, keepdims=True)
    gained = grad_rows * gain_ref[...]
    gmid_ref[...] = (
        cot_ref[own_rows, :]
        + scale2 * gained
        - mid * (scale2 * scale2 * scale2) * jnp.mean(gained * mid, -1, keepdims=True)
    )

    for k in range(1, nz):
        piece_ref = xbuf.at[e, own_rows]
        peer = (e, lax.rem(z + k, nz))
        remote(piece_ref, piece_ref, zs.at[k - 1], zr.at[k - 1], peer).wait_send()
        remote(wbuf.at[e, z], wbuf.at[e, z], zws.at[k - 1], zwr.at[k - 1], peer).wait_send()
        remote(zsend.at[k - 1], zin.at[k - 1], zgs.at[k - 1], zgr.at[k - 1], peer).wait_send()
    for s in range(half):
        peer = (lax.rem(e + 2 * s, n), z) if s else (sib, z)
        if s:
            remote(xbuf.at[e], xbuf.at[e], xs.at[s], xr.at[s], peer).wait_send()
            remote(wbuf.at[e], wbuf.at[e], ws.at[s], wr.at[s], peer).wait_send()
        remote(xbuf.at[e], xbuf.at[e], fs.at[s], fr.at[s], (sib, z)).wait_send()
        remote(wbuf.at[e], wbuf.at[e], wfs.at[s], wfr.at[s], (sib, z)).wait_send()
    for s in range(max(0, half - 2), half):
        slot = s % 2
        remote(osend.at[slot], sin.at[slot], os_.at[slot], or_.at[slot], (sib, z)).wait_send()
    for s in range(max(1, half - slots), half):
        fslot = (s - 1) % slots
        remote(fbuf.at[fslot], fin.at[s - 1], fsem.at[fslot], frem.at[s - 1], (sib, z)).wait_send()


def expert_layer(n, nz, mid, gain, router, routes, gate, up, down, cot, cot_all):
    rows, width = mid.shape
    tok = rows * nz
    experts = router.shape[1]
    local_experts, _, hid = gate.shape
    inner_w = local_experts * hid
    half = n // 2
    big = n > 8
    slots = min(half - 1, 3)
    pay = 2 * tok + experts
    dma = pltpu.SemaphoreType.DMA
    vmem = pl.BlockSpec(memory_space=pltpu.VMEM)
    hbm = pl.BlockSpec(memory_space=pl.ANY)
    sds = jax.ShapeDtypeStruct
    out_shape = [
        sds((rows, width), f32),
        sds((rows, width), f32),
        sds((experts, width), f32),
        sds((1, width), f32),
        sds((1, experts), f32),
        sds((local_experts, width, hid), f32),
        sds((local_experts, width, hid), f32),
        sds((inner_w, width), f32),
    ]
    out_specs = [vmem] * 8
    scratch = []
    if big:
        out_shape.append(sds((n, tok, width), bf16))
        out_specs.append(hbm)
        scratch.append(pltpu.VMEM((tok, width), bf16))
    else:
        scratch.append(pltpu.VMEM((n, tok, width), bf16))
    scratch += [
        pltpu.VMEM((n, nz, experts + 16, 128), bf16),
        pltpu.VMEM((rows, width), bf16),
        pltpu.VMEM((width, inner_w), bf16),
        pltpu.VMEM((width, inner_w), bf16),
        pltpu.VMEM((2, tok, width), bf16),
        pltpu.VMEM((tok, inner_w), bf16),
        pltpu.VMEM((tok, inner_w), bf16),
        pltpu.VMEM((tok, inner_w), bf16),
        pltpu.VMEM((2, pay, width), bf16),
        pltpu.VMEM((2, pay, width), bf16),
        pltpu.VMEM((2, pay, width), bf16),
        pltpu.VMEM((slots, pay, width), bf16),
        pltpu.VMEM((half - 1, pay, width), bf16),
        pltpu.VMEM((pay, width), f32),
        pltpu.VMEM((nz - 1, 2 * rows + experts, width), bf16),
        pltpu.VMEM((nz - 1, 2 * rows + experts, width), bf16),
    ]
    scratch += [dma((nz - 1,))] * 4
    scratch += [dma((half,))] * 8
    scratch += [dma((2,))] * 3
    scratch += [dma((slots,)), dma((half - 1,)), dma((nz - 1,)), dma((nz - 1,)), dma]
    return pl.pallas_call(
        functools.partial(expert_kernel, n, nz, big),
        out_shape=out_shape,
        in_specs=[vmem] * 8 + [hbm],
        out_specs=out_specs,
        scratch_shapes=scratch,
        compiler_params=pltpu.CompilerParams(
            collective_id=1, has_side_effects=True, vmem_limit_bytes=62 << 20
        ),
        name="experts",
    )(mid, gain[None], router, routes, gate, up, down.reshape(inner_w, width), cot, cot_all)[:8]


def turn(values, cos, sin, last, forward):
    lane = lax.broadcasted_iota(jnp.int32, (values.shape[0], 128), 1)
    first_half = lax.rem(lane, HD) < HD // 2
    parts = []
    for g in range(values.shape[1] // 128):
        v = values[:, g * 128 : (g + 1) * 128]
        if g * 128 >= last:
            parts.append(v)
            continue
        turned = jnp.where(
            first_half, -pltpu.roll(v, 128 - HD // 2, 1), pltpu.roll(v, HD // 2, 1)
        )
        new = v * cos + turned * sin if forward else v * cos - turned * sin
        if (g + 1) * 128 > last:
            new = jnp.where(lane + g * 128 < last, new, v)
        parts.append(new)
    return jnp.concatenate(parts, 1) if len(parts) > 1 else parts[0]


def greet(n, nz, e, z, sib):
    barrier = pltpu.get_barrier_semaphore()
    pl.semaphore_signal(barrier, inc=1, device_id=(sib, z), device_id_type=MESH)
    for s in range(1, n // 2):
        pl.semaphore_signal(
            barrier, inc=1, device_id=(lax.rem(e + 2 * s, n), z), device_id_type=MESH
        )
    for k in range(1, nz):
        pl.semaphore_signal(barrier, inc=1, device_id=(e, lax.rem(z + k, nz)), device_id_type=MESH)
    return barrier


def attend_kernel(
    n,
    nz,
    x_ref,
    gain_ref,
    wq_ref,
    wk_ref,
    wv_ref,
    wo_ref,
    cos_ref,
    sin_ref,
    lens_ref,
    mid_ref,
    q_ref,
    kv_ref,
    lrow_ref,
    att_ref,
    wqkv,
    part,
    m_s,
    l_s,
    o_s,
    zsend,
    zin,
    ks,
    kr,
    kfs,
    kfr,
    zgs,
    zgr,
):
    e = lax.axis_index("expert")
    z = lax.axis_index("tensor")
    sib = e + 1 - 2 * lax.rem(e, 2)
    half = n // 2
    tok, width = x_ref.shape
    rows = tok // nz
    qw = wq_ref.shape[1]
    kw = wk_ref.shape[1]
    seqs = kv_ref.shape[0]
    span = tok // seqs
    heads = kw // HD
    groups = qw // kw
    barrier = greet(n, nz, e, z, sib)

    wqkv[:, 0:qw] = wq_ref[...]
    wqkv[:, qw : qw + kw] = wk_ref[...]
    wqkv[:, qw + kw :] = wv_ref[...]
    x = x_ref[...].astype(f32)
    scale1 = lax.rsqrt(jnp.mean(x * x, -1, keepdims=True) + EPS)
    normed = (x * scale1 * gain_ref[...]).astype(bf16)
    lin = dot_nn(normed, wqkv[...])
    turned = turn(lin, cos_ref[...], sin_ref[...], qw + kw, True).astype(bf16)
    q_ref[...] = turned[:, :qw]
    for s in range(seqs):
        kv_ref[s, pl.ds(pl.multiple_of(e * span, 16), span)] = turned[
            s * span : (s + 1) * span, qw:
        ]
    pl.semaphore_wait(barrier, half + nz - 1)

    def rows_of(j, s):
        return kv_ref.at[s, pl.ds(pl.multiple_of(j * span, 16), span)]

    for t in range(1, half):
        to = (lax.rem(e + 2 * t, n), z)
        for s in range(seqs):
            remote(rows_of(e, s), rows_of(e, s), ks.at[t, s], kr.at[t, s], to).start()
    for s in range(seqs):
        remote(rows_of(e, s), rows_of(e, s), kfs.at[0, s], kfr.at[0, s], (sib, z)).start()

    def forward(t, carry):
        src = lax.rem(e - 2 * t + n, n)
        for s in range(seqs):
            remote(rows_of(src, s), rows_of(src, s), ks.at[t, s], kr.at[t, s], (src, z)).wait_recv()
            remote(rows_of(src, s), rows_of(src, s), kfs.at[t, s], kfr.at[t, s], (sib, z)).start()
        return carry

    lax.fori_loop(1, half, forward, 0)

    def arrive(t, carry):
        src = lax.rem(sib - 2 * t + n, n)
        for s in range(seqs):
            remote(
                rows_of(src, s), rows_of(src, s), kfs.at[t, s], kfr.at[t, s], (sib, z)
            ).wait_recv()
        return carry

    lax.fori_loop(0, half, arrive, 0)

    ck = 2 * span
    trip = (e * span + span - 1) // ck + 1
    stacked = groups * span
    qpos = lax.broadcasted_iota(jnp.int32, (stacked, ck), 0)
    qpos = e * span + lax.rem(qpos, span)
    kiota = lax.broadcasted_iota(jnp.int32, (stacked, ck), 1)
    for s in range(seqs):
        for h in range(heads):
            srows = slice(s * span, (s + 1) * span)
            qst = jnp.concatenate(
                [
                    q_ref[srows, (h * groups + g) * HD : (h * groups + g + 1) * HD]
                    for g in range(groups)
                ],
                0,
            )
            m_s[...] = jnp.full_like(m_s, -1e30)
            l_s[...] = jnp.zeros_like(l_s)
            o_s[...] = jnp.zeros_like(o_s)

            def chunk(c, carry):
                at = pl.ds(pl.multiple_of(c * ck, 16), ck)
                keys = kv_ref[s, at, h * HD : (h + 1) * HD]
                vals = kv_ref[s, at, kw + h * HD : kw + (h + 1) * HD]
                scores = dot_nt(qst, keys) * HD ** (-0.5)
                kpos = kiota + c * ck
                scores = jnp.where((kpos <= qpos) & (kpos < lens_ref[s]), scores, -1e30)
                old = m_s[:, 0:1]
                new = jnp.maximum(old, jnp.max(scores, -1, keepdims=True))
                weights = jnp.exp(scores - new)
                shrink = jnp.exp(old - new)
                m_s[...] = jnp.broadcast_to(new, m_s.shape)
                l_s[...] = l_s[...] * shrink + jnp.sum(weights, -1, keepdims=True)
                o_s[...] = o_s[...] * shrink + dot_nn(weights.astype(bf16), vals)
                return carry

            lax.fori_loop(0, trip, chunk, 0)
            result = o_s[...] / l_s[:, 0:HD]
            for g in range(groups):
                cols = slice((h * groups + g) * HD, (h * groups + g + 1) * HD)
                att_ref[srows, cols] = result[g * span : (g + 1) * span]
            logs = m_s[...] + jnp.log(l_s[...])
            lrow_ref[s * heads + h] = logs.T[0:8]

    part[...] = dot_nn(att_ref[...].astype(bf16), wo_ref[...])
    for k in range(1, nz):
        zz = lax.rem(z + k, nz)
        zsend[k - 1] = part[pl.ds(pl.multiple_of(zz * rows, 16), rows), :].astype(bf16)
        remote(zsend.at[k - 1], zin.at[k - 1], zgs.at[k - 1], zgr.at[k - 1], (e, zz)).start()
    own_rows = pl.ds(pl.multiple_of(z * rows, 16), rows)
    mid = x_ref[own_rows, :].astype(f32) + part[own_rows, :]
    for k in range(1, nz):
        remote(zsend.at[k - 1], zin.at[k - 1], zgs.at[k - 1], zgr.at[k - 1], (e, z)).wait_recv()
        mid = mid + zin[k - 1].astype(f32)
    mid_ref[...] = mid
    for k in range(1, nz):
        remote(zsend.at[k - 1], zin.at[k - 1], zgs.at[k - 1], zgr.at[k - 1], (e, z)).wait_send()

    def sent(t, carry):
        for s in range(seqs):

            @pl.when(t > 0)
            def _():
                remote(
                    rows_of(e, s), rows_of(e, s), ks.at[t, s], kr.at[t, s], (sib, z)
                ).wait_send()

            remote(rows_of(e, s), rows_of(e, s), kfs.at[t, s], kfr.at[t, s], (sib, z)).wait_send()
        return carry

    lax.fori_loop(0, half, sent, 0)


def attend_layer(n, nz, x, gain, wq, wk, wv, wo, cos, sin, lens):
    tok, width = x.shape
    rows = tok // nz
    qw, kw = wq.shape[1], wk.shape[1]
    seqs = lens.shape[0]
    span = tok // seqs
    half = n // 2
    stacked = (qw // kw) * span
    dma = pltpu.SemaphoreType.DMA
    vmem = pl.BlockSpec(memory_space=pltpu.VMEM)
    sds = jax.ShapeDtypeStruct
    return pl.pallas_call(
        functools.partial(attend_kernel, n, nz),
        out_shape=[
            sds((rows, width), f32),
            sds((tok, qw), bf16),
            sds((seqs, n * span, 2 * kw), bf16),
            sds((seqs * (kw // HD), 8, stacked), f32),
            sds((tok, qw), f32),
        ],
        in_specs=[vmem] * 8 + [pl.BlockSpec(memory_space=pltpu.SMEM)],
        out_specs=[vmem] * 5,
        scratch_shapes=[
            pltpu.VMEM((width, qw + 2 * kw), bf16),
            pltpu.VMEM((tok, width), f32),
            pltpu.VMEM((stacked, 128), f32),
            pltpu.VMEM((stacked, 128), f32),
            pltpu.VMEM((stacked, HD), f32),
            pltpu.VMEM((nz - 1, rows, width), bf16),
            pltpu.VMEM((nz - 1, rows, width), bf16),
        ]
        + [dma((half, seqs))] * 4
        + [dma((nz - 1,))] * 2,
        compiler_params=pltpu.CompilerParams(
            collective_id=2, has_side_effects=True, vmem_limit_bytes=48 << 20
        ),
        name="attend",
    )(x, gain[None], wq, wk, wv, wo, cos, sin, lens)


def return_kernel(
    n,
    nz,
    gmid_ref,
    mixed_ref,
    rgrad_ref,
    ggrad_ref,
    x_ref,
    gain_ref,
    wq_ref,
    wk_ref,
    wv_ref,
    wo_ref,
    cos_ref,
    sin_ref,
    q_ref,
    kv_ref,
    lrow_ref,
    att_ref,
    lens_ref,
    out_ref,
    igrad_ref,
    wsum_ref,
    small_ref,
    wqkv,
    gat,
    obuf,
    igbuf,
    datt,
    dq_s,
    acc_q,
    dkv,
    kvo,
    kvi,
    kvf,
    kvr,
    part,
    zsend,
    zin,
    wpack,
    wsi,
    wsf,
    wsr,
    wall,
    sz1,
    sz2,
    sown,
    ssib,
    schip,
    zas,
    zar,
    zos,
    zor,
    zis,
    zir,
    zps,
    zpr,
    z1s,
    z1r,
    z2s,
    z2r,
    kos,
    kor,
    kfs,
    kfr,
    wos,
    wor,
    wfs,
    wfr,
    was,
    war,
    wbs,
    wbr,
    sbs,
    sbr,
    scs,
    scr,
):
    e = lax.axis_index("expert")
    z = lax.axis_index("tensor")
    core = lax.rem(e, 2)
    sib = e + 1 - 2 * core
    half = n // 2
    rows, width = gmid_ref.shape
    tok = rows * nz
    qw = wq_ref.shape[1]
    kw = wk_ref.shape[1]
    seqs = kv_ref.shape[0]
    span = tok // seqs
    heads = kw // HD
    groups = qw // kw
    dn = width // n
    experts = rgrad_ref.shape[0]
    own_rows = pl.ds(pl.multiple_of(z * rows, 16), rows)
    barrier = greet(n, nz, e, z, sib)

    gat[own_rows, :] = gmid_ref[...].astype(bf16)
    obuf[own_rows, :] = mixed_ref[...].astype(bf16)
    sz1[z] = jnp.concatenate(
        [rgrad_ref[...], ggrad_ref[...], jnp.zeros((15, width), f32)], 0
    ).astype(bf16)
    pl.semaphore_wait(barrier, half + nz - 1)

    def z_copies(buf_of, send, recv):
        return [
            remote(
                buf_of(z), buf_of(z), send.at[k - 1], recv.at[k - 1], (e, lax.rem(z + k, nz))
            )
            for k in range(1, nz)
        ]

    def z_arrivals(buf_of, send, recv):
        return [
            remote(
                buf_of(lax.rem(z + nz - k, nz)),
                buf_of(lax.rem(z + nz - k, nz)),
                send.at[k - 1],
                recv.at[k - 1],
                (e, lax.rem(z + nz - k, nz)),
            )
            for k in range(1, nz)
        ]

    def part_of(ref):
        return lambda zz: ref.at[pl.ds(pl.multiple_of(zz * rows, 16), rows)]

    def slot_of(ref):
        return lambda zz: ref.at[zz]

    for copy in z_copies(part_of(gat), zas, zar):
        copy.start()
    for copy in z_copies(slot_of(sz1), z1s, z1r):
        copy.start()
    for copy in z_copies(part_of(obuf), zos, zor):
        copy.start()

    wqkv[:, 0:qw] = wq_ref[...]
    wqkv[:, qw : qw + kw] = wk_ref[...]
    wqkv[:, qw + kw :] = wv_ref[...]
    x = x_ref[...].astype(f32)
    scale1 = lax.rsqrt(jnp.mean(x * x, -1, keepdims=True) + EPS)
    normed = (x * scale1 * gain_ref[...]).astype(bf16)
    dkv[...] = jnp.zeros_like(dkv)

    for copy in z_arrivals(part_of(gat), zas, zar):
        copy.wait_recv()
    datt[...] = dot_nt(gat[...], wo_ref[...]).astype(bf16)

    ck = 2 * span
    trip = (e * span + span - 1) // ck + 1
    stacked = groups * span
    kiota = lax.broadcasted_iota(jnp.int32, (ck, stacked), 0)
    qpos = e * span + lax.rem(lax.broadcasted_iota(jnp.int32, (ck, stacked), 1), span)
    for s in range(seqs):
        for h in range(heads):
            srows = slice(s * span, (s + 1) * span)

            def gather(ref):
                return jnp.concatenate(
                    [
                        ref[srows, (h * groups + g) * HD : (h * groups + g + 1) * HD]
                        for g in range(groups)
                    ],
                    0,
                )

            qst = gather(q_ref)
            dst = gather(datt)
            delta = jnp.sum(dst.astype(f32) * gather(att_ref), -1, keepdims=True)
            drow = jnp.broadcast_to(delta, (stacked, 128)).T[0:1]
            lrow = lrow_ref[s * heads + h, 0:1, :]
            acc_q[...] = jnp.zeros_like(acc_q)

            def chunk(c, carry):
                at = pl.ds(pl.multiple_of(c * ck, 16), ck)
                keys = kv_ref[s, at, h * HD : (h + 1) * HD]
                vals = kv_ref[s, at, kw + h * HD : kw + (h + 1) * HD]
                scores = dot_nt(keys, qst) * HD ** (-0.5)
                kpos = kiota + c * ck
                soft = jnp.where(
                    (kpos <= qpos) & (kpos < lens_ref[s]), jnp.exp(scores - lrow), 0.0
                )
                grad_probs = dot_nt(vals, dst)
                grad_scores = (soft * (grad_probs - drow)).astype(bf16)
                dkv[s, at, h * HD : (h + 1) * HD] = dot_nn(grad_scores, qst) * HD ** (-0.5)
                dkv[s, at, kw + h * HD : kw + (h + 1) * HD] = dot_nn(soft.astype(bf16), dst)
                acc_q[...] += dot_tn(grad_scores, keys)
                return carry

            lax.fori_loop(0, trip, chunk, 0)
            result = acc_q[...] * HD ** (-0.5)
            for g in range(groups):
                cols = slice((h * groups + g) * HD, (h * groups + g + 1) * HD)
                dq_s[srows, cols] = result[g * span : (g + 1) * span]

    def key_rows(j, s):
        return dkv[s, pl.ds(pl.multiple_of(j * span, 16), span), :]

    def key_send(t):
        return remote(kvo.at[t], kvi.at[t], kos.at[t], kor.at[t], (sib, z))

    def key_final(t):
        to = (lax.rem(e - 2 * t + n, n), z)
        return remote(kvf.at[t - 1], kvr.at[t - 1], kfs.at[t - 1], kfr.at[t - 1], to)

    def key_give(i, carry):
        t = half - 1 - i
        oth = lax.rem(sib - 2 * t + n, n)
        for s in range(seqs):
            kvo[t, s] = key_rows(oth, s).astype(bf16)
        key_send(t).start()
        return carry

    lax.fori_loop(0, half, key_give, 0)

    def key_pass(i, carry):
        t = half - 1 - i
        key_send(t).wait_recv()
        own = lax.rem(e - 2 * t + n, n)
        for s in range(seqs):
            kvf[t - 1, s] = (key_rows(own, s) + kvi[t, s].astype(f32)).astype(bf16)
        key_final(t).start()
        return carry

    lax.fori_loop(0, half - 1, key_pass, 0)

    for copy in z_arrivals(slot_of(sz1), z1s, z1r):
        copy.wait_recv()
    first = sz1[0].astype(f32)
    for zz in range(1, nz):
        first = first + sz1[zz].astype(f32)

    out_grad = dot_tn(gat[...], att_ref[...].astype(bf16))
    for j in range(n):
        wpack[j, :, qw + 2 * kw :] = out_grad[j * dn : (j + 1) * dn].astype(bf16)

    key_send(0).wait_recv()
    own_kv = [key_rows(e, s) + kvi[0, s].astype(f32) for s in range(seqs)]
    for t in range(1, half):
        key_final(t).wait_recv()
        for s in range(seqs):
            own_kv[s] = own_kv[s] + kvr[t - 1, s].astype(f32)
    lin = jnp.concatenate([dq_s[...], jnp.concatenate(own_kv, 0)], 1)
    glin = turn(lin, cos_ref[...], sin_ref[...], qw + kw, False).astype(bf16)
    part[...] = dot_nt(glin, wqkv[...])
    for k in range(1, nz):
        zz = lax.rem(z + k, nz)
        zsend[k - 1] = part[pl.ds(pl.multiple_of(zz * rows, 16), rows), :].astype(bf16)
        remote(zsend.at[k - 1], zin.at[k - 1], zps.at[k - 1], zpr.at[k - 1], (e, zz)).start()
    again = jnp.sum(part[...] * x * scale1, 0, keepdims=True)
    sz2[z] = jnp.concatenate([again, jnp.zeros((15, width), f32)], 0).astype(bf16)
    for copy in z_copies(slot_of(sz2), z2s, z2r):
        copy.start()

    lin_grad = dot_tn(normed, glin)
    for j in range(n):
        wpack[j, :, : qw + 2 * kw] = lin_grad[j * dn : (j + 1) * dn].astype(bf16)

    def weight_send(t):
        oth = lax.rem(sib - 2 * t + n, n)
        return remote(wpack.at[oth], wsi.at[t], wos.at[t], wor.at[t], (sib, z))

    def weight_final(t):
        to = (lax.rem(e - 2 * t + n, n), z)
        return remote(wsf.at[t - 1], wsr.at[t - 1], wfs.at[t - 1], wfr.at[t - 1], to)

    def weight_give(i, carry):
        weight_send(half - 1 - i).start()
        return carry

    lax.fori_loop(0, half, weight_give, 0)

    def weight_pass(i, carry):
        t = half - 1 - i
        weight_send(t).wait_recv()
        own = lax.rem(e - 2 * t + n, n)
        wsf[t - 1] = (wpack[own].astype(f32) + wsi[t].astype(f32)).astype(bf16)
        weight_final(t).start()
        return carry

    lax.fori_loop(0, half - 1, weight_pass, 0)

    for copy in z_arrivals(slot_of(sz2), z2s, z2r):
        copy.wait_recv()
    second = sz2[0].astype(f32)
    for zz in range(1, nz):
        second = second + sz2[zz].astype(f32)
    sown[...] = jnp.concatenate(
        [first[: experts + 1], second[0:1], jnp.zeros((14, width), f32)], 0
    ).astype(bf16)
    small_sib = remote(sown, ssib, sbs, sbr, (sib, z))
    small_sib.start()

    own_x = x_ref[own_rows, :].astype(f32)
    own_scale = lax.rsqrt(jnp.mean(own_x * own_x, -1, keepdims=True) + EPS)
    grad_normed = part[own_rows, :]
    for k in range(1, nz):
        remote(zsend.at[k - 1], zin.at[k - 1], zps.at[k - 1], zpr.at[k - 1], (e, z)).wait_recv()
        grad_normed = grad_normed + zin[k - 1].astype(f32)
    gained = grad_normed * gain_ref[...]
    igrad = (
        gmid_ref[...]
        + own_scale * gained
        - own_x
        * (own_scale * own_scale * own_scale)
        * jnp.mean(gained * own_x, -1, keepdims=True)
    )
    igbuf[own_rows, :] = igrad.astype(bf16)
    for copy in z_copies(part_of(igbuf), zis, zir):
        copy.start()

    small_sib.wait_recv()
    me = e // 2
    schip[me] = (sown[...].astype(f32) + ssib[...].astype(f32)).astype(bf16)

    def small_send(t):
        to = (lax.rem(e + 2 * t, n), z)
        return remote(schip.at[me], schip.at[me], scs.at[t - 1], scr.at[t - 1], to)

    for t in range(1, half):
        small_send(t).start()

    weight_send(0).wait_recv()
    total = wpack[e].astype(f32) + wsi[0].astype(f32)
    for t in range(1, half):
        weight_final(t).wait_recv()
        total = total + wsr[t - 1].astype(f32)
    wall[e] = total.astype(bf16)

    def all_send(t):
        to = (lax.rem(e + 2 * t, n), z)
        return remote(wall.at[e], wall.at[e], was.at[t], war.at[t], to)

    def all_pass(src, t):
        return remote(wall.at[src], wall.at[src], wbs.at[t], wbr.at[t], (sib, z))

    for t in range(1, half):
        all_send(t).start()
    all_pass(e, 0).start()
    for copy in z_arrivals(part_of(obuf), zos, zor):
        copy.wait_recv()
    out_ref[...] = obuf[...].astype(f32)

    def all_forward(t, carry):
        src = lax.rem(e - 2 * t + n, n)
        remote(wall.at[src], wall.at[src], was.at[t], war.at[t], (src, z)).wait_recv()
        all_pass(src, t).start()
        return carry

    lax.fori_loop(1, half, all_forward, 0)

    for t in range(1, half):
        src = lax.rem(me + half - t, half)
        remote(
            schip.at[src], schip.at[src], scs.at[t - 1], scr.at[t - 1], (sib, z)
        ).wait_recv()
    small = schip[0].astype(f32)
    for t in range(1, half):
        small = small + schip[t].astype(f32)
    small_ref[...] = small

    for copy in z_arrivals(part_of(igbuf), zis, zir):
        copy.wait_recv()
    igrad_ref[...] = igbuf[...].astype(f32)

    def all_arrive(t, carry):
        src = lax.rem(sib - 2 * t + n, n)
        all_pass(src, t).wait_recv()
        return carry

    lax.fori_loop(0, half, all_arrive, 0)
    for j in range(n):
        wsum_ref[j * dn : (j + 1) * dn, :] = wall[j].astype(f32)

    for copy in (
        z_copies(part_of(gat), zas, zar)
        + z_copies(slot_of(sz1), z1s, z1r)
        + z_copies(part_of(obuf), zos, zor)
        + z_copies(slot_of(sz2), z2s, z2r)
        + z_copies(part_of(igbuf), zis, zir)
    ):
        copy.wait_send()
    for k in range(1, nz):
        remote(zsend.at[k - 1], zin.at[k - 1], zps.at[k - 1], zpr.at[k - 1], (e, z)).wait_send()
    small_sib.wait_send()

    def drained(t, carry):
        key_send(t).wait_send()
        weight_send(t).wait_send()
        all_pass(e, t).wait_send()

        @pl.when(t > 0)
        def _():
            key_final(t).wait_send()
            weight_final(t).wait_send()
            all_send(t).wait_send()
            small_send(t).wait_send()

        return carry

    lax.fori_loop(0, half, drained, 0)


def return_layer(
    n, nz, gmid, mixed, rgrad, ggrad, x, gain, wq, wk, wv, wo, cos, sin, q, kv, lrow, att, lens
):
    tok, width = x.shape
    rows = tok // nz
    qw, kw = wq.shape[1], wk.shape[1]
    seqs = lens.shape[0]
    span = tok // seqs
    half = n // 2
    stacked = (qw // kw) * span
    pack = 2 * qw + 2 * kw
    small_rows = rgrad.shape[0] + 16
    dma = pltpu.SemaphoreType.DMA
    vmem = pl.BlockSpec(memory_space=pltpu.VMEM)
    sds = jax.ShapeDtypeStruct
    zdma = dma((nz - 1,))
    hdma = dma((half,))
    fdma = dma((half - 1,))
    return pl.pallas_call(
        functools.partial(return_kernel, n, nz),
        out_shape=[
            sds((tok, width), f32),
            sds((tok, width), f32),
            sds((width, pack), f32),
            sds((small_rows, width), f32),
        ],
        in_specs=[vmem] * 16 + [pl.BlockSpec(memory_space=pltpu.SMEM)],
        out_specs=[vmem] * 4,
        scratch_shapes=[
            pltpu.VMEM((width, qw + 2 * kw), bf16),
            pltpu.VMEM((tok, width), bf16),
            pltpu.VMEM((tok, width), bf16),
            pltpu.VMEM((tok, width), bf16),
            pltpu.VMEM((tok, qw), bf16),
            pltpu.VMEM((tok, qw), f32),
            pltpu.VMEM((stacked, HD), f32),
            pltpu.VMEM((seqs, n * span, 2 * kw), f32),
            pltpu.VMEM((half, seqs, span, 2 * kw), bf16),
            pltpu.VMEM((half, seqs, span, 2 * kw), bf16),
            pltpu.VMEM((half - 1, seqs, span, 2 * kw), bf16),
            pltpu.VMEM((half - 1, seqs, span, 2 * kw), bf16),
            pltpu.VMEM((tok, width), f32),
            pltpu.VMEM((nz - 1, rows, width), bf16),
            pltpu.VMEM((nz - 1, rows, width), bf16),
            pltpu.VMEM((n, width // n, pack), bf16),
            pltpu.VMEM((half, width // n, pack), bf16),
            pltpu.VMEM((half - 1, width // n, pack), bf16),
            pltpu.VMEM((half - 1, width // n, pack), bf16),
            pltpu.VMEM((n, width // n, pack), bf16),
            pltpu.VMEM((nz, small_rows, width), bf16),
            pltpu.VMEM((nz, 16, width), bf16),
            pltpu.VMEM((small_rows, width), bf16),
            pltpu.VMEM((small_rows, width), bf16),
            pltpu.VMEM((half, small_rows, width), bf16),
        ]
        + [zdma] * 12
        + [hdma, hdma, fdma, fdma]
        + [hdma, hdma, fdma, fdma]
        + [hdma] * 4
        + [dma, dma, fdma, fdma],
        compiler_params=pltpu.CompilerParams(
            collective_id=3, has_side_effects=True, vmem_limit_bytes=56 << 20
        ),
        name="attend_back",
    )(
        gmid,
        mixed,
        rgrad,
        ggrad,
        x,
        gain[None],
        wq,
        wk,
        wv,
        wo,
        cos,
        sin,
        q,
        kv,
        lrow,
        att,
        lens,
    )


def shards(
    inputs,
    attention_gain,
    query_weight,
    key_weight,
    value_weight,
    out_weight,
    expert_gain,
    router_weight,
    gate_weight,
    up_weight,
    down_weight,
    routes,
    seq_lens,
    cotangent,
):
    n = lax.axis_size("expert")
    nz = lax.axis_size("tensor")
    tok_rows = inputs.shape[0]
    seq_count = seq_lens.shape[0]
    span_rows = tok_rows // seq_count
    query_width = query_weight.shape[1]
    key_width = key_weight.shape[1]
    experts = router_weight.shape[1]
    local_pos = lax.axis_index("expert") * span_rows + jnp.arange(span_rows, dtype=jnp.int32)
    frequency = THETA ** (-2.0 * jnp.arange(HD // 2, dtype=jnp.float32) / HD)
    angles = local_pos.astype(f32)[:, None] * frequency[None, :]
    cosines = jnp.tile(jnp.cos(angles), (seq_count, 4))
    sines = jnp.tile(jnp.sin(angles), (seq_count, 4))
    cot_all = lax.all_gather(cotangent.astype(bf16), "expert", axis=0, tiled=True)
    weights = (query_weight, key_weight, value_weight, out_weight, cosines, sines)
    middle, queries, pairs, logs, attended = attend_layer(
        n, nz, inputs, attention_gain, *weights, seq_lens
    )
    (
        out_part,
        grad_middle,
        router_part,
        expert_gain_part,
        expert_load,
        gate_grad,
        up_grad,
        down_grad,
    ) = expert_layer(
        n,
        nz,
        middle,
        expert_gain,
        router_weight,
        routes,
        gate_weight,
        up_weight,
        down_weight,
        cotangent,
        cot_all,
    )
    output, input_grad, packed, small = return_layer(
        n,
        nz,
        grad_middle,
        out_part,
        router_part,
        expert_gain_part,
        inputs,
        attention_gain,
        *weights,
        queries,
        pairs,
        logs,
        attended,
        seq_lens,
    )
    cuts = (query_width, query_width + key_width, query_width + 2 * key_width)
    return (
        output,
        input_grad,
        jnp.mean(expert_load),
        expert_load[0],
        small[experts + 1],
        packed[:, : cuts[0]],
        packed[:, cuts[0] : cuts[1]],
        packed[:, cuts[1] : cuts[2]],
        packed[:, cuts[2] :].T,
        small[experts],
        small[:experts].T,
        gate_grad,
        up_grad,
        down_grad.reshape(down_weight.shape),
    )


def solution(mesh):
    placed = (
        P("expert", None),
        P(),
        P(None, "tensor"),
        P(None, "tensor"),
        P(None, "tensor"),
        P("tensor", None),
        P(),
        P(),
        P("expert", None, "tensor"),
        P("expert", None, "tensor"),
        P("expert", "tensor", None),
        P("expert", None),
        P(),
        P("expert", None),
    )
    return jax.shard_map(
        shards,
        mesh=mesh,
        in_specs=placed,
        out_specs=(
            P("expert", None),
            P("expert", None),
            P(),
            P(),
            P(),
            P(None, "tensor"),
            P(None, "tensor"),
            P(None, "tensor"),
            P("tensor", None),
            P(),
            P(),
            P("expert", None, "tensor"),
            P("expert", None, "tensor"),
            P("expert", "tensor", None),
        ),
        check_vma=False,
    )
```

```python
import functools

import jax
import jax.numpy as jnp
from jax import lax
from jax.experimental import pallas as pl
from jax.experimental.pallas import tpu as pltpu
from jax.sharding import PartitionSpec as P

HD = 64
EPS = 1e-06
THETA = 10000.0
MESH = pl.DeviceIdType.MESH
f32 = jnp.float32
bf16 = jnp.bfloat16


def dot_nn(left, right):
    return lax.dot_general(left, right, (((1,), (0,)), ((), ())), preferred_element_type=f32)


def dot_nt(left, right):
    return lax.dot_general(left, right, (((1,), (1,)), ((), ())), preferred_element_type=f32)


def dot_tn(left, right):
    return lax.dot_general(left, right, (((0,), (0,)), ((), ())), preferred_element_type=f32)


def remote(src, dst, send_sem, recv_sem, device):
    return pltpu.make_async_remote_copy(
        src_ref=src,
        dst_ref=dst,
        send_sem=send_sem,
        recv_sem=recv_sem,
        device_id=device,
        device_id_type=MESH,
    )


def turn(values, cos, sin, last, forward):
    lane = lax.broadcasted_iota(jnp.int32, (values.shape[0], 128), 1)
    first_half = lax.rem(lane, HD) < HD // 2
    parts = []
    for g in range(values.shape[1] // 128):
        v = values[:, g * 128 : (g + 1) * 128]
        if g * 128 >= last:
            parts.append(v)
            continue
        turned = jnp.where(
            first_half, -pltpu.roll(v, 128 - HD // 2, 1), pltpu.roll(v, HD // 2, 1)
        )
        new = v * cos + turned * sin if forward else v * cos - turned * sin
        if (g + 1) * 128 > last:
            new = jnp.where(lane + g * 128 < last, new, v)
        parts.append(new)
    return jnp.concatenate(parts, 1) if len(parts) > 1 else parts[0]


def greet(n, nz, e, z, sib):
    barrier = pltpu.get_barrier_semaphore()
    pl.semaphore_signal(barrier, inc=1, device_id=(sib, z), device_id_type=MESH)
    for s in range(1, n // 2):
        pl.semaphore_signal(
            barrier, inc=1, device_id=(lax.rem(e + 2 * s, n), z), device_id_type=MESH
        )
    for k in range(1, nz):
        pl.semaphore_signal(barrier, inc=1, device_id=(e, lax.rem(z + k, nz)), device_id_type=MESH)
    return barrier


def expert_kernel(
    n,
    nz,
    big,
    mid_ref,
    gain_ref,
    router_ref,
    routes_ref,
    cot_ref,
    gate_hbm,
    up_hbm,
    down_hbm,
    cot_all,
    *rest,
):
    outs, rest = rest[:8], rest[8:]
    gmid_ref, rgrad_ref, ggrad_ref, load_ref, dgate_hbm, dup_hbm, ddown_hbm, mixed_hbm = outs
    xbuf, rest = rest[0], rest[1:]
    if big:
        xstage, rest = rest[0], rest[1:]
    (
        wbuf,
        xn_s,
        wg,
        wu,
        down_ref,
        dgate,
        dup,
        ddown,
        cbuf,
        dg_s,
        du_s,
        wi_s,
        hold,
        osend,
        sin,
        hold_o,
        osend_o,
        sin_o,
        hold_g,
        osend_g,
        sin_g,
        own_s,
        own_g,
        fsend,
        fin,
        fsend_g,
        fin_g,
        zsend,
        zin,
        zsend_g,
        zin_g,
        wsem,
        gsem,
        csem,
        msem,
        lsem,
        zs,
        zr,
        zws,
        zwr,
        xs,
        xr,
        ws,
        wr,
        fs,
        fr,
        wfs,
        wfr,
        gs,
        gr,
        oss,
        osr,
        ggs,
        ggr,
        ps,
        pr,
        pgs,
        pgr,
        zgs,
        zgr,
        zggs,
        zggr,
    ) = rest
    e = lax.axis_index("expert")
    z = lax.axis_index("tensor")
    core = lax.rem(e, 2)
    other = 1 - core
    me = e // 2
    sib = e + 1 - 2 * core
    half = n // 2
    rows, width = mid_ref.shape
    tok = rows * nz
    experts = router_ref.shape[1]
    local_experts, _, hid = gate_hbm.shape
    inner_w = local_experts * hid
    fc = min(inner_w, 256)
    fslots = fsend.shape[0]

    loads = []
    for el in range(local_experts):
        cols = pl.ds(el * hid, hid)
        loads.append(pltpu.make_async_copy(gate_hbm.at[el], wg.at[:, cols], wsem.at[0, el]))
        loads.append(pltpu.make_async_copy(up_hbm.at[el], wu.at[:, cols], wsem.at[1, el]))
    loads.append(pltpu.make_async_copy(down_hbm, down_ref, wsem.at[2, 0]))
    for copy in loads:
        copy.start()

    def piece_of(g):
        return lax.rem(z + nz - g, nz)

    def cot_start(g, parity, slot):
        zz = piece_of(g)
        for h in range(half):
            start = (2 * h + parity) * tok + zz * rows
            pltpu.make_async_copy(
                cot_all.at[pl.ds(pl.multiple_of(start, 16), rows)],
                cbuf.at[slot, pl.ds(h * rows, rows)],
                csem.at[slot],
            ).start()

    def cot_wait(slot):
        pltpu.make_async_copy(
            cot_all.at[pl.ds(0, half * rows)], cbuf.at[slot], csem.at[slot]
        ).wait()

    cot_start(0, core, 0)
    barrier = greet(n, nz, e, z, sib)

    own_rows = pl.ds(pl.multiple_of(z * rows, 16), rows)
    my_rows = pl.ds(pl.multiple_of(me * rows, 16), rows)
    mid = mid_ref[...]
    scale2 = lax.rsqrt(jnp.mean(mid * mid, -1, keepdims=True) + EPS)
    xn = (mid * scale2 * gain_ref[...]).astype(bf16)
    xn_s[...] = xn
    logits = dot_nn(xn, router_ref[...])
    picks = routes_ref[own_rows, :]
    lanes = lax.broadcasted_iota(jnp.int32, (rows, experts), 1)
    chosen = jnp.zeros((rows, experts), f32)
    for k in range(picks.shape[1]):
        chosen = jnp.where(picks[:, k : k + 1] == lanes, 1.0, chosen)
    top = jnp.max(logits, -1, keepdims=True)
    powers = jnp.exp(logits - top)
    probs = powers / jnp.sum(powers, -1, keepdims=True)
    low_logits = jnp.where(chosen > 0.0, logits, -1e30)
    ctop = jnp.max(low_logits, -1, keepdims=True)
    cpow = jnp.exp(low_logits - ctop)
    comb = cpow / jnp.sum(cpow, -1, keepdims=True)
    padded = jnp.concatenate([comb, jnp.zeros((rows, 128 - experts), f32)], 1)
    if rows < 128:
        padded = jnp.concatenate([padded, jnp.zeros((128 - rows, 128), f32)], 0)
    piece = padded.T[:experts]
    lane_pad = jnp.zeros((1, 128 - experts), f32)
    cnt = jnp.concatenate([jnp.sum(chosen, 0, keepdims=True), lane_pad], 1)
    psum = jnp.concatenate([jnp.sum(probs, 0, keepdims=True), lane_pad], 1)
    psum_hi = psum.astype(bf16).astype(f32)
    stats = jnp.concatenate([cnt, psum_hi, psum - psum_hi, jnp.zeros((13, 128), f32)], 0)
    wbuf[z, core, me] = jnp.concatenate([piece, stats], 0).astype(bf16)
    if big:
        copy = pltpu.make_async_copy(xn_s, xbuf.at[z, core, my_rows], lsem)
        copy.start()
        copy.wait()
    else:
        xbuf[z, core, my_rows] = xn
    pl.semaphore_wait(barrier, half + nz - 1)

    def z_row(zz, k, to):
        ref = xbuf.at[zz, core, my_rows]
        return remote(ref, ref, zs.at[k - 1], zr.at[k - 1], (e, to))

    def z_small(zz, k, to):
        ref = wbuf.at[zz, core, me]
        return remote(ref, ref, zws.at[k - 1], zwr.at[k - 1], (e, to))

    def x_row(zz, h, g, s, to):
        ref = xbuf.at[zz, core, pl.ds(pl.multiple_of(h * rows, 16), rows)]
        return remote(ref, ref, xs.at[g, s], xr.at[g, s], (to, z))

    def x_small(zz, h, g, s, to):
        ref = wbuf.at[zz, core, h]
        return remote(ref, ref, ws.at[g, s], wr.at[g, s], (to, z))

    def push_piece(g):
        zz = piece_of(g)
        for s in range(1, half):
            to = lax.rem(e + 2 * s, n)
            x_row(zz, me, g, s, to).start()
            x_small(zz, me, g, s, to).start()

    push_piece(jnp.int32(0))
    for k in range(1, nz):
        z_row(z, k, lax.rem(z + k, nz)).start()
        z_small(z, k, lax.rem(z + k, nz)).start()

    dgate[...] = jnp.zeros_like(dgate)
    dup[...] = jnp.zeros_like(dup)
    ddown[...] = jnp.zeros_like(ddown)
    for copy in loads:
        copy.wait()

    sel_row = lax.broadcasted_iota(jnp.int32, (experts, fc), 0)
    sel_col = lax.broadcasted_iota(jnp.int32, (experts, fc), 1)

    def block(zz, parity, slot, dst, dst_o, dst_g, dslot):
        if big:
            copy = pltpu.make_async_copy(xbuf.at[zz, parity], xstage, lsem)
            copy.start()
            copy.wait()
            x_ref = xstage
        else:
            x_ref = xbuf.at[zz, parity]
        c_ref = cbuf.at[slot]
        sums = [jnp.zeros((experts, rows), f32) for _ in range(half)]
        for q in range(inner_w // fc):
            cols = slice(q * fc, (q + 1) * fc)
            x = x_ref[...]
            gate_val = dot_nn(x, wg[:, cols])
            up_val = dot_nn(x, wu[:, cols])
            back = dot_nt(c_ref[...], down_ref[cols, :])
            select = jnp.where(
                sel_row == e * local_experts + (q * fc + sel_col) // hid, 1.0, 0.0
            ).astype(bf16)
            wide = jnp.concatenate(
                [dot_tn(wbuf[zz, parity, h, :experts, :], select)[:rows] for h in range(half)], 0
            )
            sig = 1.0 / (1.0 + jnp.exp(-gate_val))
            silu = gate_val * sig
            inner = silu * up_val
            wi_s[:, cols] = (inner * wide).astype(bf16)
            scaled = back * wide
            dg_s[:, cols] = (scaled * up_val * (sig * (1.0 + gate_val * (1.0 - sig)))).astype(bf16)
            du_s[:, cols] = (scaled * silu).astype(bf16)
            both = (inner * back).astype(bf16)
            for h in range(half):
                sums[h] = sums[h] + dot_nt(select, both[h * rows : (h + 1) * rows])
        for h in range(half):
            gap = jnp.zeros((experts, 128 - rows), f32)
            dst_g[dslot, h] = jnp.concatenate([sums[h], gap], 1).astype(bf16)
        for h in range(width // 256):
            cols = slice(h * 256, (h + 1) * 256)
            dst[dslot, :, cols] = (
                dot_nt(dg_s[...], wg[cols, :]) + dot_nt(du_s[...], wu[cols, :])
            ).astype(bf16)
            dst_o[dslot, :, cols] = dot_nn(wi_s[...], down_ref[:, cols]).astype(bf16)
        for h in range(width // 256):
            cols = slice(h * 256, (h + 1) * 256)
            x_part = x_ref[:, cols]
            gate_part = dot_tn(x_part, dg_s[...])
            up_part = dot_tn(x_part, du_s[...])
            for el in range(local_experts):
                dgate[el, cols, :] += gate_part[:, el * hid : (el + 1) * hid]
                dup[el, cols, :] += up_part[:, el * hid : (el + 1) * hid]
            ddown[:, cols] += dot_tn(wi_s[...], c_ref[:, cols])

    def gives(slot):
        return [
            remote(osend.at[slot], sin.at[slot], gs.at[slot], gr.at[slot], (sib, z)),
            remote(osend_g.at[slot], sin_g.at[slot], ggs.at[slot], ggr.at[slot], (sib, z)),
            remote(osend_o.at[slot], sin_o.at[slot], oss.at[slot], osr.at[slot], (sib, z)),
        ]

    def finals(g, s, to):
        at = lax.rem(g, fslots)
        return [
            remote(
                fsend.at[at, s - 1], fin.at[g, s - 1], ps.at[g, s - 1], pr.at[g, s - 1], (to, z)
            ),
            remote(
                fsend_g.at[at, s - 1],
                fin_g.at[g, s - 1],
                pgs.at[g, s - 1],
                pgr.at[g, s - 1],
                (to, z),
            ),
        ]

    def lasts(k, to):
        return [
            remote(zsend.at[k - 1], zin.at[k - 1], zgs.at[k - 1], zgr.at[k - 1], (e, to)),
            remote(zsend_g.at[k - 1], zin_g.at[k - 1], zggs.at[k - 1], zggr.at[k - 1], (e, to)),
        ]

    def mixed_copy(g, slot):
        return pltpu.make_async_copy(hold_o.at[slot], mixed_hbm.at[piece_of(g)], msem.at[slot])

    def plane_stage(g):
        slot = lax.rem(g, 2)
        for copy in gives(slot):
            copy.wait_recv()
        if fslots < nz:

            @pl.when(g >= fslots)
            def _():
                for s in range(1, half):
                    for copy in finals(g - fslots, s, sib):
                        copy.wait_send()

        spot = lax.rem(g, fslots)
        for s in range(1, half):
            h = lax.rem(me + half - s, half)
            at = pl.ds(pl.multiple_of(h * rows, 16), rows)
            fsend[spot, s - 1] = (hold[slot, at, :].astype(f32) + sin[slot, at, :].astype(f32)).astype(
                bf16
            )
            fsend_g[spot, s - 1] = (hold_g[slot, h].astype(f32) + sin_g[slot, h].astype(f32)).astype(
                bf16
            )
            for copy in finals(g, s, lax.rem(e - 2 * s + n, n)):
                copy.start()
        own_s[g] = hold[slot, my_rows, :].astype(f32) + sin[slot, my_rows, :].astype(f32)
        own_g[g] = hold_g[slot, me].astype(f32) + sin_g[slot, me].astype(f32)
        hold_o[slot] = (hold_o[slot].astype(f32) + sin_o[slot].astype(f32)).astype(bf16)
        mixed_copy(g, slot).start()

    def tensor_stage(g):
        total = own_s[g]
        total_g = own_g[g]
        for s in range(1, half):
            for copy in finals(g, s, sib):
                copy.wait_recv()
            total = total + fin[g, s - 1].astype(f32)
            total_g = total_g + fin_g[g, s - 1].astype(f32)

        @pl.when(g == 0)
        def _():
            own_s[0] = total
            own_g[0] = total_g

        @pl.when(g > 0)
        def _():
            zsend[g - 1] = total.astype(bf16)
            zsend_g[g - 1] = total_g.astype(bf16)
            for copy in lasts(g, piece_of(g)):
                copy.start()

    def step(g, carry):
        zz = piece_of(g)
        slot = lax.rem(g, 2)

        @pl.when(g < nz - 1)
        def _():
            coming = piece_of(g + 1)
            z_row(coming, g + 1, coming).wait_recv()
            z_small(coming, g + 1, coming).wait_recv()
            push_piece(g + 1)

        for s in range(1, half):
            h = lax.rem(me + half - s, half)
            src = 2 * h + core
            x_row(zz, h, g, s, src).wait_recv()
            x_small(zz, h, g, s, src).wait_recv()
        for copy in forward(zz, core, g):
            copy.start()
        cot_start(g, other, 1)
        cot_wait(0)

        @pl.when(g >= 2)
        def _():
            mixed_copy(g - 2, slot).wait()

        block(zz, core, 0, hold, hold_o, hold_g, slot)

        @pl.when(g < nz - 1)
        def _():
            cot_start(g + 1, core, 0)

        @pl.when(g >= 2)
        def _():
            tensor_stage(g - 2)

        @pl.when(g >= 1)
        def _():
            plane_stage(g - 1)

        @pl.when(g >= 2)
        def _():
            for copy in gives(slot):
                copy.wait_send()

        for copy in forward(zz, other, g):
            copy.wait_recv()
        cot_wait(1)
        block(zz, other, 1, osend, osend_o, osend_g, slot)
        for copy in gives(slot):
            copy.start()
        return carry

    def forward(zz, parity, g):
        ref = xbuf.at[zz, parity]
        small = wbuf.at[zz, parity]
        return (
            remote(ref, ref, fs.at[g], fr.at[g], (sib, z)),
            remote(small, small, wfs.at[g], wfr.at[g], (sib, z)),
        )

    lax.fori_loop(0, nz, step, 0)
    grads = [
        pltpu.make_async_copy(dgate, dgate_hbm, gsem.at[0]),
        pltpu.make_async_copy(dup, dup_hbm, gsem.at[1]),
        pltpu.make_async_copy(ddown, ddown_hbm, gsem.at[2]),
    ]
    plane_stage(jnp.int32(nz - 1))
    for copy in grads:
        copy.start()
    if nz >= 2:
        tensor_stage(jnp.int32(nz - 2))

    def total_stats(j, carry):
        for zz in range(nz):
            for parity in range(2):
                carry = carry + wbuf[zz, parity, j, experts:, :].astype(f32)
        return carry

    stats = lax.fori_loop(0, half, total_stats, jnp.zeros((16, 128), f32))
    total_rows = n * tok
    share = stats[0:1, :experts] / (total_rows * routes_ref.shape[1])
    load_ref[...] = (
        experts * experts * share * ((stats[1:2, :experts] + stats[2:3, :experts]) / total_rows)
    )
    loss_w = experts * share / total_rows
    tensor_stage(jnp.int32(nz - 1))

    gate_sums = own_g[0]
    grad_rows = own_s[0]
    for k in range(1, nz):
        for copy in lasts(k, z):
            copy.wait_recv()
        gate_sums = gate_sums + zin_g[k - 1].astype(f32)
        grad_rows = grad_rows + zin[k - 1].astype(f32)
    grow = jnp.concatenate([gate_sums, jnp.zeros((128 - experts, 128), f32)], 0).T
    grad_gates = grow[:rows, :experts]
    grad_logits = comb * (grad_gates - jnp.sum(grad_gates * comb, -1, keepdims=True))
    grad_logits = grad_logits + probs * (loss_w - jnp.sum(loss_w * probs, -1, keepdims=True))
    low_grad = grad_logits.astype(bf16)
    rgrad_ref[...] = dot_tn(low_grad, xn_s[...])
    grad_rows = grad_rows + dot_nt(low_grad, router_ref[...])
    mid = mid_ref[...]
    ggrad_ref[...] = jnp.sum(grad_rows * mid * scale2, 0, keepdims=True)
    gained = grad_rows * gain_ref[...]
    gmid_ref[...] = (
        cot_ref[own_rows, :]
        + scale2 * gained
        - mid * (scale2 * scale2 * scale2) * jnp.mean(gained * mid, -1, keepdims=True)
    )

    for copy in grads:
        copy.wait()
    for k in range(1, nz):
        z_row(z, k, z).wait_send()
        z_small(z, k, z).wait_send()
        for copy in lasts(k, z):
            copy.wait_send()
    for g in range(max(0, nz - 2), nz):
        mixed_copy(jnp.int32(g), g % 2).wait()
        for copy in gives(g % 2):
            copy.wait_send()

    def drained(g, carry):
        for s in range(1, half):
            x_row(z, me, g, s, sib).wait_send()
            x_small(z, me, g, s, sib).wait_send()
        for copy in forward(z, core, g):
            copy.wait_send()
        return carry

    lax.fori_loop(0, nz, drained, 0)

    def sums_sent(g, carry):
        for s in range(1, half):
            for copy in finals(g, s, sib):
                copy.wait_send()
        return carry

    lax.fori_loop(nz - fslots, nz, sums_sent, 0)


def expert_layer(n, nz, mid, gain, router, routes, gate, up, down, cot, cot_all):
    rows, width = mid.shape
    experts = router.shape[1]
    local_experts, _, hid = gate.shape
    inner_w = local_experts * hid
    half = n // 2
    batch = half * rows
    big = n > 8
    fslots = 2 if big else nz
    dma = pltpu.SemaphoreType.DMA
    vmem = pl.BlockSpec(memory_space=pltpu.VMEM)
    hbm = pl.BlockSpec(memory_space=pl.ANY)
    sds = jax.ShapeDtypeStruct
    out_shape = [
        sds((rows, width), f32),
        sds((experts, width), f32),
        sds((1, width), f32),
        sds((1, experts), f32),
        sds((local_experts, width, hid), f32),
        sds((local_experts, width, hid), f32),
        sds((inner_w, width), f32),
        sds((nz, batch, width), bf16),
    ]
    out_specs = [vmem] * 4 + [hbm] * 4
    scratch = []
    if big:
        out_shape.append(sds((nz, 2, batch, width), bf16))
        out_specs.append(hbm)
        scratch.append(pltpu.VMEM((batch, width), bf16))
    else:
        scratch.append(pltpu.VMEM((nz, 2, batch, width), bf16))
    pair = pltpu.VMEM((2, batch, width), bf16)
    small = pltpu.VMEM((2, half, experts, 128), bf16)
    scratch += [
        pltpu.VMEM((nz, 2, half, experts + 16, 128), bf16),
        pltpu.VMEM((rows, width), bf16),
        pltpu.VMEM((width, inner_w), bf16),
        pltpu.VMEM((width, inner_w), bf16),
        pltpu.VMEM((inner_w, width), bf16),
        pltpu.VMEM((local_experts, width, hid), f32),
        pltpu.VMEM((local_experts, width, hid), f32),
        pltpu.VMEM((inner_w, width), f32),
        pair,
        pltpu.VMEM((batch, inner_w), bf16),
        pltpu.VMEM((batch, inner_w), bf16),
        pltpu.VMEM((batch, inner_w), bf16),
        pair,
        pair,
        pair,
        pair,
        pair,
        pair,
        small,
        small,
        small,
        pltpu.VMEM((nz, rows, width), f32),
        pltpu.VMEM((nz, experts, 128), f32),
        pltpu.VMEM((fslots, half - 1, rows, width), bf16),
        pltpu.VMEM((nz, half - 1, rows, width), bf16),
        pltpu.VMEM((fslots, half - 1, experts, 128), bf16),
        pltpu.VMEM((nz, half - 1, experts, 128), bf16),
        pltpu.VMEM((nz - 1, rows, width), bf16),
        pltpu.VMEM((nz - 1, rows, width), bf16),
        pltpu.VMEM((nz - 1, experts, 128), bf16),
        pltpu.VMEM((nz - 1, experts, 128), bf16),
        dma((3, local_experts)),
        dma((3,)),
        dma((2,)),
        dma((2,)),
        dma,
    ]
    scratch += [dma((nz - 1,))] * 4
    scratch += [dma((nz, half))] * 4
    scratch += [dma((nz,))] * 4
    scratch += [dma((2,))] * 6
    scratch += [dma((nz, half - 1))] * 4
    scratch += [dma((nz - 1,))] * 4
    return pl.pallas_call(
        functools.partial(expert_kernel, n, nz, big),
        out_shape=out_shape,
        in_specs=[vmem] * 5 + [hbm] * 4,
        out_specs=out_specs,
        scratch_shapes=scratch,
        compiler_params=pltpu.CompilerParams(
            collective_id=1, has_side_effects=True, vmem_limit_bytes=60 << 20
        ),
        name="experts",
    )(mid, gain[None], router, routes, cot, gate, up, down.reshape(inner_w, width), cot_all)[:8]


def attend_kernel(
    n,
    nz,
    x_ref,
    gain_ref,
    wq_ref,
    wk_ref,
    wv_ref,
    wo_ref,
    cos_ref,
    sin_ref,
    lens_ref,
    mid_ref,
    q_ref,
    kv_ref,
    lrow_ref,
    att_ref,
    wqkv,
    part,
    m_s,
    l_s,
    o_s,
    zsend,
    zin,
    ks,
    kr,
    kfs,
    kfr,
    zgs,
    zgr,
):
    e = lax.axis_index("expert")
    z = lax.axis_index("tensor")
    sib = e + 1 - 2 * lax.rem(e, 2)
    half = n // 2
    tok, width = x_ref.shape
    rows = tok // nz
    qw = wq_ref.shape[1]
    kw = wk_ref.shape[1]
    seqs = kv_ref.shape[0]
    span = tok // seqs
    heads = kw // HD
    groups = qw // kw
    barrier = greet(n, nz, e, z, sib)

    wqkv[:, 0:qw] = wq_ref[...]
    wqkv[:, qw : qw + kw] = wk_ref[...]
    wqkv[:, qw + kw :] = wv_ref[...]
    x = x_ref[...].astype(f32)
    scale1 = lax.rsqrt(jnp.mean(x * x, -1, keepdims=True) + EPS)
    normed = (x * scale1 * gain_ref[...]).astype(bf16)
    lin = dot_nn(normed, wqkv[...])
    turned = turn(lin, cos_ref[...], sin_ref[...], qw + kw, True).astype(bf16)
    q_ref[...] = turned[:, :qw]
    for s in range(seqs):
        kv_ref[s, pl.ds(pl.multiple_of(e * span, 16), span)] = turned[
            s * span : (s + 1) * span, qw:
        ]
    pl.semaphore_wait(barrier, half + nz - 1)

    def rows_of(j, s):
        return kv_ref.at[s, pl.ds(pl.multiple_of(j * span, 16), span)]

    for t in range(1, half):
        to = (lax.rem(e + 2 * t, n), z)
        for s in range(seqs):
            remote(rows_of(e, s), rows_of(e, s), ks.at[t, s], kr.at[t, s], to).start()
    for s in range(seqs):
        remote(rows_of(e, s), rows_of(e, s), kfs.at[0, s], kfr.at[0, s], (sib, z)).start()

    def forward(t, carry):
        src = lax.rem(e - 2 * t + n, n)
        for s in range(seqs):
            remote(rows_of(src, s), rows_of(src, s), ks.at[t, s], kr.at[t, s], (src, z)).wait_recv()
            remote(rows_of(src, s), rows_of(src, s), kfs.at[t, s], kfr.at[t, s], (sib, z)).start()
        return carry

    lax.fori_loop(1, half, forward, 0)

    def arrive(t, carry):
        src = lax.rem(sib - 2 * t + n, n)
        for s in range(seqs):
            remote(
                rows_of(src, s), rows_of(src, s), kfs.at[t, s], kfr.at[t, s], (sib, z)
            ).wait_recv()
        return carry

    lax.fori_loop(0, half, arrive, 0)

    ck = 2 * span
    trip = (e * span + span - 1) // ck + 1
    stacked = groups * span
    qpos = lax.broadcasted_iota(jnp.int32, (stacked, ck), 0)
    qpos = e * span + lax.rem(qpos, span)
    kiota = lax.broadcasted_iota(jnp.int32, (stacked, ck), 1)
    for s in range(seqs):
        for h in range(heads):
            srows = slice(s * span, (s + 1) * span)
            qst = jnp.concatenate(
                [
                    q_ref[srows, (h * groups + g) * HD : (h * groups + g + 1) * HD]
                    for g in range(groups)
                ],
                0,
            )
            m_s[...] = jnp.full_like(m_s, -1e30)
            l_s[...] = jnp.zeros_like(l_s)
            o_s[...] = jnp.zeros_like(o_s)

            def chunk(c, carry):
                at = pl.ds(pl.multiple_of(c * ck, 16), ck)
                keys = kv_ref[s, at, h * HD : (h + 1) * HD]
                vals = kv_ref[s, at, kw + h * HD : kw + (h + 1) * HD]
                scores = dot_nt(qst, keys) * HD ** (-0.5)
                kpos = kiota + c * ck
                scores = jnp.where((kpos <= qpos) & (kpos < lens_ref[s]), scores, -1e30)
                old = m_s[:, 0:1]
                new = jnp.maximum(old, jnp.max(scores, -1, keepdims=True))
                weights = jnp.exp(scores - new)
                shrink = jnp.exp(old - new)
                m_s[...] = jnp.broadcast_to(new, m_s.shape)
                l_s[...] = l_s[...] * shrink + jnp.sum(weights, -1, keepdims=True)
                o_s[...] = o_s[...] * shrink + dot_nn(weights.astype(bf16), vals)
                return carry

            lax.fori_loop(0, trip, chunk, 0)
            result = o_s[...] / l_s[:, 0:HD]
            for g in range(groups):
                cols = slice((h * groups + g) * HD, (h * groups + g + 1) * HD)
                att_ref[srows, cols] = result[g * span : (g + 1) * span]
            logs = m_s[...] + jnp.log(l_s[...])
            lrow_ref[s * heads + h] = logs.T[0:8]

    part[...] = dot_nn(att_ref[...].astype(bf16), wo_ref[...])
    for k in range(1, nz):
        zz = lax.rem(z + k, nz)
        zsend[k - 1] = part[pl.ds(pl.multiple_of(zz * rows, 16), rows), :].astype(bf16)
        remote(zsend.at[k - 1], zin.at[k - 1], zgs.at[k - 1], zgr.at[k - 1], (e, zz)).start()
    own_rows = pl.ds(pl.multiple_of(z * rows, 16), rows)
    mid = x_ref[own_rows, :].astype(f32) + part[own_rows, :]
    for k in range(1, nz):
        remote(zsend.at[k - 1], zin.at[k - 1], zgs.at[k - 1], zgr.at[k - 1], (e, z)).wait_recv()
        mid = mid + zin[k - 1].astype(f32)
    mid_ref[...] = mid
    for k in range(1, nz):
        remote(zsend.at[k - 1], zin.at[k - 1], zgs.at[k - 1], zgr.at[k - 1], (e, z)).wait_send()

    def sent(t, carry):
        for s in range(seqs):

            @pl.when(t > 0)
            def _():
                remote(
                    rows_of(e, s), rows_of(e, s), ks.at[t, s], kr.at[t, s], (sib, z)
                ).wait_send()

            remote(rows_of(e, s), rows_of(e, s), kfs.at[t, s], kfr.at[t, s], (sib, z)).wait_send()
        return carry

    lax.fori_loop(0, half, sent, 0)


def attend_layer(n, nz, x, gain, wq, wk, wv, wo, cos, sin, lens):
    tok, width = x.shape
    rows = tok // nz
    qw, kw = wq.shape[1], wk.shape[1]
    seqs = lens.shape[0]
    span = tok // seqs
    half = n // 2
    stacked = (qw // kw) * span
    dma = pltpu.SemaphoreType.DMA
    vmem = pl.BlockSpec(memory_space=pltpu.VMEM)
    sds = jax.ShapeDtypeStruct
    return pl.pallas_call(
        functools.partial(attend_kernel, n, nz),
        out_shape=[
            sds((rows, width), f32),
            sds((tok, qw), bf16),
            sds((seqs, n * span, 2 * kw), bf16),
            sds((seqs * (kw // HD), 8, stacked), f32),
            sds((tok, qw), f32),
        ],
        in_specs=[vmem] * 8 + [pl.BlockSpec(memory_space=pltpu.SMEM)],
        out_specs=[vmem] * 5,
        scratch_shapes=[
            pltpu.VMEM((width, qw + 2 * kw), bf16),
            pltpu.VMEM((tok, width), f32),
            pltpu.VMEM((stacked, 128), f32),
            pltpu.VMEM((stacked, 128), f32),
            pltpu.VMEM((stacked, HD), f32),
            pltpu.VMEM((nz - 1, rows, width), bf16),
            pltpu.VMEM((nz - 1, rows, width), bf16),
        ]
        + [dma((half, seqs))] * 4
        + [dma((nz - 1,))] * 2,
        compiler_params=pltpu.CompilerParams(
            collective_id=2, has_side_effects=True, vmem_limit_bytes=48 << 20
        ),
        name="attend",
    )(x, gain[None], wq, wk, wv, wo, cos, sin, lens)


def return_kernel(
    n,
    nz,
    gmid_ref,
    mid_ref,
    rgrad_ref,
    ggrad_ref,
    x_ref,
    gain_ref,
    wq_ref,
    wk_ref,
    wv_ref,
    wo_ref,
    cos_ref,
    sin_ref,
    q_ref,
    kv_ref,
    lrow_ref,
    att_ref,
    lens_ref,
    mixed_hbm,
    out_ref,
    igrad_ref,
    wsum_ref,
    small_ref,
    wqkv,
    gat,
    obuf,
    igbuf,
    datt,
    dq_s,
    acc_q,
    dkv,
    kvo,
    kvi,
    kvf,
    kvr,
    part,
    zsend,
    zin,
    wpack,
    wsi,
    wsf,
    wsr,
    wall,
    sz1,
    sz2,
    sown,
    ssib,
    schip,
    zas,
    zar,
    zos,
    zor,
    zis,
    zir,
    zps,
    zpr,
    z1s,
    z1r,
    z2s,
    z2r,
    kos,
    kor,
    kfs,
    kfr,
    wos,
    wor,
    wfs,
    wfr,
    was,
    war,
    wbs,
    wbr,
    sbs,
    sbr,
    scs,
    scr,
    ofin,
    ozs,
    ozi,
    ofs,
    ofr,
    ozsem,
    ozrem,
    olsem,
):
    e = lax.axis_index("expert")
    z = lax.axis_index("tensor")
    core = lax.rem(e, 2)
    me = e // 2
    sib = e + 1 - 2 * core
    half = n // 2
    rows, width = gmid_ref.shape
    tok = rows * nz
    qw = wq_ref.shape[1]
    kw = wk_ref.shape[1]
    seqs = kv_ref.shape[0]
    span = tok // seqs
    heads = kw // HD
    groups = qw // kw
    dn = width // n
    experts = rgrad_ref.shape[0]
    own_rows = pl.ds(pl.multiple_of(z * rows, 16), rows)
    barrier = greet(n, nz, e, z, sib)

    gat[own_rows, :] = gmid_ref[...].astype(bf16)
    sz1[z] = jnp.concatenate(
        [rgrad_ref[...], ggrad_ref[...], jnp.zeros((15, width), f32)], 0
    ).astype(bf16)
    pl.semaphore_wait(barrier, half + nz - 1)

    def z_copies(buf_of, send, recv):
        return [
            remote(
                buf_of(z), buf_of(z), send.at[k - 1], recv.at[k - 1], (e, lax.rem(z + k, nz))
            )
            for k in range(1, nz)
        ]

    def z_arrivals(buf_of, send, recv):
        return [
            remote(
                buf_of(lax.rem(z + nz - k, nz)),
                buf_of(lax.rem(z + nz - k, nz)),
                send.at[k - 1],
                recv.at[k - 1],
                (e, lax.rem(z + nz - k, nz)),
            )
            for k in range(1, nz)
        ]

    def part_of(ref):
        return lambda zz: ref.at[pl.ds(pl.multiple_of(zz * rows, 16), rows)]

    def slot_of(ref):
        return lambda zz: ref.at[zz]

    for copy in z_copies(part_of(gat), zas, zar):
        copy.start()
    for copy in z_copies(slot_of(sz1), z1s, z1r):
        copy.start()
    def mixed_send(t):
        h = lax.rem(me + half - t, half)
        return remote(
            mixed_hbm.at[:, pl.ds(pl.multiple_of(h * rows, 16), rows), :],
            ofin.at[t],
            ofs.at[t - 1],
            ofr.at[t - 1],
            (lax.rem(e - 2 * t + n, n), z),
        )

    for t in range(1, half):
        mixed_send(t).start()
    mixed_own = pltpu.make_async_copy(
        mixed_hbm.at[:, pl.ds(pl.multiple_of(me * rows, 16), rows), :], ofin.at[0], olsem
    )
    mixed_own.start()

    def mixed_last(k):
        to = (e, lax.rem(z + k, nz))
        return remote(ozs.at[k - 1], ozi.at[k - 1], ozsem.at[k - 1], ozrem.at[k - 1], to)

    def mixed_sum(zz):
        total = ofin[0, zz].astype(f32)
        for t in range(1, half):
            total = total + ofin[t, zz].astype(f32)
        return total

    wqkv[:, 0:qw] = wq_ref[...]
    wqkv[:, qw : qw + kw] = wk_ref[...]
    wqkv[:, qw + kw :] = wv_ref[...]
    x = x_ref[...].astype(f32)
    scale1 = lax.rsqrt(jnp.mean(x * x, -1, keepdims=True) + EPS)
    normed = (x * scale1 * gain_ref[...]).astype(bf16)
    dkv[...] = jnp.zeros_like(dkv)

    for copy in z_arrivals(part_of(gat), zas, zar):
        copy.wait_recv()
    datt[...] = dot_nt(gat[...], wo_ref[...]).astype(bf16)

    ck = 2 * span
    trip = (e * span + span - 1) // ck + 1
    stacked = groups * span
    kiota = lax.broadcasted_iota(jnp.int32, (ck, stacked), 0)
    qpos = e * span + lax.rem(lax.broadcasted_iota(jnp.int32, (ck, stacked), 1), span)
    for s in range(seqs):
        if s == seqs - 1:
            mixed_own.wait()
            for t in range(1, half):
                mixed_send(t).wait_recv()
            for k in range(1, nz):
                ozs[k - 1] = mixed_sum(lax.rem(z + k, nz)).astype(bf16)
                mixed_last(k).start()
        for h in range(heads):
            srows = slice(s * span, (s + 1) * span)

            def gather(ref):
                return jnp.concatenate(
                    [
                        ref[srows, (h * groups + g) * HD : (h * groups + g + 1) * HD]
                        for g in range(groups)
                    ],
                    0,
                )

            qst = gather(q_ref)
            dst = gather(datt)
            delta = jnp.sum(dst.astype(f32) * gather(att_ref), -1, keepdims=True)
            drow = jnp.broadcast_to(delta, (stacked, 128)).T[0:1]
            lrow = lrow_ref[s * heads + h, 0:1, :]
            acc_q[...] = jnp.zeros_like(acc_q)

            def chunk(c, carry):
                at = pl.ds(pl.multiple_of(c * ck, 16), ck)
                keys = kv_ref[s, at, h * HD : (h + 1) * HD]
                vals = kv_ref[s, at, kw + h * HD : kw + (h + 1) * HD]
                scores = dot_nt(keys, qst) * HD ** (-0.5)
                kpos = kiota + c * ck
                soft = jnp.where(
                    (kpos <= qpos) & (kpos < lens_ref[s]), jnp.exp(scores - lrow), 0.0
                )
                grad_probs = dot_nt(vals, dst)
                grad_scores = (soft * (grad_probs - drow)).astype(bf16)
                dkv[s, at, h * HD : (h + 1) * HD] = dot_nn(grad_scores, qst) * HD ** (-0.5)
                dkv[s, at, kw + h * HD : kw + (h + 1) * HD] = dot_nn(soft.astype(bf16), dst)
                acc_q[...] += dot_tn(grad_scores, keys)
                return carry

            lax.fori_loop(0, trip, chunk, 0)
            result = acc_q[...] * HD ** (-0.5)
            for g in range(groups):
                cols = slice((h * groups + g) * HD, (h * groups + g + 1) * HD)
                dq_s[srows, cols] = result[g * span : (g + 1) * span]

    def key_rows(j, s):
        return dkv[s, pl.ds(pl.multiple_of(j * span, 16), span), :]

    def key_send(t):
        return remote(kvo.at[t], kvi.at[t], kos.at[t], kor.at[t], (sib, z))

    def key_final(t):
        to = (lax.rem(e - 2 * t + n, n), z)
        return remote(kvf.at[t - 1], kvr.at[t - 1], kfs.at[t - 1], kfr.at[t - 1], to)

    def key_give(i, carry):
        t = half - 1 - i
        oth = lax.rem(sib - 2 * t + n, n)
        for s in range(seqs):
            kvo[t, s] = key_rows(oth, s).astype(bf16)
        key_send(t).start()
        return carry

    lax.fori_loop(0, half, key_give, 0)

    def key_pass(i, carry):
        t = half - 1 - i
        key_send(t).wait_recv()
        own = lax.rem(e - 2 * t + n, n)
        for s in range(seqs):
            kvf[t - 1, s] = (key_rows(own, s) + kvi[t, s].astype(f32)).astype(bf16)
        key_final(t).start()
        return carry

    lax.fori_loop(0, half - 1, key_pass, 0)

    for copy in z_arrivals(slot_of(sz1), z1s, z1r):
        copy.wait_recv()
    first = sz1[0].astype(f32)
    for zz in range(1, nz):
        first = first + sz1[zz].astype(f32)

    out_grad = dot_tn(gat[...], att_ref[...].astype(bf16))
    for j in range(n):
        wpack[j, :, qw + 2 * kw :] = out_grad[j * dn : (j + 1) * dn].astype(bf16)

    mixed = mid_ref[...] + mixed_sum(z)
    for k in range(1, nz):
        mixed_last(k).wait_recv()
        mixed = mixed + ozi[k - 1].astype(f32)
    obuf[own_rows, :] = mixed.astype(bf16)

    key_send(0).wait_recv()
    own_kv = [key_rows(e, s) + kvi[0, s].astype(f32) for s in range(seqs)]
    for t in range(1, half):
        key_final(t).wait_recv()
        for s in range(seqs):
            own_kv[s] = own_kv[s] + kvr[t - 1, s].astype(f32)
    lin = jnp.concatenate([dq_s[...], jnp.concatenate(own_kv, 0)], 1)
    glin = turn(lin, cos_ref[...], sin_ref[...], qw + kw, False).astype(bf16)
    part[...] = dot_nt(glin, wqkv[...])
    for k in range(1, nz):
        zz = lax.rem(z + k, nz)
        zsend[k - 1] = part[pl.ds(pl.multiple_of(zz * rows, 16), rows), :].astype(bf16)
        remote(zsend.at[k - 1], zin.at[k - 1], zps.at[k - 1], zpr.at[k - 1], (e, zz)).start()
    again = jnp.sum(part[...] * x * scale1, 0, keepdims=True)
    sz2[z] = jnp.concatenate([again, jnp.zeros((15, width), f32)], 0).astype(bf16)
    for copy in z_copies(slot_of(sz2), z2s, z2r):
        copy.start()
    for copy in z_copies(part_of(obuf), zos, zor):
        copy.start()

    lin_grad = dot_tn(normed, glin)
    for j in range(n):
        wpack[j, :, : qw + 2 * kw] = lin_grad[j * dn : (j + 1) * dn].astype(bf16)

    def weight_send(t):
        oth = lax.rem(sib - 2 * t + n, n)
        return remote(wpack.at[oth], wsi.at[t], wos.at[t], wor.at[t], (sib, z))

    def weight_final(t):
        to = (lax.rem(e - 2 * t + n, n), z)
        return remote(wsf.at[t - 1], wsr.at[t - 1], wfs.at[t - 1], wfr.at[t - 1], to)

    def weight_give(i, carry):
        weight_send(half - 1 - i).start()
        return carry

    lax.fori_loop(0, half, weight_give, 0)

    def weight_pass(i, carry):
        t = half - 1 - i
        weight_send(t).wait_recv()
        own = lax.rem(e - 2 * t + n, n)
        wsf[t - 1] = (wpack[own].astype(f32) + wsi[t].astype(f32)).astype(bf16)
        weight_final(t).start()
        return carry

    lax.fori_loop(0, half - 1, weight_pass, 0)

    for copy in z_arrivals(slot_of(sz2), z2s, z2r):
        copy.wait_recv()
    second = sz2[0].astype(f32)
    for zz in range(1, nz):
        second = second + sz2[zz].astype(f32)
    sown[...] = jnp.concatenate(
        [first[: experts + 1], second[0:1], jnp.zeros((14, width), f32)], 0
    ).astype(bf16)
    small_sib = remote(sown, ssib, sbs, sbr, (sib, z))
    small_sib.start()

    own_x = x_ref[own_rows, :].astype(f32)
    own_scale = lax.rsqrt(jnp.mean(own_x * own_x, -1, keepdims=True) + EPS)
    grad_normed = part[own_rows, :]
    for k in range(1, nz):
        remote(zsend.at[k - 1], zin.at[k - 1], zps.at[k - 1], zpr.at[k - 1], (e, z)).wait_recv()
        grad_normed = grad_normed + zin[k - 1].astype(f32)
    gained = grad_normed * gain_ref[...]
    igrad = (
        gmid_ref[...]
        + own_scale * gained
        - own_x
        * (own_scale * own_scale * own_scale)
        * jnp.mean(gained * own_x, -1, keepdims=True)
    )
    igbuf[own_rows, :] = igrad.astype(bf16)
    for copy in z_copies(part_of(igbuf), zis, zir):
        copy.start()

    small_sib.wait_recv()
    schip[me] = (sown[...].astype(f32) + ssib[...].astype(f32)).astype(bf16)

    def small_send(t):
        to = (lax.rem(e + 2 * t, n), z)
        return remote(schip.at[me], schip.at[me], scs.at[t - 1], scr.at[t - 1], to)

    for t in range(1, half):
        small_send(t).start()

    weight_send(0).wait_recv()
    total = wpack[e].astype(f32) + wsi[0].astype(f32)
    for t in range(1, half):
        weight_final(t).wait_recv()
        total = total + wsr[t - 1].astype(f32)
    wall[e] = total.astype(bf16)

    def all_send(t):
        to = (lax.rem(e + 2 * t, n), z)
        return remote(wall.at[e], wall.at[e], was.at[t], war.at[t], to)

    def all_pass(src, t):
        return remote(wall.at[src], wall.at[src], wbs.at[t], wbr.at[t], (sib, z))

    for t in range(1, half):
        all_send(t).start()
    all_pass(e, 0).start()
    for copy in z_arrivals(part_of(obuf), zos, zor):
        copy.wait_recv()
    out_ref[...] = obuf[...].astype(f32)

    def all_forward(t, carry):
        src = lax.rem(e - 2 * t + n, n)
        remote(wall.at[src], wall.at[src], was.at[t], war.at[t], (src, z)).wait_recv()
        all_pass(src, t).start()
        return carry

    lax.fori_loop(1, half, all_forward, 0)

    for t in range(1, half):
        src = lax.rem(me + half - t, half)
        remote(
            schip.at[src], schip.at[src], scs.at[t - 1], scr.at[t - 1], (sib, z)
        ).wait_recv()
    small = schip[0].astype(f32)
    for t in range(1, half):
        small = small + schip[t].astype(f32)
    small_ref[...] = small

    for copy in z_arrivals(part_of(igbuf), zis, zir):
        copy.wait_recv()
    igrad_ref[...] = igbuf[...].astype(f32)

    def all_arrive(t, carry):
        src = lax.rem(sib - 2 * t + n, n)
        all_pass(src, t).wait_recv()
        return carry

    lax.fori_loop(0, half, all_arrive, 0)
    for j in range(n):
        wsum_ref[j * dn : (j + 1) * dn, :] = wall[j].astype(f32)

    for copy in (
        z_copies(part_of(gat), zas, zar)
        + z_copies(slot_of(sz1), z1s, z1r)
        + z_copies(part_of(obuf), zos, zor)
        + z_copies(slot_of(sz2), z2s, z2r)
        + z_copies(part_of(igbuf), zis, zir)
    ):
        copy.wait_send()
    for k in range(1, nz):
        remote(zsend.at[k - 1], zin.at[k - 1], zps.at[k - 1], zpr.at[k - 1], (e, z)).wait_send()
    small_sib.wait_send()
    for t in range(1, half):
        mixed_send(t).wait_send()
    for k in range(1, nz):
        mixed_last(k).wait_send()

    def drained(t, carry):
        key_send(t).wait_send()
        weight_send(t).wait_send()
        all_pass(e, t).wait_send()

        @pl.when(t > 0)
        def _():
            key_final(t).wait_send()
            weight_final(t).wait_send()
            all_send(t).wait_send()
            small_send(t).wait_send()

        return carry

    lax.fori_loop(0, half, drained, 0)


def return_layer(
    n, nz, gmid, mid, rgrad, ggrad, x, gain, wq, wk, wv, wo, cos, sin, q, kv, lrow, att, lens, mixed
):
    tok, width = x.shape
    rows = tok // nz
    qw, kw = wq.shape[1], wk.shape[1]
    seqs = lens.shape[0]
    span = tok // seqs
    half = n // 2
    stacked = (qw // kw) * span
    pack = 2 * qw + 2 * kw
    small_rows = rgrad.shape[0] + 16
    dma = pltpu.SemaphoreType.DMA
    vmem = pl.BlockSpec(memory_space=pltpu.VMEM)
    sds = jax.ShapeDtypeStruct
    zdma = dma((nz - 1,))
    hdma = dma((half,))
    fdma = dma((half - 1,))
    return pl.pallas_call(
        functools.partial(return_kernel, n, nz),
        out_shape=[
            sds((tok, width), f32),
            sds((tok, width), f32),
            sds((width, pack), f32),
            sds((small_rows, width), f32),
        ],
        in_specs=[vmem] * 16
        + [pl.BlockSpec(memory_space=pltpu.SMEM), pl.BlockSpec(memory_space=pl.ANY)],
        out_specs=[vmem] * 4,
        scratch_shapes=[
            pltpu.VMEM((width, qw + 2 * kw), bf16),
            pltpu.VMEM((tok, width), bf16),
            pltpu.VMEM((tok, width), bf16),
            pltpu.VMEM((tok, width), bf16),
            pltpu.VMEM((tok, qw), bf16),
            pltpu.VMEM((tok, qw), f32),
            pltpu.VMEM((stacked, HD), f32),
            pltpu.VMEM((seqs, n * span, 2 * kw), f32),
            pltpu.VMEM((half, seqs, span, 2 * kw), bf16),
            pltpu.VMEM((half, seqs, span, 2 * kw), bf16),
            pltpu.VMEM((half - 1, seqs, span, 2 * kw), bf16),
            pltpu.VMEM((half - 1, seqs, span, 2 * kw), bf16),
            pltpu.VMEM((tok, width), f32),
            pltpu.VMEM((nz - 1, rows, width), bf16),
            pltpu.VMEM((nz - 1, rows, width), bf16),
            pltpu.VMEM((n, width // n, pack), bf16),
            pltpu.VMEM((half, width // n, pack), bf16),
            pltpu.VMEM((half - 1, width // n, pack), bf16),
            pltpu.VMEM((half - 1, width // n, pack), bf16),
            pltpu.VMEM((n, width // n, pack), bf16),
            pltpu.VMEM((nz, small_rows, width), bf16),
            pltpu.VMEM((nz, 16, width), bf16),
            pltpu.VMEM((small_rows, width), bf16),
            pltpu.VMEM((small_rows, width), bf16),
            pltpu.VMEM((half, small_rows, width), bf16),
        ]
        + [zdma] * 12
        + [hdma, hdma, fdma, fdma]
        + [hdma, hdma, fdma, fdma]
        + [hdma] * 4
        + [dma, dma, fdma, fdma]
        + [
            pltpu.VMEM((half, nz, rows, width), bf16),
            pltpu.VMEM((nz - 1, rows, width), bf16),
            pltpu.VMEM((nz - 1, rows, width), bf16),
            fdma,
            fdma,
            zdma,
            zdma,
            dma,
        ],
        compiler_params=pltpu.CompilerParams(
            collective_id=3, has_side_effects=True, vmem_limit_bytes=56 << 20
        ),
        name="attend_back",
    )(
        gmid,
        mid,
        rgrad,
        ggrad,
        x,
        gain[None],
        wq,
        wk,
        wv,
        wo,
        cos,
        sin,
        q,
        kv,
        lrow,
        att,
        lens,
        mixed,
    )


def shards(
    inputs,
    attention_gain,
    query_weight,
    key_weight,
    value_weight,
    out_weight,
    expert_gain,
    router_weight,
    gate_weight,
    up_weight,
    down_weight,
    routes,
    seq_lens,
    cotangent,
):
    n = lax.axis_size("expert")
    nz = lax.axis_size("tensor")
    tok_rows = inputs.shape[0]
    seq_count = seq_lens.shape[0]
    span_rows = tok_rows // seq_count
    query_width = query_weight.shape[1]
    key_width = key_weight.shape[1]
    experts = router_weight.shape[1]
    local_pos = lax.axis_index("expert") * span_rows + jnp.arange(span_rows, dtype=jnp.int32)
    frequency = THETA ** (-2.0 * jnp.arange(HD // 2, dtype=jnp.float32) / HD)
    angles = local_pos.astype(f32)[:, None] * frequency[None, :]
    cosines = jnp.tile(jnp.cos(angles), (seq_count, 4))
    sines = jnp.tile(jnp.sin(angles), (seq_count, 4))
    cot_all = lax.all_gather(cotangent.astype(bf16), "expert", axis=0, tiled=True)
    weights = (query_weight, key_weight, value_weight, out_weight, cosines, sines)
    middle, queries, pairs, logs, attended = attend_layer(
        n, nz, inputs, attention_gain, *weights, seq_lens
    )
    (
        grad_middle,
        router_part,
        expert_gain_part,
        expert_load,
        gate_grad,
        up_grad,
        down_grad,
        mixed,
    ) = expert_layer(
        n,
        nz,
        middle,
        expert_gain,
        router_weight,
        routes,
        gate_weight,
        up_weight,
        down_weight,
        cotangent,
        cot_all,
    )
    output, input_grad, packed, small = return_layer(
        n,
        nz,
        grad_middle,
        middle,
        router_part,
        expert_gain_part,
        inputs,
        attention_gain,
        *weights,
        queries,
        pairs,
        logs,
        attended,
        seq_lens,
        mixed,
    )
    cuts = (query_width, query_width + key_width, query_width + 2 * key_width)
    return (
        output,
        input_grad,
        jnp.mean(expert_load),
        expert_load[0],
        small[experts + 1],
        packed[:, : cuts[0]],
        packed[:, cuts[0] : cuts[1]],
        packed[:, cuts[1] : cuts[2]],
        packed[:, cuts[2] :].T,
        small[experts],
        small[:experts].T,
        gate_grad,
        up_grad,
        down_grad.reshape(down_weight.shape),
    )


def solution(mesh):
    placed = (
        P("expert", None),
        P(),
        P(None, "tensor"),
        P(None, "tensor"),
        P(None, "tensor"),
        P("tensor", None),
        P(),
        P(),
        P("expert", None, "tensor"),
        P("expert", None, "tensor"),
        P("expert", "tensor", None),
        P("expert", None),
        P(),
        P("expert", None),
    )
    return jax.shard_map(
        shards,
        mesh=mesh,
        in_specs=placed,
        out_specs=(
            P("expert", None),
            P("expert", None),
            P(),
            P(),
            P(),
            P(None, "tensor"),
            P(None, "tensor"),
            P(None, "tensor"),
            P("tensor", None),
            P(),
            P(),
            P("expert", None, "tensor"),
            P("expert", None, "tensor"),
            P("expert", "tensor", None),
        ),
        check_vma=False,
    )
```

```python
import functools

import jax
import jax.numpy as jnp
from jax import lax
from jax.experimental import pallas as pl
from jax.experimental.pallas import tpu as pltpu
from jax.sharding import PartitionSpec as P

HD = 64
EPS = 1e-06
THETA = 10000.0
MESH = pl.DeviceIdType.MESH
f32 = jnp.float32
bf16 = jnp.bfloat16


def dot_nn(left, right):
    return lax.dot_general(left, right, (((1,), (0,)), ((), ())), preferred_element_type=f32)


def dot_nt(left, right):
    return lax.dot_general(left, right, (((1,), (1,)), ((), ())), preferred_element_type=f32)


def dot_tn(left, right):
    return lax.dot_general(left, right, (((0,), (0,)), ((), ())), preferred_element_type=f32)


def remote(src, dst, send_sem, recv_sem, device):
    return pltpu.make_async_remote_copy(
        src_ref=src,
        dst_ref=dst,
        send_sem=send_sem,
        recv_sem=recv_sem,
        device_id=device,
        device_id_type=MESH,
    )


def turn(values, cos, sin, last, forward):
    lane = lax.broadcasted_iota(jnp.int32, (values.shape[0], 128), 1)
    first_half = lax.rem(lane, HD) < HD // 2
    parts = []
    for g in range(values.shape[1] // 128):
        v = values[:, g * 128 : (g + 1) * 128]
        if g * 128 >= last:
            parts.append(v)
            continue
        turned = jnp.where(
            first_half, -pltpu.roll(v, 128 - HD // 2, 1), pltpu.roll(v, HD // 2, 1)
        )
        new = v * cos + turned * sin if forward else v * cos - turned * sin
        if (g + 1) * 128 > last:
            new = jnp.where(lane + g * 128 < last, new, v)
        parts.append(new)
    return jnp.concatenate(parts, 1) if len(parts) > 1 else parts[0]


def greet(n, nz, e, z, sib):
    barrier = pltpu.get_barrier_semaphore()
    pl.semaphore_signal(barrier, inc=1, device_id=(sib, z), device_id_type=MESH)
    for s in range(1, n // 2):
        pl.semaphore_signal(
            barrier, inc=1, device_id=(lax.rem(e + 2 * s, n), z), device_id_type=MESH
        )
    for k in range(1, nz):
        pl.semaphore_signal(barrier, inc=1, device_id=(e, lax.rem(z + k, nz)), device_id_type=MESH)
    return barrier


def expert_kernel(
    n,
    nz,
    big,
    mid_ref,
    gain_ref,
    router_ref,
    routes_ref,
    cot_ref,
    gate_hbm,
    up_hbm,
    down_hbm,
    cot_all,
    *rest,
):
    outs, rest = rest[:9], rest[9:]
    gmid_ref, glog_ref, ggrad_ref, load_ref = outs[:4]
    dgate_hbm, dup_hbm, ddown_hbm, mixed_hbm, normed_hbm = outs[4:]
    xbuf, rest = rest[0], rest[1:]
    if big:
        xstage, rest = rest[0], rest[1:]
    (
        wbuf,
        xn_s,
        wg,
        wu,
        down_ref,
        dgate,
        dup,
        ddown,
        cbuf,
        dg_s,
        du_s,
        wi_s,
        hold,
        osend,
        sin,
        hold_o,
        osend_o,
        sin_o,
        hold_g,
        osend_g,
        sin_g,
        own_s,
        own_g,
        fsend,
        fin,
        fsend_g,
        fin_g,
        zsend,
        zin,
        zsend_g,
        zin_g,
        wsem,
        gsem,
        csem,
        msem,
        lsem,
        zs,
        zr,
        zws,
        zwr,
        xs,
        xr,
        ws,
        wr,
        fs,
        fr,
        wfs,
        wfr,
        gs,
        gr,
        oss,
        osr,
        ggs,
        ggr,
        ps,
        pr,
        pgs,
        pgr,
        zgs,
        zgr,
        zggs,
        zggr,
    ) = rest
    e = lax.axis_index("expert")
    z = lax.axis_index("tensor")
    core = lax.rem(e, 2)
    other = 1 - core
    me = e // 2
    sib = e + 1 - 2 * core
    half = n // 2
    rows, width = mid_ref.shape
    tok = rows * nz
    experts = router_ref.shape[1]
    local_experts, _, hid = gate_hbm.shape
    inner_w = local_experts * hid
    fc = min(inner_w, 256)
    fslots = fsend.shape[0]

    loads = []
    for el in range(local_experts):
        cols = pl.ds(el * hid, hid)
        loads.append(pltpu.make_async_copy(gate_hbm.at[el], wg.at[:, cols], wsem.at[0, el]))
        loads.append(pltpu.make_async_copy(up_hbm.at[el], wu.at[:, cols], wsem.at[1, el]))
    loads.append(pltpu.make_async_copy(down_hbm, down_ref, wsem.at[2, 0]))
    for copy in loads:
        copy.start()

    def piece_of(g):
        return lax.rem(z + nz - g, nz)

    def cot_start(g, parity, slot):
        zz = piece_of(g)
        for h in range(half):
            start = (2 * h + parity) * tok + zz * rows
            pltpu.make_async_copy(
                cot_all.at[pl.ds(pl.multiple_of(start, 16), rows)],
                cbuf.at[slot, pl.ds(h * rows, rows)],
                csem.at[slot],
            ).start()

    def cot_wait(slot):
        pltpu.make_async_copy(
            cot_all.at[pl.ds(0, half * rows)], cbuf.at[slot], csem.at[slot]
        ).wait()

    cot_start(0, core, 0)
    barrier = greet(n, nz, e, z, sib)

    own_rows = pl.ds(pl.multiple_of(z * rows, 16), rows)
    my_rows = pl.ds(pl.multiple_of(me * rows, 16), rows)
    mid = mid_ref[...]
    scale2 = lax.rsqrt(jnp.mean(mid * mid, -1, keepdims=True) + EPS)
    xn = (mid * scale2 * gain_ref[...]).astype(bf16)
    xn_s[...] = xn
    logits = dot_nn(xn, router_ref[...])
    picks = routes_ref[own_rows, :]
    lanes = lax.broadcasted_iota(jnp.int32, (rows, experts), 1)
    chosen = jnp.zeros((rows, experts), f32)
    for k in range(picks.shape[1]):
        chosen = jnp.where(picks[:, k : k + 1] == lanes, 1.0, chosen)
    top = jnp.max(logits, -1, keepdims=True)
    powers = jnp.exp(logits - top)
    probs = powers / jnp.sum(powers, -1, keepdims=True)
    low_logits = jnp.where(chosen > 0.0, logits, -1e30)
    ctop = jnp.max(low_logits, -1, keepdims=True)
    cpow = jnp.exp(low_logits - ctop)
    comb = cpow / jnp.sum(cpow, -1, keepdims=True)
    padded = jnp.concatenate([comb, jnp.zeros((rows, 128 - experts), f32)], 1)
    if rows < 128:
        padded = jnp.concatenate([padded, jnp.zeros((128 - rows, 128), f32)], 0)
    piece = padded.T[:experts]
    lane_pad = jnp.zeros((1, 128 - experts), f32)
    cnt = jnp.concatenate([jnp.sum(chosen, 0, keepdims=True), lane_pad], 1)
    psum = jnp.concatenate([jnp.sum(probs, 0, keepdims=True), lane_pad], 1)
    psum_hi = psum.astype(bf16).astype(f32)
    stats = jnp.concatenate([cnt, psum_hi, psum - psum_hi, jnp.zeros((13, 128), f32)], 0)
    wbuf[z, core, me] = jnp.concatenate([piece, stats], 0).astype(bf16)
    if big:
        copy = pltpu.make_async_copy(xn_s, xbuf.at[z, core, my_rows], lsem)
        copy.start()
        copy.wait()
    else:
        xbuf[z, core, my_rows] = xn
    pl.semaphore_wait(barrier, half + nz - 1)

    def z_row(zz, k, to):
        ref = xbuf.at[zz, core, my_rows]
        return remote(ref, ref, zs.at[k - 1], zr.at[k - 1], (e, to))

    def z_small(zz, k, to):
        ref = wbuf.at[zz, core, me]
        return remote(ref, ref, zws.at[k - 1], zwr.at[k - 1], (e, to))

    def x_row(zz, h, g, s, to):
        ref = xbuf.at[zz, core, pl.ds(pl.multiple_of(h * rows, 16), rows)]
        return remote(ref, ref, xs.at[g, s], xr.at[g, s], (to, z))

    def x_small(zz, h, g, s, to):
        ref = wbuf.at[zz, core, h]
        return remote(ref, ref, ws.at[g, s], wr.at[g, s], (to, z))

    def push_piece(g):
        zz = piece_of(g)
        for s in range(1, half):
            to = lax.rem(e + 2 * s, n)
            x_row(zz, me, g, s, to).start()
            x_small(zz, me, g, s, to).start()

    push_piece(jnp.int32(0))
    for k in range(1, nz):
        z_row(z, k, lax.rem(z + k, nz)).start()
        z_small(z, k, lax.rem(z + k, nz)).start()

    dgate[...] = jnp.zeros_like(dgate)
    dup[...] = jnp.zeros_like(dup)
    ddown[...] = jnp.zeros_like(ddown)
    for copy in loads:
        copy.wait()

    sel_row = lax.broadcasted_iota(jnp.int32, (experts, fc), 0)
    sel_col = lax.broadcasted_iota(jnp.int32, (experts, fc), 1)

    def block(zz, parity, slot, dst, dst_o, dst_g, dslot):
        if big:
            copy = pltpu.make_async_copy(xbuf.at[zz, parity], xstage, lsem)
            copy.start()
            copy.wait()
            x_ref = xstage
        else:
            x_ref = xbuf.at[zz, parity]
        c_ref = cbuf.at[slot]
        sums = [jnp.zeros((experts, rows), f32) for _ in range(half)]
        for q in range(inner_w // fc):
            cols = slice(q * fc, (q + 1) * fc)
            x = x_ref[...]
            gate_val = dot_nn(x, wg[:, cols])
            up_val = dot_nn(x, wu[:, cols])
            back = dot_nt(c_ref[...], down_ref[cols, :])
            select = jnp.where(
                sel_row == e * local_experts + (q * fc + sel_col) // hid, 1.0, 0.0
            ).astype(bf16)
            wide = jnp.concatenate(
                [dot_tn(wbuf[zz, parity, h, :experts, :], select)[:rows] for h in range(half)], 0
            )
            sig = 1.0 / (1.0 + jnp.exp(-gate_val))
            silu = gate_val * sig
            inner = silu * up_val
            wi_s[:, cols] = (inner * wide).astype(bf16)
            scaled = back * wide
            dg_s[:, cols] = (scaled * up_val * (sig * (1.0 + gate_val * (1.0 - sig)))).astype(bf16)
            du_s[:, cols] = (scaled * silu).astype(bf16)
            both = (inner * back).astype(bf16)
            for h in range(half):
                sums[h] = sums[h] + dot_nt(select, both[h * rows : (h + 1) * rows])
        for h in range(half):
            gap = jnp.zeros((experts, 128 - rows), f32)
            dst_g[dslot, h] = jnp.concatenate([sums[h], gap], 1).astype(bf16)
        for h in range(width // 256):
            cols = slice(h * 256, (h + 1) * 256)
            dst[dslot, :, cols] = (
                dot_nt(dg_s[...], wg[cols, :]) + dot_nt(du_s[...], wu[cols, :])
            ).astype(bf16)
            dst_o[dslot, :, cols] = dot_nn(wi_s[...], down_ref[:, cols]).astype(bf16)
        for h in range(width // 256):
            cols = slice(h * 256, (h + 1) * 256)
            x_part = x_ref[:, cols]
            gate_part = dot_tn(x_part, dg_s[...])
            up_part = dot_tn(x_part, du_s[...])
            for el in range(local_experts):
                dgate[el, cols, :] += gate_part[:, el * hid : (el + 1) * hid]
                dup[el, cols, :] += up_part[:, el * hid : (el + 1) * hid]
            ddown[:, cols] += dot_tn(wi_s[...], c_ref[:, cols])

    def gives(slot):
        return [
            remote(osend.at[slot], sin.at[slot], gs.at[slot], gr.at[slot], (sib, z)),
            remote(osend_g.at[slot], sin_g.at[slot], ggs.at[slot], ggr.at[slot], (sib, z)),
            remote(osend_o.at[slot], sin_o.at[slot], oss.at[slot], osr.at[slot], (sib, z)),
        ]

    def finals(g, s, to):
        at = lax.rem(g, fslots)
        return [
            remote(
                fsend.at[at, s - 1], fin.at[g, s - 1], ps.at[g, s - 1], pr.at[g, s - 1], (to, z)
            ),
            remote(
                fsend_g.at[at, s - 1],
                fin_g.at[g, s - 1],
                pgs.at[g, s - 1],
                pgr.at[g, s - 1],
                (to, z),
            ),
        ]

    def lasts(k, to):
        return [
            remote(zsend.at[k - 1], zin.at[k - 1], zgs.at[k - 1], zgr.at[k - 1], (e, to)),
            remote(zsend_g.at[k - 1], zin_g.at[k - 1], zggs.at[k - 1], zggr.at[k - 1], (e, to)),
        ]

    def mixed_copy(g, slot):
        return pltpu.make_async_copy(hold_o.at[slot], mixed_hbm.at[piece_of(g)], msem.at[slot])

    def plane_stage(g):
        slot = lax.rem(g, 2)
        for copy in gives(slot):
            copy.wait_recv()
        if fslots < nz:

            @pl.when(g >= fslots)
            def _():
                for s in range(1, half):
                    for copy in finals(g - fslots, s, sib):
                        copy.wait_send()

        spot = lax.rem(g, fslots)
        for s in range(1, half):
            h = lax.rem(me + half - s, half)
            at = pl.ds(pl.multiple_of(h * rows, 16), rows)
            fsend[spot, s - 1] = (hold[slot, at, :].astype(f32) + sin[slot, at, :].astype(f32)).astype(
                bf16
            )
            fsend_g[spot, s - 1] = (hold_g[slot, h].astype(f32) + sin_g[slot, h].astype(f32)).astype(
                bf16
            )
            for copy in finals(g, s, lax.rem(e - 2 * s + n, n)):
                copy.start()
        own_s[g] = hold[slot, my_rows, :].astype(f32) + sin[slot, my_rows, :].astype(f32)
        own_g[g] = hold_g[slot, me].astype(f32) + sin_g[slot, me].astype(f32)
        hold_o[slot] = (hold_o[slot].astype(f32) + sin_o[slot].astype(f32)).astype(bf16)
        mixed_copy(g, slot).start()

    def tensor_stage(g):
        total = own_s[g]
        total_g = own_g[g]
        for s in range(1, half):
            for copy in finals(g, s, sib):
                copy.wait_recv()
            total = total + fin[g, s - 1].astype(f32)
            total_g = total_g + fin_g[g, s - 1].astype(f32)

        @pl.when(g == 0)
        def _():
            own_s[0] = total
            own_g[0] = total_g

        @pl.when(g > 0)
        def _():
            zsend[g - 1] = total.astype(bf16)
            zsend_g[g - 1] = total_g.astype(bf16)
            for copy in lasts(g, piece_of(g)):
                copy.start()

    def step(g, carry):
        zz = piece_of(g)
        slot = lax.rem(g, 2)

        @pl.when(g < nz - 1)
        def _():
            coming = piece_of(g + 1)
            z_row(coming, g + 1, coming).wait_recv()
            z_small(coming, g + 1, coming).wait_recv()
            push_piece(g + 1)

        for s in range(1, half):
            h = lax.rem(me + half - s, half)
            src = 2 * h + core
            x_row(zz, h, g, s, src).wait_recv()
            x_small(zz, h, g, s, src).wait_recv()
        for copy in forward(zz, core, g):
            copy.start()
        cot_start(g, other, 1)
        cot_wait(0)

        @pl.when(g >= 2)
        def _():
            mixed_copy(g - 2, slot).wait()

        block(zz, core, 0, hold, hold_o, hold_g, slot)

        @pl.when(g < nz - 1)
        def _():
            cot_start(g + 1, core, 0)

        @pl.when(g >= 2)
        def _():
            tensor_stage(g - 2)

        @pl.when(g >= 1)
        def _():
            plane_stage(g - 1)

        @pl.when(g >= 2)
        def _():
            for copy in gives(slot):
                copy.wait_send()

        for copy in forward(zz, other, g):
            copy.wait_recv()
        cot_wait(1)
        block(zz, other, 1, osend, osend_o, osend_g, slot)
        for copy in gives(slot):
            copy.start()
        return carry

    def forward(zz, parity, g):
        ref = xbuf.at[zz, parity]
        small = wbuf.at[zz, parity]
        return (
            remote(ref, ref, fs.at[g], fr.at[g], (sib, z)),
            remote(small, small, wfs.at[g], wfr.at[g], (sib, z)),
        )

    lax.fori_loop(0, nz, step, 0)
    grads = [
        pltpu.make_async_copy(dgate, dgate_hbm, gsem.at[0]),
        pltpu.make_async_copy(dup, dup_hbm, gsem.at[1]),
        pltpu.make_async_copy(ddown, ddown_hbm, gsem.at[2]),
        pltpu.make_async_copy(xbuf.at[:, core, my_rows, :], normed_hbm, gsem.at[3]),
    ]
    plane_stage(jnp.int32(nz - 1))
    for copy in grads:
        copy.start()
    if nz >= 2:
        tensor_stage(jnp.int32(nz - 2))

    def total_stats(j, carry):
        for zz in range(nz):
            for parity in range(2):
                carry = carry + wbuf[zz, parity, j, experts:, :].astype(f32)
        return carry

    stats = lax.fori_loop(0, half, total_stats, jnp.zeros((16, 128), f32))
    total_rows = n * tok
    share = stats[0:1, :experts] / (total_rows * routes_ref.shape[1])
    load_ref[...] = (
        experts * experts * share * ((stats[1:2, :experts] + stats[2:3, :experts]) / total_rows)
    )
    loss_w = experts * share / total_rows
    tensor_stage(jnp.int32(nz - 1))

    gate_sums = own_g[0]
    grad_rows = own_s[0]
    for k in range(1, nz):
        for copy in lasts(k, z):
            copy.wait_recv()
        gate_sums = gate_sums + zin_g[k - 1].astype(f32)
        grad_rows = grad_rows + zin[k - 1].astype(f32)
    grow = jnp.concatenate([gate_sums, jnp.zeros((128 - experts, 128), f32)], 0).T
    grad_gates = grow[:rows, :experts]
    grad_logits = comb * (grad_gates - jnp.sum(grad_gates * comb, -1, keepdims=True))
    grad_logits = grad_logits + probs * (loss_w - jnp.sum(loss_w * probs, -1, keepdims=True))
    low_grad = grad_logits.astype(bf16)
    wide_grad = jnp.concatenate([grad_logits, jnp.zeros((rows, 128 - experts), f32)], 1)
    if rows < 128:
        wide_grad = jnp.concatenate([wide_grad, jnp.zeros((128 - rows, 128), f32)], 0)
    glog_ref[...] = wide_grad.T[:experts].astype(bf16)
    grad_rows = grad_rows + dot_nt(low_grad, router_ref[...])
    mid = mid_ref[...]
    ggrad_ref[...] = jnp.sum(grad_rows * mid * scale2, 0, keepdims=True)
    gained = grad_rows * gain_ref[...]
    gmid_ref[...] = (
        cot_ref[own_rows, :]
        + scale2 * gained
        - mid * (scale2 * scale2 * scale2) * jnp.mean(gained * mid, -1, keepdims=True)
    )

    for copy in grads:
        copy.wait()
    for k in range(1, nz):
        z_row(z, k, z).wait_send()
        z_small(z, k, z).wait_send()
        for copy in lasts(k, z):
            copy.wait_send()
    for g in range(max(0, nz - 2), nz):
        mixed_copy(jnp.int32(g), g % 2).wait()
        for copy in gives(g % 2):
            copy.wait_send()

    def drained(g, carry):
        for s in range(1, half):
            x_row(z, me, g, s, sib).wait_send()
            x_small(z, me, g, s, sib).wait_send()
        for copy in forward(z, core, g):
            copy.wait_send()
        return carry

    lax.fori_loop(0, nz, drained, 0)

    def sums_sent(g, carry):
        for s in range(1, half):
            for copy in finals(g, s, sib):
                copy.wait_send()
        return carry

    lax.fori_loop(nz - fslots, nz, sums_sent, 0)


def expert_layer(n, nz, mid, gain, router, routes, gate, up, down, cot, cot_all):
    rows, width = mid.shape
    experts = router.shape[1]
    local_experts, _, hid = gate.shape
    inner_w = local_experts * hid
    half = n // 2
    batch = half * rows
    big = n > 8
    fslots = 2 if big else nz
    dma = pltpu.SemaphoreType.DMA
    vmem = pl.BlockSpec(memory_space=pltpu.VMEM)
    hbm = pl.BlockSpec(memory_space=pl.ANY)
    sds = jax.ShapeDtypeStruct
    out_shape = [
        sds((rows, width), f32),
        sds((experts, 128), bf16),
        sds((1, width), f32),
        sds((1, experts), f32),
        sds((local_experts, width, hid), f32),
        sds((local_experts, width, hid), f32),
        sds((inner_w, width), f32),
        sds((nz, batch, width), bf16),
        sds((nz, rows, width), bf16),
    ]
    out_specs = [vmem] * 4 + [hbm] * 5
    scratch = []
    if big:
        out_shape.append(sds((nz, 2, batch, width), bf16))
        out_specs.append(hbm)
        scratch.append(pltpu.VMEM((batch, width), bf16))
    else:
        scratch.append(pltpu.VMEM((nz, 2, batch, width), bf16))
    pair = pltpu.VMEM((2, batch, width), bf16)
    small = pltpu.VMEM((2, half, experts, 128), bf16)
    scratch += [
        pltpu.VMEM((nz, 2, half, experts + 16, 128), bf16),
        pltpu.VMEM((rows, width), bf16),
        pltpu.VMEM((width, inner_w), bf16),
        pltpu.VMEM((width, inner_w), bf16),
        pltpu.VMEM((inner_w, width), bf16),
        pltpu.VMEM((local_experts, width, hid), f32),
        pltpu.VMEM((local_experts, width, hid), f32),
        pltpu.VMEM((inner_w, width), f32),
        pair,
        pltpu.VMEM((batch, inner_w), bf16),
        pltpu.VMEM((batch, inner_w), bf16),
        pltpu.VMEM((batch, inner_w), bf16),
        pair,
        pair,
        pair,
        pair,
        pair,
        pair,
        small,
        small,
        small,
        pltpu.VMEM((nz, rows, width), f32),
        pltpu.VMEM((nz, experts, 128), f32),
        pltpu.VMEM((fslots, half - 1, rows, width), bf16),
        pltpu.VMEM((nz, half - 1, rows, width), bf16),
        pltpu.VMEM((fslots, half - 1, experts, 128), bf16),
        pltpu.VMEM((nz, half - 1, experts, 128), bf16),
        pltpu.VMEM((nz - 1, rows, width), bf16),
        pltpu.VMEM((nz - 1, rows, width), bf16),
        pltpu.VMEM((nz - 1, experts, 128), bf16),
        pltpu.VMEM((nz - 1, experts, 128), bf16),
        dma((3, local_experts)),
        dma((4,)),
        dma((2,)),
        dma((2,)),
        dma,
    ]
    scratch += [dma((nz - 1,))] * 4
    scratch += [dma((nz, half))] * 4
    scratch += [dma((nz,))] * 4
    scratch += [dma((2,))] * 6
    scratch += [dma((nz, half - 1))] * 4
    scratch += [dma((nz - 1,))] * 4
    return pl.pallas_call(
        functools.partial(expert_kernel, n, nz, big),
        out_shape=out_shape,
        in_specs=[vmem] * 5 + [hbm] * 4,
        out_specs=out_specs,
        scratch_shapes=scratch,
        compiler_params=pltpu.CompilerParams(
            collective_id=1, has_side_effects=True, vmem_limit_bytes=60 << 20
        ),
        name="experts",
    )(mid, gain[None], router, routes, cot, gate, up, down.reshape(inner_w, width), cot_all)[:9]


def attend_kernel(
    n,
    nz,
    x_ref,
    gain_ref,
    wq_ref,
    wk_ref,
    wv_ref,
    wo_ref,
    cos_ref,
    sin_ref,
    lens_ref,
    mid_ref,
    q_ref,
    kv_ref,
    lrow_ref,
    att_ref,
    wqkv,
    part,
    m_s,
    l_s,
    o_s,
    zsend,
    zin,
    ks,
    kr,
    kfs,
    kfr,
    zgs,
    zgr,
):
    e = lax.axis_index("expert")
    z = lax.axis_index("tensor")
    sib = e + 1 - 2 * lax.rem(e, 2)
    half = n // 2
    tok, width = x_ref.shape
    rows = tok // nz
    qw = wq_ref.shape[1]
    kw = wk_ref.shape[1]
    seqs = kv_ref.shape[0]
    span = tok // seqs
    heads = kw // HD
    groups = qw // kw
    barrier = greet(n, nz, e, z, sib)

    wqkv[:, 0:qw] = wq_ref[...]
    wqkv[:, qw : qw + kw] = wk_ref[...]
    wqkv[:, qw + kw :] = wv_ref[...]
    x = x_ref[...].astype(f32)
    scale1 = lax.rsqrt(jnp.mean(x * x, -1, keepdims=True) + EPS)
    normed = (x * scale1 * gain_ref[...]).astype(bf16)
    lin = dot_nn(normed, wqkv[...])
    turned = turn(lin, cos_ref[...], sin_ref[...], qw + kw, True).astype(bf16)
    q_ref[...] = turned[:, :qw]
    for s in range(seqs):
        kv_ref[s, pl.ds(pl.multiple_of(e * span, 16), span)] = turned[
            s * span : (s + 1) * span, qw:
        ]
    pl.semaphore_wait(barrier, half + nz - 1)

    def rows_of(j, s):
        return kv_ref.at[s, pl.ds(pl.multiple_of(j * span, 16), span)]

    for t in range(1, half):
        to = (lax.rem(e + 2 * t, n), z)
        for s in range(seqs):
            remote(rows_of(e, s), rows_of(e, s), ks.at[t, s], kr.at[t, s], to).start()
    for s in range(seqs):
        remote(rows_of(e, s), rows_of(e, s), kfs.at[0, s], kfr.at[0, s], (sib, z)).start()

    def forward(t, carry):
        src = lax.rem(e - 2 * t + n, n)
        for s in range(seqs):
            remote(rows_of(src, s), rows_of(src, s), ks.at[t, s], kr.at[t, s], (src, z)).wait_recv()
            remote(rows_of(src, s), rows_of(src, s), kfs.at[t, s], kfr.at[t, s], (sib, z)).start()
        return carry

    lax.fori_loop(1, half, forward, 0)

    def arrive(t, carry):
        src = lax.rem(sib - 2 * t + n, n)
        for s in range(seqs):
            remote(
                rows_of(src, s), rows_of(src, s), kfs.at[t, s], kfr.at[t, s], (sib, z)
            ).wait_recv()
        return carry

    lax.fori_loop(0, half, arrive, 0)

    ck = 2 * span
    trip = (e * span + span - 1) // ck + 1
    stacked = groups * span
    qpos = lax.broadcasted_iota(jnp.int32, (stacked, ck), 0)
    qpos = e * span + lax.rem(qpos, span)
    kiota = lax.broadcasted_iota(jnp.int32, (stacked, ck), 1)
    for s in range(seqs):
        for h in range(heads):
            srows = slice(s * span, (s + 1) * span)
            qst = jnp.concatenate(
                [
                    q_ref[srows, (h * groups + g) * HD : (h * groups + g + 1) * HD]
                    for g in range(groups)
                ],
                0,
            )
            m_s[...] = jnp.full_like(m_s, -1e30)
            l_s[...] = jnp.zeros_like(l_s)
            o_s[...] = jnp.zeros_like(o_s)

            def chunk(c, carry):
                at = pl.ds(pl.multiple_of(c * ck, 16), ck)
                keys = kv_ref[s, at, h * HD : (h + 1) * HD]
                vals = kv_ref[s, at, kw + h * HD : kw + (h + 1) * HD]
                scores = dot_nt(qst, keys) * HD ** (-0.5)
                kpos = kiota + c * ck
                scores = jnp.where((kpos <= qpos) & (kpos < lens_ref[s]), scores, -1e30)
                old = m_s[:, 0:1]
                new = jnp.maximum(old, jnp.max(scores, -1, keepdims=True))
                weights = jnp.exp(scores - new)
                shrink = jnp.exp(old - new)
                m_s[...] = jnp.broadcast_to(new, m_s.shape)
                l_s[...] = l_s[...] * shrink + jnp.sum(weights, -1, keepdims=True)
                o_s[...] = o_s[...] * shrink + dot_nn(weights.astype(bf16), vals)
                return carry

            lax.fori_loop(0, trip, chunk, 0)
            result = o_s[...] / l_s[:, 0:HD]
            for g in range(groups):
                cols = slice((h * groups + g) * HD, (h * groups + g + 1) * HD)
                att_ref[srows, cols] = result[g * span : (g + 1) * span]
            logs = m_s[...] + jnp.log(l_s[...])
            lrow_ref[s * heads + h] = logs.T[0:8]

    part[...] = dot_nn(att_ref[...].astype(bf16), wo_ref[...])
    for k in range(1, nz):
        zz = lax.rem(z + k, nz)
        zsend[k - 1] = part[pl.ds(pl.multiple_of(zz * rows, 16), rows), :].astype(bf16)
        remote(zsend.at[k - 1], zin.at[k - 1], zgs.at[k - 1], zgr.at[k - 1], (e, zz)).start()
    own_rows = pl.ds(pl.multiple_of(z * rows, 16), rows)
    mid = x_ref[own_rows, :].astype(f32) + part[own_rows, :]
    for k in range(1, nz):
        remote(zsend.at[k - 1], zin.at[k - 1], zgs.at[k - 1], zgr.at[k - 1], (e, z)).wait_recv()
        mid = mid + zin[k - 1].astype(f32)
    mid_ref[...] = mid
    for k in range(1, nz):
        remote(zsend.at[k - 1], zin.at[k - 1], zgs.at[k - 1], zgr.at[k - 1], (e, z)).wait_send()

    def sent(t, carry):
        for s in range(seqs):

            @pl.when(t > 0)
            def _():
                remote(
                    rows_of(e, s), rows_of(e, s), ks.at[t, s], kr.at[t, s], (sib, z)
                ).wait_send()

            remote(rows_of(e, s), rows_of(e, s), kfs.at[t, s], kfr.at[t, s], (sib, z)).wait_send()
        return carry

    lax.fori_loop(0, half, sent, 0)


def attend_layer(n, nz, x, gain, wq, wk, wv, wo, cos, sin, lens):
    tok, width = x.shape
    rows = tok // nz
    qw, kw = wq.shape[1], wk.shape[1]
    seqs = lens.shape[0]
    span = tok // seqs
    half = n // 2
    stacked = (qw // kw) * span
    dma = pltpu.SemaphoreType.DMA
    vmem = pl.BlockSpec(memory_space=pltpu.VMEM)
    sds = jax.ShapeDtypeStruct
    return pl.pallas_call(
        functools.partial(attend_kernel, n, nz),
        out_shape=[
            sds((rows, width), f32),
            sds((tok, qw), bf16),
            sds((seqs, n * span, 2 * kw), bf16),
            sds((seqs * (kw // HD), 8, stacked), f32),
            sds((tok, qw), f32),
        ],
        in_specs=[vmem] * 8 + [pl.BlockSpec(memory_space=pltpu.SMEM)],
        out_specs=[vmem] * 5,
        scratch_shapes=[
            pltpu.VMEM((width, qw + 2 * kw), bf16),
            pltpu.VMEM((tok, width), f32),
            pltpu.VMEM((stacked, 128), f32),
            pltpu.VMEM((stacked, 128), f32),
            pltpu.VMEM((stacked, HD), f32),
            pltpu.VMEM((nz - 1, rows, width), bf16),
            pltpu.VMEM((nz - 1, rows, width), bf16),
        ]
        + [dma((half, seqs))] * 4
        + [dma((nz - 1,))] * 2,
        compiler_params=pltpu.CompilerParams(
            collective_id=2, has_side_effects=True, vmem_limit_bytes=48 << 20
        ),
        name="attend",
    )(x, gain[None], wq, wk, wv, wo, cos, sin, lens)


def return_kernel(
    n,
    nz,
    gmid_ref,
    mid_ref,
    glog_ref,
    ggrad_ref,
    xn_ref,
    x_ref,
    gain_ref,
    wq_ref,
    wk_ref,
    wv_ref,
    wo_ref,
    cos_ref,
    sin_ref,
    q_ref,
    kv_ref,
    lrow_ref,
    att_ref,
    lens_ref,
    mixed_hbm,
    obuf,
    igbuf,
    wall,
    wall2,
    small_ref,
    wqkv,
    gat,
    datt,
    dq_s,
    acc_q,
    dkv,
    kvo,
    kvi,
    kvf,
    kvr,
    part,
    sums,
    osums,
    csend,
    crecv,
    osend,
    orecv,
    wbufs,
    wbufs2,
    sz1,
    sz2,
    sown,
    ssib,
    schip,
    ofin,
    zas,
    zar,
    zos,
    zor,
    zis,
    zir,
    zps,
    zpr,
    zqs,
    zqr,
    z1s,
    z1r,
    z2s,
    z2r,
    kos,
    kor,
    kfs,
    kfr,
    wsems,
    wsems2,
    sbs,
    sbr,
    scs,
    scr,
    ofs,
    ofr,
    olsem,
):
    e = lax.axis_index("expert")
    z = lax.axis_index("tensor")
    core = lax.rem(e, 2)
    me = e // 2
    sib = e + 1 - 2 * core
    half = n // 2
    rows, width = gmid_ref.shape
    tok = rows * nz
    qw = wq_ref.shape[1]
    kw = wk_ref.shape[1]
    seqs = kv_ref.shape[0]
    span = tok // seqs
    heads = kw // HD
    groups = qw // kw
    dn = width // n
    experts = glog_ref.shape[0]
    own_rows = pl.ds(pl.multiple_of(z * rows, 16), rows)
    barrier = greet(n, nz, e, z, sib)
    w1 = PlaneSum(n, e, z, sib, wall, *wbufs, *wsems)
    w2 = PlaneSum(n, e, z, sib, wall2, *wbufs2, *wsems2)

    gat[own_rows, :] = gmid_ref[...].astype(bf16)
    sz1[z] = glog_ref[...]
    pl.semaphore_wait(barrier, half + nz - 1)

    def part_of(ref):
        return lambda zz: ref.at[pl.ds(pl.multiple_of(zz * rows, 16), rows)]

    def slot_of(ref):
        return lambda zz: ref.at[zz]

    gat_line = Line(z, nz, e, part_of(gat), zas, zar)
    out_line = Line(z, nz, e, part_of(obuf), zos, zor)
    igrad_line = Line(z, nz, e, part_of(igbuf), zis, zir)
    normed_sum = LineSum(z, nz, e, csend, crecv, zps, zpr)
    out_sum = LineSum(z, nz, e, osend, orecv, zqs, zqr)

    def z_copies(buf_of, send, recv):
        return [
            remote(
                buf_of(z), buf_of(z), send.at[k - 1], recv.at[k - 1], (e, lax.rem(z + k, nz))
            )
            for k in range(1, nz)
        ]

    def z_arrivals(buf_of, send, recv):
        return [
            remote(
                buf_of(lax.rem(z + nz - k, nz)),
                buf_of(lax.rem(z + nz - k, nz)),
                send.at[k - 1],
                recv.at[k - 1],
                (e, lax.rem(z + nz - k, nz)),
            )
            for k in range(1, nz)
        ]

    gat_line.start()
    for copy in z_copies(slot_of(sz1), z1s, z1r):
        copy.start()

    def mixed_send(t):
        h = lax.rem(me + half - t, half)
        return remote(
            mixed_hbm.at[:, pl.ds(pl.multiple_of(h * rows, 16), rows), :],
            ofin.at[t],
            ofs.at[t - 1],
            ofr.at[t - 1],
            (lax.rem(e - 2 * t + n, n), z),
        )

    for t in range(1, half):
        mixed_send(t).start()
    mixed_own = pltpu.make_async_copy(
        mixed_hbm.at[:, pl.ds(pl.multiple_of(me * rows, 16), rows), :], ofin.at[0], olsem
    )
    mixed_own.start()

    def mixed_sum(zz):
        total = ofin[0, zz].astype(f32)
        for t in range(1, half):
            total = total + ofin[t, zz].astype(f32)
        return total

    wqkv[:, 0:qw] = wq_ref[...]
    wqkv[:, qw : qw + kw] = wk_ref[...]
    wqkv[:, qw + kw :] = wv_ref[...]
    x = x_ref[...].astype(f32)
    scale1 = lax.rsqrt(jnp.mean(x * x, -1, keepdims=True) + EPS)
    normed = (x * scale1 * gain_ref[...]).astype(bf16)
    dkv[...] = jnp.zeros_like(dkv)

    for hop in range(1, nz):
        gat_line.hop(hop)
    datt[...] = dot_nt(gat[...], wo_ref[...]).astype(bf16)

    ck = 2 * span
    trip = (e * span + span - 1) // ck + 1
    stacked = groups * span
    kiota = lax.broadcasted_iota(jnp.int32, (ck, stacked), 0)
    qpos = e * span + lax.rem(lax.broadcasted_iota(jnp.int32, (ck, stacked), 1), span)
    for s in range(seqs):
        for h in range(heads):
            srows = slice(s * span, (s + 1) * span)

            def gather(ref):
                return jnp.concatenate(
                    [
                        ref[srows, (h * groups + g) * HD : (h * groups + g + 1) * HD]
                        for g in range(groups)
                    ],
                    0,
                )

            qst = gather(q_ref)
            dst = gather(datt)
            delta = jnp.sum(dst.astype(f32) * gather(att_ref), -1, keepdims=True)
            drow = jnp.broadcast_to(delta, (stacked, 128)).T[0:1]
            lrow = lrow_ref[s * heads + h, 0:1, :]
            acc_q[...] = jnp.zeros_like(acc_q)

            def chunk(c, carry):
                at = pl.ds(pl.multiple_of(c * ck, 16), ck)
                keys = kv_ref[s, at, h * HD : (h + 1) * HD]
                vals = kv_ref[s, at, kw + h * HD : kw + (h + 1) * HD]
                scores = dot_nt(keys, qst) * HD ** (-0.5)
                kpos = kiota + c * ck
                soft = jnp.where(
                    (kpos <= qpos) & (kpos < lens_ref[s]), jnp.exp(scores - lrow), 0.0
                )
                grad_probs = dot_nt(vals, dst)
                grad_scores = (soft * (grad_probs - drow)).astype(bf16)
                dkv[s, at, h * HD : (h + 1) * HD] = dot_nn(grad_scores, qst) * HD ** (-0.5)
                dkv[s, at, kw + h * HD : kw + (h + 1) * HD] = dot_nn(soft.astype(bf16), dst)
                acc_q[...] += dot_tn(grad_scores, keys)
                return carry

            lax.fori_loop(0, trip, chunk, 0)
            result = acc_q[...] * HD ** (-0.5)
            for g in range(groups):
                cols = slice((h * groups + g) * HD, (h * groups + g + 1) * HD)
                dq_s[srows, cols] = result[g * span : (g + 1) * span]

    def key_rows(j, s):
        return dkv[s, pl.ds(pl.multiple_of(j * span, 16), span), :]

    def key_send(t):
        return remote(kvo.at[t], kvi.at[t], kos.at[t], kor.at[t], (sib, z))

    def key_final(t):
        to = (lax.rem(e - 2 * t + n, n), z)
        return remote(kvf.at[t - 1], kvr.at[t - 1], kfs.at[t - 1], kfr.at[t - 1], to)

    def key_give(i, carry):
        t = half - 1 - i
        oth = lax.rem(sib - 2 * t + n, n)
        for s in range(seqs):
            kvo[t, s] = key_rows(oth, s).astype(bf16)
        key_send(t).start()
        return carry

    lax.fori_loop(0, half, key_give, 0)

    def key_pass(i, carry):
        t = half - 1 - i
        key_send(t).wait_recv()
        own = lax.rem(e - 2 * t + n, n)
        for s in range(seqs):
            kvf[t - 1, s] = (key_rows(own, s) + kvi[t, s].astype(f32)).astype(bf16)
        key_final(t).start()
        return carry

    cos, sin = cos_ref[...], sin_ref[...]
    gq = turn(dq_s[...], cos, sin, qw, False).astype(bf16)
    query_part = dot_tn(normed, gq)
    out_part = dot_tn(gat[...], att_ref[...].astype(bf16))
    for j in range(n):
        w1.pack[j, :, :qw] = query_part[j * dn : (j + 1) * dn].astype(bf16)
        w1.pack[j, :, qw:] = out_part[j * dn : (j + 1) * dn].astype(bf16)
    lax.fori_loop(0, half - 1, key_pass, 0)
    w1.give()

    mixed_own.wait()
    for t in range(1, half):
        mixed_send(t).wait_recv()
    out_sum.hop(0, mixed_sum)
    w1.spread()
    for copy in z_arrivals(slot_of(sz1), z1s, z1r):
        copy.wait_recv()
    rgrad = dot_nn(sz1[0][:, :rows], xn_ref[0])
    for zz in range(1, nz):
        rgrad = rgrad + dot_nn(sz1[zz][:, :rows], xn_ref[zz])
    sown[0:experts, :] = rgrad.astype(bf16)
    for hop in range(1, nz - 1):
        out_sum.hop(hop, mixed_sum)
    out_sum.total(osums, mixed_sum)
    obuf[own_rows, :] = (mid_ref[...] + osums[...]).astype(bf16)
    out_line.start()

    key_send(0).wait_recv()
    own_kv = [key_rows(e, s) + kvi[0, s].astype(f32) for s in range(seqs)]
    for t in range(1, half):
        key_final(t).wait_recv()
        for s in range(seqs):
            own_kv[s] = own_kv[s] + kvr[t - 1, s].astype(f32)
    gkv = turn(jnp.concatenate(own_kv, 0), cos, sin, kw, False).astype(bf16)
    part[...] = dot_nt(gq, wqkv[:, :qw]) + dot_nt(gkv, wqkv[:, qw:])

    def normed_part(zz):
        return part[pl.ds(pl.multiple_of(zz * rows, 16), rows), :]

    for hop in range(nz - 1):
        normed_sum.hop(hop, normed_part)
        out_line.hop(hop + 1)
        if hop == 0:
            again = jnp.sum(part[...] * x * scale1, 0, keepdims=True)
            sz2[z] = jnp.concatenate([again, ggrad_ref[...], jnp.zeros((14, width), f32)], 0).astype(
                bf16
            )
            for copy in z_copies(slot_of(sz2), z2s, z2r):
                copy.start()
            pair_part = dot_tn(normed, gkv)
            for j in range(n):
                w2.pack[j] = pair_part[j * dn : (j + 1) * dn].astype(bf16)
            w2.give()
            w1.total()
    w2.spread()
    normed_sum.total(sums, normed_part)

    own_x = x_ref[own_rows, :].astype(f32)
    own_scale = lax.rsqrt(jnp.mean(own_x * own_x, -1, keepdims=True) + EPS)
    grad_normed = sums[...]
    gained = grad_normed * gain_ref[...]
    igrad = (
        gmid_ref[...]
        + own_scale * gained
        - own_x
        * (own_scale * own_scale * own_scale)
        * jnp.mean(gained * own_x, -1, keepdims=True)
    )
    igbuf[own_rows, :] = igrad.astype(bf16)
    igrad_line.start()

    w1.forward()
    for copy in z_arrivals(slot_of(sz2), z2s, z2r):
        copy.wait_recv()
    second = sz2[0].astype(f32)
    for zz in range(1, nz):
        second = second + sz2[zz].astype(f32)
    sown[experts:, :] = second.astype(bf16)
    small_sib = remote(sown, ssib, sbs, sbr, (sib, z))
    small_sib.start()
    if nz > 2:
        igrad_line.hop(1)
    small_sib.wait_recv()
    schip[me] = (sown[...].astype(f32) + ssib[...].astype(f32)).astype(bf16)

    def small_send(t):
        to = (lax.rem(e + 2 * t, n), z)
        return remote(schip.at[me], schip.at[me], scs.at[t - 1], scr.at[t - 1], to)

    for t in range(1, half):
        small_send(t).start()

    w2.total()
    for hop in range(2, nz - 1):
        igrad_line.hop(hop)
    igrad_line.hop(nz - 1)

    w2.forward()
    for t in range(1, half):
        src = lax.rem(me + half - t, half)
        remote(
            schip.at[src], schip.at[src], scs.at[t - 1], scr.at[t - 1], (sib, z)
        ).wait_recv()
    small = schip[0].astype(f32)
    for t in range(1, half):
        small = small + schip[t].astype(f32)
    small_ref[...] = small

    w1.arrive()
    w2.arrive()
    for line in (gat_line, out_line, igrad_line, normed_sum, out_sum, w1, w2):
        line.drain()
    for copy in z_copies(slot_of(sz1), z1s, z1r) + z_copies(slot_of(sz2), z2s, z2r):
        copy.wait_send()
    small_sib.wait_send()
    for t in range(1, half):
        mixed_send(t).wait_send()

    def drained(t, carry):
        key_send(t).wait_send()

        @pl.when(t > 0)
        def _():
            key_final(t).wait_send()
            small_send(t).wait_send()

        return carry

    lax.fori_loop(0, half, drained, 0)


class PlaneSum:
    def __init__(self, n, e, z, sib, wall, pack, near, send, recv, *sems):
        self.n, self.e, self.z, self.sib, self.half = n, e, z, sib, n // 2
        self.wall, self.pack, self.near, self.send, self.recv = wall, pack, near, send, recv
        self.sems = sems

    def peer(self, base, t):
        return lax.rem(base - 2 * t + self.n, self.n)

    def near_copy(self, t):
        src = self.pack.at[self.peer(self.sib, t)]
        return remote(
            src, self.near.at[t], self.sems[0].at[t], self.sems[1].at[t], (self.sib, self.z)
        )

    def far_copy(self, t):
        return remote(
            self.send.at[t - 1],
            self.recv.at[t - 1],
            self.sems[2].at[t],
            self.sems[3].at[t],
            (self.peer(self.e, t), self.z),
        )

    def all_copy(self, src, t, to):
        ref = self.wall.at[src]
        return remote(ref, ref, self.sems[4].at[t], self.sems[5].at[t], (to, self.z))

    def pass_copy(self, src, t):
        ref = self.wall.at[src]
        return remote(ref, ref, self.sems[6].at[t], self.sems[7].at[t], (self.sib, self.z))

    def give(self):
        def one(i, carry):
            self.near_copy(self.half - 1 - i).start()
            return carry

        lax.fori_loop(0, self.half, one, 0)

    def spread(self):
        def one(i, carry):
            t = self.half - 1 - i
            self.near_copy(t).wait_recv()
            own = self.pack[self.peer(self.e, t)].astype(f32)
            self.send[t - 1] = (own + self.near[t].astype(f32)).astype(bf16)
            self.far_copy(t).start()
            return carry

        lax.fori_loop(0, self.half - 1, one, 0)

    def total(self):
        self.near_copy(0).wait_recv()
        total = self.pack[self.e].astype(f32) + self.near[0].astype(f32)
        for t in range(1, self.half):
            self.far_copy(t).wait_recv()
            total = total + self.recv[t - 1].astype(f32)
        self.wall[self.e] = total.astype(bf16)
        for t in range(1, self.half):
            self.all_copy(self.e, t, lax.rem(self.e + 2 * t, self.n)).start()
        self.pass_copy(self.e, 0).start()

    def forward(self):
        def one(t, carry):
            src = self.peer(self.e, t)
            self.all_copy(src, t, src).wait_recv()
            self.pass_copy(src, t).start()
            return carry

        lax.fori_loop(1, self.half, one, 0)

    def arrive(self):
        def one(t, carry):
            self.pass_copy(self.peer(self.sib, t), t).wait_recv()
            return carry

        lax.fori_loop(0, self.half, one, 0)

    def drain(self):
        def one(t, carry):
            self.near_copy(t).wait_send()
            self.pass_copy(self.e, t).wait_send()

            @pl.when(t > 0)
            def _():
                self.far_copy(t).wait_send()
                self.all_copy(self.e, t, self.sib).wait_send()

            return carry

        lax.fori_loop(0, self.half, one, 0)


class Line:
    def __init__(self, z, nz, e, buf_of, send, recv):
        self.z, self.nz, self.e = z, nz, e
        self.buf_of, self.send, self.recv = buf_of, send, recv

    def copy(self, way, piece):
        to = self.z + 1 if way == 0 else self.z - 1
        ref = self.buf_of(piece)
        return remote(ref, ref, self.send.at[way, piece], self.recv.at[way, piece], (self.e, to))

    def push(self, piece, ways=(0, 1)):
        for way in ways:

            @pl.when(self.z < self.nz - 1 if way == 0 else self.z > 0)
            def _():
                self.copy(way, piece).start()

    def start(self):
        self.push(self.z)

    def hop(self, i):
        @pl.when(self.z >= i)
        def _():
            self.copy(0, self.z - i).wait_recv()
            self.push(self.z - i, (0,))

        @pl.when(self.z + i <= self.nz - 1)
        def _():
            self.copy(1, self.z + i).wait_recv()
            self.push(self.z + i, (1,))

    def drain(self):
        for piece in range(self.nz):

            @pl.when((self.z >= piece) & (self.z < self.nz - 1))
            def _():
                self.copy(0, piece).wait_send()

            @pl.when((self.z <= piece) & (self.z > 0))
            def _():
                self.copy(1, piece).wait_send()


class LineSum:
    def __init__(self, z, nz, e, send_buf, recv_buf, send, recv):
        self.z, self.nz, self.e = z, nz, e
        self.send_buf, self.recv_buf, self.send, self.recv = send_buf, recv_buf, send, recv

    def copy(self, way, target):
        to = self.z + 1 if way == 0 else self.z - 1
        return remote(
            self.send_buf.at[way, target],
            self.recv_buf.at[way, target],
            self.send.at[way, target],
            self.recv.at[way, target],
            (self.e, to),
        )

    def hop(self, i, own_of):
        for way, target in ((0, self.nz - 1 - i), (1, i)):
            passes = self.z < target if way == 0 else self.z > target
            first = self.z == 0 if way == 0 else self.z == self.nz - 1
            inner = self.z > 0 if way == 0 else self.z < self.nz - 1

            @pl.when(passes & first)
            def _():
                self.send_buf[way, target] = own_of(target).astype(bf16)
                self.copy(way, target).start()

            @pl.when(passes & inner)
            def _():
                self.copy(way, target).wait_recv()
                self.send_buf[way, target] = (
                    own_of(target) + self.recv_buf[way, target].astype(f32)
                ).astype(bf16)
                self.copy(way, target).start()

    def total(self, ref, own_of):
        ref[...] = own_of(self.z)

        @pl.when(self.z > 0)
        def _():
            self.copy(0, self.z).wait_recv()
            ref[...] += self.recv_buf[0, self.z].astype(f32)

        @pl.when(self.z < self.nz - 1)
        def _():
            self.copy(1, self.z).wait_recv()
            ref[...] += self.recv_buf[1, self.z].astype(f32)

    def drain(self):
        for target in range(self.nz):

            @pl.when(self.z < target)
            def _():
                self.copy(0, target).wait_send()

            @pl.when(self.z > target)
            def _():
                self.copy(1, target).wait_send()


def return_layer(
    n, nz, gmid, mid, glog, ggrad, xn, x, gain, wq, wk, wv, wo, cos, sin, q, kv, lrow, att, lens, mixed
):
    tok, width = x.shape
    rows = tok // nz
    qw, kw = wq.shape[1], wk.shape[1]
    seqs = lens.shape[0]
    span = tok // seqs
    half = n // 2
    stacked = (qw // kw) * span
    experts = glog.shape[0]
    small_rows = experts + 16
    dma = pltpu.SemaphoreType.DMA
    vmem = pl.BlockSpec(memory_space=pltpu.VMEM)
    sds = jax.ShapeDtypeStruct
    zdma = dma((nz - 1,))
    line = dma((2, nz))
    hdma = dma((half,))
    fdma = dma((half - 1,))
    def plane_bufs(cols):
        return [
            pltpu.VMEM((n, width // n, cols), bf16),
            pltpu.VMEM((half, width // n, cols), bf16),
            pltpu.VMEM((half - 1, width // n, cols), bf16),
            pltpu.VMEM((half - 1, width // n, cols), bf16),
        ]

    line_buf = pltpu.VMEM((2, nz, rows, width), bf16)
    return pl.pallas_call(
        functools.partial(return_kernel, n, nz),
        out_shape=[
            sds((tok, width), bf16),
            sds((tok, width), bf16),
            sds((n, width // n, 2 * qw), bf16),
            sds((n, width // n, 2 * kw), bf16),
            sds((small_rows, width), f32),
        ],
        in_specs=[vmem] * 17
        + [pl.BlockSpec(memory_space=pltpu.SMEM), pl.BlockSpec(memory_space=pl.ANY)],
        out_specs=[vmem] * 5,
        scratch_shapes=[
            pltpu.VMEM((width, qw + 2 * kw), bf16),
            pltpu.VMEM((tok, width), bf16),
            pltpu.VMEM((tok, qw), bf16),
            pltpu.VMEM((tok, qw), f32),
            pltpu.VMEM((stacked, HD), f32),
            pltpu.VMEM((seqs, n * span, 2 * kw), f32),
            pltpu.VMEM((half, seqs, span, 2 * kw), bf16),
            pltpu.VMEM((half, seqs, span, 2 * kw), bf16),
            pltpu.VMEM((half - 1, seqs, span, 2 * kw), bf16),
            pltpu.VMEM((half - 1, seqs, span, 2 * kw), bf16),
            pltpu.VMEM((tok, width), f32),
            pltpu.VMEM((rows, width), f32),
            pltpu.VMEM((rows, width), f32),
            line_buf,
            line_buf,
            line_buf,
            line_buf,
            plane_bufs(2 * qw),
            plane_bufs(2 * kw),
            pltpu.VMEM((nz, experts, 128), bf16),
            pltpu.VMEM((nz, 16, width), bf16),
            pltpu.VMEM((small_rows, width), bf16),
            pltpu.VMEM((small_rows, width), bf16),
            pltpu.VMEM((half, small_rows, width), bf16),
            pltpu.VMEM((half, nz, rows, width), bf16),
        ]
        + [line] * 10
        + [zdma] * 4
        + [hdma, hdma, fdma, fdma]
        + [[hdma] * 8, [hdma] * 8]
        + [dma, dma, fdma, fdma]
        + [fdma, fdma, dma],
        compiler_params=pltpu.CompilerParams(
            collective_id=3, has_side_effects=True, vmem_limit_bytes=58 << 20
        ),
        name="attend_back",
    )(
        gmid,
        mid,
        glog,
        ggrad,
        xn,
        x,
        gain[None],
        wq,
        wk,
        wv,
        wo,
        cos,
        sin,
        q,
        kv,
        lrow,
        att,
        lens,
        mixed,
    )


def finish_kernel(
    out_low,
    igrad_low,
    wall,
    wall2,
    small,
    load,
    dgate_in,
    dup_in,
    ddown_in,
    out_ref,
    igrad_ref,
    q_ref,
    k_ref,
    v_ref,
    o_ref,
    router_ref,
    again_ref,
    egain_ref,
    loss_ref,
    load_ref,
    dgate,
    dup,
    ddown,
    dgate_s,
    dup_s,
    ddown_s,
    sems,
):
    pairs = ((dgate_in, dgate_s, dgate), (dup_in, dup_s, dup), (ddown_in, ddown_s, ddown))
    reads = [pltpu.make_async_copy(p[0], p[1], sems.at[0, i]) for i, p in enumerate(pairs)]
    writes = [pltpu.make_async_copy(p[1], p[2], sems.at[1, i]) for i, p in enumerate(pairs)]
    for copy in reads:
        copy.start()
    qw, kw = q_ref.shape[1], k_ref.shape[1]
    experts = load.shape[1]
    out_ref[...] = out_low[...].astype(f32)
    for read, write in zip(reads, writes):
        read.wait()
        write.start()
    igrad_ref[...] = igrad_low[...].astype(f32)
    chunks, dn, _ = wall.shape
    flat = wall[...].reshape(chunks * dn, 2 * qw).astype(f32)
    q_ref[...] = flat[:, :qw]
    o_ref[...] = flat[:, qw:].T
    flat = wall2[...].reshape(chunks * dn, 2 * kw).astype(f32)
    k_ref[...] = flat[:, :kw]
    v_ref[...] = flat[:, kw:]
    router_ref[...] = small[0:experts, :].T
    again_ref[...] = small[experts : experts + 1, :]
    egain_ref[...] = small[experts + 1 : experts + 2, :]
    load_ref[...] = load[...]
    loss_ref[...] = jnp.mean(load[...], -1, keepdims=True)
    for copy in writes:
        copy.wait()


def finish_layer(out_low, igrad_low, wall, wall2, small, load, dgate, dup, ddown, qw, kw):
    tok, width = out_low.shape
    experts = load.shape[1]
    vmem = pl.BlockSpec(memory_space=pltpu.VMEM)
    hbm = pl.BlockSpec(memory_space=pl.ANY)
    sds = jax.ShapeDtypeStruct
    return pl.pallas_call(
        finish_kernel,
        out_shape=[
            sds((tok, width), f32),
            sds((tok, width), f32),
            sds((width, qw), f32),
            sds((width, kw), f32),
            sds((width, kw), f32),
            sds((qw, width), f32),
            sds((width, experts), f32),
            sds((1, width), f32),
            sds((1, width), f32),
            sds((1, 1), f32),
            sds((1, experts), f32),
            sds(dgate.shape, f32),
            sds(dup.shape, f32),
            sds(ddown.shape, f32),
        ],
        in_specs=[vmem] * 6 + [hbm] * 3,
        out_specs=[vmem] * 11 + [hbm] * 3,
        scratch_shapes=[
            pltpu.VMEM(dgate.shape, f32),
            pltpu.VMEM(dup.shape, f32),
            pltpu.VMEM(ddown.shape, f32),
            pltpu.SemaphoreType.DMA((2, 3)),
        ],
        compiler_params=pltpu.CompilerParams(vmem_limit_bytes=48 << 20),
        name="finish",
    )(out_low, igrad_low, wall, wall2, small, load, dgate, dup, ddown)


def shards(
    inputs,
    attention_gain,
    query_weight,
    key_weight,
    value_weight,
    out_weight,
    expert_gain,
    router_weight,
    gate_weight,
    up_weight,
    down_weight,
    routes,
    seq_lens,
    cotangent,
):
    n = lax.axis_size("expert")
    nz = lax.axis_size("tensor")
    tok_rows = inputs.shape[0]
    seq_count = seq_lens.shape[0]
    span_rows = tok_rows // seq_count
    local_pos = lax.axis_index("expert") * span_rows + jnp.arange(span_rows, dtype=jnp.int32)
    frequency = THETA ** (-2.0 * jnp.arange(HD // 2, dtype=jnp.float32) / HD)
    angles = local_pos.astype(f32)[:, None] * frequency[None, :]
    cosines = jnp.tile(jnp.cos(angles), (seq_count, 4))
    sines = jnp.tile(jnp.sin(angles), (seq_count, 4))
    cot_all = lax.all_gather(cotangent.astype(bf16), "expert", axis=0, tiled=True)
    weights = (query_weight, key_weight, value_weight, out_weight, cosines, sines)
    middle, queries, pairs, logs, attended = attend_layer(
        n, nz, inputs, attention_gain, *weights, seq_lens
    )
    (
        grad_middle,
        logit_grads,
        expert_gain_part,
        expert_load,
        gate_grad,
        up_grad,
        down_grad,
        mixed,
        normed2,
    ) = expert_layer(
        n,
        nz,
        middle,
        expert_gain,
        router_weight,
        routes,
        gate_weight,
        up_weight,
        down_weight,
        cotangent,
        cot_all,
    )
    out_low, igrad_low, packed, packed2, small = return_layer(
        n,
        nz,
        grad_middle,
        middle,
        logit_grads,
        expert_gain_part,
        normed2,
        inputs,
        attention_gain,
        *weights,
        queries,
        pairs,
        logs,
        attended,
        seq_lens,
        mixed,
    )
    (
        output,
        input_grad,
        query_grad,
        key_grad,
        value_grad,
        out_weight_grad,
        router_grad,
        attention_gain_grad,
        expert_gain_grad,
        balance_loss,
        expert_load,
        gate_grad,
        up_grad,
        down_grad,
    ) = finish_layer(
        out_low,
        igrad_low,
        packed,
        packed2,
        small,
        expert_load,
        gate_grad,
        up_grad,
        down_grad,
        query_weight.shape[1],
        key_weight.shape[1],
    )
    return (
        output,
        input_grad,
        balance_loss[0, 0],
        expert_load[0],
        attention_gain_grad[0],
        query_grad,
        key_grad,
        value_grad,
        out_weight_grad,
        expert_gain_grad[0],
        router_grad,
        gate_grad,
        up_grad,
        down_grad.reshape(down_weight.shape),
    )


def solution(mesh):
    placed = (
        P("expert", None),
        P(),
        P(None, "tensor"),
        P(None, "tensor"),
        P(None, "tensor"),
        P("tensor", None),
        P(),
        P(),
        P("expert", None, "tensor"),
        P("expert", None, "tensor"),
        P("expert", "tensor", None),
        P("expert", None),
        P(),
        P("expert", None),
    )
    return jax.shard_map(
        shards,
        mesh=mesh,
        in_specs=placed,
        out_specs=(
            P("expert", None),
            P("expert", None),
            P(),
            P(),
            P(),
            P(None, "tensor"),
            P(None, "tensor"),
            P(None, "tensor"),
            P("tensor", None),
            P(),
            P(),
            P("expert", None, "tensor"),
            P("expert", None, "tensor"),
            P("expert", "tensor", None),
        ),
        check_vma=False,
    )
```

```python
import functools

import jax
import jax.numpy as jnp
from jax import lax
from jax.experimental import pallas as pl
from jax.experimental.pallas import tpu as pltpu
from jax.sharding import PartitionSpec as P

HD = 64
EPS = 1e-06
THETA = 10000.0
MESH = pl.DeviceIdType.MESH
f32 = jnp.float32
bf16 = jnp.bfloat16


def dot_nn(left, right):
    return lax.dot_general(left, right, (((1,), (0,)), ((), ())), preferred_element_type=f32)


def dot_nt(left, right):
    return lax.dot_general(left, right, (((1,), (1,)), ((), ())), preferred_element_type=f32)


def dot_tn(left, right):
    return lax.dot_general(left, right, (((0,), (0,)), ((), ())), preferred_element_type=f32)


def remote(src, dst, send_sem, recv_sem, device):
    return pltpu.make_async_remote_copy(
        src_ref=src,
        dst_ref=dst,
        send_sem=send_sem,
        recv_sem=recv_sem,
        device_id=device,
        device_id_type=MESH,
    )


def turn(values, cos, sin, last, forward):
    lane = lax.broadcasted_iota(jnp.int32, (values.shape[0], 128), 1)
    first_half = lax.rem(lane, HD) < HD // 2
    parts = []
    for g in range(values.shape[1] // 128):
        v = values[:, g * 128 : (g + 1) * 128]
        if g * 128 >= last:
            parts.append(v)
            continue
        turned = jnp.where(
            first_half, -pltpu.roll(v, 128 - HD // 2, 1), pltpu.roll(v, HD // 2, 1)
        )
        new = v * cos + turned * sin if forward else v * cos - turned * sin
        if (g + 1) * 128 > last:
            new = jnp.where(lane + g * 128 < last, new, v)
        parts.append(new)
    return jnp.concatenate(parts, 1) if len(parts) > 1 else parts[0]


def greet(n, nz, e, z, sib):
    barrier = pltpu.get_barrier_semaphore()
    pl.semaphore_signal(barrier, inc=1, device_id=(sib, z), device_id_type=MESH)
    for s in range(1, n // 2):
        pl.semaphore_signal(
            barrier, inc=1, device_id=(lax.rem(e + 2 * s, n), z), device_id_type=MESH
        )
    for k in range(1, nz):
        pl.semaphore_signal(barrier, inc=1, device_id=(e, lax.rem(z + k, nz)), device_id_type=MESH)
    return barrier


def expert_kernel(
    n,
    nz,
    big,
    mid_ref,
    gain_ref,
    router_ref,
    routes_ref,
    cot_ref,
    gate_hbm,
    up_hbm,
    down_hbm,
    cot_all,
    *rest,
):
    outs, rest = rest[:9], rest[9:]
    gmid_ref, glog_ref, ggrad_ref, load_ref = outs[:4]
    dgate_hbm, dup_hbm, ddown_hbm, mixed_hbm, normed_hbm = outs[4:]
    xbuf, rest = rest[0], rest[1:]
    if big:
        xstage, rest = rest[0], rest[1:]
    (
        wbuf,
        xn_s,
        wg,
        wu,
        down_ref,
        dgate,
        dup,
        ddown,
        cbuf,
        dg_s,
        du_s,
        wi_s,
        hold,
        osend,
        sin,
        hold_o,
        osend_o,
        sin_o,
        hold_g,
        osend_g,
        sin_g,
        own_s,
        own_g,
        fsend,
        fin,
        fsend_g,
        fin_g,
        zsend,
        zin,
        zsend_g,
        zin_g,
        wsem,
        gsem,
        csem,
        msem,
        lsem,
        zs,
        zr,
        zws,
        zwr,
        xs,
        xr,
        ws,
        wr,
        fs,
        fr,
        wfs,
        wfr,
        gs,
        gr,
        oss,
        osr,
        ggs,
        ggr,
        ps,
        pr,
        pgs,
        pgr,
        zgs,
        zgr,
        zggs,
        zggr,
        zds,
        zdr,
        picks_s,
    ) = rest
    e = lax.axis_index("expert")
    z = lax.axis_index("tensor")
    core = lax.rem(e, 2)
    other = 1 - core
    me = e // 2
    sib = e + 1 - 2 * core
    half = n // 2
    rows, width = mid_ref.shape
    tok = rows * nz
    experts = router_ref.shape[0]
    local_experts, _, hid = gate_hbm.shape
    inner_w = local_experts * hid
    fc = min(inner_w, 256)
    fslots = fsend.shape[0]
    square = half == 4
    chip_x = me + 1 - 2 * lax.rem(me, 2)
    chip_y = lax.rem(me + 2, 4)
    chip_d = 3 - me
    mid_row = rows // 2

    loads = []
    for el in range(local_experts):
        cols = pl.ds(el * hid, hid)
        loads.append(pltpu.make_async_copy(gate_hbm.at[el], wg.at[:, cols], wsem.at[0, el]))
        loads.append(pltpu.make_async_copy(up_hbm.at[el], wu.at[:, cols], wsem.at[1, el]))
    loads.append(pltpu.make_async_copy(down_hbm, down_ref, wsem.at[2, 0]))
    for copy in loads:
        copy.start()

    def piece_of(g):
        return lax.rem(z + nz - g, nz)

    def cot_start(g, parity, slot):
        zz = piece_of(g)
        for h in range(half):
            start = (2 * h + parity) * tok + zz * rows
            pltpu.make_async_copy(
                cot_all.at[pl.ds(pl.multiple_of(start, 16), rows)],
                cbuf.at[slot, pl.ds(h * rows, rows)],
                csem.at[slot],
            ).start()

    def cot_wait(slot):
        pltpu.make_async_copy(
            cot_all.at[pl.ds(0, half * rows)], cbuf.at[slot], csem.at[slot]
        ).wait()

    cot_start(0, core, 0)
    barrier = greet(n, nz, e, z, sib)

    own_rows = pl.ds(pl.multiple_of(z * rows, 16), rows)
    my_rows = pl.ds(pl.multiple_of(me * rows, 16), rows)
    mid = mid_ref[...]
    scale2 = lax.rsqrt(jnp.mean(mid * mid, -1, keepdims=True) + EPS)
    xn = (mid * scale2 * gain_ref[...]).astype(bf16)
    xn_s[...] = xn
    logits = dot_nt(xn, router_ref[...])
    choices = routes_ref[...].astype(f32)
    top_count = choices.shape[0]
    picks_s[...] = jnp.concatenate([choices, jnp.zeros((128 - top_count, tok), f32)], 0).T
    picks = picks_s[own_rows, 0:top_count].astype(jnp.int32)
    lanes = lax.broadcasted_iota(jnp.int32, (rows, experts), 1)
    chosen = jnp.zeros((rows, experts), f32)
    for k in range(picks.shape[1]):
        chosen = jnp.where(picks[:, k : k + 1] == lanes, 1.0, chosen)
    top = jnp.max(logits, -1, keepdims=True)
    powers = jnp.exp(logits - top)
    probs = powers / jnp.sum(powers, -1, keepdims=True)
    low_logits = jnp.where(chosen > 0.0, logits, -1e30)
    ctop = jnp.max(low_logits, -1, keepdims=True)
    cpow = jnp.exp(low_logits - ctop)
    comb = cpow / jnp.sum(cpow, -1, keepdims=True)
    padded = jnp.concatenate([comb, jnp.zeros((rows, 128 - experts), f32)], 1)
    if rows < 128:
        padded = jnp.concatenate([padded, jnp.zeros((128 - rows, 128), f32)], 0)
    piece = padded.T[:experts]
    lane_pad = jnp.zeros((1, 128 - experts), f32)
    cnt = jnp.concatenate([jnp.sum(chosen, 0, keepdims=True), lane_pad], 1)
    psum = jnp.concatenate([jnp.sum(probs, 0, keepdims=True), lane_pad], 1)
    psum_hi = psum.astype(bf16).astype(f32)
    stats = jnp.concatenate([cnt, psum_hi, psum - psum_hi, jnp.zeros((13, 128), f32)], 0)
    wbuf[z, core, me] = jnp.concatenate([piece, stats], 0).astype(bf16)
    if big:
        copy = pltpu.make_async_copy(xn_s, xbuf.at[z, core, my_rows], lsem)
        copy.start()
        copy.wait()
    else:
        xbuf[z, core, my_rows] = xn
    pl.semaphore_wait(barrier, half + nz - 1)

    def z_row(zz, k, to):
        ref = xbuf.at[zz, core, my_rows]
        return remote(ref, ref, zs.at[k - 1], zr.at[k - 1], (e, to))

    def z_small(zz, k, to):
        ref = wbuf.at[zz, core, me]
        return remote(ref, ref, zws.at[k - 1], zwr.at[k - 1], (e, to))

    def x_row(zz, h, g, s, to):
        ref = xbuf.at[zz, core, pl.ds(pl.multiple_of(h * rows, 16), rows)]
        return remote(ref, ref, xs.at[g, s], xr.at[g, s], (to, z))

    def x_small(zz, h, g, s, to):
        ref = wbuf.at[zz, core, h]
        return remote(ref, ref, ws.at[g, s], wr.at[g, s], (to, z))

    def x_part(zz, h, first, count, g, i, to):
        start = pl.multiple_of(h * rows + first, 16)
        ref = xbuf.at[zz, core, pl.ds(start, count)]
        return remote(ref, ref, xs.at[g, i], xr.at[g, i], (2 * to + core, z))

    def push_piece(g):
        zz = piece_of(g)
        if square:
            x_part(zz, me, 0, rows, g, 0, chip_x).start()
            x_part(zz, me, 0, rows, g, 1, chip_y).start()
        for s in range(1, half):
            to = lax.rem(e + 2 * s, n)
            if not square:
                x_row(zz, me, g, s, to).start()
            x_small(zz, me, g, s, to).start()

    def relays():
        low = x_part(z, chip_x, 0, mid_row, 0, 2, chip_y)
        high = x_part(z, chip_y, mid_row, rows - mid_row, 0, 3, chip_x)
        return low, high

    def z_diag(zz, k, to):
        ref = xbuf.at[zz, core, pl.ds(pl.multiple_of(chip_d * rows, 16), rows)]
        return remote(ref, ref, zds.at[k - 1], zdr.at[k - 1], (e, to))

    push_piece(jnp.int32(0))
    for k in range(1, nz):
        z_row(z, k, lax.rem(z + k, nz)).start()
        z_small(z, k, lax.rem(z + k, nz)).start()

    if square:
        low, high = relays()
        x_part(z, chip_x, 0, rows, 0, 0, chip_x).wait_recv()
        low.start()
        x_part(z, chip_y, 0, rows, 0, 1, chip_y).wait_recv()
        high.start()

    dgate[...] = jnp.zeros_like(dgate)
    dup[...] = jnp.zeros_like(dup)
    ddown[...] = jnp.zeros_like(ddown)
    for copy in loads:
        copy.wait()
    if square:
        x_part(z, chip_d, 0, mid_row, 0, 2, chip_y).wait_recv()
        x_part(z, chip_d, mid_row, rows - mid_row, 0, 3, chip_x).wait_recv()
        z_diag(z, 1, lax.rem(z + 1, nz)).start()

    sel_row = lax.broadcasted_iota(jnp.int32, (experts, fc), 0)
    sel_col = lax.broadcasted_iota(jnp.int32, (experts, fc), 1)

    def block(zz, parity, slot, dst, dst_o, dst_g, dslot):
        if big:
            copy = pltpu.make_async_copy(xbuf.at[zz, parity], xstage, lsem)
            copy.start()
            copy.wait()
            x_ref = xstage
        else:
            x_ref = xbuf.at[zz, parity]
        c_ref = cbuf.at[slot]
        sums = [jnp.zeros((experts, rows), f32) for _ in range(half)]
        for q in range(inner_w // fc):
            cols = slice(q * fc, (q + 1) * fc)
            x = x_ref[...]
            gate_val = dot_nn(x, wg[:, cols])
            up_val = dot_nn(x, wu[:, cols])
            back = dot_nt(c_ref[...], down_ref[cols, :])
            select = jnp.where(
                sel_row == e * local_experts + (q * fc + sel_col) // hid, 1.0, 0.0
            ).astype(bf16)
            wide = jnp.concatenate(
                [dot_tn(wbuf[zz, parity, h, :experts, :], select)[:rows] for h in range(half)], 0
            )
            sig = 1.0 / (1.0 + jnp.exp(-gate_val))
            silu = gate_val * sig
            inner = silu * up_val
            wi_s[:, cols] = (inner * wide).astype(bf16)
            scaled = back * wide
            dg_s[:, cols] = (scaled * up_val * (sig * (1.0 + gate_val * (1.0 - sig)))).astype(bf16)
            du_s[:, cols] = (scaled * silu).astype(bf16)
            both = (inner * back).astype(bf16)
            for h in range(half):
                sums[h] = sums[h] + dot_nt(select, both[h * rows : (h + 1) * rows])
        for h in range(half):
            gap = jnp.zeros((experts, 128 - rows), f32)
            dst_g[dslot, h] = jnp.concatenate([sums[h], gap], 1).astype(bf16)
        for h in range(width // 256):
            cols = slice(h * 256, (h + 1) * 256)
            dst[dslot, :, cols] = (
                dot_nt(dg_s[...], wg[cols, :]) + dot_nt(du_s[...], wu[cols, :])
            ).astype(bf16)
            dst_o[dslot, :, cols] = dot_nn(wi_s[...], down_ref[:, cols]).astype(bf16)
        for h in range(width // 256):
            cols = slice(h * 256, (h + 1) * 256)
            x_part = x_ref[:, cols]
            gate_part = dot_tn(x_part, dg_s[...])
            up_part = dot_tn(x_part, du_s[...])
            for el in range(local_experts):
                dgate[el, cols, :] += gate_part[:, el * hid : (el + 1) * hid]
                dup[el, cols, :] += up_part[:, el * hid : (el + 1) * hid]
            ddown[:, cols] += dot_tn(wi_s[...], c_ref[:, cols])

    def gives(slot):
        return [
            remote(osend.at[slot], sin.at[slot], gs.at[slot], gr.at[slot], (sib, z)),
            remote(osend_g.at[slot], sin_g.at[slot], ggs.at[slot], ggr.at[slot], (sib, z)),
            remote(osend_o.at[slot], sin_o.at[slot], oss.at[slot], osr.at[slot], (sib, z)),
        ]

    def finals(g, s, to):
        at = lax.rem(g, fslots)
        rows_copy = []
        if not square:
            rows_copy = [
                remote(
                    fsend.at[at, s - 1], fin.at[g, s - 1], ps.at[g, s - 1], pr.at[g, s - 1], (to, z)
                )
            ]
        return rows_copy + [
            remote(
                fsend_g.at[at, s - 1],
                fin_g.at[g, s - 1],
                pgs.at[g, s - 1],
                pgr.at[g, s - 1],
                (to, z),
            ),
        ]

    def half_copy(g, buf, upper, i, chip):
        first, count = (mid_row, rows - mid_row) if upper else (0, mid_row)
        return remote(
            fsend.at[g, buf, pl.ds(first, count)],
            fin.at[g, buf, pl.ds(first, count)],
            ps.at[g, i],
            pr.at[g, i],
            (2 * chip + core, z),
        )

    def half_copies(g):
        return [
            half_copy(g, 2, False, 0, chip_x),
            half_copy(g, 2, True, 1, chip_y),
            half_copy(g, 0, False, 2, chip_x),
            half_copy(g, 1, True, 3, chip_y),
            half_copy(g, 1, False, 4, chip_y),
            half_copy(g, 0, True, 5, chip_x),
        ]

    def chip_sum(slot, chip, upper):
        first, count = (mid_row, rows - mid_row) if upper else (0, mid_row)
        at = pl.ds(pl.multiple_of(chip * rows + first, 16), count)
        return hold[slot, at, :].astype(f32) + sin[slot, at, :].astype(f32)

    def direct_stage(g):
        slot = lax.rem(g, 2)
        copies = half_copies(g)
        fsend[g, 2, :mid_row] = chip_sum(slot, chip_d, False).astype(bf16)
        copies[0].start()
        fsend[g, 2, mid_row:] = chip_sum(slot, chip_d, True).astype(bf16)
        copies[1].start()
        fsend[g, 0, :mid_row] = chip_sum(slot, chip_x, False).astype(bf16)
        copies[2].start()
        fsend[g, 1, mid_row:] = chip_sum(slot, chip_y, True).astype(bf16)
        copies[3].start()

    def relay_stage(g):
        slot = lax.rem(g, 2)
        copies = half_copies(g)
        copies[0].wait_recv()
        passed = chip_sum(slot, chip_y, False) + fin[g, 2, :mid_row].astype(f32)
        fsend[g, 1, :mid_row] = passed.astype(bf16)
        copies[4].start()
        copies[1].wait_recv()
        passed = chip_sum(slot, chip_x, True) + fin[g, 2, mid_row:].astype(f32)
        fsend[g, 0, mid_row:] = passed.astype(bf16)
        copies[5].start()

    def lasts(k, to):
        return [
            remote(zsend.at[k - 1], zin.at[k - 1], zgs.at[k - 1], zgr.at[k - 1], (e, to)),
            remote(zsend_g.at[k - 1], zin_g.at[k - 1], zggs.at[k - 1], zggr.at[k - 1], (e, to)),
        ]

    def mixed_copy(g, slot):
        return pltpu.make_async_copy(hold_o.at[slot], mixed_hbm.at[piece_of(g)], msem.at[slot])

    def plane_stage(g):
        slot = lax.rem(g, 2)
        for copy in gives(slot)[:2]:
            copy.wait_recv()
        if fslots < nz:

            @pl.when(g >= fslots)
            def _():
                for s in range(1, half):
                    for copy in finals(g - fslots, s, sib):
                        copy.wait_send()

        spot = lax.rem(g, fslots)
        if square:
            direct_stage(g)
        for s in range(1, half):
            h = lax.rem(me + half - s, half)
            at = pl.ds(pl.multiple_of(h * rows, 16), rows)
            if not square:
                fsend[spot, s - 1] = (
                    hold[slot, at, :].astype(f32) + sin[slot, at, :].astype(f32)
                ).astype(bf16)
            fsend_g[spot, s - 1] = (hold_g[slot, h].astype(f32) + sin_g[slot, h].astype(f32)).astype(
                bf16
            )
            for copy in finals(g, s, lax.rem(e - 2 * s + n, n)):
                copy.start()
        own_s[g] = hold[slot, my_rows, :].astype(f32) + sin[slot, my_rows, :].astype(f32)
        own_g[g] = hold_g[slot, me].astype(f32) + sin_g[slot, me].astype(f32)

    def mixed_stage(g):
        slot = lax.rem(g, 2)
        gives(slot)[2].wait_recv()
        hold_o[slot] = (hold_o[slot].astype(f32) + sin_o[slot].astype(f32)).astype(bf16)
        mixed_copy(g, slot).start()

    def tensor_stage(g):
        total = own_s[g]
        total_g = own_g[g]
        for s in range(1, half):
            for copy in finals(g, s, sib):
                copy.wait_recv()
            if not square:
                total = total + fin[g, s - 1].astype(f32)
            total_g = total_g + fin_g[g, s - 1].astype(f32)

        if square:
            for copy in half_copies(g)[2:]:
                copy.wait_recv()
            total = total + fin[g, 0].astype(f32) + fin[g, 1].astype(f32)

        @pl.when(g == 0)
        def _():
            own_s[0] = total
            own_g[0] = total_g

        @pl.when(g > 0)
        def _():
            zsend[g - 1] = total.astype(bf16)
            zsend_g[g - 1] = total_g.astype(bf16)
            for copy in lasts(g, piece_of(g)):
                copy.start()

    def step(g, carry):
        zz = piece_of(g)
        slot = lax.rem(g, 2)

        @pl.when(g < nz - 1)
        def _():
            coming = piece_of(g + 1)
            z_row(coming, g + 1, coming).wait_recv()
            z_small(coming, g + 1, coming).wait_recv()
            push_piece(g + 1)

        if square:

            @pl.when(g > 0)
            def _():
                x_part(zz, chip_x, 0, rows, g, 0, chip_x).wait_recv()
                x_part(zz, chip_y, 0, rows, g, 1, chip_y).wait_recv()
                z_diag(zz, g, zz).wait_recv()

        for s in range(1, half):
            h = lax.rem(me + half - s, half)
            src = 2 * h + core
            if not square:
                x_row(zz, h, g, s, src).wait_recv()
            x_small(zz, h, g, s, src).wait_recv()
        for copy in forward(zz, core, g):
            copy.start()
        cot_start(g, other, 1)
        cot_wait(0)

        @pl.when(g >= 2)
        def _():
            mixed_copy(g - 2, slot).wait()

        block(zz, core, 0, hold, hold_o, hold_g, slot)
        if square:
            for k in range(2, nz):

                @pl.when(g == k - 2)
                def _():
                    z_diag(z, k, lax.rem(z + k, nz)).start()


        @pl.when(g < nz - 1)
        def _():
            cot_start(g + 1, core, 0)

        @pl.when(g >= 2)
        def _():
            tensor_stage(g - 2)

        @pl.when(g >= 1)
        def _():
            plane_stage(g - 1)
            mixed_stage(g - 1)

        @pl.when(g >= 2)
        def _():
            for copy in gives(slot):
                copy.wait_send()

        for copy in forward(zz, other, g):
            copy.wait_recv()
        cot_wait(1)
        block(zz, other, 1, osend, osend_o, osend_g, slot)
        for copy in gives(slot):
            copy.start()
        if square:

            @pl.when(g >= 1)
            def _():
                relay_stage(g - 1)

        return carry

    def forward(zz, parity, g):
        ref = xbuf.at[zz, parity]
        small = wbuf.at[zz, parity]
        return (
            remote(ref, ref, fs.at[g], fr.at[g], (sib, z)),
            remote(small, small, wfs.at[g], wfr.at[g], (sib, z)),
        )

    lax.fori_loop(0, nz, step, 0)
    grads = [
        pltpu.make_async_copy(dgate, dgate_hbm, gsem.at[0]),
        pltpu.make_async_copy(dup, dup_hbm, gsem.at[1]),
        pltpu.make_async_copy(ddown, ddown_hbm, gsem.at[2]),
        pltpu.make_async_copy(xbuf.at[:, core, my_rows, :], normed_hbm, gsem.at[3]),
    ]
    plane_stage(jnp.int32(nz - 1))
    for copy in grads:
        copy.start()
    if nz >= 2:
        tensor_stage(jnp.int32(nz - 2))
    if square:
        relay_stage(jnp.int32(nz - 1))

    def total_stats(j, carry):
        for zz in range(nz):
            for parity in range(2):
                carry = carry + wbuf[zz, parity, j, experts:, :].astype(f32)
        return carry

    stats = lax.fori_loop(0, half, total_stats, jnp.zeros((16, 128), f32))
    total_rows = n * tok
    share = stats[0:1, :experts] / (total_rows * top_count)
    load_ref[...] = (
        experts * experts * share * ((stats[1:2, :experts] + stats[2:3, :experts]) / total_rows)
    )
    loss_w = experts * share / total_rows
    mixed_stage(jnp.int32(nz - 1))
    tensor_stage(jnp.int32(nz - 1))

    gate_sums = own_g[0]
    grad_rows = own_s[0]
    for k in range(1, nz):
        for copy in lasts(k, z):
            copy.wait_recv()
        gate_sums = gate_sums + zin_g[k - 1].astype(f32)
        grad_rows = grad_rows + zin[k - 1].astype(f32)
    grow = jnp.concatenate([gate_sums, jnp.zeros((128 - experts, 128), f32)], 0).T
    grad_gates = grow[:rows, :experts]
    grad_logits = comb * (grad_gates - jnp.sum(grad_gates * comb, -1, keepdims=True))
    grad_logits = grad_logits + probs * (loss_w - jnp.sum(loss_w * probs, -1, keepdims=True))
    low_grad = grad_logits.astype(bf16)
    wide_grad = jnp.concatenate([grad_logits, jnp.zeros((rows, 128 - experts), f32)], 1)
    if rows < 128:
        wide_grad = jnp.concatenate([wide_grad, jnp.zeros((128 - rows, 128), f32)], 0)
    glog_ref[...] = wide_grad.T[:experts].astype(bf16)
    grad_rows = grad_rows + dot_nn(low_grad, router_ref[...])
    mid = mid_ref[...]
    ggrad_ref[...] = jnp.sum(grad_rows * mid * scale2, 0, keepdims=True)
    gained = grad_rows * gain_ref[...]
    gmid_ref[...] = (
        cot_ref[own_rows, :]
        + scale2 * gained
        - mid * (scale2 * scale2 * scale2) * jnp.mean(gained * mid, -1, keepdims=True)
    )

    for copy in grads:
        copy.wait()
    if square:
        for copy in relays():
            copy.wait_send()
        for k in range(1, nz):
            z_diag(z, k, z).wait_send()
    for k in range(1, nz):
        z_row(z, k, z).wait_send()
        z_small(z, k, z).wait_send()
        for copy in lasts(k, z):
            copy.wait_send()
    for g in range(max(0, nz - 2), nz):
        mixed_copy(jnp.int32(g), g % 2).wait()
        for copy in gives(g % 2):
            copy.wait_send()

    def drained(g, carry):
        if square:
            x_part(z, me, 0, rows, g, 0, chip_x).wait_send()
            x_part(z, me, 0, rows, g, 1, chip_y).wait_send()
            for copy in half_copies(g):
                copy.wait_send()
        for s in range(1, half):
            if not square:
                x_row(z, me, g, s, sib).wait_send()
            x_small(z, me, g, s, sib).wait_send()
        for copy in forward(z, core, g):
            copy.wait_send()
        return carry

    lax.fori_loop(0, nz, drained, 0)

    def sums_sent(g, carry):
        for s in range(1, half):
            for copy in finals(g, s, sib):
                copy.wait_send()
        return carry

    lax.fori_loop(nz - fslots, nz, sums_sent, 0)


def expert_layer(n, nz, mid, gain, router, routes, gate, up, down, cot, cot_all):
    rows, width = mid.shape
    experts = router.shape[1]
    local_experts, _, hid = gate.shape
    inner_w = local_experts * hid
    half = n // 2
    batch = half * rows
    big = n > 8
    fslots = 2 if big else nz
    dma = pltpu.SemaphoreType.DMA
    vmem = pl.BlockSpec(memory_space=pltpu.VMEM)
    hbm = pl.BlockSpec(memory_space=pl.ANY)
    sds = jax.ShapeDtypeStruct
    out_shape = [
        sds((rows, width), f32),
        sds((experts, 128), bf16),
        sds((1, width), f32),
        sds((1, experts), f32),
        sds((local_experts, width, hid), f32),
        sds((local_experts, width, hid), f32),
        sds((inner_w, width), f32),
        sds((nz, batch, width), bf16),
        sds((nz, rows, width), bf16),
    ]
    out_specs = [vmem] * 4 + [hbm] * 5
    scratch = []
    if big:
        out_shape.append(sds((nz, 2, batch, width), bf16))
        out_specs.append(hbm)
        scratch.append(pltpu.VMEM((batch, width), bf16))
    else:
        scratch.append(pltpu.VMEM((nz, 2, batch, width), bf16))
    pair = pltpu.VMEM((2, batch, width), bf16)
    small = pltpu.VMEM((2, half, experts, 128), bf16)
    scratch += [
        pltpu.VMEM((nz, 2, half, experts + 16, 128), bf16),
        pltpu.VMEM((rows, width), bf16),
        pltpu.VMEM((width, inner_w), bf16),
        pltpu.VMEM((width, inner_w), bf16),
        pltpu.VMEM((inner_w, width), bf16),
        pltpu.VMEM((local_experts, width, hid), f32),
        pltpu.VMEM((local_experts, width, hid), f32),
        pltpu.VMEM((inner_w, width), f32),
        pair,
        pltpu.VMEM((batch, inner_w), bf16),
        pltpu.VMEM((batch, inner_w), bf16),
        pltpu.VMEM((batch, inner_w), bf16),
        pair,
        pair,
        pair,
        pair,
        pair,
        pair,
        small,
        small,
        small,
        pltpu.VMEM((nz, rows, width), f32),
        pltpu.VMEM((nz, experts, 128), f32),
        pltpu.VMEM((fslots, half - 1, rows, width), bf16),
        pltpu.VMEM((nz, half - 1, rows, width), bf16),
        pltpu.VMEM((fslots, half - 1, experts, 128), bf16),
        pltpu.VMEM((nz, half - 1, experts, 128), bf16),
        pltpu.VMEM((nz - 1, rows, width), bf16),
        pltpu.VMEM((nz - 1, rows, width), bf16),
        pltpu.VMEM((nz - 1, experts, 128), bf16),
        pltpu.VMEM((nz - 1, experts, 128), bf16),
        dma((3, local_experts)),
        dma((4,)),
        dma((2,)),
        dma((2,)),
        dma,
    ]
    scratch += [dma((nz - 1,))] * 4
    scratch += [dma((nz, half))] * 4
    scratch += [dma((nz,))] * 4
    scratch += [dma((2,))] * 6
    scratch += [dma((nz, 6 if half == 4 else half - 1))] * 2
    scratch += [dma((nz, half - 1))] * 2
    scratch += [dma((nz - 1,))] * 6 + [pltpu.VMEM((nz * rows, 128), f32)]
    return pl.pallas_call(
        functools.partial(expert_kernel, n, nz, big),
        out_shape=out_shape,
        in_specs=[vmem] * 5 + [hbm] * 4,
        out_specs=out_specs,
        scratch_shapes=scratch,
        compiler_params=pltpu.CompilerParams(
            collective_id=1, has_side_effects=True, vmem_limit_bytes=60 << 20
        ),
        name="experts",
    )(mid, gain[None], router.T, routes.T, cot, gate, up, down.reshape(inner_w, width), cot_all)[:9]


def attend_kernel(
    n,
    nz,
    x_ref,
    gain_ref,
    wq_ref,
    wk_ref,
    wv_ref,
    wo_ref,
    cos_ref,
    sin_ref,
    lens_ref,
    mid_ref,
    q_ref,
    kv_ref,
    lrow_ref,
    att_ref,
    wqkv,
    part,
    qst_s,
    m_s,
    l_s,
    o_s,
    zsend,
    zin,
    ks,
    kr,
    kfs,
    kfr,
    zgs,
    zgr,
):
    e = lax.axis_index("expert")
    z = lax.axis_index("tensor")
    sib = e + 1 - 2 * lax.rem(e, 2)
    half = n // 2
    tok, width = x_ref.shape
    rows = tok // nz
    qw = wq_ref.shape[1]
    kw = wk_ref.shape[1]
    seqs = kv_ref.shape[0]
    span = tok // seqs
    heads = kw // HD
    groups = qw // kw
    barrier = greet(n, nz, e, z, sib)

    wqkv[:, 0:qw] = wq_ref[...]
    wqkv[:, qw : qw + kw] = wk_ref[...]
    wqkv[:, qw + kw :] = wv_ref[...]
    x = x_ref[...].astype(f32)
    scale1 = lax.rsqrt(jnp.mean(x * x, -1, keepdims=True) + EPS)
    normed = (x * scale1 * gain_ref[...]).astype(bf16)
    lin = dot_nn(normed, wqkv[...])
    turned = turn(lin, cos_ref[...], sin_ref[...], qw + kw, True).astype(bf16)
    q_ref[...] = turned[:, :qw]
    for s in range(seqs):
        kv_ref[s, pl.ds(pl.multiple_of(e * span, 16), span)] = turned[
            s * span : (s + 1) * span, qw:
        ]
    pl.semaphore_wait(barrier, half + nz - 1)

    def rows_of(j, s):
        return kv_ref.at[s, pl.ds(pl.multiple_of(j * span, 16), span)]

    for t in range(1, half):
        to = (lax.rem(e + 2 * t, n), z)
        for s in range(seqs):
            remote(rows_of(e, s), rows_of(e, s), ks.at[t, s], kr.at[t, s], to).start()
    for s in range(seqs):
        remote(rows_of(e, s), rows_of(e, s), kfs.at[0, s], kfr.at[0, s], (sib, z)).start()

    def forward(t, carry):
        src = lax.rem(e - 2 * t + n, n)
        for s in range(seqs):
            remote(rows_of(src, s), rows_of(src, s), ks.at[t, s], kr.at[t, s], (src, z)).wait_recv()
            remote(rows_of(src, s), rows_of(src, s), kfs.at[t, s], kfr.at[t, s], (sib, z)).start()
        return carry

    lax.fori_loop(1, half, forward, 0)

    def arrive(t, carry):
        src = lax.rem(sib - 2 * t + n, n)
        for s in range(seqs):
            remote(
                rows_of(src, s), rows_of(src, s), kfs.at[t, s], kfr.at[t, s], (sib, z)
            ).wait_recv()
        return carry

    lax.fori_loop(0, half, arrive, 0)

    ck = 2 * span
    last = (e * span + span - 1) // ck
    stacked = groups * span
    qpos = lax.broadcasted_iota(jnp.int32, (stacked, ck), 0)
    qpos = e * span + lax.rem(qpos, span)
    kiota = lax.broadcasted_iota(jnp.int32, (stacked, ck), 1)
    klane = lax.broadcasted_iota(jnp.int32, (1, ck), 1)
    m_s[...] = jnp.full_like(m_s, -1e30)
    l_s[...] = jnp.zeros_like(l_s)
    o_s[...] = jnp.zeros_like(o_s)
    for s in range(seqs):
        for h in range(heads):
            qst_s[s * heads + h] = jnp.concatenate(
                [
                    q_ref[
                        s * span : (s + 1) * span,
                        (h * groups + g) * HD : (h * groups + g + 1) * HD,
                    ]
                    for g in range(groups)
                ],
                0,
            ) * jnp.array(HD ** (-0.5), bf16)

    def chunk(c, diagonal):
        at = pl.ds(pl.multiple_of(c * ck, 16), ck)
        for s in range(seqs):
            for h in range(heads):
                i = s * heads + h
                keys = kv_ref[s, at, h * HD : (h + 1) * HD]
                vals = kv_ref[s, at, kw + h * HD : kw + (h + 1) * HD]
                scores = dot_nt(qst_s[i], keys)
                if diagonal:
                    kpos = kiota + c * ck
                    scores = jnp.where((kpos <= qpos) & (kpos < lens_ref[s]), scores, -1e30)
                else:
                    scores = scores + jnp.where(klane + c * ck < lens_ref[s], 0.0, -1e30)
                old = m_s[i, :, 0:1]
                new = jnp.maximum(old, jnp.max(scores, -1, keepdims=True))
                weights = jnp.exp(scores - new)
                shrink = jnp.exp(old - new)
                m_s[i] = jnp.broadcast_to(new, (stacked, 128))
                l_s[i] = l_s[i] * shrink + jnp.sum(weights, -1, keepdims=True)
                o_s[i] = o_s[i] * shrink + dot_nn(weights.astype(bf16), vals)

    def whole_chunk(c, carry):
        chunk(c, False)
        return carry

    lax.fori_loop(0, last, whole_chunk, 0)
    chunk(last, True)
    for s in range(seqs):
        for h in range(heads):
            i = s * heads + h
            result = o_s[i] / l_s[i, :, 0:HD]
            for g in range(groups):
                cols = slice((h * groups + g) * HD, (h * groups + g + 1) * HD)
                att_ref[s * span : (s + 1) * span, cols] = result[g * span : (g + 1) * span]
            logs = m_s[i] + jnp.log(l_s[i])
            lrow_ref[i] = logs.T[0:8]

    part[...] = dot_nn(att_ref[...].astype(bf16), wo_ref[...])
    for k in range(1, nz):
        zz = lax.rem(z + k, nz)
        zsend[k - 1] = part[pl.ds(pl.multiple_of(zz * rows, 16), rows), :].astype(bf16)
        remote(zsend.at[k - 1], zin.at[k - 1], zgs.at[k - 1], zgr.at[k - 1], (e, zz)).start()
    own_rows = pl.ds(pl.multiple_of(z * rows, 16), rows)
    mid = x_ref[own_rows, :].astype(f32) + part[own_rows, :]
    for k in range(1, nz):
        remote(zsend.at[k - 1], zin.at[k - 1], zgs.at[k - 1], zgr.at[k - 1], (e, z)).wait_recv()
        mid = mid + zin[k - 1].astype(f32)
    mid_ref[...] = mid
    for k in range(1, nz):
        remote(zsend.at[k - 1], zin.at[k - 1], zgs.at[k - 1], zgr.at[k - 1], (e, z)).wait_send()

    def sent(t, carry):
        for s in range(seqs):

            @pl.when(t > 0)
            def _():
                remote(
                    rows_of(e, s), rows_of(e, s), ks.at[t, s], kr.at[t, s], (sib, z)
                ).wait_send()

            remote(rows_of(e, s), rows_of(e, s), kfs.at[t, s], kfr.at[t, s], (sib, z)).wait_send()
        return carry

    lax.fori_loop(0, half, sent, 0)


def attend_layer(n, nz, x, gain, wq, wk, wv, wo, cos, sin, lens):
    tok, width = x.shape
    rows = tok // nz
    qw, kw = wq.shape[1], wk.shape[1]
    seqs = lens.shape[0]
    span = tok // seqs
    half = n // 2
    stacked = (qw // kw) * span
    pairs = seqs * (kw // HD)
    dma = pltpu.SemaphoreType.DMA
    vmem = pl.BlockSpec(memory_space=pltpu.VMEM)
    sds = jax.ShapeDtypeStruct
    return pl.pallas_call(
        functools.partial(attend_kernel, n, nz),
        out_shape=[
            sds((rows, width), f32),
            sds((tok, qw), bf16),
            sds((seqs, n * span, 2 * kw), bf16),
            sds((seqs * (kw // HD), 8, stacked), f32),
            sds((tok, qw), f32),
        ],
        in_specs=[vmem] * 8 + [pl.BlockSpec(memory_space=pltpu.SMEM)],
        out_specs=[vmem] * 5,
        scratch_shapes=[
            pltpu.VMEM((width, qw + 2 * kw), bf16),
            pltpu.VMEM((tok, width), f32),
            pltpu.VMEM((pairs, stacked, HD), bf16),
            pltpu.VMEM((pairs, stacked, 128), f32),
            pltpu.VMEM((pairs, stacked, 128), f32),
            pltpu.VMEM((pairs, stacked, HD), f32),
            pltpu.VMEM((nz - 1, rows, width), bf16),
            pltpu.VMEM((nz - 1, rows, width), bf16),
        ]
        + [dma((half, seqs))] * 4
        + [dma((nz - 1,))] * 2,
        compiler_params=pltpu.CompilerParams(
            collective_id=2, has_side_effects=True, vmem_limit_bytes=60 << 20
        ),
        name="attend",
    )(x, gain[None], wq, wk, wv, wo, cos, sin, lens)


def return_kernel(
    n,
    nz,
    gmid_ref,
    mid_ref,
    glog_ref,
    ggrad_ref,
    xn_ref,
    x_ref,
    gain_ref,
    wq_ref,
    wk_ref,
    wv_ref,
    wo_ref,
    cos_ref,
    sin_ref,
    q_ref,
    kv_ref,
    lrow_ref,
    att_ref,
    lens_ref,
    mixed_hbm,
    obuf,
    igbuf,
    wall,
    wall2,
    small_ref,
    wqkv,
    gat,
    datt,
    dq_s,
    qst_s,
    dst_s,
    acc_q,
    dkv,
    kvo,
    kvi,
    kvf,
    kvr,
    part,
    sums,
    csend,
    crecv,
    osend,
    orecv,
    wbufs,
    wbufs2,
    sz1,
    sz2,
    sown,
    ssib,
    schip,
    ofin,
    zas,
    zar,
    zos,
    zor,
    zis,
    zir,
    zps,
    zpr,
    zqs,
    zqr,
    z1s,
    z1r,
    z2s,
    z2r,
    kos,
    kor,
    kfs,
    kfr,
    wsems,
    wsems2,
    sbs,
    sbr,
    scs,
    scr,
    ofs,
    ofr,
    olsem,
):
    e = lax.axis_index("expert")
    z = lax.axis_index("tensor")
    core = lax.rem(e, 2)
    me = e // 2
    sib = e + 1 - 2 * core
    half = n // 2
    rows, width = gmid_ref.shape
    tok = rows * nz
    qw = wq_ref.shape[1]
    kw = wk_ref.shape[1]
    seqs = kv_ref.shape[0]
    span = tok // seqs
    heads = kw // HD
    groups = qw // kw
    dn = width // n
    experts = glog_ref.shape[0]
    own_rows = pl.ds(pl.multiple_of(z * rows, 16), rows)
    barrier = greet(n, nz, e, z, sib)
    w1 = PlaneSum(n, e, z, sib, wall, *wbufs, *wsems)
    w2 = PlaneSum(n, e, z, sib, wall2, *wbufs2, *wsems2)

    gat[own_rows, :] = gmid_ref[...].astype(bf16)
    sz1[z] = glog_ref[...]
    pl.semaphore_wait(barrier, half + nz - 1)

    def part_of(ref):
        return lambda zz: ref.at[pl.ds(pl.multiple_of(zz * rows, 16), rows)]

    def slot_of(ref):
        return lambda zz: ref.at[zz]

    gat_line = Line(z, nz, e, part_of(gat), zas, zar)
    out_line = Line(z, nz, e, part_of(obuf), zos, zor)
    igrad_line = Line(z, nz, e, part_of(igbuf), zis, zir)
    normed_sum = LineSum(z, nz, e, csend, crecv, zps, zpr)

    def z_copies(buf_of, send, recv):
        return [
            remote(
                buf_of(z), buf_of(z), send.at[k - 1], recv.at[k - 1], (e, lax.rem(z + k, nz))
            )
            for k in range(1, nz)
        ]

    def z_arrivals(buf_of, send, recv):
        return [
            remote(
                buf_of(lax.rem(z + nz - k, nz)),
                buf_of(lax.rem(z + nz - k, nz)),
                send.at[k - 1],
                recv.at[k - 1],
                (e, lax.rem(z + nz - k, nz)),
            )
            for k in range(1, nz)
        ]

    gat_line.start()
    for copy in z_copies(slot_of(sz1), z1s, z1r):
        copy.start()

    def mixed_send(t):
        h = lax.rem(me + half - t, half)
        return remote(
            mixed_hbm.at[:, pl.ds(pl.multiple_of(h * rows, 16), rows), :],
            ofin.at[t],
            ofs.at[t - 1],
            ofr.at[t - 1],
            (lax.rem(e - 2 * t + n, n), z),
        )

    for t in range(1, half):
        mixed_send(t).start()
    mixed_own = pltpu.make_async_copy(
        mixed_hbm.at[:, pl.ds(pl.multiple_of(me * rows, 16), rows), :], ofin.at[0], olsem
    )
    mixed_own.start()

    def mixed_sum(zz):
        total = ofin[0, zz].astype(f32)
        for t in range(1, half):
            total = total + ofin[t, zz].astype(f32)
        return total

    wqkv[:, 0:qw] = wq_ref[...]
    wqkv[:, qw : qw + kw] = wk_ref[...]
    wqkv[:, qw + kw :] = wv_ref[...]
    x = x_ref[...].astype(f32)
    scale1 = lax.rsqrt(jnp.mean(x * x, -1, keepdims=True) + EPS)
    normed = (x * scale1 * gain_ref[...]).astype(bf16)
    dkv[...] = jnp.zeros_like(dkv)

    for hop in range(1, nz):
        gat_line.hop(hop)
    datt[...] = dot_nt(gat[...], wo_ref[...]).astype(bf16)

    ck = 2 * span
    last = (e * span + span - 1) // ck
    stacked = groups * span
    kiota = lax.broadcasted_iota(jnp.int32, (ck, stacked), 0)
    krow = lax.broadcasted_iota(jnp.int32, (ck, 1), 0)
    qpos = e * span + lax.rem(lax.broadcasted_iota(jnp.int32, (ck, stacked), 1), span)
    drows = []
    for s in range(seqs):
        for h in range(heads):

            def gather(ref):
                return jnp.concatenate(
                    [
                        ref[
                            s * span : (s + 1) * span,
                            (h * groups + g) * HD : (h * groups + g + 1) * HD,
                        ]
                        for g in range(groups)
                    ],
                    0,
                )

            i = s * heads + h
            qst_s[i] = gather(q_ref) * jnp.array(HD ** (-0.5), bf16)
            dst = gather(datt)
            dst_s[i] = dst
            delta = jnp.sum(dst.astype(f32) * gather(att_ref), -1, keepdims=True)
            drows.append(jnp.broadcast_to(delta, (stacked, 128)).T[0:1])
    acc_q[...] = jnp.zeros_like(acc_q)

    def chunk(c, diagonal):
        at = pl.ds(pl.multiple_of(c * ck, 16), ck)
        for s in range(seqs):
            for h in range(heads):
                i = s * heads + h
                keys = kv_ref[s, at, h * HD : (h + 1) * HD]
                vals = kv_ref[s, at, kw + h * HD : kw + (h + 1) * HD]
                scores = dot_nt(keys, qst_s[i]) - lrow_ref[i, 0:1, :]
                if diagonal:
                    kpos = kiota + c * ck
                    allowed = (kpos <= qpos) & (kpos < lens_ref[s])
                    soft = jnp.where(allowed, jnp.exp(scores), 0.0)
                else:
                    soft = jnp.exp(scores + jnp.where(krow + c * ck < lens_ref[s], 0.0, -1e30))
                grad_probs = dot_nt(vals, dst_s[i])
                grad_scores = (soft * (grad_probs - drows[i])).astype(bf16)
                dkv[s, at, h * HD : (h + 1) * HD] = dot_nn(grad_scores, qst_s[i])
                dkv[s, at, kw + h * HD : kw + (h + 1) * HD] = dot_nn(soft.astype(bf16), dst_s[i])
                acc_q[i] += dot_tn(grad_scores, keys)

    def whole_chunk(c, carry):
        chunk(c, False)
        return carry

    lax.fori_loop(0, last, whole_chunk, 0)
    chunk(last, True)
    for s in range(seqs):
        for h in range(heads):
            result = acc_q[s * heads + h] * HD ** (-0.5)
            for g in range(groups):
                cols = slice((h * groups + g) * HD, (h * groups + g + 1) * HD)
                dq_s[s * span : (s + 1) * span, cols] = result[g * span : (g + 1) * span]

    def key_rows(j, s):
        return dkv[s, pl.ds(pl.multiple_of(j * span, 16), span), :]

    def key_send(t):
        return remote(kvo.at[t], kvi.at[t], kos.at[t], kor.at[t], (sib, z))

    def key_final(t):
        to = (lax.rem(e - 2 * t + n, n), z)
        return remote(kvf.at[t - 1], kvr.at[t - 1], kfs.at[t - 1], kfr.at[t - 1], to)

    def key_give(i, carry):
        t = half - 1 - i
        oth = lax.rem(sib - 2 * t + n, n)
        for s in range(seqs):
            kvo[t, s] = key_rows(oth, s).astype(bf16)
        key_send(t).start()
        return carry

    lax.fori_loop(0, half, key_give, 0)

    def key_pass(i, carry):
        t = half - 1 - i
        key_send(t).wait_recv()
        own = lax.rem(e - 2 * t + n, n)
        for s in range(seqs):
            kvf[t - 1, s] = (key_rows(own, s) + kvi[t, s].astype(f32)).astype(bf16)
        key_final(t).start()
        return carry

    cos, sin = cos_ref[...], sin_ref[...]
    gq = turn(dq_s[...], cos, sin, qw, False).astype(bf16)
    query_part = dot_tn(normed, gq)
    out_part = dot_tn(gat[...], att_ref[...].astype(bf16))
    for j in range(n):
        w1.pack[j, :, :qw] = query_part[j * dn : (j + 1) * dn].astype(bf16)
        w1.pack[j, :, qw:] = out_part[j * dn : (j + 1) * dn].astype(bf16)
    lax.fori_loop(0, half - 1, key_pass, 0)
    w1.give()

    def mixed_last(k, to):
        return remote(osend.at[k - 1], orecv.at[k - 1], zqs.at[k - 1], zqr.at[k - 1], (e, to))

    mixed_own.wait()
    for t in range(1, half):
        mixed_send(t).wait_recv()
    for k in range(1, nz):
        zz = lax.rem(z + k, nz)
        osend[k - 1] = mixed_sum(zz).astype(bf16)
        mixed_last(k, zz).start()
    own_mixed = mid_ref[...] + mixed_sum(z)
    w1.spread()
    for copy in z_arrivals(slot_of(sz1), z1s, z1r):
        copy.wait_recv()
    rgrad = dot_nn(sz1[0][:, :rows], xn_ref[0])
    for zz in range(1, nz):
        rgrad = rgrad + dot_nn(sz1[zz][:, :rows], xn_ref[zz])
    sown[0:experts, :] = rgrad.astype(bf16)

    key_send(0).wait_recv()
    own_kv = [key_rows(e, s) + kvi[0, s].astype(f32) for s in range(seqs)]
    for t in range(1, half):
        key_final(t).wait_recv()
        for s in range(seqs):
            own_kv[s] = own_kv[s] + kvr[t - 1, s].astype(f32)
    gkv = turn(jnp.concatenate(own_kv, 0), cos, sin, kw, False).astype(bf16)
    part[...] = dot_nt(gq, wqkv[:, :qw]) + dot_nt(gkv, wqkv[:, qw:])

    def normed_part(zz):
        return part[pl.ds(pl.multiple_of(zz * rows, 16), rows), :]

    for hop in range(nz - 1):
        normed_sum.hop(hop, normed_part)
        if hop > 0:
            out_line.hop(hop)
        if hop == 0:
            for k in range(1, nz):
                mixed_last(k, z).wait_recv()
                own_mixed = own_mixed + orecv[k - 1].astype(f32)
            obuf[own_rows, :] = own_mixed.astype(bf16)
            out_line.start()
            again = jnp.sum(part[...] * x * scale1, 0, keepdims=True)
            sz2[z] = jnp.concatenate([again, ggrad_ref[...], jnp.zeros((14, width), f32)], 0).astype(
                bf16
            )
            for copy in z_copies(slot_of(sz2), z2s, z2r):
                copy.start()
            pair_part = dot_tn(normed, gkv)
            for j in range(n):
                w2.pack[j] = pair_part[j * dn : (j + 1) * dn].astype(bf16)
            w2.give()
            w1.total()
    w2.spread()
    normed_sum.total(sums, normed_part)

    own_x = x_ref[own_rows, :].astype(f32)
    own_scale = lax.rsqrt(jnp.mean(own_x * own_x, -1, keepdims=True) + EPS)
    grad_normed = sums[...]
    gained = grad_normed * gain_ref[...]
    igrad = (
        gmid_ref[...]
        + own_scale * gained
        - own_x
        * (own_scale * own_scale * own_scale)
        * jnp.mean(gained * own_x, -1, keepdims=True)
    )
    igbuf[own_rows, :] = igrad.astype(bf16)
    igrad_line.start()
    out_line.hop(nz - 1)

    w1.forward()
    for copy in z_arrivals(slot_of(sz2), z2s, z2r):
        copy.wait_recv()
    second = sz2[0].astype(f32)
    for zz in range(1, nz):
        second = second + sz2[zz].astype(f32)
    sown[experts:, :] = second.astype(bf16)
    small_sib = remote(sown, ssib, sbs, sbr, (sib, z))
    small_sib.start()
    if nz > 2:
        igrad_line.hop(1)
    small_sib.wait_recv()
    schip[me] = (sown[...].astype(f32) + ssib[...].astype(f32)).astype(bf16)

    def small_send(t):
        to = (lax.rem(e + 2 * t, n), z)
        return remote(schip.at[me], schip.at[me], scs.at[t - 1], scr.at[t - 1], to)

    for t in range(1, half):
        small_send(t).start()

    w2.total()
    for hop in range(2, nz - 1):
        igrad_line.hop(hop)
    igrad_line.hop(nz - 1)

    w2.forward()
    for t in range(1, half):
        src = lax.rem(me + half - t, half)
        remote(
            schip.at[src], schip.at[src], scs.at[t - 1], scr.at[t - 1], (sib, z)
        ).wait_recv()
    small = schip[0].astype(f32)
    for t in range(1, half):
        small = small + schip[t].astype(f32)
    small_ref[...] = small

    w1.arrive()
    w2.arrive()
    for k in range(1, nz):
        mixed_last(k, z).wait_send()
    for line in (gat_line, out_line, igrad_line, normed_sum, w1, w2):
        line.drain()
    for copy in z_copies(slot_of(sz1), z1s, z1r) + z_copies(slot_of(sz2), z2s, z2r):
        copy.wait_send()
    small_sib.wait_send()
    for t in range(1, half):
        mixed_send(t).wait_send()

    def drained(t, carry):
        key_send(t).wait_send()

        @pl.when(t > 0)
        def _():
            key_final(t).wait_send()
            small_send(t).wait_send()

        return carry

    lax.fori_loop(0, half, drained, 0)


class PlaneSum:
    def __init__(self, n, e, z, sib, wall, pack, near, send, recv, *sems):
        self.n, self.e, self.z, self.sib, self.half = n, e, z, sib, n // 2
        self.wall, self.pack, self.near, self.send, self.recv = wall, pack, near, send, recv
        self.sems = sems

    def peer(self, base, t):
        return lax.rem(base - 2 * t + self.n, self.n)

    def near_copy(self, t):
        src = self.pack.at[self.peer(self.sib, t)]
        return remote(
            src, self.near.at[t], self.sems[0].at[t], self.sems[1].at[t], (self.sib, self.z)
        )

    def far_copy(self, t):
        return remote(
            self.send.at[t - 1],
            self.recv.at[t - 1],
            self.sems[2].at[t],
            self.sems[3].at[t],
            (self.peer(self.e, t), self.z),
        )

    def all_copy(self, src, t, to):
        ref = self.wall.at[src]
        return remote(ref, ref, self.sems[4].at[t], self.sems[5].at[t], (to, self.z))

    def pass_copy(self, src, t):
        ref = self.wall.at[src]
        return remote(ref, ref, self.sems[6].at[t], self.sems[7].at[t], (self.sib, self.z))

    def give(self):
        def one(i, carry):
            self.near_copy(self.half - 1 - i).start()
            return carry

        lax.fori_loop(0, self.half, one, 0)

    def spread(self):
        def one(i, carry):
            t = self.half - 1 - i
            self.near_copy(t).wait_recv()
            own = self.pack[self.peer(self.e, t)].astype(f32)
            self.send[t - 1] = (own + self.near[t].astype(f32)).astype(bf16)
            self.far_copy(t).start()
            return carry

        lax.fori_loop(0, self.half - 1, one, 0)

    def total(self):
        self.near_copy(0).wait_recv()
        total = self.pack[self.e].astype(f32) + self.near[0].astype(f32)
        for t in range(1, self.half):
            self.far_copy(t).wait_recv()
            total = total + self.recv[t - 1].astype(f32)
        self.wall[self.e] = total.astype(bf16)
        for t in range(1, self.half):
            self.all_copy(self.e, t, lax.rem(self.e + 2 * t, self.n)).start()
        self.pass_copy(self.e, 0).start()

    def forward(self):
        def one(t, carry):
            src = self.peer(self.e, t)
            self.all_copy(src, t, src).wait_recv()
            self.pass_copy(src, t).start()
            return carry

        lax.fori_loop(1, self.half, one, 0)

    def arrive(self):
        def one(t, carry):
            self.pass_copy(self.peer(self.sib, t), t).wait_recv()
            return carry

        lax.fori_loop(0, self.half, one, 0)

    def drain(self):
        def one(t, carry):
            self.near_copy(t).wait_send()
            self.pass_copy(self.e, t).wait_send()

            @pl.when(t > 0)
            def _():
                self.far_copy(t).wait_send()
                self.all_copy(self.e, t, self.sib).wait_send()

            return carry

        lax.fori_loop(0, self.half, one, 0)


class Line:
    def __init__(self, z, nz, e, buf_of, send, recv):
        self.z, self.nz, self.e = z, nz, e
        self.buf_of, self.send, self.recv = buf_of, send, recv

    def copy(self, way, piece):
        to = self.z + 1 if way == 0 else self.z - 1
        ref = self.buf_of(piece)
        return remote(ref, ref, self.send.at[way, piece], self.recv.at[way, piece], (self.e, to))

    def push(self, piece, ways=(0, 1)):
        for way in ways:

            @pl.when(self.z < self.nz - 1 if way == 0 else self.z > 0)
            def _():
                self.copy(way, piece).start()

    def start(self):
        self.push(self.z)

    def hop(self, i):
        @pl.when(self.z >= i)
        def _():
            self.copy(0, self.z - i).wait_recv()
            self.push(self.z - i, (0,))

        @pl.when(self.z + i <= self.nz - 1)
        def _():
            self.copy(1, self.z + i).wait_recv()
            self.push(self.z + i, (1,))

    def drain(self):
        for piece in range(self.nz):

            @pl.when((self.z >= piece) & (self.z < self.nz - 1))
            def _():
                self.copy(0, piece).wait_send()

            @pl.when((self.z <= piece) & (self.z > 0))
            def _():
                self.copy(1, piece).wait_send()


class LineSum:
    def __init__(self, z, nz, e, send_buf, recv_buf, send, recv):
        self.z, self.nz, self.e = z, nz, e
        self.send_buf, self.recv_buf, self.send, self.recv = send_buf, recv_buf, send, recv

    def copy(self, way, target):
        to = self.z + 1 if way == 0 else self.z - 1
        return remote(
            self.send_buf.at[way, target],
            self.recv_buf.at[way, target],
            self.send.at[way, target],
            self.recv.at[way, target],
            (self.e, to),
        )

    def hop(self, i, own_of):
        for way, target in ((0, self.nz - 1 - i), (1, i)):
            passes = self.z < target if way == 0 else self.z > target
            first = self.z == 0 if way == 0 else self.z == self.nz - 1
            inner = self.z > 0 if way == 0 else self.z < self.nz - 1

            @pl.when(passes & first)
            def _():
                self.send_buf[way, target] = own_of(target).astype(bf16)
                self.copy(way, target).start()

            @pl.when(passes & inner)
            def _():
                self.copy(way, target).wait_recv()
                self.send_buf[way, target] = (
                    own_of(target) + self.recv_buf[way, target].astype(f32)
                ).astype(bf16)
                self.copy(way, target).start()

    def total(self, ref, own_of):
        ref[...] = own_of(self.z)

        @pl.when(self.z > 0)
        def _():
            self.copy(0, self.z).wait_recv()
            ref[...] += self.recv_buf[0, self.z].astype(f32)

        @pl.when(self.z < self.nz - 1)
        def _():
            self.copy(1, self.z).wait_recv()
            ref[...] += self.recv_buf[1, self.z].astype(f32)

    def drain(self):
        for target in range(self.nz):

            @pl.when(self.z < target)
            def _():
                self.copy(0, target).wait_send()

            @pl.when(self.z > target)
            def _():
                self.copy(1, target).wait_send()


def return_layer(
    n, nz, gmid, mid, glog, ggrad, xn, x, gain, wq, wk, wv, wo, cos, sin, q, kv, lrow, att, lens, mixed
):
    tok, width = x.shape
    rows = tok // nz
    qw, kw = wq.shape[1], wk.shape[1]
    seqs = lens.shape[0]
    span = tok // seqs
    half = n // 2
    stacked = (qw // kw) * span
    pairs = seqs * (kw // HD)
    experts = glog.shape[0]
    small_rows = experts + 16
    dma = pltpu.SemaphoreType.DMA
    vmem = pl.BlockSpec(memory_space=pltpu.VMEM)
    sds = jax.ShapeDtypeStruct
    zdma = dma((nz - 1,))
    line = dma((2, nz))
    hdma = dma((half,))
    fdma = dma((half - 1,))
    def plane_bufs(cols):
        return [
            pltpu.VMEM((n, width // n, cols), bf16),
            pltpu.VMEM((half, width // n, cols), bf16),
            pltpu.VMEM((half - 1, width // n, cols), bf16),
            pltpu.VMEM((half - 1, width // n, cols), bf16),
        ]

    line_buf = pltpu.VMEM((2, nz, rows, width), bf16)
    return pl.pallas_call(
        functools.partial(return_kernel, n, nz),
        out_shape=[
            sds((tok, width), bf16),
            sds((tok, width), bf16),
            sds((n, width // n, 2 * qw), bf16),
            sds((n, width // n, 2 * kw), bf16),
            sds((small_rows, width), f32),
        ],
        in_specs=[vmem] * 17
        + [pl.BlockSpec(memory_space=pltpu.SMEM), pl.BlockSpec(memory_space=pl.ANY)],
        out_specs=[vmem] * 5,
        scratch_shapes=[
            pltpu.VMEM((width, qw + 2 * kw), bf16),
            pltpu.VMEM((tok, width), bf16),
            pltpu.VMEM((tok, qw), bf16),
            pltpu.VMEM((tok, qw), f32),
            pltpu.VMEM((pairs, stacked, HD), bf16),
            pltpu.VMEM((pairs, stacked, HD), bf16),
            pltpu.VMEM((pairs, stacked, HD), f32),
            pltpu.VMEM((seqs, n * span, 2 * kw), f32),
            pltpu.VMEM((half, seqs, span, 2 * kw), bf16),
            pltpu.VMEM((half, seqs, span, 2 * kw), bf16),
            pltpu.VMEM((half - 1, seqs, span, 2 * kw), bf16),
            pltpu.VMEM((half - 1, seqs, span, 2 * kw), bf16),
            pltpu.VMEM((tok, width), f32),
            pltpu.VMEM((rows, width), f32),
            line_buf,
            line_buf,
            pltpu.VMEM((nz - 1, rows, width), bf16),
            pltpu.VMEM((nz - 1, rows, width), bf16),
            plane_bufs(2 * qw),
            plane_bufs(2 * kw),
            pltpu.VMEM((nz, experts, 128), bf16),
            pltpu.VMEM((nz, 16, width), bf16),
            pltpu.VMEM((small_rows, width), bf16),
            pltpu.VMEM((small_rows, width), bf16),
            pltpu.VMEM((half, small_rows, width), bf16),
            pltpu.VMEM((half, nz, rows, width), bf16),
        ]
        + [line] * 8
        + [zdma] * 6
        + [hdma, hdma, fdma, fdma]
        + [[hdma] * 8, [hdma] * 8]
        + [dma, dma, fdma, fdma]
        + [fdma, fdma, dma],
        compiler_params=pltpu.CompilerParams(
            collective_id=3, has_side_effects=True, vmem_limit_bytes=58 << 20
        ),
        name="attend_back",
    )(
        gmid,
        mid,
        glog,
        ggrad,
        xn,
        x,
        gain[None],
        wq,
        wk,
        wv,
        wo,
        cos,
        sin,
        q,
        kv,
        lrow,
        att,
        lens,
        mixed,
    )


def finish_kernel(
    out_low,
    igrad_low,
    wall,
    wall2,
    small,
    load,
    dgate_in,
    dup_in,
    ddown_in,
    out_ref,
    igrad_ref,
    q_ref,
    k_ref,
    v_ref,
    o_ref,
    router_ref,
    again_ref,
    egain_ref,
    loss_ref,
    load_ref,
    dgate,
    dup,
    ddown,
    dgate_s,
    dup_s,
    ddown_s,
    sems,
):
    pairs = ((dgate_in, dgate_s, dgate), (dup_in, dup_s, dup), (ddown_in, ddown_s, ddown))
    reads = [pltpu.make_async_copy(p[0], p[1], sems.at[0, i]) for i, p in enumerate(pairs)]
    writes = [pltpu.make_async_copy(p[1], p[2], sems.at[1, i]) for i, p in enumerate(pairs)]
    for copy in reads:
        copy.start()
    qw, kw = q_ref.shape[1], k_ref.shape[1]
    experts = load.shape[1]
    out_ref[...] = out_low[...].astype(f32)
    for read, write in zip(reads, writes):
        read.wait()
        write.start()
    igrad_ref[...] = igrad_low[...].astype(f32)
    chunks, dn, _ = wall.shape
    flat = wall[...].reshape(chunks * dn, 2 * qw).astype(f32)
    q_ref[...] = flat[:, :qw]
    o_ref[...] = flat[:, qw:].T
    flat = wall2[...].reshape(chunks * dn, 2 * kw).astype(f32)
    k_ref[...] = flat[:, :kw]
    v_ref[...] = flat[:, kw:]
    router_ref[...] = small[0:experts, :].T
    again_ref[...] = small[experts : experts + 1, :]
    egain_ref[...] = small[experts + 1 : experts + 2, :]
    load_ref[...] = load[...]
    loss_ref[...] = jnp.mean(load[...], -1, keepdims=True)
    for copy in writes:
        copy.wait()


def finish_layer(out_low, igrad_low, wall, wall2, small, load, dgate, dup, ddown, qw, kw):
    tok, width = out_low.shape
    experts = load.shape[1]
    vmem = pl.BlockSpec(memory_space=pltpu.VMEM)
    hbm = pl.BlockSpec(memory_space=pl.ANY)
    sds = jax.ShapeDtypeStruct
    return pl.pallas_call(
        finish_kernel,
        out_shape=[
            sds((tok, width), f32),
            sds((tok, width), f32),
            sds((width, qw), f32),
            sds((width, kw), f32),
            sds((width, kw), f32),
            sds((qw, width), f32),
            sds((width, experts), f32),
            sds((1, width), f32),
            sds((1, width), f32),
            sds((1, 1), f32),
            sds((1, experts), f32),
            sds(dgate.shape, f32),
            sds(dup.shape, f32),
            sds(ddown.shape, f32),
        ],
        in_specs=[vmem] * 6 + [hbm] * 3,
        out_specs=[vmem] * 11 + [hbm] * 3,
        scratch_shapes=[
            pltpu.VMEM(dgate.shape, f32),
            pltpu.VMEM(dup.shape, f32),
            pltpu.VMEM(ddown.shape, f32),
            pltpu.SemaphoreType.DMA((2, 3)),
        ],
        compiler_params=pltpu.CompilerParams(vmem_limit_bytes=60 << 20),
        name="finish",
    )(out_low, igrad_low, wall, wall2, small, load, dgate, dup, ddown)


def shards(
    inputs,
    attention_gain,
    query_weight,
    key_weight,
    value_weight,
    out_weight,
    expert_gain,
    router_weight,
    gate_weight,
    up_weight,
    down_weight,
    routes,
    seq_lens,
    cotangent,
):
    n = lax.axis_size("expert")
    nz = lax.axis_size("tensor")
    tok_rows = inputs.shape[0]
    seq_count = seq_lens.shape[0]
    span_rows = tok_rows // seq_count
    local_pos = lax.axis_index("expert") * span_rows + jnp.arange(span_rows, dtype=jnp.int32)
    frequency = THETA ** (-2.0 * jnp.arange(HD // 2, dtype=jnp.float32) / HD)
    angles = local_pos.astype(f32)[:, None] * frequency[None, :]
    cosines = jnp.tile(jnp.cos(angles), (seq_count, 4))
    sines = jnp.tile(jnp.sin(angles), (seq_count, 4))
    cot_all = lax.all_gather(cotangent.astype(bf16), "expert", axis=0, tiled=True)
    weights = (query_weight, key_weight, value_weight, out_weight, cosines, sines)
    middle, queries, pairs, logs, attended = attend_layer(
        n, nz, inputs, attention_gain, *weights, seq_lens
    )
    (
        grad_middle,
        logit_grads,
        expert_gain_part,
        expert_load,
        gate_grad,
        up_grad,
        down_grad,
        mixed,
        normed2,
    ) = expert_layer(
        n,
        nz,
        middle,
        expert_gain,
        router_weight,
        routes,
        gate_weight,
        up_weight,
        down_weight,
        cotangent,
        cot_all,
    )
    out_low, igrad_low, packed, packed2, small = return_layer(
        n,
        nz,
        grad_middle,
        middle,
        logit_grads,
        expert_gain_part,
        normed2,
        inputs,
        attention_gain,
        *weights,
        queries,
        pairs,
        logs,
        attended,
        seq_lens,
        mixed,
    )
    (
        output,
        input_grad,
        query_grad,
        key_grad,
        value_grad,
        out_weight_grad,
        router_grad,
        attention_gain_grad,
        expert_gain_grad,
        balance_loss,
        expert_load,
        gate_grad,
        up_grad,
        down_grad,
    ) = finish_layer(
        out_low,
        igrad_low,
        packed,
        packed2,
        small,
        expert_load,
        gate_grad,
        up_grad,
        down_grad,
        query_weight.shape[1],
        key_weight.shape[1],
    )
    return (
        output,
        input_grad,
        balance_loss[0, 0],
        expert_load[0],
        attention_gain_grad[0],
        query_grad,
        key_grad,
        value_grad,
        out_weight_grad,
        expert_gain_grad[0],
        router_grad,
        gate_grad,
        up_grad,
        down_grad.reshape(down_weight.shape),
    )


def solution(mesh):
    placed = (
        P("expert", None),
        P(),
        P(None, "tensor"),
        P(None, "tensor"),
        P(None, "tensor"),
        P("tensor", None),
        P(),
        P(),
        P("expert", None, "tensor"),
        P("expert", None, "tensor"),
        P("expert", "tensor", None),
        P("expert", None),
        P(),
        P("expert", None),
    )
    return jax.shard_map(
        shards,
        mesh=mesh,
        in_specs=placed,
        out_specs=(
            P("expert", None),
            P("expert", None),
            P(),
            P(),
            P(),
            P(None, "tensor"),
            P(None, "tensor"),
            P(None, "tensor"),
            P("tensor", None),
            P(),
            P(),
            P("expert", None, "tensor"),
            P("expert", None, "tensor"),
            P("expert", "tensor", None),
        ),
        check_vma=False,
    )
```

```python
import functools

import jax
import jax.numpy as jnp
from jax import lax
from jax.experimental import pallas as pl
from jax.experimental.pallas import tpu as pltpu
from jax.sharding import PartitionSpec as P

HD = 64
EPS = 1e-06
THETA = 10000.0
MESH = pl.DeviceIdType.MESH
f32 = jnp.float32
bf16 = jnp.bfloat16


def dot_nn(left, right):
    return lax.dot_general(left, right, (((1,), (0,)), ((), ())), preferred_element_type=f32)


def dot_nt(left, right):
    return lax.dot_general(left, right, (((1,), (1,)), ((), ())), preferred_element_type=f32)


def dot_tn(left, right):
    return lax.dot_general(left, right, (((0,), (0,)), ((), ())), preferred_element_type=f32)


def remote(src, dst, send_sem, recv_sem, device):
    return pltpu.make_async_remote_copy(
        src_ref=src,
        dst_ref=dst,
        send_sem=send_sem,
        recv_sem=recv_sem,
        device_id=device,
        device_id_type=MESH,
    )


def turn(values, cos, sin, last, forward):
    lane = lax.broadcasted_iota(jnp.int32, (values.shape[0], 128), 1)
    first_half = lax.rem(lane, HD) < HD // 2
    parts = []
    for g in range(values.shape[1] // 128):
        v = values[:, g * 128 : (g + 1) * 128]
        if g * 128 >= last:
            parts.append(v)
            continue
        turned = jnp.where(
            first_half, -pltpu.roll(v, 128 - HD // 2, 1), pltpu.roll(v, HD // 2, 1)
        )
        new = v * cos + turned * sin if forward else v * cos - turned * sin
        if (g + 1) * 128 > last:
            new = jnp.where(lane + g * 128 < last, new, v)
        parts.append(new)
    return jnp.concatenate(parts, 1) if len(parts) > 1 else parts[0]


def greet(n, nz, e, z, sib):
    barrier = pltpu.get_barrier_semaphore()
    pl.semaphore_signal(barrier, inc=1, device_id=(sib, z), device_id_type=MESH)
    for s in range(1, n // 2):
        pl.semaphore_signal(
            barrier, inc=1, device_id=(lax.rem(e + 2 * s, n), z), device_id_type=MESH
        )
    for k in range(1, nz):
        pl.semaphore_signal(barrier, inc=1, device_id=(e, lax.rem(z + k, nz)), device_id_type=MESH)
    return barrier


def expert_kernel(
    n,
    nz,
    big,
    mid_ref,
    gain_ref,
    router_ref,
    routes_ref,
    cot_ref,
    gate_hbm,
    up_hbm,
    down_hbm,
    cot_all,
    *rest,
):
    outs, rest = rest[:9], rest[9:]
    gmid_ref, glog_ref, ggrad_ref, load_ref = outs[:4]
    dgate_hbm, dup_hbm, ddown_hbm, mixed_hbm, normed_hbm = outs[4:]
    xbuf, rest = rest[0], rest[1:]
    if big:
        xstage, rest = rest[0], rest[1:]
    (
        wbuf,
        xn_s,
        wg,
        wu,
        down_ref,
        dgate,
        dup,
        ddown,
        cbuf,
        dg_s,
        du_s,
        wi_s,
        hold,
        osend,
        sin,
        hold_o,
        osend_o,
        sin_o,
        hold_g,
        osend_g,
        sin_g,
        own_s,
        own_g,
        fsend,
        fin,
        fsend_g,
        fin_g,
        zsend,
        zin,
        zsend_g,
        zin_g,
        wsem,
        gsem,
        csem,
        msem,
        lsem,
        zs,
        zr,
        zws,
        zwr,
        xs,
        xr,
        ws,
        wr,
        fs,
        fr,
        wfs,
        wfr,
        gs,
        gr,
        oss,
        osr,
        ggs,
        ggr,
        ps,
        pr,
        pgs,
        pgr,
        zgs,
        zgr,
        zggs,
        zggr,
        zds,
        zdr,
        picks_s,
    ) = rest
    e = lax.axis_index("expert")
    z = lax.axis_index("tensor")
    core = lax.rem(e, 2)
    other = 1 - core
    me = e // 2
    sib = e + 1 - 2 * core
    half = n // 2
    rows, width = mid_ref.shape
    tok = rows * nz
    experts = router_ref.shape[0]
    local_experts, _, hid = gate_hbm.shape
    inner_w = local_experts * hid
    fc = min(inner_w, 256)
    fslots = fsend.shape[0]
    square = half == 4
    chip_x = me + 1 - 2 * lax.rem(me, 2)
    chip_y = lax.rem(me + 2, 4)
    chip_d = 3 - me
    mid_row = rows // 2

    loads = []
    for el in range(local_experts):
        cols = pl.ds(el * hid, hid)
        loads.append(pltpu.make_async_copy(gate_hbm.at[el], wg.at[:, cols], wsem.at[0, el]))
        loads.append(pltpu.make_async_copy(up_hbm.at[el], wu.at[:, cols], wsem.at[1, el]))
    loads.append(pltpu.make_async_copy(down_hbm, down_ref, wsem.at[2, 0]))
    for copy in loads:
        copy.start()

    def piece_of(g):
        return lax.rem(z + nz - g, nz)

    def cot_start(g, parity, slot):
        zz = piece_of(g)
        for h in range(half):
            start = (2 * h + parity) * tok + zz * rows
            pltpu.make_async_copy(
                cot_all.at[pl.ds(pl.multiple_of(start, 16), rows)],
                cbuf.at[slot, pl.ds(h * rows, rows)],
                csem.at[slot],
            ).start()

    def cot_wait(slot):
        pltpu.make_async_copy(
            cot_all.at[pl.ds(0, half * rows)], cbuf.at[slot], csem.at[slot]
        ).wait()

    cot_start(0, core, 0)
    barrier = greet(n, nz, e, z, sib)

    own_rows = pl.ds(pl.multiple_of(z * rows, 16), rows)
    my_rows = pl.ds(pl.multiple_of(me * rows, 16), rows)
    mid = mid_ref[...]
    scale2 = lax.rsqrt(jnp.mean(mid * mid, -1, keepdims=True) + EPS)
    xn = (mid * scale2 * gain_ref[...]).astype(bf16)
    xn_s[...] = xn
    logits = dot_nt(xn, router_ref[...])
    choices = routes_ref[...].astype(f32)
    top_count = choices.shape[0]
    picks_s[...] = jnp.concatenate([choices, jnp.zeros((128 - top_count, tok), f32)], 0).T
    picks = picks_s[own_rows, 0:top_count].astype(jnp.int32)
    lanes = lax.broadcasted_iota(jnp.int32, (rows, experts), 1)
    chosen = jnp.zeros((rows, experts), f32)
    for k in range(picks.shape[1]):
        chosen = jnp.where(picks[:, k : k + 1] == lanes, 1.0, chosen)
    top = jnp.max(logits, -1, keepdims=True)
    powers = jnp.exp(logits - top)
    probs = powers / jnp.sum(powers, -1, keepdims=True)
    low_logits = jnp.where(chosen > 0.0, logits, -1e30)
    ctop = jnp.max(low_logits, -1, keepdims=True)
    cpow = jnp.exp(low_logits - ctop)
    comb = cpow / jnp.sum(cpow, -1, keepdims=True)
    padded = jnp.concatenate([comb, jnp.zeros((rows, 128 - experts), f32)], 1)
    if rows < 128:
        padded = jnp.concatenate([padded, jnp.zeros((128 - rows, 128), f32)], 0)
    piece = padded.T[:experts]
    lane_pad = jnp.zeros((1, 128 - experts), f32)
    cnt = jnp.concatenate([jnp.sum(chosen, 0, keepdims=True), lane_pad], 1)
    psum = jnp.concatenate([jnp.sum(probs, 0, keepdims=True), lane_pad], 1)
    psum_hi = psum.astype(bf16).astype(f32)
    stats = jnp.concatenate([cnt, psum_hi, psum - psum_hi, jnp.zeros((13, 128), f32)], 0)
    wbuf[z, core, me] = jnp.concatenate([piece, stats], 0).astype(bf16)
    if big:
        copy = pltpu.make_async_copy(xn_s, xbuf.at[z, core, my_rows], lsem)
        copy.start()
        copy.wait()
    else:
        xbuf[z, core, my_rows] = xn
    pl.semaphore_wait(barrier, half + nz - 1)

    def z_row(zz, k, to):
        ref = xbuf.at[zz, core, my_rows]
        return remote(ref, ref, zs.at[k - 1], zr.at[k - 1], (e, to))

    def z_small(zz, k, to):
        ref = wbuf.at[zz, core, me]
        return remote(ref, ref, zws.at[k - 1], zwr.at[k - 1], (e, to))

    def x_row(zz, h, g, s, to):
        ref = xbuf.at[zz, core, pl.ds(pl.multiple_of(h * rows, 16), rows)]
        return remote(ref, ref, xs.at[g, s], xr.at[g, s], (to, z))

    def x_small(zz, h, g, s, to):
        ref = wbuf.at[zz, core, h]
        return remote(ref, ref, ws.at[g, s], wr.at[g, s], (to, z))

    def x_part(zz, h, first, count, g, i, to):
        start = pl.multiple_of(h * rows + first, 16)
        ref = xbuf.at[zz, core, pl.ds(start, count)]
        return remote(ref, ref, xs.at[g, i], xr.at[g, i], (2 * to + core, z))

    def push_piece(g):
        zz = piece_of(g)
        if square:
            x_part(zz, me, 0, rows, g, 0, chip_x).start()
            x_part(zz, me, 0, rows, g, 1, chip_y).start()
        for s in range(1, half):
            to = lax.rem(e + 2 * s, n)
            if not square:
                x_row(zz, me, g, s, to).start()
            x_small(zz, me, g, s, to).start()

    def relays():
        low = x_part(z, chip_x, 0, mid_row, 0, 2, chip_y)
        high = x_part(z, chip_y, mid_row, rows - mid_row, 0, 3, chip_x)
        return low, high

    def z_diag(zz, k, to):
        ref = xbuf.at[zz, core, pl.ds(pl.multiple_of(chip_d * rows, 16), rows)]
        return remote(ref, ref, zds.at[k - 1], zdr.at[k - 1], (e, to))

    push_piece(jnp.int32(0))
    for k in range(1, nz):
        z_row(z, k, lax.rem(z + k, nz)).start()
        z_small(z, k, lax.rem(z + k, nz)).start()

    if square:
        low, high = relays()
        x_part(z, chip_x, 0, rows, 0, 0, chip_x).wait_recv()
        low.start()
        x_part(z, chip_y, 0, rows, 0, 1, chip_y).wait_recv()
        high.start()

    dgate[...] = jnp.zeros_like(dgate)
    dup[...] = jnp.zeros_like(dup)
    ddown[...] = jnp.zeros_like(ddown)
    for copy in loads:
        copy.wait()
    if square:
        x_part(z, chip_d, 0, mid_row, 0, 2, chip_y).wait_recv()
        x_part(z, chip_d, mid_row, rows - mid_row, 0, 3, chip_x).wait_recv()
        z_diag(z, 1, lax.rem(z + 1, nz)).start()

    sel_row = lax.broadcasted_iota(jnp.int32, (experts, fc), 0)
    sel_col = lax.broadcasted_iota(jnp.int32, (experts, fc), 1)

    def block(zz, parity, slot, dst, dst_o, dst_g, dslot):
        if big:
            copy = pltpu.make_async_copy(xbuf.at[zz, parity], xstage, lsem)
            copy.start()
            copy.wait()
            x_ref = xstage
        else:
            x_ref = xbuf.at[zz, parity]
        c_ref = cbuf.at[slot]
        sums = [jnp.zeros((experts, rows), f32) for _ in range(half)]
        for q in range(inner_w // fc):
            cols = slice(q * fc, (q + 1) * fc)
            x = x_ref[...]
            gate_val = dot_nn(x, wg[:, cols])
            up_val = dot_nn(x, wu[:, cols])
            back = dot_nt(c_ref[...], down_ref[cols, :])
            select = jnp.where(
                sel_row == e * local_experts + (q * fc + sel_col) // hid, 1.0, 0.0
            ).astype(bf16)
            wide = jnp.concatenate(
                [dot_tn(wbuf[zz, parity, h, :experts, :], select)[:rows] for h in range(half)], 0
            )
            sig = 1.0 / (1.0 + jnp.exp(-gate_val))
            silu = gate_val * sig
            inner = silu * up_val
            wi_s[:, cols] = (inner * wide).astype(bf16)
            scaled = back * wide
            dg_s[:, cols] = (scaled * up_val * (sig * (1.0 + gate_val * (1.0 - sig)))).astype(bf16)
            du_s[:, cols] = (scaled * silu).astype(bf16)
            both = (inner * back).astype(bf16)
            for h in range(half):
                sums[h] = sums[h] + dot_nt(select, both[h * rows : (h + 1) * rows])
        for h in range(half):
            gap = jnp.zeros((experts, 128 - rows), f32)
            dst_g[dslot, h] = jnp.concatenate([sums[h], gap], 1).astype(bf16)
        for h in range(width // 256):
            cols = slice(h * 256, (h + 1) * 256)
            dst[dslot, :, cols] = (
                dot_nt(dg_s[...], wg[cols, :]) + dot_nt(du_s[...], wu[cols, :])
            ).astype(bf16)
            dst_o[dslot, :, cols] = dot_nn(wi_s[...], down_ref[:, cols]).astype(bf16)
        for h in range(width // 256):
            cols = slice(h * 256, (h + 1) * 256)
            x_part = x_ref[:, cols]
            gate_part = dot_tn(x_part, dg_s[...])
            up_part = dot_tn(x_part, du_s[...])
            for el in range(local_experts):
                dgate[el, cols, :] += gate_part[:, el * hid : (el + 1) * hid]
                dup[el, cols, :] += up_part[:, el * hid : (el + 1) * hid]
            ddown[:, cols] += dot_tn(wi_s[...], c_ref[:, cols])

    def gives(slot):
        return [
            remote(osend.at[slot], sin.at[slot], gs.at[slot], gr.at[slot], (sib, z)),
            remote(osend_g.at[slot], sin_g.at[slot], ggs.at[slot], ggr.at[slot], (sib, z)),
            remote(osend_o.at[slot], sin_o.at[slot], oss.at[slot], osr.at[slot], (sib, z)),
        ]

    def finals(g, s, to):
        at = lax.rem(g, fslots)
        rows_copy = []
        if not square:
            rows_copy = [
                remote(
                    fsend.at[at, s - 1], fin.at[g, s - 1], ps.at[g, s - 1], pr.at[g, s - 1], (to, z)
                )
            ]
        return rows_copy + [
            remote(
                fsend_g.at[at, s - 1],
                fin_g.at[g, s - 1],
                pgs.at[g, s - 1],
                pgr.at[g, s - 1],
                (to, z),
            ),
        ]

    def half_copy(g, buf, upper, i, chip):
        first, count = (mid_row, rows - mid_row) if upper else (0, mid_row)
        return remote(
            fsend.at[g, buf, pl.ds(first, count)],
            fin.at[g, buf, pl.ds(first, count)],
            ps.at[g, i],
            pr.at[g, i],
            (2 * chip + core, z),
        )

    def half_copies(g):
        return [
            half_copy(g, 2, False, 0, chip_x),
            half_copy(g, 2, True, 1, chip_y),
            half_copy(g, 0, False, 2, chip_x),
            half_copy(g, 1, True, 3, chip_y),
            half_copy(g, 1, False, 4, chip_y),
            half_copy(g, 0, True, 5, chip_x),
        ]

    def chip_sum(slot, chip, upper):
        first, count = (mid_row, rows - mid_row) if upper else (0, mid_row)
        at = pl.ds(pl.multiple_of(chip * rows + first, 16), count)
        return hold[slot, at, :].astype(f32) + sin[slot, at, :].astype(f32)

    def direct_stage(g):
        slot = lax.rem(g, 2)
        copies = half_copies(g)
        fsend[g, 2, :mid_row] = chip_sum(slot, chip_d, False).astype(bf16)
        copies[0].start()
        fsend[g, 2, mid_row:] = chip_sum(slot, chip_d, True).astype(bf16)
        copies[1].start()
        fsend[g, 0, :mid_row] = chip_sum(slot, chip_x, False).astype(bf16)
        copies[2].start()
        fsend[g, 1, mid_row:] = chip_sum(slot, chip_y, True).astype(bf16)
        copies[3].start()

    def relay_stage(g):
        slot = lax.rem(g, 2)
        copies = half_copies(g)
        copies[0].wait_recv()
        passed = chip_sum(slot, chip_y, False) + fin[g, 2, :mid_row].astype(f32)
        fsend[g, 1, :mid_row] = passed.astype(bf16)
        copies[4].start()
        copies[1].wait_recv()
        passed = chip_sum(slot, chip_x, True) + fin[g, 2, mid_row:].astype(f32)
        fsend[g, 0, mid_row:] = passed.astype(bf16)
        copies[5].start()

    def lasts(k, to):
        return [
            remote(zsend.at[k - 1], zin.at[k - 1], zgs.at[k - 1], zgr.at[k - 1], (e, to)),
            remote(zsend_g.at[k - 1], zin_g.at[k - 1], zggs.at[k - 1], zggr.at[k - 1], (e, to)),
        ]

    def mixed_copy(g, slot):
        return pltpu.make_async_copy(hold_o.at[slot], mixed_hbm.at[piece_of(g)], msem.at[slot])

    def plane_stage(g):
        slot = lax.rem(g, 2)
        for copy in gives(slot)[:2]:
            copy.wait_recv()
        if fslots < nz:

            @pl.when(g >= fslots)
            def _():
                for s in range(1, half):
                    for copy in finals(g - fslots, s, sib):
                        copy.wait_send()

        spot = lax.rem(g, fslots)
        if square:
            direct_stage(g)
        for s in range(1, half):
            h = lax.rem(me + half - s, half)
            at = pl.ds(pl.multiple_of(h * rows, 16), rows)
            if not square:
                fsend[spot, s - 1] = (
                    hold[slot, at, :].astype(f32) + sin[slot, at, :].astype(f32)
                ).astype(bf16)
            fsend_g[spot, s - 1] = (hold_g[slot, h].astype(f32) + sin_g[slot, h].astype(f32)).astype(
                bf16
            )
            for copy in finals(g, s, lax.rem(e - 2 * s + n, n)):
                copy.start()
        own_s[g] = hold[slot, my_rows, :].astype(f32) + sin[slot, my_rows, :].astype(f32)
        own_g[g] = hold_g[slot, me].astype(f32) + sin_g[slot, me].astype(f32)

    def mixed_stage(g):
        slot = lax.rem(g, 2)
        gives(slot)[2].wait_recv()
        hold_o[slot] = (hold_o[slot].astype(f32) + sin_o[slot].astype(f32)).astype(bf16)
        mixed_copy(g, slot).start()

    def tensor_stage(g):
        total = own_s[g]
        total_g = own_g[g]
        for s in range(1, half):
            for copy in finals(g, s, sib):
                copy.wait_recv()
            if not square:
                total = total + fin[g, s - 1].astype(f32)
            total_g = total_g + fin_g[g, s - 1].astype(f32)

        if square:
            for copy in half_copies(g)[2:]:
                copy.wait_recv()
            total = total + fin[g, 0].astype(f32) + fin[g, 1].astype(f32)

        @pl.when(g == 0)
        def _():
            own_s[0] = total
            own_g[0] = total_g

        @pl.when(g > 0)
        def _():
            zsend[g - 1] = total.astype(bf16)
            zsend_g[g - 1] = total_g.astype(bf16)
            for copy in lasts(g, piece_of(g)):
                copy.start()

    def step(g, carry):
        zz = piece_of(g)
        slot = lax.rem(g, 2)

        @pl.when(g < nz - 1)
        def _():
            coming = piece_of(g + 1)
            z_row(coming, g + 1, coming).wait_recv()
            z_small(coming, g + 1, coming).wait_recv()
            push_piece(g + 1)

        if square:

            @pl.when(g > 0)
            def _():
                x_part(zz, chip_x, 0, rows, g, 0, chip_x).wait_recv()
                x_part(zz, chip_y, 0, rows, g, 1, chip_y).wait_recv()
                z_diag(zz, g, zz).wait_recv()

        for s in range(1, half):
            h = lax.rem(me + half - s, half)
            src = 2 * h + core
            if not square:
                x_row(zz, h, g, s, src).wait_recv()
            x_small(zz, h, g, s, src).wait_recv()
        for copy in forward(zz, core, g):
            copy.start()
        cot_start(g, other, 1)
        cot_wait(0)

        @pl.when(g >= 2)
        def _():
            mixed_copy(g - 2, slot).wait()

        block(zz, core, 0, hold, hold_o, hold_g, slot)
        if square:
            for k in range(2, nz):

                @pl.when(g == k - 2)
                def _():
                    z_diag(z, k, lax.rem(z + k, nz)).start()


        @pl.when(g < nz - 1)
        def _():
            cot_start(g + 1, core, 0)

        @pl.when(g >= 2)
        def _():
            tensor_stage(g - 2)

        @pl.when(g >= 1)
        def _():
            plane_stage(g - 1)
            mixed_stage(g - 1)

        @pl.when(g >= 2)
        def _():
            for copy in gives(slot):
                copy.wait_send()

        for copy in forward(zz, other, g):
            copy.wait_recv()
        cot_wait(1)
        block(zz, other, 1, osend, osend_o, osend_g, slot)
        for copy in gives(slot):
            copy.start()
        if square:

            @pl.when(g >= 1)
            def _():
                relay_stage(g - 1)

        return carry

    def forward(zz, parity, g):
        ref = xbuf.at[zz, parity]
        small = wbuf.at[zz, parity]
        return (
            remote(ref, ref, fs.at[g], fr.at[g], (sib, z)),
            remote(small, small, wfs.at[g], wfr.at[g], (sib, z)),
        )

    lax.fori_loop(0, nz, step, 0)
    grads = [
        pltpu.make_async_copy(dgate, dgate_hbm, gsem.at[0]),
        pltpu.make_async_copy(dup, dup_hbm, gsem.at[1]),
        pltpu.make_async_copy(ddown, ddown_hbm, gsem.at[2]),
        pltpu.make_async_copy(xbuf.at[:, core, my_rows, :], normed_hbm, gsem.at[3]),
    ]
    plane_stage(jnp.int32(nz - 1))
    for copy in grads:
        copy.start()
    if nz >= 2:
        tensor_stage(jnp.int32(nz - 2))
    if square:
        relay_stage(jnp.int32(nz - 1))

    def total_stats(j, carry):
        for zz in range(nz):
            for parity in range(2):
                carry = carry + wbuf[zz, parity, j, experts:, :].astype(f32)
        return carry

    stats = lax.fori_loop(0, half, total_stats, jnp.zeros((16, 128), f32))
    total_rows = n * tok
    share = stats[0:1, :experts] / (total_rows * top_count)
    load_ref[...] = (
        experts * experts * share * ((stats[1:2, :experts] + stats[2:3, :experts]) / total_rows)
    )
    loss_w = experts * share / total_rows
    mixed_stage(jnp.int32(nz - 1))
    tensor_stage(jnp.int32(nz - 1))

    gate_sums = own_g[0]
    grad_rows = own_s[0]
    for k in range(1, nz):
        for copy in lasts(k, z):
            copy.wait_recv()
        gate_sums = gate_sums + zin_g[k - 1].astype(f32)
        grad_rows = grad_rows + zin[k - 1].astype(f32)
    grow = jnp.concatenate([gate_sums, jnp.zeros((128 - experts, 128), f32)], 0).T
    grad_gates = grow[:rows, :experts]
    grad_logits = comb * (grad_gates - jnp.sum(grad_gates * comb, -1, keepdims=True))
    grad_logits = grad_logits + probs * (loss_w - jnp.sum(loss_w * probs, -1, keepdims=True))
    low_grad = grad_logits.astype(bf16)
    wide_grad = jnp.concatenate([grad_logits, jnp.zeros((rows, 128 - experts), f32)], 1)
    if rows < 128:
        wide_grad = jnp.concatenate([wide_grad, jnp.zeros((128 - rows, 128), f32)], 0)
    glog_ref[...] = wide_grad.T[:experts].astype(bf16)
    grad_rows = grad_rows + dot_nn(low_grad, router_ref[...])
    mid = mid_ref[...]
    ggrad_ref[...] = jnp.sum(grad_rows * mid * scale2, 0, keepdims=True)
    gained = grad_rows * gain_ref[...]
    gmid_ref[...] = (
        cot_ref[own_rows, :]
        + scale2 * gained
        - mid * (scale2 * scale2 * scale2) * jnp.mean(gained * mid, -1, keepdims=True)
    )

    for copy in grads:
        copy.wait()
    if square:
        for copy in relays():
            copy.wait_send()
        for k in range(1, nz):
            z_diag(z, k, z).wait_send()
    for k in range(1, nz):
        z_row(z, k, z).wait_send()
        z_small(z, k, z).wait_send()
        for copy in lasts(k, z):
            copy.wait_send()
    for g in range(max(0, nz - 2), nz):
        mixed_copy(jnp.int32(g), g % 2).wait()
        for copy in gives(g % 2):
            copy.wait_send()

    def drained(g, carry):
        if square:
            x_part(z, me, 0, rows, g, 0, chip_x).wait_send()
            x_part(z, me, 0, rows, g, 1, chip_y).wait_send()
            for copy in half_copies(g):
                copy.wait_send()
        for s in range(1, half):
            if not square:
                x_row(z, me, g, s, sib).wait_send()
            x_small(z, me, g, s, sib).wait_send()
        for copy in forward(z, core, g):
            copy.wait_send()
        return carry

    lax.fori_loop(0, nz, drained, 0)

    def sums_sent(g, carry):
        for s in range(1, half):
            for copy in finals(g, s, sib):
                copy.wait_send()
        return carry

    lax.fori_loop(nz - fslots, nz, sums_sent, 0)


def expert_layer(n, nz, mid, gain, router, routes, gate, up, down, cot, cot_all):
    rows, width = mid.shape
    experts = router.shape[1]
    local_experts, _, hid = gate.shape
    inner_w = local_experts * hid
    half = n // 2
    batch = half * rows
    big = n > 8
    fslots = 2 if big else nz
    dma = pltpu.SemaphoreType.DMA
    vmem = pl.BlockSpec(memory_space=pltpu.VMEM)
    hbm = pl.BlockSpec(memory_space=pl.ANY)
    sds = jax.ShapeDtypeStruct
    out_shape = [
        sds((rows, width), f32),
        sds((experts, 128), bf16),
        sds((1, width), f32),
        sds((1, experts), f32),
        sds((local_experts, width, hid), f32),
        sds((local_experts, width, hid), f32),
        sds((inner_w, width), f32),
        sds((nz, batch, width), bf16),
        sds((nz, rows, width), bf16),
    ]
    out_specs = [vmem] * 4 + [hbm] * 5
    scratch = []
    if big:
        out_shape.append(sds((nz, 2, batch, width), bf16))
        out_specs.append(hbm)
        scratch.append(pltpu.VMEM((batch, width), bf16))
    else:
        scratch.append(pltpu.VMEM((nz, 2, batch, width), bf16))
    pair = pltpu.VMEM((2, batch, width), bf16)
    small = pltpu.VMEM((2, half, experts, 128), bf16)
    scratch += [
        pltpu.VMEM((nz, 2, half, experts + 16, 128), bf16),
        pltpu.VMEM((rows, width), bf16),
        pltpu.VMEM((width, inner_w), bf16),
        pltpu.VMEM((width, inner_w), bf16),
        pltpu.VMEM((inner_w, width), bf16),
        pltpu.VMEM((local_experts, width, hid), f32),
        pltpu.VMEM((local_experts, width, hid), f32),
        pltpu.VMEM((inner_w, width), f32),
        pair,
        pltpu.VMEM((batch, inner_w), bf16),
        pltpu.VMEM((batch, inner_w), bf16),
        pltpu.VMEM((batch, inner_w), bf16),
        pair,
        pair,
        pair,
        pair,
        pair,
        pair,
        small,
        small,
        small,
        pltpu.VMEM((nz, rows, width), f32),
        pltpu.VMEM((nz, experts, 128), f32),
        pltpu.VMEM((fslots, half - 1, rows, width), bf16),
        pltpu.VMEM((nz, half - 1, rows, width), bf16),
        pltpu.VMEM((fslots, half - 1, experts, 128), bf16),
        pltpu.VMEM((nz, half - 1, experts, 128), bf16),
        pltpu.VMEM((nz - 1, rows, width), bf16),
        pltpu.VMEM((nz - 1, rows, width), bf16),
        pltpu.VMEM((nz - 1, experts, 128), bf16),
        pltpu.VMEM((nz - 1, experts, 128), bf16),
        dma((3, local_experts)),
        dma((4,)),
        dma((2,)),
        dma((2,)),
        dma,
    ]
    scratch += [dma((nz - 1,))] * 4
    scratch += [dma((nz, half))] * 4
    scratch += [dma((nz,))] * 4
    scratch += [dma((2,))] * 6
    scratch += [dma((nz, 6 if half == 4 else half - 1))] * 2
    scratch += [dma((nz, half - 1))] * 2
    scratch += [dma((nz - 1,))] * 6 + [pltpu.VMEM((nz * rows, 128), f32)]
    return pl.pallas_call(
        functools.partial(expert_kernel, n, nz, big),
        out_shape=out_shape,
        in_specs=[vmem] * 5 + [hbm] * 4,
        out_specs=out_specs,
        scratch_shapes=scratch,
        compiler_params=pltpu.CompilerParams(
            collective_id=1, has_side_effects=True, vmem_limit_bytes=60 << 20
        ),
        name="experts",
    )(mid, gain[None], router.T, routes.T, cot, gate, up, down.reshape(inner_w, width), cot_all)[:9]


def attend_kernel(
    n,
    nz,
    x_ref,
    gain_ref,
    wq_ref,
    wk_ref,
    wv_ref,
    wo_ref,
    cos_ref,
    sin_ref,
    lens_ref,
    mid_ref,
    q_ref,
    kv_ref,
    lrow_ref,
    att_ref,
    wqkv,
    wfull,
    qst_s,
    m_s,
    l_s,
    o_s,
    att_low,
    acol,
    ks,
    kr,
    kfs,
    kfr,
    zgs,
    zgr,
    gos,
    gor,
    gps,
    gpr,
):
    e = lax.axis_index("expert")
    z = lax.axis_index("tensor")
    core = lax.rem(e, 2)
    sib = e + 1 - 2 * core
    half = n // 2
    tok, width = x_ref.shape
    rows = tok // nz
    qw = wq_ref.shape[1]
    kw = wk_ref.shape[1]
    seqs = kv_ref.shape[0]
    span = tok // seqs
    heads = kw // HD
    groups = qw // kw
    barrier = greet(n, nz, e, z, sib)

    wqkv[:, 0:qw] = wq_ref[...]
    wqkv[:, qw : qw + kw] = wk_ref[...]
    wqkv[:, qw + kw :] = wv_ref[...]
    x = x_ref[...].astype(f32)
    scale1 = lax.rsqrt(jnp.mean(x * x, -1, keepdims=True) + EPS)
    normed = (x * scale1 * gain_ref[...]).astype(bf16)
    lin = dot_nn(normed, wqkv[...])
    turned = turn(lin, cos_ref[...], sin_ref[...], qw + kw, True).astype(bf16)
    q_ref[...] = turned[:, :qw]
    for s in range(seqs):
        kv_ref[s, pl.ds(pl.multiple_of(e * span, 16), span)] = turned[
            s * span : (s + 1) * span, qw:
        ]
    pl.semaphore_wait(barrier, half + nz - 1)

    def rows_of(j, s):
        return kv_ref.at[s, pl.ds(pl.multiple_of(j * span, 16), span)]

    half_rows = qw // 2
    my_half = pl.ds(pl.multiple_of(core * half_rows, 16), half_rows)

    def weight_send(k):
        to = (e, lax.rem(z + k, nz))
        return remote(
            wo_ref.at[my_half], wfull.at[z, my_half], gos.at[k - 1], gor.at[k - 1], to
        )

    def weight_copy(zz, k, to):
        ref = wfull.at[zz, my_half]
        return remote(ref, ref, gos.at[k - 1], gor.at[k - 1], (e, to))

    def weight_pass(zz, which, k):
        at = pl.ds(pl.multiple_of(which * half_rows, 16), half_rows)
        ref = wfull.at[zz, at]
        return remote(ref, ref, gps.at[k - 1], gpr.at[k - 1], (sib, z))

    for t in range(1, half):
        to = (lax.rem(e + 2 * t, n), z)
        for s in range(seqs):
            remote(rows_of(e, s), rows_of(e, s), ks.at[t, s], kr.at[t, s], to).start()
    for s in range(seqs):
        remote(rows_of(e, s), rows_of(e, s), kfs.at[0, s], kfr.at[0, s], (sib, z)).start()
    for k in range(1, nz):
        weight_send(k).start()
    wfull[z] = wo_ref[...]

    def forward(t, carry):
        src = lax.rem(e - 2 * t + n, n)
        for s in range(seqs):
            remote(rows_of(src, s), rows_of(src, s), ks.at[t, s], kr.at[t, s], (src, z)).wait_recv()
            remote(rows_of(src, s), rows_of(src, s), kfs.at[t, s], kfr.at[t, s], (sib, z)).start()
        return carry

    lax.fori_loop(1, half, forward, 0)

    def arrive(t, carry):
        src = lax.rem(sib - 2 * t + n, n)
        for s in range(seqs):
            remote(
                rows_of(src, s), rows_of(src, s), kfs.at[t, s], kfr.at[t, s], (sib, z)
            ).wait_recv()
        return carry

    lax.fori_loop(0, half, arrive, 0)

    ck = 2 * span
    last = (e * span + span - 1) // ck
    stacked = groups * span
    qpos = lax.broadcasted_iota(jnp.int32, (stacked, ck), 0)
    qpos = e * span + lax.rem(qpos, span)
    kiota = lax.broadcasted_iota(jnp.int32, (stacked, ck), 1)
    klane = lax.broadcasted_iota(jnp.int32, (1, ck), 1)
    m_s[...] = jnp.full_like(m_s, -1e30)
    l_s[...] = jnp.zeros_like(l_s)
    o_s[...] = jnp.zeros_like(o_s)
    for s in range(seqs):
        for h in range(heads):
            qst_s[s * heads + h] = jnp.concatenate(
                [
                    q_ref[
                        s * span : (s + 1) * span,
                        (h * groups + g) * HD : (h * groups + g + 1) * HD,
                    ]
                    for g in range(groups)
                ],
                0,
            ) * jnp.array(HD ** (-0.5), bf16)

    def chunk(c, diagonal):
        at = pl.ds(pl.multiple_of(c * ck, 16), ck)
        for s in range(seqs):
            for h in range(heads):
                i = s * heads + h
                keys = kv_ref[s, at, h * HD : (h + 1) * HD]
                vals = kv_ref[s, at, kw + h * HD : kw + (h + 1) * HD]
                scores = dot_nt(qst_s[i], keys)
                if diagonal:
                    kpos = kiota + c * ck
                    scores = jnp.where((kpos <= qpos) & (kpos < lens_ref[s]), scores, -1e30)
                else:
                    scores = scores + jnp.where(klane + c * ck < lens_ref[s], 0.0, -1e30)
                old = m_s[i, :, 0:1]
                new = jnp.maximum(old, jnp.max(scores, -1, keepdims=True))
                weights = jnp.exp(scores - new)
                shrink = jnp.exp(old - new)
                m_s[i] = jnp.broadcast_to(new, (stacked, 128))
                l_s[i] = l_s[i] * shrink + jnp.sum(weights, -1, keepdims=True)
                o_s[i] = o_s[i] * shrink + dot_nn(weights.astype(bf16), vals)

    def whole_chunk(c, carry):
        chunk(c, False)
        return carry

    lax.fori_loop(0, last, whole_chunk, 0)
    chunk(last, True)
    for s in range(seqs):
        for h in range(heads):
            i = s * heads + h
            result = o_s[i] / l_s[i, :, 0:HD]
            for g in range(groups):
                cols = slice((h * groups + g) * HD, (h * groups + g + 1) * HD)
                att_ref[s * span : (s + 1) * span, cols] = result[g * span : (g + 1) * span]
            logs = m_s[i] + jnp.log(l_s[i])
            lrow_ref[i] = logs.T[0:8]

    att_low[...] = att_ref[...].astype(bf16)
    own_rows = pl.ds(pl.multiple_of(z * rows, 16), rows)

    def row_copy(k, to):
        src = att_low.at[pl.ds(pl.multiple_of(to * rows, 16), rows)]
        return remote(src, acol.at[z], zgs.at[k - 1], zgr.at[k - 1], (e, to))

    for k in range(1, nz):
        row_copy(k, lax.rem(z + k, nz)).start()
    acol[z] = att_low[own_rows, :]
    for k in range(1, nz):
        zz = lax.rem(z + nz - k, nz)
        weight_copy(zz, k, zz).wait_recv()
        weight_pass(zz, core, k).start()
    for k in range(1, nz):
        row_copy(k, lax.rem(z + nz - k, nz)).wait_recv()
        weight_pass(lax.rem(z + nz - k, nz), 1 - core, k).wait_recv()
    mid = x_ref[own_rows, :].astype(f32)
    for zz in range(nz):
        mid = mid + dot_nn(acol[zz], wfull[zz])
    mid_ref[...] = mid
    for k in range(1, nz):
        row_copy(k, lax.rem(z + k, nz)).wait_send()
        weight_send(k).wait_send()
        weight_pass(lax.rem(z + nz - k, nz), core, k).wait_send()

    def sent(t, carry):
        for s in range(seqs):

            @pl.when(t > 0)
            def _():
                remote(
                    rows_of(e, s), rows_of(e, s), ks.at[t, s], kr.at[t, s], (sib, z)
                ).wait_send()

            remote(rows_of(e, s), rows_of(e, s), kfs.at[t, s], kfr.at[t, s], (sib, z)).wait_send()
        return carry

    lax.fori_loop(0, half, sent, 0)


def attend_layer(n, nz, x, gain, wq, wk, wv, wo, cos, sin, lens):
    tok, width = x.shape
    rows = tok // nz
    qw, kw = wq.shape[1], wk.shape[1]
    seqs = lens.shape[0]
    span = tok // seqs
    half = n // 2
    stacked = (qw // kw) * span
    pairs = seqs * (kw // HD)
    dma = pltpu.SemaphoreType.DMA
    vmem = pl.BlockSpec(memory_space=pltpu.VMEM)
    sds = jax.ShapeDtypeStruct
    return pl.pallas_call(
        functools.partial(attend_kernel, n, nz),
        out_shape=[
            sds((rows, width), f32),
            sds((tok, qw), bf16),
            sds((seqs, n * span, 2 * kw), bf16),
            sds((seqs * (kw // HD), 8, stacked), f32),
            sds((tok, qw), f32),
        ],
        in_specs=[vmem] * 8 + [pl.BlockSpec(memory_space=pltpu.SMEM)],
        out_specs=[vmem] * 5,
        scratch_shapes=[
            pltpu.VMEM((width, qw + 2 * kw), bf16),
            pltpu.VMEM((nz, qw, width), bf16),
            pltpu.VMEM((pairs, stacked, HD), bf16),
            pltpu.VMEM((pairs, stacked, 128), f32),
            pltpu.VMEM((pairs, stacked, 128), f32),
            pltpu.VMEM((pairs, stacked, HD), f32),
            pltpu.VMEM((tok, qw), bf16),
            pltpu.VMEM((nz, rows, qw), bf16),
        ]
        + [dma((half, seqs))] * 4
        + [dma((nz - 1,))] * 6,
        compiler_params=pltpu.CompilerParams(
            collective_id=2, has_side_effects=True, vmem_limit_bytes=60 << 20
        ),
        name="attend",
    )(x, gain[None], wq, wk, wv, wo, cos, sin, lens)


def return_kernel(
    n,
    nz,
    gmid_ref,
    mid_ref,
    glog_ref,
    ggrad_ref,
    xn_ref,
    x_ref,
    gain_ref,
    wq_ref,
    wk_ref,
    wv_ref,
    wo_ref,
    cos_ref,
    sin_ref,
    q_ref,
    kv_ref,
    lrow_ref,
    att_ref,
    lens_ref,
    mixed_hbm,
    obuf,
    igbuf,
    wall,
    wall2,
    small_ref,
    wqkv,
    gat,
    datt,
    dq_s,
    qst_s,
    dst_s,
    acc_q,
    dkv,
    kvo,
    kvi,
    kvf,
    kvr,
    part,
    sums,
    csend,
    crecv,
    osend,
    orecv,
    wbufs,
    wbufs2,
    sz1,
    sz2,
    sown,
    ssib,
    schip,
    ofin,
    zas,
    zar,
    zos,
    zor,
    zis,
    zir,
    zps,
    zpr,
    zqs,
    zqr,
    z1s,
    z1r,
    z2s,
    z2r,
    kos,
    kor,
    kfs,
    kfr,
    wsems,
    wsems2,
    sbs,
    sbr,
    scs,
    scr,
    ofs,
    ofr,
    olsem,
):
    e = lax.axis_index("expert")
    z = lax.axis_index("tensor")
    core = lax.rem(e, 2)
    me = e // 2
    sib = e + 1 - 2 * core
    half = n // 2
    rows, width = gmid_ref.shape
    tok = rows * nz
    qw = wq_ref.shape[1]
    kw = wk_ref.shape[1]
    seqs = kv_ref.shape[0]
    span = tok // seqs
    heads = kw // HD
    groups = qw // kw
    dn = width // n
    experts = glog_ref.shape[0]
    own_rows = pl.ds(pl.multiple_of(z * rows, 16), rows)
    barrier = greet(n, nz, e, z, sib)
    w1 = PlaneSum(n, e, z, sib, wall, *wbufs, *wsems)
    w2 = PlaneSum(n, e, z, sib, wall2, *wbufs2, *wsems2)

    gat[own_rows, :] = gmid_ref[...].astype(bf16)
    sz1[z] = glog_ref[...]
    pl.semaphore_wait(barrier, half + nz - 1)

    def part_of(ref):
        return lambda zz: ref.at[pl.ds(pl.multiple_of(zz * rows, 16), rows)]

    def slot_of(ref):
        return lambda zz: ref.at[zz]

    gat_line = Line(z, nz, e, part_of(gat), zas, zar)
    out_line = Line(z, nz, e, part_of(obuf), zos, zor)
    igrad_line = Line(z, nz, e, part_of(igbuf), zis, zir)
    normed_sum = LineSum(z, nz, e, csend, crecv, zps, zpr)

    def z_copies(buf_of, send, recv):
        return [
            remote(
                buf_of(z), buf_of(z), send.at[k - 1], recv.at[k - 1], (e, lax.rem(z + k, nz))
            )
            for k in range(1, nz)
        ]

    def z_arrivals(buf_of, send, recv):
        return [
            remote(
                buf_of(lax.rem(z + nz - k, nz)),
                buf_of(lax.rem(z + nz - k, nz)),
                send.at[k - 1],
                recv.at[k - 1],
                (e, lax.rem(z + nz - k, nz)),
            )
            for k in range(1, nz)
        ]

    gat_line.start()
    for copy in z_copies(slot_of(sz1), z1s, z1r):
        copy.start()

    def mixed_send(t):
        h = lax.rem(me + half - t, half)
        return remote(
            mixed_hbm.at[:, pl.ds(pl.multiple_of(h * rows, 16), rows), :],
            ofin.at[t],
            ofs.at[t - 1],
            ofr.at[t - 1],
            (lax.rem(e - 2 * t + n, n), z),
        )

    for t in range(1, half):
        mixed_send(t).start()
    mixed_own = pltpu.make_async_copy(
        mixed_hbm.at[:, pl.ds(pl.multiple_of(me * rows, 16), rows), :], ofin.at[0], olsem
    )
    mixed_own.start()

    def mixed_sum(zz):
        total = ofin[0, zz].astype(f32)
        for t in range(1, half):
            total = total + ofin[t, zz].astype(f32)
        return total

    wqkv[:, 0:qw] = wq_ref[...]
    wqkv[:, qw : qw + kw] = wk_ref[...]
    wqkv[:, qw + kw :] = wv_ref[...]
    x = x_ref[...].astype(f32)
    scale1 = lax.rsqrt(jnp.mean(x * x, -1, keepdims=True) + EPS)
    normed = (x * scale1 * gain_ref[...]).astype(bf16)
    dkv[...] = jnp.zeros_like(dkv)

    for hop in range(1, nz):
        gat_line.hop(hop)
    datt[...] = dot_nt(gat[...], wo_ref[...]).astype(bf16)

    ck = 2 * span
    last = (e * span + span - 1) // ck
    stacked = groups * span
    kiota = lax.broadcasted_iota(jnp.int32, (ck, stacked), 0)
    krow = lax.broadcasted_iota(jnp.int32, (ck, 1), 0)
    qpos = e * span + lax.rem(lax.broadcasted_iota(jnp.int32, (ck, stacked), 1), span)
    drows = []
    for s in range(seqs):
        for h in range(heads):

            def gather(ref):
                return jnp.concatenate(
                    [
                        ref[
                            s * span : (s + 1) * span,
                            (h * groups + g) * HD : (h * groups + g + 1) * HD,
                        ]
                        for g in range(groups)
                    ],
                    0,
                )

            i = s * heads + h
            qst_s[i] = gather(q_ref) * jnp.array(HD ** (-0.5), bf16)
            dst = gather(datt)
            dst_s[i] = dst
            delta = jnp.sum(dst.astype(f32) * gather(att_ref), -1, keepdims=True)
            drows.append(jnp.broadcast_to(delta, (stacked, 128)).T[0:1])
    acc_q[...] = jnp.zeros_like(acc_q)

    def chunk(c, diagonal):
        at = pl.ds(pl.multiple_of(c * ck, 16), ck)
        for s in range(seqs):
            for h in range(heads):
                i = s * heads + h
                keys = kv_ref[s, at, h * HD : (h + 1) * HD]
                vals = kv_ref[s, at, kw + h * HD : kw + (h + 1) * HD]
                scores = dot_nt(keys, qst_s[i]) - lrow_ref[i, 0:1, :]
                if diagonal:
                    kpos = kiota + c * ck
                    allowed = (kpos <= qpos) & (kpos < lens_ref[s])
                    soft = jnp.where(allowed, jnp.exp(scores), 0.0)
                else:
                    soft = jnp.exp(scores + jnp.where(krow + c * ck < lens_ref[s], 0.0, -1e30))
                grad_probs = dot_nt(vals, dst_s[i])
                grad_scores = (soft * (grad_probs - drows[i])).astype(bf16)
                dkv[s, at, h * HD : (h + 1) * HD] = dot_nn(grad_scores, qst_s[i])
                dkv[s, at, kw + h * HD : kw + (h + 1) * HD] = dot_nn(soft.astype(bf16), dst_s[i])
                acc_q[i] += dot_tn(grad_scores, keys)

    def whole_chunk(c, carry):
        chunk(c, False)
        return carry

    lax.fori_loop(0, last, whole_chunk, 0)
    chunk(last, True)
    for s in range(seqs):
        for h in range(heads):
            result = acc_q[s * heads + h] * HD ** (-0.5)
            for g in range(groups):
                cols = slice((h * groups + g) * HD, (h * groups + g + 1) * HD)
                dq_s[s * span : (s + 1) * span, cols] = result[g * span : (g + 1) * span]

    def key_rows(j, s):
        return dkv[s, pl.ds(pl.multiple_of(j * span, 16), span), :]

    def key_send(t):
        return remote(kvo.at[t], kvi.at[t], kos.at[t], kor.at[t], (sib, z))

    def key_final(t):
        to = (lax.rem(e - 2 * t + n, n), z)
        return remote(kvf.at[t - 1], kvr.at[t - 1], kfs.at[t - 1], kfr.at[t - 1], to)

    def key_give(i, carry):
        t = half - 1 - i
        oth = lax.rem(sib - 2 * t + n, n)
        for s in range(seqs):
            kvo[t, s] = key_rows(oth, s).astype(bf16)
        key_send(t).start()
        return carry

    lax.fori_loop(0, half, key_give, 0)

    def key_pass(i, carry):
        t = half - 1 - i
        key_send(t).wait_recv()
        own = lax.rem(e - 2 * t + n, n)
        for s in range(seqs):
            kvf[t - 1, s] = (key_rows(own, s) + kvi[t, s].astype(f32)).astype(bf16)
        key_final(t).start()
        return carry

    cos, sin = cos_ref[...], sin_ref[...]
    gq = turn(dq_s[...], cos, sin, qw, False).astype(bf16)
    query_part = dot_tn(normed, gq)
    out_part = dot_tn(gat[...], att_ref[...].astype(bf16))
    for j in range(n):
        w1.pack[j, :, :qw] = query_part[j * dn : (j + 1) * dn].astype(bf16)
        w1.pack[j, :, qw:] = out_part[j * dn : (j + 1) * dn].astype(bf16)
    lax.fori_loop(0, half - 1, key_pass, 0)
    w1.give()

    def mixed_last(k, to):
        return remote(osend.at[k - 1], orecv.at[k - 1], zqs.at[k - 1], zqr.at[k - 1], (e, to))

    mixed_own.wait()
    for t in range(1, half):
        mixed_send(t).wait_recv()
    for k in range(1, nz):
        zz = lax.rem(z + k, nz)
        osend[k - 1] = mixed_sum(zz).astype(bf16)
        mixed_last(k, zz).start()
    own_mixed = mid_ref[...] + mixed_sum(z)
    w1.spread()
    for copy in z_arrivals(slot_of(sz1), z1s, z1r):
        copy.wait_recv()
    rgrad = dot_nn(sz1[0][:, :rows], xn_ref[0])
    for zz in range(1, nz):
        rgrad = rgrad + dot_nn(sz1[zz][:, :rows], xn_ref[zz])
    sown[0:experts, :] = rgrad.astype(bf16)

    key_send(0).wait_recv()
    own_kv = [key_rows(e, s) + kvi[0, s].astype(f32) for s in range(seqs)]
    for t in range(1, half):
        key_final(t).wait_recv()
        for s in range(seqs):
            own_kv[s] = own_kv[s] + kvr[t - 1, s].astype(f32)
    gkv = turn(jnp.concatenate(own_kv, 0), cos, sin, kw, False).astype(bf16)
    part[...] = dot_nt(gq, wqkv[:, :qw]) + dot_nt(gkv, wqkv[:, qw:])

    def normed_part(zz):
        return part[pl.ds(pl.multiple_of(zz * rows, 16), rows), :]

    for hop in range(nz - 1):
        normed_sum.hop(hop, normed_part)
        if hop > 0:
            out_line.hop(hop)
        if hop == 0:
            for k in range(1, nz):
                mixed_last(k, z).wait_recv()
                own_mixed = own_mixed + orecv[k - 1].astype(f32)
            obuf[own_rows, :] = own_mixed.astype(bf16)
            out_line.start()
            again = jnp.sum(part[...] * x * scale1, 0, keepdims=True)
            sz2[z] = jnp.concatenate([again, ggrad_ref[...], jnp.zeros((14, width), f32)], 0).astype(
                bf16
            )
            for copy in z_copies(slot_of(sz2), z2s, z2r):
                copy.start()
            pair_part = dot_tn(normed, gkv)
            for j in range(n):
                w2.pack[j] = pair_part[j * dn : (j + 1) * dn].astype(bf16)
            w2.give()
            w1.total()
    w2.spread()
    normed_sum.total(sums, normed_part)

    own_x = x_ref[own_rows, :].astype(f32)
    own_scale = lax.rsqrt(jnp.mean(own_x * own_x, -1, keepdims=True) + EPS)
    grad_normed = sums[...]
    gained = grad_normed * gain_ref[...]
    igrad = (
        gmid_ref[...]
        + own_scale * gained
        - own_x
        * (own_scale * own_scale * own_scale)
        * jnp.mean(gained * own_x, -1, keepdims=True)
    )
    igbuf[own_rows, :] = igrad.astype(bf16)
    igrad_line.start()
    out_line.hop(nz - 1)

    w1.forward()
    for copy in z_arrivals(slot_of(sz2), z2s, z2r):
        copy.wait_recv()
    second = sz2[0].astype(f32)
    for zz in range(1, nz):
        second = second + sz2[zz].astype(f32)
    sown[experts:, :] = second.astype(bf16)
    small_sib = remote(sown, ssib, sbs, sbr, (sib, z))
    small_sib.start()
    if nz > 2:
        igrad_line.hop(1)
    small_sib.wait_recv()
    schip[me] = (sown[...].astype(f32) + ssib[...].astype(f32)).astype(bf16)

    def small_send(t):
        to = (lax.rem(e + 2 * t, n), z)
        return remote(schip.at[me], schip.at[me], scs.at[t - 1], scr.at[t - 1], to)

    for t in range(1, half):
        small_send(t).start()

    w2.total()
    for hop in range(2, nz - 1):
        igrad_line.hop(hop)
    igrad_line.hop(nz - 1)

    w2.forward()
    for t in range(1, half):
        src = lax.rem(me + half - t, half)
        remote(
            schip.at[src], schip.at[src], scs.at[t - 1], scr.at[t - 1], (sib, z)
        ).wait_recv()
    small = schip[0].astype(f32)
    for t in range(1, half):
        small = small + schip[t].astype(f32)
    small_ref[...] = small

    w1.arrive()
    w2.arrive()
    for k in range(1, nz):
        mixed_last(k, z).wait_send()
    for line in (gat_line, out_line, igrad_line, normed_sum, w1, w2):
        line.drain()
    for copy in z_copies(slot_of(sz1), z1s, z1r) + z_copies(slot_of(sz2), z2s, z2r):
        copy.wait_send()
    small_sib.wait_send()
    for t in range(1, half):
        mixed_send(t).wait_send()

    def drained(t, carry):
        key_send(t).wait_send()

        @pl.when(t > 0)
        def _():
            key_final(t).wait_send()
            small_send(t).wait_send()

        return carry

    lax.fori_loop(0, half, drained, 0)


class PlaneSum:
    def __init__(self, n, e, z, sib, wall, pack, near, send, recv, *sems):
        self.n, self.e, self.z, self.sib, self.half = n, e, z, sib, n // 2
        self.wall, self.pack, self.near, self.send, self.recv = wall, pack, near, send, recv
        self.sems = sems

    def peer(self, base, t):
        return lax.rem(base - 2 * t + self.n, self.n)

    def near_copy(self, t):
        src = self.pack.at[self.peer(self.sib, t)]
        return remote(
            src, self.near.at[t], self.sems[0].at[t], self.sems[1].at[t], (self.sib, self.z)
        )

    def far_copy(self, t):
        return remote(
            self.send.at[t - 1],
            self.recv.at[t - 1],
            self.sems[2].at[t],
            self.sems[3].at[t],
            (self.peer(self.e, t), self.z),
        )

    def all_copy(self, src, t, to):
        ref = self.wall.at[src]
        return remote(ref, ref, self.sems[4].at[t], self.sems[5].at[t], (to, self.z))

    def pass_copy(self, src, t):
        ref = self.wall.at[src]
        return remote(ref, ref, self.sems[6].at[t], self.sems[7].at[t], (self.sib, self.z))

    def give(self):
        def one(i, carry):
            self.near_copy(self.half - 1 - i).start()
            return carry

        lax.fori_loop(0, self.half, one, 0)

    def spread(self):
        def one(i, carry):
            t = self.half - 1 - i
            self.near_copy(t).wait_recv()
            own = self.pack[self.peer(self.e, t)].astype(f32)
            self.send[t - 1] = (own + self.near[t].astype(f32)).astype(bf16)
            self.far_copy(t).start()
            return carry

        lax.fori_loop(0, self.half - 1, one, 0)

    def total(self):
        self.near_copy(0).wait_recv()
        total = self.pack[self.e].astype(f32) + self.near[0].astype(f32)
        for t in range(1, self.half):
            self.far_copy(t).wait_recv()
            total = total + self.recv[t - 1].astype(f32)
        self.wall[self.e] = total.astype(bf16)
        for t in range(1, self.half):
            self.all_copy(self.e, t, lax.rem(self.e + 2 * t, self.n)).start()
        self.pass_copy(self.e, 0).start()

    def forward(self):
        def one(t, carry):
            src = self.peer(self.e, t)
            self.all_copy(src, t, src).wait_recv()
            self.pass_copy(src, t).start()
            return carry

        lax.fori_loop(1, self.half, one, 0)

    def arrive(self):
        def one(t, carry):
            self.pass_copy(self.peer(self.sib, t), t).wait_recv()
            return carry

        lax.fori_loop(0, self.half, one, 0)

    def drain(self):
        def one(t, carry):
            self.near_copy(t).wait_send()
            self.pass_copy(self.e, t).wait_send()

            @pl.when(t > 0)
            def _():
                self.far_copy(t).wait_send()
                self.all_copy(self.e, t, self.sib).wait_send()

            return carry

        lax.fori_loop(0, self.half, one, 0)


class Line:
    def __init__(self, z, nz, e, buf_of, send, recv):
        self.z, self.nz, self.e = z, nz, e
        self.buf_of, self.send, self.recv = buf_of, send, recv

    def copy(self, way, piece):
        to = self.z + 1 if way == 0 else self.z - 1
        ref = self.buf_of(piece)
        return remote(ref, ref, self.send.at[way, piece], self.recv.at[way, piece], (self.e, to))

    def push(self, piece, ways=(0, 1)):
        for way in ways:

            @pl.when(self.z < self.nz - 1 if way == 0 else self.z > 0)
            def _():
                self.copy(way, piece).start()

    def start(self):
        self.push(self.z)

    def hop(self, i):
        @pl.when(self.z >= i)
        def _():
            self.copy(0, self.z - i).wait_recv()
            self.push(self.z - i, (0,))

        @pl.when(self.z + i <= self.nz - 1)
        def _():
            self.copy(1, self.z + i).wait_recv()
            self.push(self.z + i, (1,))

    def drain(self):
        for piece in range(self.nz):

            @pl.when((self.z >= piece) & (self.z < self.nz - 1))
            def _():
                self.copy(0, piece).wait_send()

            @pl.when((self.z <= piece) & (self.z > 0))
            def _():
                self.copy(1, piece).wait_send()


class LineSum:
    def __init__(self, z, nz, e, send_buf, recv_buf, send, recv):
        self.z, self.nz, self.e = z, nz, e
        self.send_buf, self.recv_buf, self.send, self.recv = send_buf, recv_buf, send, recv

    def copy(self, way, target):
        to = self.z + 1 if way == 0 else self.z - 1
        return remote(
            self.send_buf.at[way, target],
            self.recv_buf.at[way, target],
            self.send.at[way, target],
            self.recv.at[way, target],
            (self.e, to),
        )

    def hop(self, i, own_of):
        for way, target in ((0, self.nz - 1 - i), (1, i)):
            passes = self.z < target if way == 0 else self.z > target
            first = self.z == 0 if way == 0 else self.z == self.nz - 1
            inner = self.z > 0 if way == 0 else self.z < self.nz - 1

            @pl.when(passes & first)
            def _():
                self.send_buf[way, target] = own_of(target).astype(bf16)
                self.copy(way, target).start()

            @pl.when(passes & inner)
            def _():
                self.copy(way, target).wait_recv()
                self.send_buf[way, target] = (
                    own_of(target) + self.recv_buf[way, target].astype(f32)
                ).astype(bf16)
                self.copy(way, target).start()

    def total(self, ref, own_of):
        ref[...] = own_of(self.z)

        @pl.when(self.z > 0)
        def _():
            self.copy(0, self.z).wait_recv()
            ref[...] += self.recv_buf[0, self.z].astype(f32)

        @pl.when(self.z < self.nz - 1)
        def _():
            self.copy(1, self.z).wait_recv()
            ref[...] += self.recv_buf[1, self.z].astype(f32)

    def drain(self):
        for target in range(self.nz):

            @pl.when(self.z < target)
            def _():
                self.copy(0, target).wait_send()

            @pl.when(self.z > target)
            def _():
                self.copy(1, target).wait_send()


def return_layer(
    n, nz, gmid, mid, glog, ggrad, xn, x, gain, wq, wk, wv, wo, cos, sin, q, kv, lrow, att, lens, mixed
):
    tok, width = x.shape
    rows = tok // nz
    qw, kw = wq.shape[1], wk.shape[1]
    seqs = lens.shape[0]
    span = tok // seqs
    half = n // 2
    stacked = (qw // kw) * span
    pairs = seqs * (kw // HD)
    experts = glog.shape[0]
    small_rows = experts + 16
    dma = pltpu.SemaphoreType.DMA
    vmem = pl.BlockSpec(memory_space=pltpu.VMEM)
    sds = jax.ShapeDtypeStruct
    zdma = dma((nz - 1,))
    line = dma((2, nz))
    hdma = dma((half,))
    fdma = dma((half - 1,))
    def plane_bufs(cols):
        return [
            pltpu.VMEM((n, width // n, cols), bf16),
            pltpu.VMEM((half, width // n, cols), bf16),
            pltpu.VMEM((half - 1, width // n, cols), bf16),
            pltpu.VMEM((half - 1, width // n, cols), bf16),
        ]

    line_buf = pltpu.VMEM((2, nz, rows, width), bf16)
    return pl.pallas_call(
        functools.partial(return_kernel, n, nz),
        out_shape=[
            sds((tok, width), bf16),
            sds((tok, width), bf16),
            sds((n, width // n, 2 * qw), bf16),
            sds((n, width // n, 2 * kw), bf16),
            sds((small_rows, width), f32),
        ],
        in_specs=[vmem] * 17
        + [pl.BlockSpec(memory_space=pltpu.SMEM), pl.BlockSpec(memory_space=pl.ANY)],
        out_specs=[vmem] * 5,
        scratch_shapes=[
            pltpu.VMEM((width, qw + 2 * kw), bf16),
            pltpu.VMEM((tok, width), bf16),
            pltpu.VMEM((tok, qw), bf16),
            pltpu.VMEM((tok, qw), f32),
            pltpu.VMEM((pairs, stacked, HD), bf16),
            pltpu.VMEM((pairs, stacked, HD), bf16),
            pltpu.VMEM((pairs, stacked, HD), f32),
            pltpu.VMEM((seqs, n * span, 2 * kw), f32),
            pltpu.VMEM((half, seqs, span, 2 * kw), bf16),
            pltpu.VMEM((half, seqs, span, 2 * kw), bf16),
            pltpu.VMEM((half - 1, seqs, span, 2 * kw), bf16),
            pltpu.VMEM((half - 1, seqs, span, 2 * kw), bf16),
            pltpu.VMEM((tok, width), f32),
            pltpu.VMEM((rows, width), f32),
            line_buf,
            line_buf,
            pltpu.VMEM((nz - 1, rows, width), bf16),
            pltpu.VMEM((nz - 1, rows, width), bf16),
            plane_bufs(2 * qw),
            plane_bufs(2 * kw),
            pltpu.VMEM((nz, experts, 128), bf16),
            pltpu.VMEM((nz, 16, width), bf16),
            pltpu.VMEM((small_rows, width), bf16),
            pltpu.VMEM((small_rows, width), bf16),
            pltpu.VMEM((half, small_rows, width), bf16),
            pltpu.VMEM((half, nz, rows, width), bf16),
        ]
        + [line] * 8
        + [zdma] * 6
        + [hdma, hdma, fdma, fdma]
        + [[hdma] * 8, [hdma] * 8]
        + [dma, dma, fdma, fdma]
        + [fdma, fdma, dma],
        compiler_params=pltpu.CompilerParams(
            collective_id=3, has_side_effects=True, vmem_limit_bytes=58 << 20
        ),
        name="attend_back",
    )(
        gmid,
        mid,
        glog,
        ggrad,
        xn,
        x,
        gain[None],
        wq,
        wk,
        wv,
        wo,
        cos,
        sin,
        q,
        kv,
        lrow,
        att,
        lens,
        mixed,
    )


def finish_kernel(
    out_low,
    igrad_low,
    wall,
    wall2,
    small,
    load,
    dgate_in,
    dup_in,
    ddown_in,
    out_ref,
    igrad_ref,
    q_ref,
    k_ref,
    v_ref,
    o_ref,
    router_ref,
    again_ref,
    egain_ref,
    loss_ref,
    load_ref,
    dgate,
    dup,
    ddown,
    dgate_s,
    dup_s,
    ddown_s,
    sems,
):
    pairs = ((dgate_in, dgate_s, dgate), (dup_in, dup_s, dup), (ddown_in, ddown_s, ddown))
    reads = [pltpu.make_async_copy(p[0], p[1], sems.at[0, i]) for i, p in enumerate(pairs)]
    writes = [pltpu.make_async_copy(p[1], p[2], sems.at[1, i]) for i, p in enumerate(pairs)]
    for copy in reads:
        copy.start()
    qw, kw = q_ref.shape[1], k_ref.shape[1]
    experts = load.shape[1]
    out_ref[...] = out_low[...].astype(f32)
    for read, write in zip(reads, writes):
        read.wait()
        write.start()
    igrad_ref[...] = igrad_low[...].astype(f32)
    chunks, dn, _ = wall.shape
    flat = wall[...].reshape(chunks * dn, 2 * qw).astype(f32)
    q_ref[...] = flat[:, :qw]
    o_ref[...] = flat[:, qw:].T
    flat = wall2[...].reshape(chunks * dn, 2 * kw).astype(f32)
    k_ref[...] = flat[:, :kw]
    v_ref[...] = flat[:, kw:]
    router_ref[...] = small[0:experts, :]
    again_ref[...] = small[experts : experts + 1, :]
    egain_ref[...] = small[experts + 1 : experts + 2, :]
    load_ref[...] = load[...]
    loss_ref[...] = jnp.mean(load[...], -1, keepdims=True)
    for copy in writes:
        copy.wait()


def finish_layer(out_low, igrad_low, wall, wall2, small, load, dgate, dup, ddown, qw, kw):
    tok, width = out_low.shape
    experts = load.shape[1]
    vmem = pl.BlockSpec(memory_space=pltpu.VMEM)
    hbm = pl.BlockSpec(memory_space=pl.ANY)
    sds = jax.ShapeDtypeStruct
    return pl.pallas_call(
        finish_kernel,
        out_shape=[
            sds((tok, width), f32),
            sds((tok, width), f32),
            sds((width, qw), f32),
            sds((width, kw), f32),
            sds((width, kw), f32),
            sds((qw, width), f32),
            sds((experts, width), f32),
            sds((1, width), f32),
            sds((1, width), f32),
            sds((1, 1), f32),
            sds((1, experts), f32),
            sds(dgate.shape, f32),
            sds(dup.shape, f32),
            sds(ddown.shape, f32),
        ],
        in_specs=[vmem] * 6 + [hbm] * 3,
        out_specs=[vmem] * 11 + [hbm] * 3,
        scratch_shapes=[
            pltpu.VMEM(dgate.shape, f32),
            pltpu.VMEM(dup.shape, f32),
            pltpu.VMEM(ddown.shape, f32),
            pltpu.SemaphoreType.DMA((2, 3)),
        ],
        compiler_params=pltpu.CompilerParams(vmem_limit_bytes=60 << 20),
        name="finish",
    )(out_low, igrad_low, wall, wall2, small, load, dgate, dup, ddown)


def shards(
    inputs,
    attention_gain,
    query_weight,
    key_weight,
    value_weight,
    out_weight,
    expert_gain,
    router_weight,
    gate_weight,
    up_weight,
    down_weight,
    routes,
    seq_lens,
    cotangent,
):
    n = lax.axis_size("expert")
    nz = lax.axis_size("tensor")
    tok_rows = inputs.shape[0]
    seq_count = seq_lens.shape[0]
    span_rows = tok_rows // seq_count
    row = lax.broadcasted_iota(jnp.int32, (tok_rows, 128), 0) % span_rows
    lane = lax.broadcasted_iota(jnp.int32, (tok_rows, 128), 1) % (HD // 2)
    frequency = THETA ** (-2.0 * lane.astype(f32) / HD)
    angles = (lax.axis_index("expert") * span_rows + row).astype(f32) * frequency
    cosines = jnp.cos(angles)
    sines = jnp.sin(angles)
    cot_all = lax.all_gather(cotangent.astype(bf16), "expert", axis=0, tiled=True)
    weights = (query_weight, key_weight, value_weight, out_weight, cosines, sines)
    middle, queries, pairs, logs, attended = attend_layer(
        n, nz, inputs, attention_gain, *weights, seq_lens
    )
    (
        grad_middle,
        logit_grads,
        expert_gain_part,
        expert_load,
        gate_grad,
        up_grad,
        down_grad,
        mixed,
        normed2,
    ) = expert_layer(
        n,
        nz,
        middle,
        expert_gain,
        router_weight,
        routes,
        gate_weight,
        up_weight,
        down_weight,
        cotangent,
        cot_all,
    )
    out_low, igrad_low, packed, packed2, small = return_layer(
        n,
        nz,
        grad_middle,
        middle,
        logit_grads,
        expert_gain_part,
        normed2,
        inputs,
        attention_gain,
        *weights,
        queries,
        pairs,
        logs,
        attended,
        seq_lens,
        mixed,
    )
    (
        output,
        input_grad,
        query_grad,
        key_grad,
        value_grad,
        out_weight_grad,
        router_grad,
        attention_gain_grad,
        expert_gain_grad,
        balance_loss,
        expert_load,
        gate_grad,
        up_grad,
        down_grad,
    ) = finish_layer(
        out_low,
        igrad_low,
        packed,
        packed2,
        small,
        expert_load,
        gate_grad,
        up_grad,
        down_grad,
        query_weight.shape[1],
        key_weight.shape[1],
    )
    return (
        output,
        input_grad,
        balance_loss[0, 0],
        expert_load[0],
        attention_gain_grad[0],
        query_grad,
        key_grad,
        value_grad,
        out_weight_grad,
        expert_gain_grad[0],
        router_grad.T,
        gate_grad,
        up_grad,
        down_grad.reshape(down_weight.shape),
    )


def solution(mesh):
    placed = (
        P("expert", None),
        P(),
        P(None, "tensor"),
        P(None, "tensor"),
        P(None, "tensor"),
        P("tensor", None),
        P(),
        P(),
        P("expert", None, "tensor"),
        P("expert", None, "tensor"),
        P("expert", "tensor", None),
        P("expert", None),
        P(),
        P("expert", None),
    )
    return jax.shard_map(
        shards,
        mesh=mesh,
        in_specs=placed,
        out_specs=(
            P("expert", None),
            P("expert", None),
            P(),
            P(),
            P(),
            P(None, "tensor"),
            P(None, "tensor"),
            P(None, "tensor"),
            P("tensor", None),
            P(),
            P(),
            P("expert", None, "tensor"),
            P("expert", None, "tensor"),
            P("expert", "tensor", None),
        ),
        check_vma=False,
    )
```

```python
import functools

import jax
import jax.numpy as jnp
from jax import lax
from jax.experimental import pallas as pl
from jax.experimental.pallas import tpu as pltpu
from jax.sharding import PartitionSpec as P

HD = 64
EPS = 1e-06
THETA = 10000.0
MESH = pl.DeviceIdType.MESH
f32 = jnp.float32
bf16 = jnp.bfloat16


def dot_nn(left, right):
    return lax.dot_general(left, right, (((1,), (0,)), ((), ())), preferred_element_type=f32)


def dot_nt(left, right):
    return lax.dot_general(left, right, (((1,), (1,)), ((), ())), preferred_element_type=f32)


def dot_tn(left, right):
    return lax.dot_general(left, right, (((0,), (0,)), ((), ())), preferred_element_type=f32)


def remote(src, dst, send_sem, recv_sem, device):
    return pltpu.make_async_remote_copy(
        src_ref=src,
        dst_ref=dst,
        send_sem=send_sem,
        recv_sem=recv_sem,
        device_id=device,
        device_id_type=MESH,
    )


def turn(values, cos, sin, last, forward):
    lane = lax.broadcasted_iota(jnp.int32, (values.shape[0], 128), 1)
    first_half = lax.rem(lane, HD) < HD // 2
    parts = []
    for g in range(values.shape[1] // 128):
        v = values[:, g * 128 : (g + 1) * 128]
        if g * 128 >= last:
            parts.append(v)
            continue
        turned = jnp.where(
            first_half, -pltpu.roll(v, 128 - HD // 2, 1), pltpu.roll(v, HD // 2, 1)
        )
        new = v * cos + turned * sin if forward else v * cos - turned * sin
        if (g + 1) * 128 > last:
            new = jnp.where(lane + g * 128 < last, new, v)
        parts.append(new)
    return jnp.concatenate(parts, 1) if len(parts) > 1 else parts[0]


def greet(n, nz, e, z, sib):
    barrier = pltpu.get_barrier_semaphore()
    pl.semaphore_signal(barrier, inc=1, device_id=(sib, z), device_id_type=MESH)
    for s in range(1, n // 2):
        pl.semaphore_signal(
            barrier, inc=1, device_id=(lax.rem(e + 2 * s, n), z), device_id_type=MESH
        )
    for k in range(1, nz):
        pl.semaphore_signal(barrier, inc=1, device_id=(e, lax.rem(z + k, nz)), device_id_type=MESH)
    return barrier


def expert_kernel(
    n,
    nz,
    big,
    mid_ref,
    gain_ref,
    router_ref,
    routes_ref,
    cot_ref,
    gate_hbm,
    up_hbm,
    down_hbm,
    cot_all,
    *rest,
):
    outs, rest = rest[:9], rest[9:]
    gmid_ref, glog_ref, ggrad_ref, load_ref = outs[:4]
    dgate_hbm, dup_hbm, ddown_hbm, mixed_hbm, normed_hbm = outs[4:]
    xbuf, rest = rest[0], rest[1:]
    if big:
        xstage, rest = rest[0], rest[1:]
    (
        wbuf,
        xn_s,
        wg,
        wu,
        down_ref,
        dgate,
        dup,
        ddown,
        cbuf,
        dg_s,
        du_s,
        wi_s,
        hold,
        osend,
        sin,
        hold_o,
        osend_o,
        sin_o,
        hold_g,
        osend_g,
        sin_g,
        own_s,
        own_g,
        fsend,
        fin,
        fsend_g,
        fin_g,
        zsend,
        zin,
        zsend_g,
        zin_g,
        wsem,
        gsem,
        csem,
        msem,
        lsem,
        zs,
        zr,
        zws,
        zwr,
        xs,
        xr,
        ws,
        wr,
        fs,
        fr,
        wfs,
        wfr,
        gs,
        gr,
        oss,
        osr,
        ggs,
        ggr,
        ps,
        pr,
        pgs,
        pgr,
        zgs,
        zgr,
        zggs,
        zggr,
        zds,
        zdr,
        picks_s,
    ) = rest
    e = lax.axis_index("expert")
    z = lax.axis_index("tensor")
    core = lax.rem(e, 2)
    other = 1 - core
    me = e // 2
    sib = e + 1 - 2 * core
    half = n // 2
    rows, width = mid_ref.shape
    tok = rows * nz
    experts = router_ref.shape[0]
    local_experts, _, hid = gate_hbm.shape
    inner_w = local_experts * hid
    fc = min(inner_w, 256)
    fslots = fsend.shape[0]
    square = half == 4
    chip_x = me + 1 - 2 * lax.rem(me, 2)
    chip_y = lax.rem(me + 2, 4)
    chip_d = 3 - me
    mid_row = rows // 2

    loads = []
    for el in range(local_experts):
        cols = pl.ds(el * hid, hid)
        loads.append(pltpu.make_async_copy(gate_hbm.at[el], wg.at[:, cols], wsem.at[0, el]))
        loads.append(pltpu.make_async_copy(up_hbm.at[el], wu.at[:, cols], wsem.at[1, el]))
    loads.append(pltpu.make_async_copy(down_hbm, down_ref, wsem.at[2, 0]))
    for copy in loads:
        copy.start()

    def piece_of(g):
        return lax.rem(z + nz - g, nz)

    def cot_start(g, parity, slot):
        zz = piece_of(g)
        for h in range(half):
            start = (2 * h + parity) * tok + zz * rows
            pltpu.make_async_copy(
                cot_all.at[pl.ds(pl.multiple_of(start, 16), rows)],
                cbuf.at[slot, pl.ds(h * rows, rows)],
                csem.at[slot],
            ).start()

    def cot_wait(slot):
        pltpu.make_async_copy(
            cot_all.at[pl.ds(0, half * rows)], cbuf.at[slot], csem.at[slot]
        ).wait()

    cot_start(0, core, 0)
    barrier = greet(n, nz, e, z, sib)

    own_rows = pl.ds(pl.multiple_of(z * rows, 16), rows)
    my_rows = pl.ds(pl.multiple_of(me * rows, 16), rows)
    mid = mid_ref[...]
    scale2 = lax.rsqrt(jnp.mean(mid * mid, -1, keepdims=True) + EPS)
    xn = (mid * scale2 * gain_ref[...]).astype(bf16)
    xn_s[...] = xn
    logits = dot_nt(xn, router_ref[...])
    choices = routes_ref[...].astype(f32)
    top_count = choices.shape[0]
    picks_s[...] = jnp.concatenate([choices, jnp.zeros((128 - top_count, tok), f32)], 0).T
    picks = picks_s[own_rows, 0:top_count].astype(jnp.int32)
    lanes = lax.broadcasted_iota(jnp.int32, (rows, experts), 1)
    chosen = jnp.zeros((rows, experts), f32)
    for k in range(picks.shape[1]):
        chosen = jnp.where(picks[:, k : k + 1] == lanes, 1.0, chosen)
    top = jnp.max(logits, -1, keepdims=True)
    powers = jnp.exp(logits - top)
    probs = powers / jnp.sum(powers, -1, keepdims=True)
    low_logits = jnp.where(chosen > 0.0, logits, -1e30)
    ctop = jnp.max(low_logits, -1, keepdims=True)
    cpow = jnp.exp(low_logits - ctop)
    comb = cpow / jnp.sum(cpow, -1, keepdims=True)
    padded = jnp.concatenate([comb, jnp.zeros((rows, 128 - experts), f32)], 1)
    if rows < 128:
        padded = jnp.concatenate([padded, jnp.zeros((128 - rows, 128), f32)], 0)
    piece = padded.T[:experts]
    lane_pad = jnp.zeros((1, 128 - experts), f32)
    cnt = jnp.concatenate([jnp.sum(chosen, 0, keepdims=True), lane_pad], 1)
    psum = jnp.concatenate([jnp.sum(probs, 0, keepdims=True), lane_pad], 1)
    psum_hi = psum.astype(bf16).astype(f32)
    stats = jnp.concatenate([cnt, psum_hi, psum - psum_hi, jnp.zeros((13, 128), f32)], 0)
    wbuf[z, core, me] = jnp.concatenate([piece, stats], 0).astype(bf16)
    if big:
        copy = pltpu.make_async_copy(xn_s, xbuf.at[z, core, my_rows], lsem)
        copy.start()
        copy.wait()
    else:
        xbuf[z, core, my_rows] = xn
    pl.semaphore_wait(barrier, half + nz - 1)

    def z_row(zz, k, to):
        ref = xbuf.at[zz, core, my_rows]
        return remote(ref, ref, zs.at[k - 1], zr.at[k - 1], (e, to))

    def z_small(zz, k, to):
        ref = wbuf.at[zz, core, me]
        return remote(ref, ref, zws.at[k - 1], zwr.at[k - 1], (e, to))

    def x_row(zz, h, g, s, to):
        ref = xbuf.at[zz, core, pl.ds(pl.multiple_of(h * rows, 16), rows)]
        return remote(ref, ref, xs.at[g, s], xr.at[g, s], (to, z))

    def x_small(zz, h, g, s, to):
        ref = wbuf.at[zz, core, h]
        return remote(ref, ref, ws.at[g, s], wr.at[g, s], (to, z))

    def x_part(zz, h, first, count, g, i, to):
        start = pl.multiple_of(h * rows + first, 16)
        ref = xbuf.at[zz, core, pl.ds(start, count)]
        return remote(ref, ref, xs.at[g, i], xr.at[g, i], (2 * to + core, z))

    def push_piece(g):
        zz = piece_of(g)
        if square:
            x_part(zz, me, 0, rows, g, 0, chip_x).start()
            x_part(zz, me, 0, rows, g, 1, chip_y).start()
        for s in range(1, half):
            to = lax.rem(e + 2 * s, n)
            if not square:
                x_row(zz, me, g, s, to).start()
            x_small(zz, me, g, s, to).start()

    def relays():
        low = x_part(z, chip_x, 0, mid_row, 0, 2, chip_y)
        high = x_part(z, chip_y, mid_row, rows - mid_row, 0, 3, chip_x)
        return low, high

    def z_diag(zz, k, to):
        ref = xbuf.at[zz, core, pl.ds(pl.multiple_of(chip_d * rows, 16), rows)]
        return remote(ref, ref, zds.at[k - 1], zdr.at[k - 1], (e, to))

    push_piece(jnp.int32(0))
    for k in range(1, nz):
        z_row(z, k, lax.rem(z + k, nz)).start()
        z_small(z, k, lax.rem(z + k, nz)).start()

    if square:
        low, high = relays()
        x_part(z, chip_x, 0, rows, 0, 0, chip_x).wait_recv()
        low.start()
        x_part(z, chip_y, 0, rows, 0, 1, chip_y).wait_recv()
        high.start()

    dgate[...] = jnp.zeros_like(dgate)
    dup[...] = jnp.zeros_like(dup)
    ddown[...] = jnp.zeros_like(ddown)
    for copy in loads:
        copy.wait()
    if square:
        x_part(z, chip_d, 0, mid_row, 0, 2, chip_y).wait_recv()
        x_part(z, chip_d, mid_row, rows - mid_row, 0, 3, chip_x).wait_recv()
        z_diag(z, 1, lax.rem(z + 1, nz)).start()

    sel_row = lax.broadcasted_iota(jnp.int32, (experts, fc), 0)
    sel_col = lax.broadcasted_iota(jnp.int32, (experts, fc), 1)

    def block(zz, parity, slot, dst, dst_o, dst_g, dslot):
        if big:
            copy = pltpu.make_async_copy(xbuf.at[zz, parity], xstage, lsem)
            copy.start()
            copy.wait()
            x_ref = xstage
        else:
            x_ref = xbuf.at[zz, parity]
        c_ref = cbuf.at[slot]
        sums = [jnp.zeros((experts, rows), f32) for _ in range(half)]
        for q in range(inner_w // fc):
            cols = slice(q * fc, (q + 1) * fc)
            x = x_ref[...]
            gate_val = dot_nn(x, wg[:, cols])
            up_val = dot_nn(x, wu[:, cols])
            back = dot_nt(c_ref[...], down_ref[cols, :])
            select = jnp.where(
                sel_row == e * local_experts + (q * fc + sel_col) // hid, 1.0, 0.0
            ).astype(bf16)
            wide = jnp.concatenate(
                [dot_tn(wbuf[zz, parity, h, :experts, :], select)[:rows] for h in range(half)], 0
            )
            sig = 1.0 / (1.0 + jnp.exp(-gate_val))
            silu = gate_val * sig
            inner = silu * up_val
            wi_s[:, cols] = (inner * wide).astype(bf16)
            scaled = back * wide
            dg_s[:, cols] = (scaled * up_val * (sig * (1.0 + gate_val * (1.0 - sig)))).astype(bf16)
            du_s[:, cols] = (scaled * silu).astype(bf16)
            both = (inner * back).astype(bf16)
            for h in range(half):
                sums[h] = sums[h] + dot_nt(select, both[h * rows : (h + 1) * rows])
        for h in range(half):
            gap = jnp.zeros((experts, 128 - rows), f32)
            dst_g[dslot, h] = jnp.concatenate([sums[h], gap], 1).astype(bf16)
        for h in range(width // 256):
            cols = slice(h * 256, (h + 1) * 256)
            dst[dslot, :, cols] = (
                dot_nt(dg_s[...], wg[cols, :]) + dot_nt(du_s[...], wu[cols, :])
            ).astype(bf16)
            dst_o[dslot, :, cols] = dot_nn(wi_s[...], down_ref[:, cols]).astype(bf16)
        for h in range(width // 256):
            cols = slice(h * 256, (h + 1) * 256)
            x_part = x_ref[:, cols]
            gate_part = dot_tn(x_part, dg_s[...])
            up_part = dot_tn(x_part, du_s[...])
            for el in range(local_experts):
                dgate[el, cols, :] += gate_part[:, el * hid : (el + 1) * hid]
                dup[el, cols, :] += up_part[:, el * hid : (el + 1) * hid]
            ddown[:, cols] += dot_tn(wi_s[...], c_ref[:, cols])

    def gives(slot):
        return [
            remote(osend.at[slot], sin.at[slot], gs.at[slot], gr.at[slot], (sib, z)),
            remote(osend_g.at[slot], sin_g.at[slot], ggs.at[slot], ggr.at[slot], (sib, z)),
            remote(osend_o.at[slot], sin_o.at[slot], oss.at[slot], osr.at[slot], (sib, z)),
        ]

    def finals(g, s, to):
        at = lax.rem(g, fslots)
        rows_copy = []
        if not square:
            rows_copy = [
                remote(
                    fsend.at[at, s - 1], fin.at[g, s - 1], ps.at[g, s - 1], pr.at[g, s - 1], (to, z)
                )
            ]
        return rows_copy + [
            remote(
                fsend_g.at[at, s - 1],
                fin_g.at[g, s - 1],
                pgs.at[g, s - 1],
                pgr.at[g, s - 1],
                (to, z),
            ),
        ]

    def half_copy(g, buf, upper, i, chip):
        first, count = (mid_row, rows - mid_row) if upper else (0, mid_row)
        return remote(
            fsend.at[g, buf, pl.ds(first, count)],
            fin.at[g, buf, pl.ds(first, count)],
            ps.at[g, i],
            pr.at[g, i],
            (2 * chip + core, z),
        )

    def half_copies(g):
        return [
            half_copy(g, 2, False, 0, chip_x),
            half_copy(g, 2, True, 1, chip_y),
            half_copy(g, 0, False, 2, chip_x),
            half_copy(g, 1, True, 3, chip_y),
            half_copy(g, 1, False, 4, chip_y),
            half_copy(g, 0, True, 5, chip_x),
        ]

    def chip_sum(slot, chip, upper):
        first, count = (mid_row, rows - mid_row) if upper else (0, mid_row)
        at = pl.ds(pl.multiple_of(chip * rows + first, 16), count)
        return hold[slot, at, :].astype(f32) + sin[slot, at, :].astype(f32)

    def direct_stage(g):
        slot = lax.rem(g, 2)
        copies = half_copies(g)
        fsend[g, 2, :mid_row] = chip_sum(slot, chip_d, False).astype(bf16)
        copies[0].start()
        fsend[g, 2, mid_row:] = chip_sum(slot, chip_d, True).astype(bf16)
        copies[1].start()
        fsend[g, 0, :mid_row] = chip_sum(slot, chip_x, False).astype(bf16)
        copies[2].start()
        fsend[g, 1, mid_row:] = chip_sum(slot, chip_y, True).astype(bf16)
        copies[3].start()

    def relay_stage(g):
        slot = lax.rem(g, 2)
        copies = half_copies(g)
        copies[0].wait_recv()
        passed = chip_sum(slot, chip_y, False) + fin[g, 2, :mid_row].astype(f32)
        fsend[g, 1, :mid_row] = passed.astype(bf16)
        copies[4].start()
        copies[1].wait_recv()
        passed = chip_sum(slot, chip_x, True) + fin[g, 2, mid_row:].astype(f32)
        fsend[g, 0, mid_row:] = passed.astype(bf16)
        copies[5].start()

    def lasts(k, to):
        return [
            remote(zsend.at[k - 1], zin.at[k - 1], zgs.at[k - 1], zgr.at[k - 1], (e, to)),
            remote(zsend_g.at[k - 1], zin_g.at[k - 1], zggs.at[k - 1], zggr.at[k - 1], (e, to)),
        ]

    def mixed_copy(g, slot):
        return pltpu.make_async_copy(hold_o.at[slot], mixed_hbm.at[piece_of(g)], msem.at[slot])

    def plane_stage(g):
        slot = lax.rem(g, 2)
        for copy in gives(slot)[:2]:
            copy.wait_recv()
        if fslots < nz:

            @pl.when(g >= fslots)
            def _():
                for s in range(1, half):
                    for copy in finals(g - fslots, s, sib):
                        copy.wait_send()

        spot = lax.rem(g, fslots)
        if square:
            direct_stage(g)
        for s in range(1, half):
            h = lax.rem(me + half - s, half)
            at = pl.ds(pl.multiple_of(h * rows, 16), rows)
            if not square:
                fsend[spot, s - 1] = (
                    hold[slot, at, :].astype(f32) + sin[slot, at, :].astype(f32)
                ).astype(bf16)
            fsend_g[spot, s - 1] = (hold_g[slot, h].astype(f32) + sin_g[slot, h].astype(f32)).astype(
                bf16
            )
            for copy in finals(g, s, lax.rem(e - 2 * s + n, n)):
                copy.start()
        own_s[g] = hold[slot, my_rows, :].astype(f32) + sin[slot, my_rows, :].astype(f32)
        own_g[g] = hold_g[slot, me].astype(f32) + sin_g[slot, me].astype(f32)

    def mixed_stage(g):
        slot = lax.rem(g, 2)
        gives(slot)[2].wait_recv()
        hold_o[slot] = (hold_o[slot].astype(f32) + sin_o[slot].astype(f32)).astype(bf16)
        mixed_copy(g, slot).start()

    def tensor_stage(g):
        total = own_s[g]
        total_g = own_g[g]
        for s in range(1, half):
            for copy in finals(g, s, sib):
                copy.wait_recv()
            if not square:
                total = total + fin[g, s - 1].astype(f32)
            total_g = total_g + fin_g[g, s - 1].astype(f32)

        if square:
            for copy in half_copies(g)[2:]:
                copy.wait_recv()
            total = total + fin[g, 0].astype(f32) + fin[g, 1].astype(f32)

        @pl.when(g == 0)
        def _():
            own_s[0] = total
            own_g[0] = total_g

        @pl.when(g > 0)
        def _():
            zsend[g - 1] = total.astype(bf16)
            zsend_g[g - 1] = total_g.astype(bf16)
            for copy in lasts(g, piece_of(g)):
                copy.start()

    def step(g, carry):
        zz = piece_of(g)
        slot = lax.rem(g, 2)

        @pl.when(g < nz - 1)
        def _():
            coming = piece_of(g + 1)
            z_row(coming, g + 1, coming).wait_recv()
            z_small(coming, g + 1, coming).wait_recv()
            push_piece(g + 1)

        if square:

            @pl.when(g > 0)
            def _():
                x_part(zz, chip_x, 0, rows, g, 0, chip_x).wait_recv()
                x_part(zz, chip_y, 0, rows, g, 1, chip_y).wait_recv()
                z_diag(zz, g, zz).wait_recv()

        for s in range(1, half):
            h = lax.rem(me + half - s, half)
            src = 2 * h + core
            if not square:
                x_row(zz, h, g, s, src).wait_recv()
            x_small(zz, h, g, s, src).wait_recv()
        for copy in forward(zz, core, g):
            copy.start()
        cot_start(g, other, 1)
        cot_wait(0)

        @pl.when(g >= 2)
        def _():
            mixed_copy(g - 2, slot).wait()

        block(zz, core, 0, hold, hold_o, hold_g, slot)
        if square:
            for k in range(2, nz):

                @pl.when(g == k - 2)
                def _():
                    z_diag(z, k, lax.rem(z + k, nz)).start()


        @pl.when(g < nz - 1)
        def _():
            cot_start(g + 1, core, 0)

        @pl.when(g >= 2)
        def _():
            tensor_stage(g - 2)

        @pl.when(g >= 1)
        def _():
            plane_stage(g - 1)
            mixed_stage(g - 1)

        @pl.when(g >= 2)
        def _():
            for copy in gives(slot):
                copy.wait_send()

        for copy in forward(zz, other, g):
            copy.wait_recv()
        cot_wait(1)
        block(zz, other, 1, osend, osend_o, osend_g, slot)
        for copy in gives(slot):
            copy.start()
        if square:

            @pl.when(g >= 1)
            def _():
                relay_stage(g - 1)

        return carry

    def forward(zz, parity, g):
        ref = xbuf.at[zz, parity]
        small = wbuf.at[zz, parity]
        return (
            remote(ref, ref, fs.at[g], fr.at[g], (sib, z)),
            remote(small, small, wfs.at[g], wfr.at[g], (sib, z)),
        )

    lax.fori_loop(0, nz, step, 0)
    grads = [
        pltpu.make_async_copy(dgate, dgate_hbm, gsem.at[0]),
        pltpu.make_async_copy(dup, dup_hbm, gsem.at[1]),
        pltpu.make_async_copy(ddown, ddown_hbm, gsem.at[2]),
        pltpu.make_async_copy(xbuf.at[:, core, my_rows, :], normed_hbm, gsem.at[3]),
    ]
    plane_stage(jnp.int32(nz - 1))
    for copy in grads:
        copy.start()
    if nz >= 2:
        tensor_stage(jnp.int32(nz - 2))
    if square:
        relay_stage(jnp.int32(nz - 1))

    def total_stats(j, carry):
        for zz in range(nz):
            for parity in range(2):
                carry = carry + wbuf[zz, parity, j, experts:, :].astype(f32)
        return carry

    stats = lax.fori_loop(0, half, total_stats, jnp.zeros((16, 128), f32))
    total_rows = n * tok
    share = stats[0:1, :experts] / (total_rows * top_count)
    load_ref[...] = (
        experts * experts * share * ((stats[1:2, :experts] + stats[2:3, :experts]) / total_rows)
    )
    loss_w = experts * share / total_rows
    mixed_stage(jnp.int32(nz - 1))
    tensor_stage(jnp.int32(nz - 1))

    gate_sums = own_g[0]
    grad_rows = own_s[0]
    for k in range(1, nz):
        for copy in lasts(k, z):
            copy.wait_recv()
        gate_sums = gate_sums + zin_g[k - 1].astype(f32)
        grad_rows = grad_rows + zin[k - 1].astype(f32)
    grow = jnp.concatenate([gate_sums, jnp.zeros((128 - experts, 128), f32)], 0).T
    grad_gates = grow[:rows, :experts]
    grad_logits = comb * (grad_gates - jnp.sum(grad_gates * comb, -1, keepdims=True))
    grad_logits = grad_logits + probs * (loss_w - jnp.sum(loss_w * probs, -1, keepdims=True))
    low_grad = grad_logits.astype(bf16)
    wide_grad = jnp.concatenate([grad_logits, jnp.zeros((rows, 128 - experts), f32)], 1)
    if rows < 128:
        wide_grad = jnp.concatenate([wide_grad, jnp.zeros((128 - rows, 128), f32)], 0)
    glog_ref[...] = wide_grad.T[:experts].astype(bf16)
    grad_rows = grad_rows + dot_nn(low_grad, router_ref[...])
    mid = mid_ref[...]
    ggrad_ref[...] = jnp.sum(grad_rows * mid * scale2, 0, keepdims=True)
    gained = grad_rows * gain_ref[...]
    gmid_ref[...] = (
        cot_ref[own_rows, :]
        + scale2 * gained
        - mid * (scale2 * scale2 * scale2) * jnp.mean(gained * mid, -1, keepdims=True)
    )

    for copy in grads:
        copy.wait()
    if square:
        for copy in relays():
            copy.wait_send()
        for k in range(1, nz):
            z_diag(z, k, z).wait_send()
    for k in range(1, nz):
        z_row(z, k, z).wait_send()
        z_small(z, k, z).wait_send()
        for copy in lasts(k, z):
            copy.wait_send()
    for g in range(max(0, nz - 2), nz):
        mixed_copy(jnp.int32(g), g % 2).wait()
        for copy in gives(g % 2):
            copy.wait_send()

    def drained(g, carry):
        if square:
            x_part(z, me, 0, rows, g, 0, chip_x).wait_send()
            x_part(z, me, 0, rows, g, 1, chip_y).wait_send()
            for copy in half_copies(g):
                copy.wait_send()
        for s in range(1, half):
            if not square:
                x_row(z, me, g, s, sib).wait_send()
            x_small(z, me, g, s, sib).wait_send()
        for copy in forward(z, core, g):
            copy.wait_send()
        return carry

    lax.fori_loop(0, nz, drained, 0)

    def sums_sent(g, carry):
        for s in range(1, half):
            for copy in finals(g, s, sib):
                copy.wait_send()
        return carry

    lax.fori_loop(nz - fslots, nz, sums_sent, 0)


def expert_layer(n, nz, mid, gain, router, routes, gate, up, down, cot, cot_all):
    rows, width = mid.shape
    experts = router.shape[1]
    local_experts, _, hid = gate.shape
    inner_w = local_experts * hid
    half = n // 2
    batch = half * rows
    big = n > 8
    fslots = 2 if big else nz
    dma = pltpu.SemaphoreType.DMA
    vmem = pl.BlockSpec(memory_space=pltpu.VMEM)
    hbm = pl.BlockSpec(memory_space=pl.ANY)
    sds = jax.ShapeDtypeStruct
    out_shape = [
        sds((rows, width), f32),
        sds((experts, 128), bf16),
        sds((1, width), f32),
        sds((1, experts), f32),
        sds((local_experts, width, hid), f32),
        sds((local_experts, width, hid), f32),
        sds((inner_w, width), f32),
        sds((nz, batch, width), bf16),
        sds((nz, rows, width), bf16),
    ]
    out_specs = [vmem] * 4 + [hbm] * 5
    scratch = []
    if big:
        out_shape.append(sds((nz, 2, batch, width), bf16))
        out_specs.append(hbm)
        scratch.append(pltpu.VMEM((batch, width), bf16))
    else:
        scratch.append(pltpu.VMEM((nz, 2, batch, width), bf16))
    pair = pltpu.VMEM((2, batch, width), bf16)
    small = pltpu.VMEM((2, half, experts, 128), bf16)
    scratch += [
        pltpu.VMEM((nz, 2, half, experts + 16, 128), bf16),
        pltpu.VMEM((rows, width), bf16),
        pltpu.VMEM((width, inner_w), bf16),
        pltpu.VMEM((width, inner_w), bf16),
        pltpu.VMEM((inner_w, width), bf16),
        pltpu.VMEM((local_experts, width, hid), f32),
        pltpu.VMEM((local_experts, width, hid), f32),
        pltpu.VMEM((inner_w, width), f32),
        pair,
        pltpu.VMEM((batch, inner_w), bf16),
        pltpu.VMEM((batch, inner_w), bf16),
        pltpu.VMEM((batch, inner_w), bf16),
        pair,
        pair,
        pair,
        pair,
        pair,
        pair,
        small,
        small,
        small,
        pltpu.VMEM((nz, rows, width), f32),
        pltpu.VMEM((nz, experts, 128), f32),
        pltpu.VMEM((fslots, half - 1, rows, width), bf16),
        pltpu.VMEM((nz, half - 1, rows, width), bf16),
        pltpu.VMEM((fslots, half - 1, experts, 128), bf16),
        pltpu.VMEM((nz, half - 1, experts, 128), bf16),
        pltpu.VMEM((nz - 1, rows, width), bf16),
        pltpu.VMEM((nz - 1, rows, width), bf16),
        pltpu.VMEM((nz - 1, experts, 128), bf16),
        pltpu.VMEM((nz - 1, experts, 128), bf16),
        dma((3, local_experts)),
        dma((4,)),
        dma((2,)),
        dma((2,)),
        dma,
    ]
    scratch += [dma((nz - 1,))] * 4
    scratch += [dma((nz, half))] * 4
    scratch += [dma((nz,))] * 4
    scratch += [dma((2,))] * 6
    scratch += [dma((nz, 6 if half == 4 else half - 1))] * 2
    scratch += [dma((nz, half - 1))] * 2
    scratch += [dma((nz - 1,))] * 6 + [pltpu.VMEM((nz * rows, 128), f32)]
    return pl.pallas_call(
        functools.partial(expert_kernel, n, nz, big),
        out_shape=out_shape,
        in_specs=[vmem] * 5 + [hbm] * 4,
        out_specs=out_specs,
        scratch_shapes=scratch,
        compiler_params=pltpu.CompilerParams(
            collective_id=1, has_side_effects=True, vmem_limit_bytes=60 << 20
        ),
        name="experts",
    )(mid, gain[None], router.T, routes.T, cot, gate, up, down.reshape(inner_w, width), cot_all)[:9]


def attend_kernel(
    n,
    nz,
    x_ref,
    gain_ref,
    wq_ref,
    wk_ref,
    wv_ref,
    wo_ref,
    cos_ref,
    sin_ref,
    lens_ref,
    mid_ref,
    q_ref,
    kv_ref,
    lrow_ref,
    att_ref,
    wqkv,
    wfull,
    qst_s,
    m_s,
    l_s,
    o_s,
    att_low,
    acol,
    ks,
    kr,
    kfs,
    kfr,
    zgs,
    zgr,
    gos,
    gor,
    gps,
    gpr,
):
    e = lax.axis_index("expert")
    z = lax.axis_index("tensor")
    core = lax.rem(e, 2)
    sib = e + 1 - 2 * core
    half = n // 2
    tok, width = x_ref.shape
    rows = tok // nz
    qw = wq_ref.shape[1]
    kw = wk_ref.shape[1]
    seqs = kv_ref.shape[0]
    span = tok // seqs
    heads = kw // HD
    groups = qw // kw
    barrier = greet(n, nz, e, z, sib)

    wqkv[:, 0:qw] = wq_ref[...]
    wqkv[:, qw : qw + kw] = wk_ref[...]
    wqkv[:, qw + kw :] = wv_ref[...]
    x = x_ref[...].astype(f32)
    scale1 = lax.rsqrt(jnp.mean(x * x, -1, keepdims=True) + EPS)
    normed = (x * scale1 * gain_ref[...]).astype(bf16)
    lin = dot_nn(normed, wqkv[...])
    turned = turn(lin, cos_ref[...], sin_ref[...], qw + kw, True).astype(bf16)
    q_ref[...] = turned[:, :qw]
    for s in range(seqs):
        kv_ref[s, pl.ds(pl.multiple_of(e * span, 16), span)] = turned[
            s * span : (s + 1) * span, qw:
        ]
    pl.semaphore_wait(barrier, half + nz - 1)

    def rows_of(j, s):
        return kv_ref.at[s, pl.ds(pl.multiple_of(j * span, 16), span)]

    half_rows = qw // 2
    my_half = pl.ds(pl.multiple_of(core * half_rows, 16), half_rows)

    def weight_send(k):
        to = (e, lax.rem(z + k, nz))
        return remote(
            wo_ref.at[my_half], wfull.at[z, my_half], gos.at[k - 1], gor.at[k - 1], to
        )

    def weight_copy(zz, k, to):
        ref = wfull.at[zz, my_half]
        return remote(ref, ref, gos.at[k - 1], gor.at[k - 1], (e, to))

    def weight_pass(zz, which, k):
        at = pl.ds(pl.multiple_of(which * half_rows, 16), half_rows)
        ref = wfull.at[zz, at]
        return remote(ref, ref, gps.at[k - 1], gpr.at[k - 1], (sib, z))

    for t in range(1, half):
        to = (lax.rem(e + 2 * t, n), z)
        for s in range(seqs):
            remote(rows_of(e, s), rows_of(e, s), ks.at[t, s], kr.at[t, s], to).start()
    for s in range(seqs):
        remote(rows_of(e, s), rows_of(e, s), kfs.at[0, s], kfr.at[0, s], (sib, z)).start()
    for k in range(1, nz):
        weight_send(k).start()
    wfull[z] = wo_ref[...]

    def forward(t, carry):
        src = lax.rem(e - 2 * t + n, n)
        for s in range(seqs):
            remote(rows_of(src, s), rows_of(src, s), ks.at[t, s], kr.at[t, s], (src, z)).wait_recv()
            remote(rows_of(src, s), rows_of(src, s), kfs.at[t, s], kfr.at[t, s], (sib, z)).start()
        return carry

    lax.fori_loop(1, half, forward, 0)

    def arrive(t, carry):
        src = lax.rem(sib - 2 * t + n, n)
        for s in range(seqs):
            remote(
                rows_of(src, s), rows_of(src, s), kfs.at[t, s], kfr.at[t, s], (sib, z)
            ).wait_recv()
        return carry

    lax.fori_loop(0, half, arrive, 0)

    ck = 2 * span
    last = (e * span + span - 1) // ck
    stacked = groups * span
    qpos = lax.broadcasted_iota(jnp.int32, (stacked, ck), 0)
    qpos = e * span + lax.rem(qpos, span)
    kiota = lax.broadcasted_iota(jnp.int32, (stacked, ck), 1)
    klane = lax.broadcasted_iota(jnp.int32, (1, ck), 1)
    m_s[...] = jnp.full_like(m_s, -1e30)
    l_s[...] = jnp.zeros_like(l_s)
    o_s[...] = jnp.zeros_like(o_s)
    for s in range(seqs):
        for h in range(heads):
            qst_s[s * heads + h] = jnp.concatenate(
                [
                    q_ref[
                        s * span : (s + 1) * span,
                        (h * groups + g) * HD : (h * groups + g + 1) * HD,
                    ]
                    for g in range(groups)
                ],
                0,
            ) * jnp.array(HD ** (-0.5), bf16)

    def chunk(c, diagonal):
        at = pl.ds(pl.multiple_of(c * ck, 16), ck)
        for s in range(seqs):
            for h in range(heads):
                i = s * heads + h
                keys = kv_ref[s, at, h * HD : (h + 1) * HD]
                vals = kv_ref[s, at, kw + h * HD : kw + (h + 1) * HD]
                scores = dot_nt(qst_s[i], keys)
                if diagonal:
                    kpos = kiota + c * ck
                    scores = jnp.where((kpos <= qpos) & (kpos < lens_ref[s]), scores, -1e30)
                else:
                    scores = scores + jnp.where(klane + c * ck < lens_ref[s], 0.0, -1e30)
                old = m_s[i, :, 0:1]
                new = jnp.maximum(old, jnp.max(scores, -1, keepdims=True))
                weights = jnp.exp(scores - new)
                shrink = jnp.exp(old - new)
                m_s[i] = jnp.broadcast_to(new, (stacked, 128))
                l_s[i] = l_s[i] * shrink + jnp.sum(weights, -1, keepdims=True)
                o_s[i] = o_s[i] * shrink + dot_nn(weights.astype(bf16), vals)

    def whole_chunk(c, carry):
        chunk(c, False)
        return carry

    lax.fori_loop(0, last, whole_chunk, 0)
    chunk(last, True)
    for s in range(seqs):
        for h in range(heads):
            i = s * heads + h
            result = o_s[i] / l_s[i, :, 0:HD]
            for g in range(groups):
                cols = slice((h * groups + g) * HD, (h * groups + g + 1) * HD)
                att_ref[s * span : (s + 1) * span, cols] = result[g * span : (g + 1) * span]
            logs = m_s[i] + jnp.log(l_s[i])
            lrow_ref[i] = logs.T[0:8]

    att_low[...] = att_ref[...].astype(bf16)
    own_rows = pl.ds(pl.multiple_of(z * rows, 16), rows)

    def row_copy(k, to):
        src = att_low.at[pl.ds(pl.multiple_of(to * rows, 16), rows)]
        return remote(src, acol.at[z], zgs.at[k - 1], zgr.at[k - 1], (e, to))

    for k in range(1, nz):
        row_copy(k, lax.rem(z + k, nz)).start()
    acol[z] = att_low[own_rows, :]
    for k in range(1, nz):
        zz = lax.rem(z + nz - k, nz)
        weight_copy(zz, k, zz).wait_recv()
        weight_pass(zz, core, k).start()
    for k in range(1, nz):
        row_copy(k, lax.rem(z + nz - k, nz)).wait_recv()
        weight_pass(lax.rem(z + nz - k, nz), 1 - core, k).wait_recv()
    mid = x_ref[own_rows, :].astype(f32)
    for zz in range(nz):
        mid = mid + dot_nn(acol[zz], wfull[zz])
    mid_ref[...] = mid
    for k in range(1, nz):
        row_copy(k, lax.rem(z + k, nz)).wait_send()
        weight_send(k).wait_send()
        weight_pass(lax.rem(z + nz - k, nz), core, k).wait_send()

    def sent(t, carry):
        for s in range(seqs):

            @pl.when(t > 0)
            def _():
                remote(
                    rows_of(e, s), rows_of(e, s), ks.at[t, s], kr.at[t, s], (sib, z)
                ).wait_send()

            remote(rows_of(e, s), rows_of(e, s), kfs.at[t, s], kfr.at[t, s], (sib, z)).wait_send()
        return carry

    lax.fori_loop(0, half, sent, 0)


def attend_layer(n, nz, x, gain, wq, wk, wv, wo, cos, sin, lens):
    tok, width = x.shape
    rows = tok // nz
    qw, kw = wq.shape[1], wk.shape[1]
    seqs = lens.shape[0]
    span = tok // seqs
    half = n // 2
    stacked = (qw // kw) * span
    pairs = seqs * (kw // HD)
    dma = pltpu.SemaphoreType.DMA
    vmem = pl.BlockSpec(memory_space=pltpu.VMEM)
    sds = jax.ShapeDtypeStruct
    return pl.pallas_call(
        functools.partial(attend_kernel, n, nz),
        out_shape=[
            sds((rows, width), f32),
            sds((tok, qw), bf16),
            sds((seqs, n * span, 2 * kw), bf16),
            sds((seqs * (kw // HD), 8, stacked), f32),
            sds((tok, qw), f32),
        ],
        in_specs=[vmem] * 8 + [pl.BlockSpec(memory_space=pltpu.SMEM)],
        out_specs=[vmem] * 5,
        scratch_shapes=[
            pltpu.VMEM((width, qw + 2 * kw), bf16),
            pltpu.VMEM((nz, qw, width), bf16),
            pltpu.VMEM((pairs, stacked, HD), bf16),
            pltpu.VMEM((pairs, stacked, 128), f32),
            pltpu.VMEM((pairs, stacked, 128), f32),
            pltpu.VMEM((pairs, stacked, HD), f32),
            pltpu.VMEM((tok, qw), bf16),
            pltpu.VMEM((nz, rows, qw), bf16),
        ]
        + [dma((half, seqs))] * 4
        + [dma((nz - 1,))] * 6,
        compiler_params=pltpu.CompilerParams(
            collective_id=2, has_side_effects=True, vmem_limit_bytes=60 << 20
        ),
        name="attend",
    )(x, gain[None], wq, wk, wv, wo, cos, sin, lens)


def return_kernel(
    n,
    nz,
    gmid_ref,
    mid_ref,
    glog_ref,
    ggrad_ref,
    xn_ref,
    x_ref,
    gain_ref,
    wq_ref,
    wk_ref,
    wv_ref,
    wo_ref,
    cos_ref,
    sin_ref,
    q_ref,
    kv_ref,
    lrow_ref,
    att_ref,
    lens_ref,
    mixed_hbm,
    obuf,
    igbuf,
    wall,
    wall2,
    small_ref,
    wqkv,
    gat,
    datt,
    dq_s,
    qst_s,
    dst_s,
    acc_q,
    dkv,
    kvo,
    kvi,
    kvf,
    kvr,
    part,
    sums,
    csend,
    crecv,
    osend,
    orecv,
    wbufs,
    wbufs2,
    sz1,
    sz2,
    sown,
    ssib,
    schip,
    ofin,
    zas,
    zar,
    zos,
    zor,
    zis,
    zir,
    zps,
    zpr,
    zqs,
    zqr,
    z1s,
    z1r,
    z2s,
    z2r,
    kos,
    kor,
    kfs,
    kfr,
    wsems,
    wsems2,
    sbs,
    sbr,
    scs,
    scr,
    ofs,
    ofr,
    olsem,
    obase,
):
    e = lax.axis_index("expert")
    z = lax.axis_index("tensor")
    core = lax.rem(e, 2)
    me = e // 2
    sib = e + 1 - 2 * core
    half = n // 2
    rows, width = gmid_ref.shape
    tok = rows * nz
    qw = wq_ref.shape[1]
    kw = wk_ref.shape[1]
    seqs = kv_ref.shape[0]
    span = tok // seqs
    heads = kw // HD
    groups = qw // kw
    dn = width // n
    experts = glog_ref.shape[0]
    own_rows = pl.ds(pl.multiple_of(z * rows, 16), rows)
    barrier = greet(n, nz, e, z, sib)
    w1 = PlaneSum(n, e, z, sib, wall, *wbufs, *wsems)
    w2 = PlaneSum(n, e, z, sib, wall2, *wbufs2, *wsems2)

    gat[own_rows, :] = gmid_ref[...].astype(bf16)
    sz1[z] = glog_ref[...]
    pl.semaphore_wait(barrier, half + nz - 1)

    def part_of(ref):
        return lambda zz: ref.at[pl.ds(pl.multiple_of(zz * rows, 16), rows)]

    def slot_of(ref):
        return lambda zz: ref.at[zz]

    gat_line = Line(z, nz, e, part_of(gat), zas, zar)
    out_line = Line(z, nz, e, part_of(obuf), zos, zor)
    igrad_line = Line(z, nz, e, part_of(igbuf), zis, zir)
    normed_sum = LineSum(z, nz, e, csend, crecv, zps, zpr)

    def z_copies(buf_of, send, recv):
        return [
            remote(
                buf_of(z), buf_of(z), send.at[k - 1], recv.at[k - 1], (e, lax.rem(z + k, nz))
            )
            for k in range(1, nz)
        ]

    def z_arrivals(buf_of, send, recv):
        return [
            remote(
                buf_of(lax.rem(z + nz - k, nz)),
                buf_of(lax.rem(z + nz - k, nz)),
                send.at[k - 1],
                recv.at[k - 1],
                (e, lax.rem(z + nz - k, nz)),
            )
            for k in range(1, nz)
        ]

    gat_line.start()
    for copy in z_copies(slot_of(sz1), z1s, z1r):
        copy.start()

    square = half == 4
    chip_x = me + 1 - 2 * lax.rem(me, 2)
    chip_y = lax.rem(me + 2, 4)
    chip_d = 3 - me
    low, high = pl.ds(0, nz // 2), pl.ds(nz // 2, nz - nz // 2)

    def mixed_at(chip, which=slice(None)):
        return mixed_hbm.at[which, pl.ds(pl.multiple_of(chip * rows, 16), rows), :]

    def mixed_copy(src, dst, i, chip):
        return remote(src, dst, ofs.at[i], ofr.at[i], (2 * chip + core, z))

    def mixed_sends():
        if not square:
            return [
                mixed_copy(
                    mixed_at(lax.rem(me + half - t, half)),
                    ofin.at[t],
                    t - 1,
                    lax.rem(me + half - t, half),
                )
                for t in range(1, half)
            ]
        return [
            mixed_copy(mixed_at(chip_d, low), ofin.at[3, low], 0, chip_x),
            mixed_copy(mixed_at(chip_d, high), ofin.at[3, high], 1, chip_y),
            mixed_copy(mixed_at(chip_x, low), ofin.at[1, low], 2, chip_x),
            mixed_copy(mixed_at(chip_y, high), ofin.at[2, high], 3, chip_y),
        ]

    def mixed_relays():
        return [
            mixed_copy(obase.at[low], ofin.at[2, low], 4, chip_y),
            mixed_copy(obase.at[high], ofin.at[1, high], 5, chip_x),
        ]

    for copy in mixed_sends():
        copy.start()
    mixed_own = [pltpu.make_async_copy(mixed_at(me), ofin.at[0], olsem.at[0])]
    if square:
        mixed_own += [
            pltpu.make_async_copy(mixed_at(chip_y, low), obase.at[low], olsem.at[1]),
            pltpu.make_async_copy(mixed_at(chip_x, high), obase.at[high], olsem.at[2]),
        ]
    for copy in mixed_own:
        copy.start()

    def mixed_relay():
        waits = mixed_sends()
        for copy, part, i in zip(mixed_relays(), (low, high), (0, 1)):
            waits[i].wait_recv()
            obase[part] = (obase[part].astype(f32) + ofin[3, part].astype(f32)).astype(bf16)
            copy.start()

    mixed_count = 3 if square else half

    def mixed_sum(zz):
        total = ofin[0, zz].astype(f32)
        for t in range(1, mixed_count):
            total = total + ofin[t, zz].astype(f32)
        return total

    wqkv[:, 0:qw] = wq_ref[...]
    wqkv[:, qw : qw + kw] = wk_ref[...]
    wqkv[:, qw + kw :] = wv_ref[...]
    x = x_ref[...].astype(f32)
    scale1 = lax.rsqrt(jnp.mean(x * x, -1, keepdims=True) + EPS)
    normed = (x * scale1 * gain_ref[...]).astype(bf16)
    dkv[...] = jnp.zeros_like(dkv)

    for hop in range(1, nz):
        gat_line.hop(hop)
    datt[...] = dot_nt(gat[...], wo_ref[...]).astype(bf16)

    ck = 2 * span
    last = (e * span + span - 1) // ck
    stacked = groups * span
    kiota = lax.broadcasted_iota(jnp.int32, (ck, stacked), 0)
    krow = lax.broadcasted_iota(jnp.int32, (ck, 1), 0)
    qpos = e * span + lax.rem(lax.broadcasted_iota(jnp.int32, (ck, stacked), 1), span)
    drows = []
    for s in range(seqs):
        for h in range(heads):

            def gather(ref):
                return jnp.concatenate(
                    [
                        ref[
                            s * span : (s + 1) * span,
                            (h * groups + g) * HD : (h * groups + g + 1) * HD,
                        ]
                        for g in range(groups)
                    ],
                    0,
                )

            i = s * heads + h
            qst_s[i] = gather(q_ref) * jnp.array(HD ** (-0.5), bf16)
            dst = gather(datt)
            dst_s[i] = dst
            delta = jnp.sum(dst.astype(f32) * gather(att_ref), -1, keepdims=True)
            drows.append(jnp.broadcast_to(delta, (stacked, 128)).T[0:1])
    acc_q[...] = jnp.zeros_like(acc_q)
    for copy in mixed_own:
        copy.wait()
    if square:
        mixed_relay()

    def chunk(c, diagonal):
        at = pl.ds(pl.multiple_of(c * ck, 16), ck)
        for s in range(seqs):
            for h in range(heads):
                i = s * heads + h
                keys = kv_ref[s, at, h * HD : (h + 1) * HD]
                vals = kv_ref[s, at, kw + h * HD : kw + (h + 1) * HD]
                scores = dot_nt(keys, qst_s[i]) - lrow_ref[i, 0:1, :]
                if diagonal:
                    kpos = kiota + c * ck
                    allowed = (kpos <= qpos) & (kpos < lens_ref[s])
                    soft = jnp.where(allowed, jnp.exp(scores), 0.0)
                else:
                    soft = jnp.exp(scores + jnp.where(krow + c * ck < lens_ref[s], 0.0, -1e30))
                grad_probs = dot_nt(vals, dst_s[i])
                grad_scores = (soft * (grad_probs - drows[i])).astype(bf16)
                dkv[s, at, h * HD : (h + 1) * HD] = dot_nn(grad_scores, qst_s[i])
                dkv[s, at, kw + h * HD : kw + (h + 1) * HD] = dot_nn(soft.astype(bf16), dst_s[i])
                acc_q[i] += dot_tn(grad_scores, keys)

    def whole_chunk(c, carry):
        chunk(c, False)
        return carry

    lax.fori_loop(0, last, whole_chunk, 0)
    chunk(last, True)
    for s in range(seqs):
        for h in range(heads):
            result = acc_q[s * heads + h] * HD ** (-0.5)
            for g in range(groups):
                cols = slice((h * groups + g) * HD, (h * groups + g + 1) * HD)
                dq_s[s * span : (s + 1) * span, cols] = result[g * span : (g + 1) * span]

    def key_rows(j, s):
        return dkv[s, pl.ds(pl.multiple_of(j * span, 16), span), :]

    def key_send(t):
        return remote(kvo.at[t], kvi.at[t], kos.at[t], kor.at[t], (sib, z))

    def key_final(t):
        to = (lax.rem(e - 2 * t + n, n), z)
        return remote(kvf.at[t - 1], kvr.at[t - 1], kfs.at[t - 1], kfr.at[t - 1], to)

    def key_give(i, carry):
        t = half - 1 - i
        oth = lax.rem(sib - 2 * t + n, n)
        for s in range(seqs):
            kvo[t, s] = key_rows(oth, s).astype(bf16)
        key_send(t).start()
        return carry

    lax.fori_loop(0, half, key_give, 0)

    def key_pass(i, carry):
        t = half - 1 - i
        key_send(t).wait_recv()
        own = lax.rem(e - 2 * t + n, n)
        for s in range(seqs):
            kvf[t - 1, s] = (key_rows(own, s) + kvi[t, s].astype(f32)).astype(bf16)
        key_final(t).start()
        return carry

    cos, sin = cos_ref[...], sin_ref[...]
    gq = turn(dq_s[...], cos, sin, qw, False).astype(bf16)
    query_part = dot_tn(normed, gq)
    out_part = dot_tn(gat[...], att_ref[...].astype(bf16))
    for j in range(n):
        w1.pack[j, :, :qw] = query_part[j * dn : (j + 1) * dn].astype(bf16)
        w1.pack[j, :, qw:] = out_part[j * dn : (j + 1) * dn].astype(bf16)
    lax.fori_loop(0, half - 1, key_pass, 0)
    w1.give()

    def mixed_last(k, to):
        return remote(osend.at[k - 1], orecv.at[k - 1], zqs.at[k - 1], zqr.at[k - 1], (e, to))

    for copy in mixed_sends()[2:] + mixed_relays() if square else mixed_sends():
        copy.wait_recv()
    for k in range(1, nz):
        zz = lax.rem(z + k, nz)
        osend[k - 1] = mixed_sum(zz).astype(bf16)
        mixed_last(k, zz).start()
    own_mixed = mid_ref[...] + mixed_sum(z)
    w1.spread()
    for copy in z_arrivals(slot_of(sz1), z1s, z1r):
        copy.wait_recv()
    rgrad = dot_nn(sz1[0][:, :rows], xn_ref[0])
    for zz in range(1, nz):
        rgrad = rgrad + dot_nn(sz1[zz][:, :rows], xn_ref[zz])
    sown[0:experts, :] = rgrad.astype(bf16)

    key_send(0).wait_recv()
    own_kv = [key_rows(e, s) + kvi[0, s].astype(f32) for s in range(seqs)]
    for t in range(1, half):
        key_final(t).wait_recv()
        for s in range(seqs):
            own_kv[s] = own_kv[s] + kvr[t - 1, s].astype(f32)
    gkv = turn(jnp.concatenate(own_kv, 0), cos, sin, kw, False).astype(bf16)
    part[...] = dot_nt(gq, wqkv[:, :qw]) + dot_nt(gkv, wqkv[:, qw:])

    def normed_part(zz):
        return part[pl.ds(pl.multiple_of(zz * rows, 16), rows), :]

    for hop in range(nz - 1):
        normed_sum.hop(hop, normed_part)
        if hop > 0:
            out_line.hop(hop)
        if hop == 0:
            for k in range(1, nz):
                mixed_last(k, z).wait_recv()
                own_mixed = own_mixed + orecv[k - 1].astype(f32)
            obuf[own_rows, :] = own_mixed.astype(bf16)
            out_line.start()
            again = jnp.sum(part[...] * x * scale1, 0, keepdims=True)
            sz2[z] = jnp.concatenate([again, ggrad_ref[...], jnp.zeros((14, width), f32)], 0).astype(
                bf16
            )
            for copy in z_copies(slot_of(sz2), z2s, z2r):
                copy.start()
            pair_part = dot_tn(normed, gkv)
            for j in range(n):
                w2.pack[j] = pair_part[j * dn : (j + 1) * dn].astype(bf16)
            w2.give()
            w1.total()
    w2.spread()
    normed_sum.total(sums, normed_part)

    own_x = x_ref[own_rows, :].astype(f32)
    own_scale = lax.rsqrt(jnp.mean(own_x * own_x, -1, keepdims=True) + EPS)
    grad_normed = sums[...]
    gained = grad_normed * gain_ref[...]
    igrad = (
        gmid_ref[...]
        + own_scale * gained
        - own_x
        * (own_scale * own_scale * own_scale)
        * jnp.mean(gained * own_x, -1, keepdims=True)
    )
    igbuf[own_rows, :] = igrad.astype(bf16)
    igrad_line.start()
    out_line.hop(nz - 1)

    w1.forward()
    for copy in z_arrivals(slot_of(sz2), z2s, z2r):
        copy.wait_recv()
    second = sz2[0].astype(f32)
    for zz in range(1, nz):
        second = second + sz2[zz].astype(f32)
    sown[experts:, :] = second.astype(bf16)
    small_sib = remote(sown, ssib, sbs, sbr, (sib, z))
    small_sib.start()
    if nz > 2:
        igrad_line.hop(1)
    small_sib.wait_recv()
    schip[me] = (sown[...].astype(f32) + ssib[...].astype(f32)).astype(bf16)

    def small_send(t):
        to = (lax.rem(e + 2 * t, n), z)
        return remote(schip.at[me], schip.at[me], scs.at[t - 1], scr.at[t - 1], to)

    for t in range(1, half):
        small_send(t).start()

    w2.total()
    for hop in range(2, nz - 1):
        igrad_line.hop(hop)
    igrad_line.hop(nz - 1)

    w2.forward()
    for t in range(1, half):
        src = lax.rem(me + half - t, half)
        remote(
            schip.at[src], schip.at[src], scs.at[t - 1], scr.at[t - 1], (sib, z)
        ).wait_recv()
    small = schip[0].astype(f32)
    for t in range(1, half):
        small = small + schip[t].astype(f32)
    small_ref[...] = small

    w1.arrive()
    w2.arrive()
    for k in range(1, nz):
        mixed_last(k, z).wait_send()
    for line in (gat_line, out_line, igrad_line, normed_sum, w1, w2):
        line.drain()
    for copy in z_copies(slot_of(sz1), z1s, z1r) + z_copies(slot_of(sz2), z2s, z2r):
        copy.wait_send()
    small_sib.wait_send()
    for copy in mixed_sends() + (mixed_relays() if square else []):
        copy.wait_send()

    def drained(t, carry):
        key_send(t).wait_send()

        @pl.when(t > 0)
        def _():
            key_final(t).wait_send()
            small_send(t).wait_send()

        return carry

    lax.fori_loop(0, half, drained, 0)


class PlaneSum:
    def __init__(self, n, e, z, sib, wall, pack, near, send, recv, *sems):
        self.n, self.e, self.z, self.sib, self.half = n, e, z, sib, n // 2
        self.wall, self.pack, self.near, self.send, self.recv = wall, pack, near, send, recv
        self.sems = sems

    def peer(self, base, t):
        return lax.rem(base - 2 * t + self.n, self.n)

    def near_copy(self, t):
        src = self.pack.at[self.peer(self.sib, t)]
        return remote(
            src, self.near.at[t], self.sems[0].at[t], self.sems[1].at[t], (self.sib, self.z)
        )

    def far_copy(self, t):
        return remote(
            self.send.at[t - 1],
            self.recv.at[t - 1],
            self.sems[2].at[t],
            self.sems[3].at[t],
            (self.peer(self.e, t), self.z),
        )

    def all_copy(self, src, t, to):
        ref = self.wall.at[src]
        return remote(ref, ref, self.sems[4].at[t], self.sems[5].at[t], (to, self.z))

    def pass_copy(self, src, t):
        ref = self.wall.at[src]
        return remote(ref, ref, self.sems[6].at[t], self.sems[7].at[t], (self.sib, self.z))

    def give(self):
        def one(i, carry):
            self.near_copy(self.half - 1 - i).start()
            return carry

        lax.fori_loop(0, self.half, one, 0)

    def spread(self):
        def one(i, carry):
            t = self.half - 1 - i
            self.near_copy(t).wait_recv()
            own = self.pack[self.peer(self.e, t)].astype(f32)
            self.send[t - 1] = (own + self.near[t].astype(f32)).astype(bf16)
            self.far_copy(t).start()
            return carry

        lax.fori_loop(0, self.half - 1, one, 0)

    def total(self):
        self.near_copy(0).wait_recv()
        total = self.pack[self.e].astype(f32) + self.near[0].astype(f32)
        for t in range(1, self.half):
            self.far_copy(t).wait_recv()
            total = total + self.recv[t - 1].astype(f32)
        self.wall[self.e] = total.astype(bf16)
        for t in range(1, self.half):
            self.all_copy(self.e, t, lax.rem(self.e + 2 * t, self.n)).start()
        self.pass_copy(self.e, 0).start()

    def forward(self):
        def one(t, carry):
            src = self.peer(self.e, t)
            self.all_copy(src, t, src).wait_recv()
            self.pass_copy(src, t).start()
            return carry

        lax.fori_loop(1, self.half, one, 0)

    def arrive(self):
        def one(t, carry):
            self.pass_copy(self.peer(self.sib, t), t).wait_recv()
            return carry

        lax.fori_loop(0, self.half, one, 0)

    def drain(self):
        def one(t, carry):
            self.near_copy(t).wait_send()
            self.pass_copy(self.e, t).wait_send()

            @pl.when(t > 0)
            def _():
                self.far_copy(t).wait_send()
                self.all_copy(self.e, t, self.sib).wait_send()

            return carry

        lax.fori_loop(0, self.half, one, 0)


class Line:
    def __init__(self, z, nz, e, buf_of, send, recv):
        self.z, self.nz, self.e = z, nz, e
        self.buf_of, self.send, self.recv = buf_of, send, recv

    def copy(self, way, piece):
        to = self.z + 1 if way == 0 else self.z - 1
        ref = self.buf_of(piece)
        return remote(ref, ref, self.send.at[way, piece], self.recv.at[way, piece], (self.e, to))

    def push(self, piece, ways=(0, 1)):
        for way in ways:

            @pl.when(self.z < self.nz - 1 if way == 0 else self.z > 0)
            def _():
                self.copy(way, piece).start()

    def start(self):
        self.push(self.z)

    def hop(self, i):
        @pl.when(self.z >= i)
        def _():
            self.copy(0, self.z - i).wait_recv()
            self.push(self.z - i, (0,))

        @pl.when(self.z + i <= self.nz - 1)
        def _():
            self.copy(1, self.z + i).wait_recv()
            self.push(self.z + i, (1,))

    def drain(self):
        for piece in range(self.nz):

            @pl.when((self.z >= piece) & (self.z < self.nz - 1))
            def _():
                self.copy(0, piece).wait_send()

            @pl.when((self.z <= piece) & (self.z > 0))
            def _():
                self.copy(1, piece).wait_send()


class LineSum:
    def __init__(self, z, nz, e, send_buf, recv_buf, send, recv):
        self.z, self.nz, self.e = z, nz, e
        self.send_buf, self.recv_buf, self.send, self.recv = send_buf, recv_buf, send, recv

    def copy(self, way, target):
        to = self.z + 1 if way == 0 else self.z - 1
        return remote(
            self.send_buf.at[way, target],
            self.recv_buf.at[way, target],
            self.send.at[way, target],
            self.recv.at[way, target],
            (self.e, to),
        )

    def hop(self, i, own_of):
        for way, target in ((0, self.nz - 1 - i), (1, i)):
            passes = self.z < target if way == 0 else self.z > target
            first = self.z == 0 if way == 0 else self.z == self.nz - 1
            inner = self.z > 0 if way == 0 else self.z < self.nz - 1

            @pl.when(passes & first)
            def _():
                self.send_buf[way, target] = own_of(target).astype(bf16)
                self.copy(way, target).start()

            @pl.when(passes & inner)
            def _():
                self.copy(way, target).wait_recv()
                self.send_buf[way, target] = (
                    own_of(target) + self.recv_buf[way, target].astype(f32)
                ).astype(bf16)
                self.copy(way, target).start()

    def total(self, ref, own_of):
        ref[...] = own_of(self.z)

        @pl.when(self.z > 0)
        def _():
            self.copy(0, self.z).wait_recv()
            ref[...] += self.recv_buf[0, self.z].astype(f32)

        @pl.when(self.z < self.nz - 1)
        def _():
            self.copy(1, self.z).wait_recv()
            ref[...] += self.recv_buf[1, self.z].astype(f32)

    def drain(self):
        for target in range(self.nz):

            @pl.when(self.z < target)
            def _():
                self.copy(0, target).wait_send()

            @pl.when(self.z > target)
            def _():
                self.copy(1, target).wait_send()


def return_layer(
    n, nz, gmid, mid, glog, ggrad, xn, x, gain, wq, wk, wv, wo, cos, sin, q, kv, lrow, att, lens, mixed
):
    tok, width = x.shape
    rows = tok // nz
    qw, kw = wq.shape[1], wk.shape[1]
    seqs = lens.shape[0]
    span = tok // seqs
    half = n // 2
    stacked = (qw // kw) * span
    pairs = seqs * (kw // HD)
    experts = glog.shape[0]
    small_rows = experts + 16
    dma = pltpu.SemaphoreType.DMA
    vmem = pl.BlockSpec(memory_space=pltpu.VMEM)
    sds = jax.ShapeDtypeStruct
    zdma = dma((nz - 1,))
    line = dma((2, nz))
    hdma = dma((half,))
    fdma = dma((half - 1,))
    def plane_bufs(cols):
        return [
            pltpu.VMEM((n, width // n, cols), bf16),
            pltpu.VMEM((half, width // n, cols), bf16),
            pltpu.VMEM((half - 1, width // n, cols), bf16),
            pltpu.VMEM((half - 1, width // n, cols), bf16),
        ]

    line_buf = pltpu.VMEM((2, nz, rows, width), bf16)
    return pl.pallas_call(
        functools.partial(return_kernel, n, nz),
        out_shape=[
            sds((tok, width), bf16),
            sds((tok, width), bf16),
            sds((n, width // n, 2 * qw), bf16),
            sds((n, width // n, 2 * kw), bf16),
            sds((small_rows, width), f32),
        ],
        in_specs=[vmem] * 17
        + [pl.BlockSpec(memory_space=pltpu.SMEM), pl.BlockSpec(memory_space=pl.ANY)],
        out_specs=[vmem] * 5,
        scratch_shapes=[
            pltpu.VMEM((width, qw + 2 * kw), bf16),
            pltpu.VMEM((tok, width), bf16),
            pltpu.VMEM((tok, qw), bf16),
            pltpu.VMEM((tok, qw), f32),
            pltpu.VMEM((pairs, stacked, HD), bf16),
            pltpu.VMEM((pairs, stacked, HD), bf16),
            pltpu.VMEM((pairs, stacked, HD), f32),
            pltpu.VMEM((seqs, n * span, 2 * kw), f32),
            pltpu.VMEM((half, seqs, span, 2 * kw), bf16),
            pltpu.VMEM((half, seqs, span, 2 * kw), bf16),
            pltpu.VMEM((half - 1, seqs, span, 2 * kw), bf16),
            pltpu.VMEM((half - 1, seqs, span, 2 * kw), bf16),
            pltpu.VMEM((tok, width), f32),
            pltpu.VMEM((rows, width), f32),
            line_buf,
            line_buf,
            pltpu.VMEM((nz - 1, rows, width), bf16),
            pltpu.VMEM((nz - 1, rows, width), bf16),
            plane_bufs(2 * qw),
            plane_bufs(2 * kw),
            pltpu.VMEM((nz, experts, 128), bf16),
            pltpu.VMEM((nz, 16, width), bf16),
            pltpu.VMEM((small_rows, width), bf16),
            pltpu.VMEM((small_rows, width), bf16),
            pltpu.VMEM((half, small_rows, width), bf16),
            pltpu.VMEM((half, nz, rows, width), bf16),
        ]
        + [line] * 8
        + [zdma] * 6
        + [hdma, hdma, fdma, fdma]
        + [[hdma] * 8, [hdma] * 8]
        + [dma, dma, fdma, fdma]
        + [dma((6 if half == 4 else half - 1,))] * 2
        + [dma((3,)), pltpu.VMEM((nz, rows, width), bf16)],
        compiler_params=pltpu.CompilerParams(
            collective_id=3, has_side_effects=True, vmem_limit_bytes=58 << 20
        ),
        name="attend_back",
    )(
        gmid,
        mid,
        glog,
        ggrad,
        xn,
        x,
        gain[None],
        wq,
        wk,
        wv,
        wo,
        cos,
        sin,
        q,
        kv,
        lrow,
        att,
        lens,
        mixed,
    )


def finish_kernel(
    out_low,
    igrad_low,
    wall,
    wall2,
    small,
    load,
    dgate_in,
    dup_in,
    ddown_in,
    out_ref,
    igrad_ref,
    q_ref,
    k_ref,
    v_ref,
    o_ref,
    router_ref,
    again_ref,
    egain_ref,
    loss_ref,
    load_ref,
    dgate,
    dup,
    ddown,
    dgate_s,
    dup_s,
    ddown_s,
    sems,
):
    pairs = ((dgate_in, dgate_s, dgate), (dup_in, dup_s, dup), (ddown_in, ddown_s, ddown))
    reads = [pltpu.make_async_copy(p[0], p[1], sems.at[0, i]) for i, p in enumerate(pairs)]
    writes = [pltpu.make_async_copy(p[1], p[2], sems.at[1, i]) for i, p in enumerate(pairs)]
    for copy in reads:
        copy.start()
    qw, kw = q_ref.shape[1], k_ref.shape[1]
    experts = load.shape[1]
    out_ref[...] = out_low[...].astype(f32)
    for read, write in zip(reads, writes):
        read.wait()
        write.start()
    igrad_ref[...] = igrad_low[...].astype(f32)
    chunks, dn, _ = wall.shape
    flat = wall[...].reshape(chunks * dn, 2 * qw).astype(f32)
    q_ref[...] = flat[:, :qw]
    o_ref[...] = flat[:, qw:].T
    flat = wall2[...].reshape(chunks * dn, 2 * kw).astype(f32)
    k_ref[...] = flat[:, :kw]
    v_ref[...] = flat[:, kw:]
    router_ref[...] = small[0:experts, :]
    again_ref[...] = small[experts : experts + 1, :]
    egain_ref[...] = small[experts + 1 : experts + 2, :]
    load_ref[...] = load[...]
    loss_ref[...] = jnp.mean(load[...], -1, keepdims=True)
    for copy in writes:
        copy.wait()


def finish_layer(out_low, igrad_low, wall, wall2, small, load, dgate, dup, ddown, qw, kw):
    tok, width = out_low.shape
    experts = load.shape[1]
    vmem = pl.BlockSpec(memory_space=pltpu.VMEM)
    hbm = pl.BlockSpec(memory_space=pl.ANY)
    sds = jax.ShapeDtypeStruct
    return pl.pallas_call(
        finish_kernel,
        out_shape=[
            sds((tok, width), f32),
            sds((tok, width), f32),
            sds((width, qw), f32),
            sds((width, kw), f32),
            sds((width, kw), f32),
            sds((qw, width), f32),
            sds((experts, width), f32),
            sds((1, width), f32),
            sds((1, width), f32),
            sds((1, 1), f32),
            sds((1, experts), f32),
            sds(dgate.shape, f32),
            sds(dup.shape, f32),
            sds(ddown.shape, f32),
        ],
        in_specs=[vmem] * 6 + [hbm] * 3,
        out_specs=[vmem] * 11 + [hbm] * 3,
        scratch_shapes=[
            pltpu.VMEM(dgate.shape, f32),
            pltpu.VMEM(dup.shape, f32),
            pltpu.VMEM(ddown.shape, f32),
            pltpu.SemaphoreType.DMA((2, 3)),
        ],
        compiler_params=pltpu.CompilerParams(vmem_limit_bytes=60 << 20),
        name="finish",
    )(out_low, igrad_low, wall, wall2, small, load, dgate, dup, ddown)


def shards(
    inputs,
    attention_gain,
    query_weight,
    key_weight,
    value_weight,
    out_weight,
    expert_gain,
    router_weight,
    gate_weight,
    up_weight,
    down_weight,
    routes,
    seq_lens,
    cotangent,
):
    n = lax.axis_size("expert")
    nz = lax.axis_size("tensor")
    tok_rows = inputs.shape[0]
    seq_count = seq_lens.shape[0]
    span_rows = tok_rows // seq_count
    row = lax.broadcasted_iota(jnp.int32, (tok_rows, 128), 0) % span_rows
    lane = lax.broadcasted_iota(jnp.int32, (tok_rows, 128), 1) % (HD // 2)
    frequency = THETA ** (-2.0 * lane.astype(f32) / HD)
    angles = (lax.axis_index("expert") * span_rows + row).astype(f32) * frequency
    cosines = jnp.cos(angles)
    sines = jnp.sin(angles)
    cot_all = lax.all_gather(cotangent.astype(bf16), "expert", axis=0, tiled=True)
    weights = (query_weight, key_weight, value_weight, out_weight, cosines, sines)
    middle, queries, pairs, logs, attended = attend_layer(
        n, nz, inputs, attention_gain, *weights, seq_lens
    )
    (
        grad_middle,
        logit_grads,
        expert_gain_part,
        expert_load,
        gate_grad,
        up_grad,
        down_grad,
        mixed,
        normed2,
    ) = expert_layer(
        n,
        nz,
        middle,
        expert_gain,
        router_weight,
        routes,
        gate_weight,
        up_weight,
        down_weight,
        cotangent,
        cot_all,
    )
    out_low, igrad_low, packed, packed2, small = return_layer(
        n,
        nz,
        grad_middle,
        middle,
        logit_grads,
        expert_gain_part,
        normed2,
        inputs,
        attention_gain,
        *weights,
        queries,
        pairs,
        logs,
        attended,
        seq_lens,
        mixed,
    )
    (
        output,
        input_grad,
        query_grad,
        key_grad,
        value_grad,
        out_weight_grad,
        router_grad,
        attention_gain_grad,
        expert_gain_grad,
        balance_loss,
        expert_load,
        gate_grad,
        up_grad,
        down_grad,
    ) = finish_layer(
        out_low,
        igrad_low,
        packed,
        packed2,
        small,
        expert_load,
        gate_grad,
        up_grad,
        down_grad,
        query_weight.shape[1],
        key_weight.shape[1],
    )
    return (
        output,
        input_grad,
        balance_loss[0, 0],
        expert_load[0],
        attention_gain_grad[0],
        query_grad,
        key_grad,
        value_grad,
        out_weight_grad,
        expert_gain_grad[0],
        router_grad.T,
        gate_grad,
        up_grad,
        down_grad.reshape(down_weight.shape),
    )


def solution(mesh):
    placed = (
        P("expert", None),
        P(),
        P(None, "tensor"),
        P(None, "tensor"),
        P(None, "tensor"),
        P("tensor", None),
        P(),
        P(),
        P("expert", None, "tensor"),
        P("expert", None, "tensor"),
        P("expert", "tensor", None),
        P("expert", None),
        P(),
        P("expert", None),
    )
    return jax.shard_map(
        shards,
        mesh=mesh,
        in_specs=placed,
        out_specs=(
            P("expert", None),
            P("expert", None),
            P(),
            P(),
            P(),
            P(None, "tensor"),
            P(None, "tensor"),
            P(None, "tensor"),
            P("tensor", None),
            P(),
            P(),
            P("expert", None, "tensor"),
            P("expert", None, "tensor"),
            P("expert", "tensor", None),
        ),
        check_vma=False,
    )
```

```python
import functools

import jax
import jax.numpy as jnp
from jax import lax
from jax.experimental import pallas as pl
from jax.experimental.pallas import tpu as pltpu
from jax.sharding import PartitionSpec as P

HD = 64
EPS = 1e-06
THETA = 10000.0
MESH = pl.DeviceIdType.MESH
f32 = jnp.float32
bf16 = jnp.bfloat16


def dot_nn(left, right):
    return lax.dot_general(left, right, (((1,), (0,)), ((), ())), preferred_element_type=f32)


def dot_nt(left, right):
    return lax.dot_general(left, right, (((1,), (1,)), ((), ())), preferred_element_type=f32)


def dot_tn(left, right):
    return lax.dot_general(left, right, (((0,), (0,)), ((), ())), preferred_element_type=f32)


def remote(src, dst, send_sem, recv_sem, device):
    return pltpu.make_async_remote_copy(
        src_ref=src,
        dst_ref=dst,
        send_sem=send_sem,
        recv_sem=recv_sem,
        device_id=device,
        device_id_type=MESH,
    )


def turn(values, cos, sin, last, forward):
    lane = lax.broadcasted_iota(jnp.int32, (values.shape[0], 128), 1)
    first_half = lax.rem(lane, HD) < HD // 2
    parts = []
    for g in range(values.shape[1] // 128):
        v = values[:, g * 128 : (g + 1) * 128]
        if g * 128 >= last:
            parts.append(v)
            continue
        turned = jnp.where(
            first_half, -pltpu.roll(v, 128 - HD // 2, 1), pltpu.roll(v, HD // 2, 1)
        )
        new = v * cos + turned * sin if forward else v * cos - turned * sin
        if (g + 1) * 128 > last:
            new = jnp.where(lane + g * 128 < last, new, v)
        parts.append(new)
    return jnp.concatenate(parts, 1) if len(parts) > 1 else parts[0]


def greet(n, nz, e, z, sib):
    barrier = pltpu.get_barrier_semaphore()
    pl.semaphore_signal(barrier, inc=1, device_id=(sib, z), device_id_type=MESH)
    for s in range(1, n // 2):
        pl.semaphore_signal(
            barrier, inc=1, device_id=(lax.rem(e + 2 * s, n), z), device_id_type=MESH
        )
    for k in range(1, nz):
        pl.semaphore_signal(barrier, inc=1, device_id=(e, lax.rem(z + k, nz)), device_id_type=MESH)
    return barrier


def expert_kernel(
    n,
    nz,
    big,
    mid_ref,
    gain_ref,
    router_ref,
    routes_ref,
    cot_ref,
    gate_hbm,
    up_hbm,
    down_hbm,
    cot_all,
    *rest,
):
    outs, rest = rest[:9], rest[9:]
    gmid_ref, glog_ref, ggrad_ref, load_ref = outs[:4]
    dgate_hbm, dup_hbm, ddown_hbm, mixed_hbm, normed_hbm = outs[4:]
    xbuf, rest = rest[0], rest[1:]
    if big:
        xstage, rest = rest[0], rest[1:]
    (
        wbuf,
        xn_s,
        wg,
        wu,
        down_ref,
        dgate,
        dup,
        ddown,
        cbuf,
        dg_s,
        du_s,
        wi_s,
        hold,
        osend,
        sin,
        hold_o,
        osend_o,
        sin_o,
        hold_g,
        osend_g,
        sin_g,
        own_s,
        own_g,
        fsend,
        fin,
        fsend_g,
        fin_g,
        zsend,
        zin,
        zsend_g,
        zin_g,
        wsem,
        gsem,
        csem,
        msem,
        lsem,
        zs,
        zr,
        zws,
        zwr,
        xs,
        xr,
        ws,
        wr,
        fs,
        fr,
        wfs,
        wfr,
        gs,
        gr,
        oss,
        osr,
        ggs,
        ggr,
        ps,
        pr,
        pgs,
        pgr,
        zgs,
        zgr,
        zggs,
        zggr,
        picks_s,
    ) = rest
    e = lax.axis_index("expert")
    z = lax.axis_index("tensor")
    core = lax.rem(e, 2)
    other = 1 - core
    me = e // 2
    sib = e + 1 - 2 * core
    half = n // 2
    rows, width = mid_ref.shape
    tok = rows * nz
    experts = router_ref.shape[0]
    local_experts, _, hid = gate_hbm.shape
    inner_w = local_experts * hid
    fc = min(inner_w, 256)
    fslots = fsend.shape[0]
    square = half == 4
    chip_x = me + 1 - 2 * lax.rem(me, 2)
    chip_y = lax.rem(me + 2, 4)
    chip_d = 3 - me
    mid_row = rows // 2

    loads = []
    for el in range(local_experts):
        cols = pl.ds(el * hid, hid)
        loads.append(pltpu.make_async_copy(gate_hbm.at[el], wg.at[:, cols], wsem.at[0, el]))
        loads.append(pltpu.make_async_copy(up_hbm.at[el], wu.at[:, cols], wsem.at[1, el]))
    loads.append(pltpu.make_async_copy(down_hbm, down_ref, wsem.at[2, 0]))
    for copy in loads:
        copy.start()

    def piece_of(g):
        return lax.rem(z + nz - g, nz)

    def cot_start(g, parity, slot):
        zz = piece_of(g)
        for h in range(half):
            start = (2 * h + parity) * tok + zz * rows
            pltpu.make_async_copy(
                cot_all.at[pl.ds(pl.multiple_of(start, 16), rows)],
                cbuf.at[slot, pl.ds(h * rows, rows)],
                csem.at[slot],
            ).start()

    def cot_wait(slot):
        pltpu.make_async_copy(
            cot_all.at[pl.ds(0, half * rows)], cbuf.at[slot], csem.at[slot]
        ).wait()

    cot_start(0, core, 0)
    barrier = greet(n, nz, e, z, sib)

    own_rows = pl.ds(pl.multiple_of(z * rows, 16), rows)
    my_rows = pl.ds(pl.multiple_of(me * rows, 16), rows)
    mid = mid_ref[...]
    scale2 = lax.rsqrt(jnp.mean(mid * mid, -1, keepdims=True) + EPS)
    xn = (mid * scale2 * gain_ref[...]).astype(bf16)
    xn_s[...] = xn
    logits = dot_nt(xn, router_ref[...])
    choices = routes_ref[...].astype(f32)
    top_count = choices.shape[0]
    picks_s[...] = jnp.concatenate([choices, jnp.zeros((128 - top_count, tok), f32)], 0).T
    picks = picks_s[own_rows, 0:top_count].astype(jnp.int32)
    lanes = lax.broadcasted_iota(jnp.int32, (rows, experts), 1)
    chosen = jnp.zeros((rows, experts), f32)
    for k in range(picks.shape[1]):
        chosen = jnp.where(picks[:, k : k + 1] == lanes, 1.0, chosen)
    top = jnp.max(logits, -1, keepdims=True)
    powers = jnp.exp(logits - top)
    probs = powers / jnp.sum(powers, -1, keepdims=True)
    low_logits = jnp.where(chosen > 0.0, logits, -1e30)
    ctop = jnp.max(low_logits, -1, keepdims=True)
    cpow = jnp.exp(low_logits - ctop)
    comb = cpow / jnp.sum(cpow, -1, keepdims=True)
    padded = jnp.concatenate([comb, jnp.zeros((rows, 128 - experts), f32)], 1)
    if rows < 128:
        padded = jnp.concatenate([padded, jnp.zeros((128 - rows, 128), f32)], 0)
    piece = padded.T[:experts]
    lane_pad = jnp.zeros((1, 128 - experts), f32)
    cnt = jnp.concatenate([jnp.sum(chosen, 0, keepdims=True), lane_pad], 1)
    psum = jnp.concatenate([jnp.sum(probs, 0, keepdims=True), lane_pad], 1)
    psum_hi = psum.astype(bf16).astype(f32)
    stats = jnp.concatenate([cnt, psum_hi, psum - psum_hi, jnp.zeros((13, 128), f32)], 0)
    wbuf[z, core, me] = jnp.concatenate([piece, stats], 0).astype(bf16)
    if big:
        copy = pltpu.make_async_copy(xn_s, xbuf.at[z, core, my_rows], lsem)
        copy.start()
        copy.wait()
    else:
        xbuf[z, core, my_rows] = xn
    pl.semaphore_wait(barrier, half + nz - 1)

    def z_row(zz, k, to):
        ref = xbuf.at[zz, core, my_rows]
        return remote(ref, ref, zs.at[k - 1], zr.at[k - 1], (e, to))

    def z_small(zz, k, to):
        ref = wbuf.at[zz, core, me]
        return remote(ref, ref, zws.at[k - 1], zwr.at[k - 1], (e, to))

    def x_row(zz, h, g, s, to):
        ref = xbuf.at[zz, core, pl.ds(pl.multiple_of(h * rows, 16), rows)]
        return remote(ref, ref, xs.at[g, s], xr.at[g, s], (to, z))

    def x_small(zz, h, g, s, to):
        ref = wbuf.at[zz, core, h]
        return remote(ref, ref, ws.at[g, s], wr.at[g, s], (to, z))

    def x_part(zz, h, first, count, g, i, to):
        start = pl.multiple_of(h * rows + first, 16)
        ref = xbuf.at[zz, core, pl.ds(start, count)]
        return remote(ref, ref, xs.at[g, i], xr.at[g, i], (2 * to + core, z))

    def push_piece(g):
        zz = piece_of(g)
        if square:
            x_part(zz, me, 0, rows, g, 0, chip_x).start()
            x_part(zz, me, 0, rows, g, 1, chip_y).start()
        for s in range(1, half):
            to = lax.rem(e + 2 * s, n)
            if not square:
                x_row(zz, me, g, s, to).start()
            x_small(zz, me, g, s, to).start()

    def relays(g):
        zz = piece_of(g)
        return (
            x_part(zz, chip_x, 0, mid_row, g, 2, chip_y),
            x_part(zz, chip_y, mid_row, rows - mid_row, g, 3, chip_x),
        )

    def relay_pieces(g):
        zz = piece_of(g)
        low, high = relays(g)
        x_part(zz, chip_x, 0, rows, g, 0, chip_x).wait_recv()
        low.start()
        x_part(zz, chip_y, 0, rows, g, 1, chip_y).wait_recv()
        high.start()

    push_piece(jnp.int32(0))
    def z_push(k):
        z_row(z, k, lax.rem(z + k, nz)).start()
        z_small(z, k, lax.rem(z + k, nz)).start()

    for k in range(1, min(nz, 2) if square else nz):
        z_push(k)

    if square:
        relay_pieces(jnp.int32(0))
        if nz > 2:
            z_push(2)

    dgate[...] = jnp.zeros_like(dgate)
    dup[...] = jnp.zeros_like(dup)
    ddown[...] = jnp.zeros_like(ddown)
    for copy in loads:
        copy.wait()

    sel_row = lax.broadcasted_iota(jnp.int32, (experts, fc), 0)
    sel_col = lax.broadcasted_iota(jnp.int32, (experts, fc), 1)

    def block(zz, parity, slot, dst, dst_o, dst_g, dslot):
        if big:
            copy = pltpu.make_async_copy(xbuf.at[zz, parity], xstage, lsem)
            copy.start()
            copy.wait()
            x_ref = xstage
        else:
            x_ref = xbuf.at[zz, parity]
        c_ref = cbuf.at[slot]
        sums = [jnp.zeros((experts, rows), f32) for _ in range(half)]
        for q in range(inner_w // fc):
            cols = slice(q * fc, (q + 1) * fc)
            x = x_ref[...]
            gate_val = dot_nn(x, wg[:, cols])
            up_val = dot_nn(x, wu[:, cols])
            back = dot_nt(c_ref[...], down_ref[cols, :])
            select = jnp.where(
                sel_row == e * local_experts + (q * fc + sel_col) // hid, 1.0, 0.0
            ).astype(bf16)
            wide = jnp.concatenate(
                [dot_tn(wbuf[zz, parity, h, :experts, :], select)[:rows] for h in range(half)], 0
            )
            sig = 1.0 / (1.0 + jnp.exp(-gate_val))
            silu = gate_val * sig
            inner = silu * up_val
            wi_s[:, cols] = (inner * wide).astype(bf16)
            scaled = back * wide
            dg_s[:, cols] = (scaled * up_val * (sig * (1.0 + gate_val * (1.0 - sig)))).astype(bf16)
            du_s[:, cols] = (scaled * silu).astype(bf16)
            both = (inner * back).astype(bf16)
            for h in range(half):
                sums[h] = sums[h] + dot_nt(select, both[h * rows : (h + 1) * rows])
        for h in range(half):
            gap = jnp.zeros((experts, 128 - rows), f32)
            dst_g[dslot, h] = jnp.concatenate([sums[h], gap], 1).astype(bf16)
        for h in range(width // 256):
            cols = slice(h * 256, (h + 1) * 256)
            dst[dslot, :, cols] = (
                dot_nt(dg_s[...], wg[cols, :]) + dot_nt(du_s[...], wu[cols, :])
            ).astype(bf16)
            dst_o[dslot, :, cols] = dot_nn(wi_s[...], down_ref[:, cols]).astype(bf16)
        for h in range(width // 256):
            cols = slice(h * 256, (h + 1) * 256)
            x_part = x_ref[:, cols]
            gate_part = dot_tn(x_part, dg_s[...])
            up_part = dot_tn(x_part, du_s[...])
            for el in range(local_experts):
                dgate[el, cols, :] += gate_part[:, el * hid : (el + 1) * hid]
                dup[el, cols, :] += up_part[:, el * hid : (el + 1) * hid]
            ddown[:, cols] += dot_tn(wi_s[...], c_ref[:, cols])

    def gives(slot):
        return [
            remote(osend.at[slot], sin.at[slot], gs.at[slot], gr.at[slot], (sib, z)),
            remote(osend_g.at[slot], sin_g.at[slot], ggs.at[slot], ggr.at[slot], (sib, z)),
            remote(osend_o.at[slot], sin_o.at[slot], oss.at[slot], osr.at[slot], (sib, z)),
        ]

    def finals(g, s, to):
        at = lax.rem(g, fslots)
        rows_copy = []
        if not square:
            rows_copy = [
                remote(
                    fsend.at[at, s - 1], fin.at[g, s - 1], ps.at[g, s - 1], pr.at[g, s - 1], (to, z)
                )
            ]
        return rows_copy + [
            remote(
                fsend_g.at[at, s - 1],
                fin_g.at[g, s - 1],
                pgs.at[g, s - 1],
                pgr.at[g, s - 1],
                (to, z),
            ),
        ]

    def half_copy(g, buf, upper, i, chip):
        first, count = (mid_row, rows - mid_row) if upper else (0, mid_row)
        return remote(
            fsend.at[g, buf, pl.ds(first, count)],
            fin.at[g, buf, pl.ds(first, count)],
            ps.at[g, i],
            pr.at[g, i],
            (2 * chip + core, z),
        )

    def half_copies(g):
        return [
            half_copy(g, 2, False, 0, chip_x),
            half_copy(g, 2, True, 1, chip_y),
            half_copy(g, 0, False, 2, chip_x),
            half_copy(g, 1, True, 3, chip_y),
            half_copy(g, 1, False, 4, chip_y),
            half_copy(g, 0, True, 5, chip_x),
        ]

    def chip_sum(slot, chip, upper):
        first, count = (mid_row, rows - mid_row) if upper else (0, mid_row)
        at = pl.ds(pl.multiple_of(chip * rows + first, 16), count)
        return hold[slot, at, :].astype(f32) + sin[slot, at, :].astype(f32)

    def direct_stage(g):
        slot = lax.rem(g, 2)
        copies = half_copies(g)
        fsend[g, 2, :mid_row] = chip_sum(slot, chip_d, False).astype(bf16)
        copies[0].start()
        fsend[g, 2, mid_row:] = chip_sum(slot, chip_d, True).astype(bf16)
        copies[1].start()
        fsend[g, 0, :mid_row] = chip_sum(slot, chip_x, False).astype(bf16)
        copies[2].start()
        fsend[g, 1, mid_row:] = chip_sum(slot, chip_y, True).astype(bf16)
        copies[3].start()

    def relay_stage(g):
        slot = lax.rem(g, 2)
        copies = half_copies(g)
        copies[0].wait_recv()
        passed = chip_sum(slot, chip_y, False) + fin[g, 2, :mid_row].astype(f32)
        fsend[g, 1, :mid_row] = passed.astype(bf16)
        copies[4].start()
        copies[1].wait_recv()
        passed = chip_sum(slot, chip_x, True) + fin[g, 2, mid_row:].astype(f32)
        fsend[g, 0, mid_row:] = passed.astype(bf16)
        copies[5].start()

    def lasts(k, to):
        return [
            remote(zsend.at[k - 1], zin.at[k - 1], zgs.at[k - 1], zgr.at[k - 1], (e, to)),
            remote(zsend_g.at[k - 1], zin_g.at[k - 1], zggs.at[k - 1], zggr.at[k - 1], (e, to)),
        ]

    def mixed_copy(g, slot):
        return pltpu.make_async_copy(hold_o.at[slot], mixed_hbm.at[piece_of(g)], msem.at[slot])

    def plane_stage(g):
        slot = lax.rem(g, 2)
        for copy in gives(slot)[:2]:
            copy.wait_recv()
        if fslots < nz:

            @pl.when(g >= fslots)
            def _():
                for s in range(1, half):
                    for copy in finals(g - fslots, s, sib):
                        copy.wait_send()

        spot = lax.rem(g, fslots)
        if square:
            direct_stage(g)
        for s in range(1, half):
            h = lax.rem(me + half - s, half)
            at = pl.ds(pl.multiple_of(h * rows, 16), rows)
            if not square:
                fsend[spot, s - 1] = (
                    hold[slot, at, :].astype(f32) + sin[slot, at, :].astype(f32)
                ).astype(bf16)
            fsend_g[spot, s - 1] = (hold_g[slot, h].astype(f32) + sin_g[slot, h].astype(f32)).astype(
                bf16
            )
            for copy in finals(g, s, lax.rem(e - 2 * s + n, n)):
                copy.start()
        own_s[g] = hold[slot, my_rows, :].astype(f32) + sin[slot, my_rows, :].astype(f32)
        own_g[g] = hold_g[slot, me].astype(f32) + sin_g[slot, me].astype(f32)

    def mixed_stage(g):
        slot = lax.rem(g, 2)
        gives(slot)[2].wait_recv()
        hold_o[slot] = (hold_o[slot].astype(f32) + sin_o[slot].astype(f32)).astype(bf16)
        mixed_copy(g, slot).start()

    def tensor_stage(g):
        total = own_s[g]
        total_g = own_g[g]
        for s in range(1, half):
            for copy in finals(g, s, sib):
                copy.wait_recv()
            if not square:
                total = total + fin[g, s - 1].astype(f32)
            total_g = total_g + fin_g[g, s - 1].astype(f32)

        if square:
            for copy in half_copies(g)[2:]:
                copy.wait_recv()
            total = total + fin[g, 0].astype(f32) + fin[g, 1].astype(f32)

        @pl.when(g == 0)
        def _():
            own_s[0] = total
            own_g[0] = total_g

        @pl.when(g > 0)
        def _():
            zsend[g - 1] = total.astype(bf16)
            zsend_g[g - 1] = total_g.astype(bf16)
            for copy in lasts(g, piece_of(g)):
                copy.start()

    def step(g, carry):
        zz = piece_of(g)
        slot = lax.rem(g, 2)

        @pl.when(g < nz - 1)
        def _():
            coming = piece_of(g + 1)
            z_row(coming, g + 1, coming).wait_recv()
            z_small(coming, g + 1, coming).wait_recv()
            push_piece(g + 1)

        if square:
            x_part(zz, chip_d, 0, mid_row, g, 2, chip_y).wait_recv()
            x_part(zz, chip_d, mid_row, rows - mid_row, g, 3, chip_x).wait_recv()

        for s in range(1, half):
            h = lax.rem(me + half - s, half)
            src = 2 * h + core
            if not square:
                x_row(zz, h, g, s, src).wait_recv()
            x_small(zz, h, g, s, src).wait_recv()
        for copy in forward(zz, core, g):
            copy.start()
        cot_start(g, other, 1)
        cot_wait(0)

        @pl.when(g >= 2)
        def _():
            mixed_copy(g - 2, slot).wait()

        block(zz, core, 0, hold, hold_o, hold_g, slot)
        if square:

            @pl.when(g == 0)
            def _():
                for k in range(3, nz):
                    z_push(k)

            @pl.when(g < nz - 1)
            def _():
                relay_pieces(g + 1)


        @pl.when(g < nz - 1)
        def _():
            cot_start(g + 1, core, 0)

        @pl.when(g >= 2)
        def _():
            tensor_stage(g - 2)

        @pl.when(g >= 1)
        def _():
            plane_stage(g - 1)
            mixed_stage(g - 1)

        @pl.when(g >= 2)
        def _():
            for copy in gives(slot):
                copy.wait_send()

        for copy in forward(zz, other, g):
            copy.wait_recv()
        cot_wait(1)
        block(zz, other, 1, osend, osend_o, osend_g, slot)
        for copy in gives(slot):
            copy.start()
        if square:

            @pl.when(g >= 1)
            def _():
                relay_stage(g - 1)

        return carry

    def forward(zz, parity, g):
        ref = xbuf.at[zz, parity]
        small = wbuf.at[zz, parity]
        return (
            remote(ref, ref, fs.at[g], fr.at[g], (sib, z)),
            remote(small, small, wfs.at[g], wfr.at[g], (sib, z)),
        )

    lax.fori_loop(0, nz, step, 0)
    grads = [
        pltpu.make_async_copy(dgate, dgate_hbm, gsem.at[0]),
        pltpu.make_async_copy(dup, dup_hbm, gsem.at[1]),
        pltpu.make_async_copy(ddown, ddown_hbm, gsem.at[2]),
        pltpu.make_async_copy(xbuf.at[:, core, my_rows, :], normed_hbm, gsem.at[3]),
    ]
    plane_stage(jnp.int32(nz - 1))
    for copy in grads:
        copy.start()
    if nz >= 2:
        tensor_stage(jnp.int32(nz - 2))
    if square:
        relay_stage(jnp.int32(nz - 1))

    def total_stats(j, carry):
        for zz in range(nz):
            for parity in range(2):
                carry = carry + wbuf[zz, parity, j, experts:, :].astype(f32)
        return carry

    stats = lax.fori_loop(0, half, total_stats, jnp.zeros((16, 128), f32))
    total_rows = n * tok
    share = stats[0:1, :experts] / (total_rows * top_count)
    load_ref[...] = (
        experts * experts * share * ((stats[1:2, :experts] + stats[2:3, :experts]) / total_rows)
    )
    loss_w = experts * share / total_rows
    mixed_stage(jnp.int32(nz - 1))
    tensor_stage(jnp.int32(nz - 1))

    gate_sums = own_g[0]
    grad_rows = own_s[0]
    for k in range(1, nz):
        for copy in lasts(k, z):
            copy.wait_recv()
        gate_sums = gate_sums + zin_g[k - 1].astype(f32)
        grad_rows = grad_rows + zin[k - 1].astype(f32)
    grow = jnp.concatenate([gate_sums, jnp.zeros((128 - experts, 128), f32)], 0).T
    grad_gates = grow[:rows, :experts]
    grad_logits = comb * (grad_gates - jnp.sum(grad_gates * comb, -1, keepdims=True))
    grad_logits = grad_logits + probs * (loss_w - jnp.sum(loss_w * probs, -1, keepdims=True))
    low_grad = grad_logits.astype(bf16)
    wide_grad = jnp.concatenate([grad_logits, jnp.zeros((rows, 128 - experts), f32)], 1)
    if rows < 128:
        wide_grad = jnp.concatenate([wide_grad, jnp.zeros((128 - rows, 128), f32)], 0)
    glog_ref[...] = wide_grad.T[:experts].astype(bf16)
    grad_rows = grad_rows + dot_nn(low_grad, router_ref[...])
    mid = mid_ref[...]
    ggrad_ref[...] = jnp.sum(grad_rows * mid * scale2, 0, keepdims=True)
    gained = grad_rows * gain_ref[...]
    gmid_ref[...] = (
        cot_ref[own_rows, :]
        + scale2 * gained
        - mid * (scale2 * scale2 * scale2) * jnp.mean(gained * mid, -1, keepdims=True)
    )

    for copy in grads:
        copy.wait()
    for k in range(1, nz):
        z_row(z, k, z).wait_send()
        z_small(z, k, z).wait_send()
        for copy in lasts(k, z):
            copy.wait_send()
    for g in range(max(0, nz - 2), nz):
        mixed_copy(jnp.int32(g), g % 2).wait()
        for copy in gives(g % 2):
            copy.wait_send()

    def drained(g, carry):
        if square:
            x_part(z, me, 0, rows, g, 0, chip_x).wait_send()
            x_part(z, me, 0, rows, g, 1, chip_y).wait_send()
            for copy in relays(g) + tuple(half_copies(g)):
                copy.wait_send()
        for s in range(1, half):
            if not square:
                x_row(z, me, g, s, sib).wait_send()
            x_small(z, me, g, s, sib).wait_send()
        for copy in forward(z, core, g):
            copy.wait_send()
        return carry

    lax.fori_loop(0, nz, drained, 0)

    def sums_sent(g, carry):
        for s in range(1, half):
            for copy in finals(g, s, sib):
                copy.wait_send()
        return carry

    lax.fori_loop(nz - fslots, nz, sums_sent, 0)


def expert_layer(n, nz, mid, gain, router, routes, gate, up, down, cot, cot_all):
    rows, width = mid.shape
    experts = router.shape[1]
    local_experts, _, hid = gate.shape
    inner_w = local_experts * hid
    half = n // 2
    batch = half * rows
    big = n > 8
    fslots = 2 if big else nz
    dma = pltpu.SemaphoreType.DMA
    vmem = pl.BlockSpec(memory_space=pltpu.VMEM)
    hbm = pl.BlockSpec(memory_space=pl.ANY)
    sds = jax.ShapeDtypeStruct
    out_shape = [
        sds((rows, width), f32),
        sds((experts, 128), bf16),
        sds((1, width), f32),
        sds((1, experts), f32),
        sds((local_experts, width, hid), f32),
        sds((local_experts, width, hid), f32),
        sds((inner_w, width), f32),
        sds((nz, batch, width), bf16),
        sds((nz, rows, width), bf16),
    ]
    out_specs = [vmem] * 4 + [hbm] * 5
    scratch = []
    if big:
        out_shape.append(sds((nz, 2, batch, width), bf16))
        out_specs.append(hbm)
        scratch.append(pltpu.VMEM((batch, width), bf16))
    else:
        scratch.append(pltpu.VMEM((nz, 2, batch, width), bf16))
    pair = pltpu.VMEM((2, batch, width), bf16)
    small = pltpu.VMEM((2, half, experts, 128), bf16)
    scratch += [
        pltpu.VMEM((nz, 2, half, experts + 16, 128), bf16),
        pltpu.VMEM((rows, width), bf16),
        pltpu.VMEM((width, inner_w), bf16),
        pltpu.VMEM((width, inner_w), bf16),
        pltpu.VMEM((inner_w, width), bf16),
        pltpu.VMEM((local_experts, width, hid), f32),
        pltpu.VMEM((local_experts, width, hid), f32),
        pltpu.VMEM((inner_w, width), f32),
        pair,
        pltpu.VMEM((batch, inner_w), bf16),
        pltpu.VMEM((batch, inner_w), bf16),
        pltpu.VMEM((batch, inner_w), bf16),
        pair,
        pair,
        pair,
        pair,
        pair,
        pair,
        small,
        small,
        small,
        pltpu.VMEM((nz, rows, width), f32),
        pltpu.VMEM((nz, experts, 128), f32),
        pltpu.VMEM((fslots, half - 1, rows, width), bf16),
        pltpu.VMEM((nz, half - 1, rows, width), bf16),
        pltpu.VMEM((fslots, half - 1, experts, 128), bf16),
        pltpu.VMEM((nz, half - 1, experts, 128), bf16),
        pltpu.VMEM((nz - 1, rows, width), bf16),
        pltpu.VMEM((nz - 1, rows, width), bf16),
        pltpu.VMEM((nz - 1, experts, 128), bf16),
        pltpu.VMEM((nz - 1, experts, 128), bf16),
        dma((3, local_experts)),
        dma((4,)),
        dma((2,)),
        dma((2,)),
        dma,
    ]
    scratch += [dma((nz - 1,))] * 4
    scratch += [dma((nz, half))] * 4
    scratch += [dma((nz,))] * 4
    scratch += [dma((2,))] * 6
    scratch += [dma((nz, 6 if half == 4 else half - 1))] * 2
    scratch += [dma((nz, half - 1))] * 2
    scratch += [dma((nz - 1,))] * 4 + [pltpu.VMEM((nz * rows, 128), f32)]
    return pl.pallas_call(
        functools.partial(expert_kernel, n, nz, big),
        out_shape=out_shape,
        in_specs=[vmem] * 5 + [hbm] * 4,
        out_specs=out_specs,
        scratch_shapes=scratch,
        compiler_params=pltpu.CompilerParams(
            collective_id=1, has_side_effects=True, vmem_limit_bytes=60 << 20
        ),
        name="experts",
    )(mid, gain[None], router.T, routes.T, cot, gate, up, down.reshape(inner_w, width), cot_all)[:9]


def attend_kernel(
    n,
    nz,
    x_ref,
    gain_ref,
    wq_ref,
    wk_ref,
    wv_ref,
    wo_ref,
    cos_ref,
    sin_ref,
    lens_ref,
    mid_ref,
    q_ref,
    kv_ref,
    lrow_ref,
    att_ref,
    wqkv,
    wfull,
    qst_s,
    m_s,
    l_s,
    o_s,
    att_low,
    acol,
    ks,
    kr,
    kfs,
    kfr,
    zgs,
    zgr,
    gos,
    gor,
    gps,
    gpr,
):
    e = lax.axis_index("expert")
    z = lax.axis_index("tensor")
    core = lax.rem(e, 2)
    sib = e + 1 - 2 * core
    half = n // 2
    tok, width = x_ref.shape
    rows = tok // nz
    qw = wq_ref.shape[1]
    kw = wk_ref.shape[1]
    seqs = kv_ref.shape[0]
    span = tok // seqs
    heads = kw // HD
    groups = qw // kw
    barrier = greet(n, nz, e, z, sib)

    wqkv[:, 0:qw] = wq_ref[...]
    wqkv[:, qw : qw + kw] = wk_ref[...]
    wqkv[:, qw + kw :] = wv_ref[...]
    x = x_ref[...].astype(f32)
    scale1 = lax.rsqrt(jnp.mean(x * x, -1, keepdims=True) + EPS)
    normed = (x * scale1 * gain_ref[...]).astype(bf16)
    lin = dot_nn(normed, wqkv[...])
    turned = turn(lin, cos_ref[...], sin_ref[...], qw + kw, True).astype(bf16)
    q_ref[...] = turned[:, :qw]
    for s in range(seqs):
        kv_ref[s, pl.ds(pl.multiple_of(e * span, 16), span)] = turned[
            s * span : (s + 1) * span, qw:
        ]
    pl.semaphore_wait(barrier, half + nz - 1)

    def rows_of(j, s):
        return kv_ref.at[s, pl.ds(pl.multiple_of(j * span, 16), span)]

    half_rows = qw // 2
    my_half = pl.ds(pl.multiple_of(core * half_rows, 16), half_rows)

    def weight_send(k):
        to = (e, lax.rem(z + k, nz))
        return remote(
            wo_ref.at[my_half], wfull.at[z, my_half], gos.at[k - 1], gor.at[k - 1], to
        )

    def weight_copy(zz, k, to):
        ref = wfull.at[zz, my_half]
        return remote(ref, ref, gos.at[k - 1], gor.at[k - 1], (e, to))

    def weight_pass(zz, which, k):
        at = pl.ds(pl.multiple_of(which * half_rows, 16), half_rows)
        ref = wfull.at[zz, at]
        return remote(ref, ref, gps.at[k - 1], gpr.at[k - 1], (sib, z))

    for t in range(1, half):
        to = (lax.rem(e + 2 * t, n), z)
        for s in range(seqs):
            remote(rows_of(e, s), rows_of(e, s), ks.at[t, s], kr.at[t, s], to).start()
    for s in range(seqs):
        remote(rows_of(e, s), rows_of(e, s), kfs.at[0, s], kfr.at[0, s], (sib, z)).start()
    for k in range(1, nz):
        weight_send(k).start()
    wfull[z] = wo_ref[...]

    def forward(t, carry):
        src = lax.rem(e - 2 * t + n, n)
        for s in range(seqs):
            remote(rows_of(src, s), rows_of(src, s), ks.at[t, s], kr.at[t, s], (src, z)).wait_recv()
            remote(rows_of(src, s), rows_of(src, s), kfs.at[t, s], kfr.at[t, s], (sib, z)).start()
        return carry

    lax.fori_loop(1, half, forward, 0)

    def arrive(t, carry):
        src = lax.rem(sib - 2 * t + n, n)
        for s in range(seqs):
            remote(
                rows_of(src, s), rows_of(src, s), kfs.at[t, s], kfr.at[t, s], (sib, z)
            ).wait_recv()
        return carry

    lax.fori_loop(0, half, arrive, 0)

    ck = 2 * span
    last = (e * span + span - 1) // ck
    stacked = groups * span
    qpos = lax.broadcasted_iota(jnp.int32, (stacked, ck), 0)
    qpos = e * span + lax.rem(qpos, span)
    kiota = lax.broadcasted_iota(jnp.int32, (stacked, ck), 1)
    klane = lax.broadcasted_iota(jnp.int32, (1, ck), 1)
    m_s[...] = jnp.full_like(m_s, -1e30)
    l_s[...] = jnp.zeros_like(l_s)
    o_s[...] = jnp.zeros_like(o_s)
    for s in range(seqs):
        for h in range(heads):
            qst_s[s * heads + h] = jnp.concatenate(
                [
                    q_ref[
                        s * span : (s + 1) * span,
                        (h * groups + g) * HD : (h * groups + g + 1) * HD,
                    ]
                    for g in range(groups)
                ],
                0,
            ) * jnp.array(HD ** (-0.5), bf16)

    def chunk(c, diagonal):
        at = pl.ds(pl.multiple_of(c * ck, 16), ck)
        for s in range(seqs):
            for h in range(heads):
                i = s * heads + h
                keys = kv_ref[s, at, h * HD : (h + 1) * HD]
                vals = kv_ref[s, at, kw + h * HD : kw + (h + 1) * HD]
                scores = dot_nt(qst_s[i], keys)
                if diagonal:
                    kpos = kiota + c * ck
                    scores = jnp.where((kpos <= qpos) & (kpos < lens_ref[s]), scores, -1e30)
                else:
                    scores = scores + jnp.where(klane + c * ck < lens_ref[s], 0.0, -1e30)
                old = m_s[i, :, 0:1]
                new = jnp.maximum(old, jnp.max(scores, -1, keepdims=True))
                weights = jnp.exp(scores - new)
                shrink = jnp.exp(old - new)
                m_s[i] = jnp.broadcast_to(new, (stacked, 128))
                l_s[i] = l_s[i] * shrink + jnp.sum(weights, -1, keepdims=True)
                o_s[i] = o_s[i] * shrink + dot_nn(weights.astype(bf16), vals)

    def whole_chunk(c, carry):
        chunk(c, False)
        return carry

    lax.fori_loop(0, last, whole_chunk, 0)
    chunk(last, True)
    for s in range(seqs):
        for h in range(heads):
            i = s * heads + h
            result = o_s[i] / l_s[i, :, 0:HD]
            for g in range(groups):
                cols = slice((h * groups + g) * HD, (h * groups + g + 1) * HD)
                att_ref[s * span : (s + 1) * span, cols] = result[g * span : (g + 1) * span]
            logs = m_s[i] + jnp.log(l_s[i])
            lrow_ref[i] = logs.T[0:8]

    att_low[...] = att_ref[...].astype(bf16)
    own_rows = pl.ds(pl.multiple_of(z * rows, 16), rows)

    def row_copy(k, to):
        src = att_low.at[pl.ds(pl.multiple_of(to * rows, 16), rows)]
        return remote(src, acol.at[z], zgs.at[k - 1], zgr.at[k - 1], (e, to))

    for k in range(1, nz):
        row_copy(k, lax.rem(z + k, nz)).start()
    acol[z] = att_low[own_rows, :]
    for k in range(1, nz):
        zz = lax.rem(z + nz - k, nz)
        weight_copy(zz, k, zz).wait_recv()
        weight_pass(zz, core, k).start()
    for k in range(1, nz):
        row_copy(k, lax.rem(z + nz - k, nz)).wait_recv()
        weight_pass(lax.rem(z + nz - k, nz), 1 - core, k).wait_recv()
    mid = x_ref[own_rows, :].astype(f32)
    for zz in range(nz):
        mid = mid + dot_nn(acol[zz], wfull[zz])
    mid_ref[...] = mid
    for k in range(1, nz):
        row_copy(k, lax.rem(z + k, nz)).wait_send()
        weight_send(k).wait_send()
        weight_pass(lax.rem(z + nz - k, nz), core, k).wait_send()

    def sent(t, carry):
        for s in range(seqs):

            @pl.when(t > 0)
            def _():
                remote(
                    rows_of(e, s), rows_of(e, s), ks.at[t, s], kr.at[t, s], (sib, z)
                ).wait_send()

            remote(rows_of(e, s), rows_of(e, s), kfs.at[t, s], kfr.at[t, s], (sib, z)).wait_send()
        return carry

    lax.fori_loop(0, half, sent, 0)


def attend_layer(n, nz, x, gain, wq, wk, wv, wo, cos, sin, lens):
    tok, width = x.shape
    rows = tok // nz
    qw, kw = wq.shape[1], wk.shape[1]
    seqs = lens.shape[0]
    span = tok // seqs
    half = n // 2
    stacked = (qw // kw) * span
    pairs = seqs * (kw // HD)
    dma = pltpu.SemaphoreType.DMA
    vmem = pl.BlockSpec(memory_space=pltpu.VMEM)
    sds = jax.ShapeDtypeStruct
    return pl.pallas_call(
        functools.partial(attend_kernel, n, nz),
        out_shape=[
            sds((rows, width), f32),
            sds((tok, qw), bf16),
            sds((seqs, n * span, 2 * kw), bf16),
            sds((seqs * (kw // HD), 8, stacked), f32),
            sds((tok, qw), f32),
        ],
        in_specs=[vmem] * 8 + [pl.BlockSpec(memory_space=pltpu.SMEM)],
        out_specs=[vmem] * 5,
        scratch_shapes=[
            pltpu.VMEM((width, qw + 2 * kw), bf16),
            pltpu.VMEM((nz, qw, width), bf16),
            pltpu.VMEM((pairs, stacked, HD), bf16),
            pltpu.VMEM((pairs, stacked, 128), f32),
            pltpu.VMEM((pairs, stacked, 128), f32),
            pltpu.VMEM((pairs, stacked, HD), f32),
            pltpu.VMEM((tok, qw), bf16),
            pltpu.VMEM((nz, rows, qw), bf16),
        ]
        + [dma((half, seqs))] * 4
        + [dma((nz - 1,))] * 6,
        compiler_params=pltpu.CompilerParams(
            collective_id=2, has_side_effects=True, vmem_limit_bytes=60 << 20
        ),
        name="attend",
    )(x, gain[None], wq, wk, wv, wo, cos, sin, lens)


def return_kernel(
    n,
    nz,
    gmid_ref,
    mid_ref,
    glog_ref,
    ggrad_ref,
    xn_ref,
    x_ref,
    gain_ref,
    wq_ref,
    wk_ref,
    wv_ref,
    wo_ref,
    cos_ref,
    sin_ref,
    q_ref,
    kv_ref,
    lrow_ref,
    att_ref,
    lens_ref,
    mixed_hbm,
    obuf,
    igbuf,
    wall,
    wall2,
    small_ref,
    wqkv,
    gat,
    datt,
    dq_s,
    qst_s,
    dst_s,
    acc_q,
    dkv,
    kvo,
    kvi,
    kvf,
    kvr,
    part,
    sums,
    csend,
    crecv,
    osend,
    orecv,
    wbufs,
    wbufs2,
    sz1,
    sz2,
    sown,
    ssib,
    schip,
    ofin,
    zas,
    zar,
    zos,
    zor,
    zis,
    zir,
    zps,
    zpr,
    zqs,
    zqr,
    z1s,
    z1r,
    z2s,
    z2r,
    kos,
    kor,
    kfs,
    kfr,
    wsems,
    wsems2,
    sbs,
    sbr,
    scs,
    scr,
    ofs,
    ofr,
    olsem,
    obase,
):
    e = lax.axis_index("expert")
    z = lax.axis_index("tensor")
    core = lax.rem(e, 2)
    me = e // 2
    sib = e + 1 - 2 * core
    half = n // 2
    rows, width = gmid_ref.shape
    tok = rows * nz
    qw = wq_ref.shape[1]
    kw = wk_ref.shape[1]
    seqs = kv_ref.shape[0]
    span = tok // seqs
    heads = kw // HD
    groups = qw // kw
    dn = width // n
    experts = glog_ref.shape[0]
    own_rows = pl.ds(pl.multiple_of(z * rows, 16), rows)
    barrier = greet(n, nz, e, z, sib)
    w1 = PlaneSum(n, e, z, sib, wall, *wbufs, *wsems)
    w2 = PlaneSum(n, e, z, sib, wall2, *wbufs2, *wsems2)

    gat[own_rows, :] = gmid_ref[...].astype(bf16)
    sz1[z] = glog_ref[...]
    pl.semaphore_wait(barrier, half + nz - 1)

    def part_of(ref):
        return lambda zz: ref.at[pl.ds(pl.multiple_of(zz * rows, 16), rows)]

    def slot_of(ref):
        return lambda zz: ref.at[zz]

    gat_line = Line(z, nz, e, part_of(gat), zas, zar)
    out_line = Line(z, nz, e, part_of(obuf), zos, zor)
    igrad_line = Line(z, nz, e, part_of(igbuf), zis, zir)
    normed_sum = LineSum(z, nz, e, csend, crecv, zps, zpr)

    def z_copies(buf_of, send, recv):
        return [
            remote(
                buf_of(z), buf_of(z), send.at[k - 1], recv.at[k - 1], (e, lax.rem(z + k, nz))
            )
            for k in range(1, nz)
        ]

    def z_arrivals(buf_of, send, recv):
        return [
            remote(
                buf_of(lax.rem(z + nz - k, nz)),
                buf_of(lax.rem(z + nz - k, nz)),
                send.at[k - 1],
                recv.at[k - 1],
                (e, lax.rem(z + nz - k, nz)),
            )
            for k in range(1, nz)
        ]

    gat_line.start()
    for copy in z_copies(slot_of(sz1), z1s, z1r):
        copy.start()

    square = half == 4
    chip_x = me + 1 - 2 * lax.rem(me, 2)
    chip_y = lax.rem(me + 2, 4)
    chip_d = 3 - me
    low, high = pl.ds(0, nz // 2), pl.ds(nz // 2, nz - nz // 2)

    def mixed_at(chip, which=slice(None)):
        return mixed_hbm.at[which, pl.ds(pl.multiple_of(chip * rows, 16), rows), :]

    def mixed_copy(src, dst, i, chip):
        return remote(src, dst, ofs.at[i], ofr.at[i], (2 * chip + core, z))

    def mixed_sends():
        if not square:
            return [
                mixed_copy(
                    mixed_at(lax.rem(me + half - t, half)),
                    ofin.at[t],
                    t - 1,
                    lax.rem(me + half - t, half),
                )
                for t in range(1, half)
            ]
        return [
            mixed_copy(mixed_at(chip_d, low), ofin.at[3, low], 0, chip_x),
            mixed_copy(mixed_at(chip_d, high), ofin.at[3, high], 1, chip_y),
            mixed_copy(mixed_at(chip_x, low), ofin.at[1, low], 2, chip_x),
            mixed_copy(mixed_at(chip_y, high), ofin.at[2, high], 3, chip_y),
        ]

    def mixed_relays():
        return [
            mixed_copy(obase.at[low], ofin.at[2, low], 4, chip_y),
            mixed_copy(obase.at[high], ofin.at[1, high], 5, chip_x),
        ]

    for copy in mixed_sends():
        copy.start()
    mixed_own = [pltpu.make_async_copy(mixed_at(me), ofin.at[0], olsem.at[0])]
    if square:
        mixed_own += [
            pltpu.make_async_copy(mixed_at(chip_y, low), obase.at[low], olsem.at[1]),
            pltpu.make_async_copy(mixed_at(chip_x, high), obase.at[high], olsem.at[2]),
        ]
    for copy in mixed_own:
        copy.start()

    def mixed_relay():
        waits = mixed_sends()
        for copy, part, i in zip(mixed_relays(), (low, high), (0, 1)):
            waits[i].wait_recv()
            obase[part] = (obase[part].astype(f32) + ofin[3, part].astype(f32)).astype(bf16)
            copy.start()

    mixed_count = 3 if square else half

    def mixed_sum(zz):
        total = ofin[0, zz].astype(f32)
        for t in range(1, mixed_count):
            total = total + ofin[t, zz].astype(f32)
        return total

    wqkv[:, 0:qw] = wq_ref[...]
    wqkv[:, qw : qw + kw] = wk_ref[...]
    wqkv[:, qw + kw :] = wv_ref[...]
    x = x_ref[...].astype(f32)
    scale1 = lax.rsqrt(jnp.mean(x * x, -1, keepdims=True) + EPS)
    normed = (x * scale1 * gain_ref[...]).astype(bf16)
    dkv[...] = jnp.zeros_like(dkv)

    for hop in range(1, nz):
        gat_line.hop(hop)
    datt[...] = dot_nt(gat[...], wo_ref[...]).astype(bf16)

    ck = 2 * span
    last = (e * span + span - 1) // ck
    stacked = groups * span
    kiota = lax.broadcasted_iota(jnp.int32, (ck, stacked), 0)
    krow = lax.broadcasted_iota(jnp.int32, (ck, 1), 0)
    qpos = e * span + lax.rem(lax.broadcasted_iota(jnp.int32, (ck, stacked), 1), span)
    drows = []
    for s in range(seqs):
        for h in range(heads):

            def gather(ref):
                return jnp.concatenate(
                    [
                        ref[
                            s * span : (s + 1) * span,
                            (h * groups + g) * HD : (h * groups + g + 1) * HD,
                        ]
                        for g in range(groups)
                    ],
                    0,
                )

            i = s * heads + h
            qst_s[i] = gather(q_ref) * jnp.array(HD ** (-0.5), bf16)
            dst = gather(datt)
            dst_s[i] = dst
            delta = jnp.sum(dst.astype(f32) * gather(att_ref), -1, keepdims=True)
            drows.append(jnp.broadcast_to(delta, (stacked, 128)).T[0:1])
    acc_q[...] = jnp.zeros_like(acc_q)
    for copy in mixed_own:
        copy.wait()
    if square:
        mixed_relay()

    def chunk(c, diagonal):
        at = pl.ds(pl.multiple_of(c * ck, 16), ck)
        for s in range(seqs):
            for h in range(heads):
                i = s * heads + h
                keys = kv_ref[s, at, h * HD : (h + 1) * HD]
                vals = kv_ref[s, at, kw + h * HD : kw + (h + 1) * HD]
                scores = dot_nt(keys, qst_s[i]) - lrow_ref[i, 0:1, :]
                if diagonal:
                    kpos = kiota + c * ck
                    allowed = (kpos <= qpos) & (kpos < lens_ref[s])
                    soft = jnp.where(allowed, jnp.exp(scores), 0.0)
                else:
                    soft = jnp.exp(scores + jnp.where(krow + c * ck < lens_ref[s], 0.0, -1e30))
                grad_probs = dot_nt(vals, dst_s[i])
                grad_scores = (soft * (grad_probs - drows[i])).astype(bf16)
                dkv[s, at, h * HD : (h + 1) * HD] = dot_nn(grad_scores, qst_s[i])
                dkv[s, at, kw + h * HD : kw + (h + 1) * HD] = dot_nn(soft.astype(bf16), dst_s[i])
                acc_q[i] += dot_tn(grad_scores, keys)

    def whole_chunk(c, carry):
        chunk(c, False)
        return carry

    lax.fori_loop(0, last, whole_chunk, 0)
    chunk(last, True)
    for s in range(seqs):
        for h in range(heads):
            result = acc_q[s * heads + h] * HD ** (-0.5)
            for g in range(groups):
                cols = slice((h * groups + g) * HD, (h * groups + g + 1) * HD)
                dq_s[s * span : (s + 1) * span, cols] = result[g * span : (g + 1) * span]

    def key_rows(j, s):
        return dkv[s, pl.ds(pl.multiple_of(j * span, 16), span), :]

    def key_send(t):
        return remote(kvo.at[t], kvi.at[t], kos.at[t], kor.at[t], (sib, z))

    def key_final(t):
        to = (lax.rem(e - 2 * t + n, n), z)
        return remote(kvf.at[t - 1], kvr.at[t - 1], kfs.at[t - 1], kfr.at[t - 1], to)

    def key_give(i, carry):
        t = half - 1 - i
        oth = lax.rem(sib - 2 * t + n, n)
        for s in range(seqs):
            kvo[t, s] = key_rows(oth, s).astype(bf16)
        key_send(t).start()
        return carry

    lax.fori_loop(0, half, key_give, 0)

    def key_pass(i, carry):
        t = half - 1 - i
        key_send(t).wait_recv()
        own = lax.rem(e - 2 * t + n, n)
        for s in range(seqs):
            kvf[t - 1, s] = (key_rows(own, s) + kvi[t, s].astype(f32)).astype(bf16)
        key_final(t).start()
        return carry

    cos, sin = cos_ref[...], sin_ref[...]
    gq = turn(dq_s[...], cos, sin, qw, False).astype(bf16)
    query_part = dot_tn(normed, gq)
    out_part = dot_tn(gat[...], att_ref[...].astype(bf16))
    for j in range(n):
        w1.pack[j, :, :qw] = query_part[j * dn : (j + 1) * dn].astype(bf16)
        w1.pack[j, :, qw:] = out_part[j * dn : (j + 1) * dn].astype(bf16)
    lax.fori_loop(0, half - 1, key_pass, 0)
    w1.give()

    def mixed_last(k, to):
        return remote(osend.at[k - 1], orecv.at[k - 1], zqs.at[k - 1], zqr.at[k - 1], (e, to))

    for copy in mixed_sends()[2:] + mixed_relays() if square else mixed_sends():
        copy.wait_recv()
    for k in range(1, nz):
        zz = lax.rem(z + k, nz)
        osend[k - 1] = mixed_sum(zz).astype(bf16)
        mixed_last(k, zz).start()
    own_mixed = mid_ref[...] + mixed_sum(z)
    w1.spread()
    for copy in z_arrivals(slot_of(sz1), z1s, z1r):
        copy.wait_recv()
    rgrad = dot_nn(sz1[0][:, :rows], xn_ref[0])
    for zz in range(1, nz):
        rgrad = rgrad + dot_nn(sz1[zz][:, :rows], xn_ref[zz])
    sown[0:experts, :] = rgrad.astype(bf16)

    key_send(0).wait_recv()
    own_kv = [key_rows(e, s) + kvi[0, s].astype(f32) for s in range(seqs)]
    for t in range(1, half):
        key_final(t).wait_recv()
        for s in range(seqs):
            own_kv[s] = own_kv[s] + kvr[t - 1, s].astype(f32)
    gkv = turn(jnp.concatenate(own_kv, 0), cos, sin, kw, False).astype(bf16)
    part[...] = dot_nt(gq, wqkv[:, :qw]) + dot_nt(gkv, wqkv[:, qw:])

    def normed_part(zz):
        return part[pl.ds(pl.multiple_of(zz * rows, 16), rows), :]

    for hop in range(nz - 1):
        normed_sum.hop(hop, normed_part)
        if hop > 0:
            out_line.hop(hop)
        if hop == 0:
            for k in range(1, nz):
                mixed_last(k, z).wait_recv()
                own_mixed = own_mixed + orecv[k - 1].astype(f32)
            obuf[own_rows, :] = own_mixed.astype(bf16)
            out_line.start()
            again = jnp.sum(part[...] * x * scale1, 0, keepdims=True)
            sz2[z] = jnp.concatenate([again, ggrad_ref[...], jnp.zeros((14, width), f32)], 0).astype(
                bf16
            )
            for copy in z_copies(slot_of(sz2), z2s, z2r):
                copy.start()
            pair_part = dot_tn(normed, gkv)
            for j in range(n):
                w2.pack[j] = pair_part[j * dn : (j + 1) * dn].astype(bf16)
            w2.give()
            w1.total()
    w2.spread()
    normed_sum.total(sums, normed_part)

    own_x = x_ref[own_rows, :].astype(f32)
    own_scale = lax.rsqrt(jnp.mean(own_x * own_x, -1, keepdims=True) + EPS)
    grad_normed = sums[...]
    gained = grad_normed * gain_ref[...]
    igrad = (
        gmid_ref[...]
        + own_scale * gained
        - own_x
        * (own_scale * own_scale * own_scale)
        * jnp.mean(gained * own_x, -1, keepdims=True)
    )
    igbuf[own_rows, :] = igrad.astype(bf16)
    igrad_line.start()
    out_line.hop(nz - 1)

    w1.forward()
    for copy in z_arrivals(slot_of(sz2), z2s, z2r):
        copy.wait_recv()
    second = sz2[0].astype(f32)
    for zz in range(1, nz):
        second = second + sz2[zz].astype(f32)
    sown[experts:, :] = second.astype(bf16)
    small_sib = remote(sown, ssib, sbs, sbr, (sib, z))
    small_sib.start()
    if nz > 2:
        igrad_line.hop(1)
    small_sib.wait_recv()
    schip[me] = (sown[...].astype(f32) + ssib[...].astype(f32)).astype(bf16)

    def small_send(t):
        to = (lax.rem(e + 2 * t, n), z)
        return remote(schip.at[me], schip.at[me], scs.at[t - 1], scr.at[t - 1], to)

    for t in range(1, half):
        small_send(t).start()

    w2.total()
    for hop in range(2, nz - 1):
        igrad_line.hop(hop)
    igrad_line.hop(nz - 1)

    w2.forward()
    for t in range(1, half):
        src = lax.rem(me + half - t, half)
        remote(
            schip.at[src], schip.at[src], scs.at[t - 1], scr.at[t - 1], (sib, z)
        ).wait_recv()
    small = schip[0].astype(f32)
    for t in range(1, half):
        small = small + schip[t].astype(f32)
    small_ref[...] = small

    w1.arrive()
    w2.arrive()
    for k in range(1, nz):
        mixed_last(k, z).wait_send()
    for line in (gat_line, out_line, igrad_line, normed_sum, w1, w2):
        line.drain()
    for copy in z_copies(slot_of(sz1), z1s, z1r) + z_copies(slot_of(sz2), z2s, z2r):
        copy.wait_send()
    small_sib.wait_send()
    for copy in mixed_sends() + (mixed_relays() if square else []):
        copy.wait_send()

    def drained(t, carry):
        key_send(t).wait_send()

        @pl.when(t > 0)
        def _():
            key_final(t).wait_send()
            small_send(t).wait_send()

        return carry

    lax.fori_loop(0, half, drained, 0)


class PlaneSum:
    def __init__(self, n, e, z, sib, wall, pack, near, send, recv, *sems):
        self.n, self.e, self.z, self.sib, self.half = n, e, z, sib, n // 2
        self.wall, self.pack, self.near, self.send, self.recv = wall, pack, near, send, recv
        self.sems = sems

    def peer(self, base, t):
        return lax.rem(base - 2 * t + self.n, self.n)

    def near_copy(self, t):
        src = self.pack.at[self.peer(self.sib, t)]
        return remote(
            src, self.near.at[t], self.sems[0].at[t], self.sems[1].at[t], (self.sib, self.z)
        )

    def far_copy(self, t):
        return remote(
            self.send.at[t - 1],
            self.recv.at[t - 1],
            self.sems[2].at[t],
            self.sems[3].at[t],
            (self.peer(self.e, t), self.z),
        )

    def all_copy(self, src, t, to):
        ref = self.wall.at[src]
        return remote(ref, ref, self.sems[4].at[t], self.sems[5].at[t], (to, self.z))

    def pass_copy(self, src, t):
        ref = self.wall.at[src]
        return remote(ref, ref, self.sems[6].at[t], self.sems[7].at[t], (self.sib, self.z))

    def give(self):
        def one(i, carry):
            self.near_copy(self.half - 1 - i).start()
            return carry

        lax.fori_loop(0, self.half, one, 0)

    def spread(self):
        def one(i, carry):
            t = self.half - 1 - i
            self.near_copy(t).wait_recv()
            own = self.pack[self.peer(self.e, t)].astype(f32)
            self.send[t - 1] = (own + self.near[t].astype(f32)).astype(bf16)
            self.far_copy(t).start()
            return carry

        lax.fori_loop(0, self.half - 1, one, 0)

    def total(self):
        self.near_copy(0).wait_recv()
        total = self.pack[self.e].astype(f32) + self.near[0].astype(f32)
        for t in range(1, self.half):
            self.far_copy(t).wait_recv()
            total = total + self.recv[t - 1].astype(f32)
        self.wall[self.e] = total.astype(bf16)
        for t in range(1, self.half):
            self.all_copy(self.e, t, lax.rem(self.e + 2 * t, self.n)).start()
        self.pass_copy(self.e, 0).start()

    def forward(self):
        def one(t, carry):
            src = self.peer(self.e, t)
            self.all_copy(src, t, src).wait_recv()
            self.pass_copy(src, t).start()
            return carry

        lax.fori_loop(1, self.half, one, 0)

    def arrive(self):
        def one(t, carry):
            self.pass_copy(self.peer(self.sib, t), t).wait_recv()
            return carry

        lax.fori_loop(0, self.half, one, 0)

    def drain(self):
        def one(t, carry):
            self.near_copy(t).wait_send()
            self.pass_copy(self.e, t).wait_send()

            @pl.when(t > 0)
            def _():
                self.far_copy(t).wait_send()
                self.all_copy(self.e, t, self.sib).wait_send()

            return carry

        lax.fori_loop(0, self.half, one, 0)


class Line:
    def __init__(self, z, nz, e, buf_of, send, recv):
        self.z, self.nz, self.e = z, nz, e
        self.buf_of, self.send, self.recv = buf_of, send, recv

    def copy(self, way, piece):
        to = self.z + 1 if way == 0 else self.z - 1
        ref = self.buf_of(piece)
        return remote(ref, ref, self.send.at[way, piece], self.recv.at[way, piece], (self.e, to))

    def push(self, piece, ways=(0, 1)):
        for way in ways:

            @pl.when(self.z < self.nz - 1 if way == 0 else self.z > 0)
            def _():
                self.copy(way, piece).start()

    def start(self):
        self.push(self.z)

    def hop(self, i):
        @pl.when(self.z >= i)
        def _():
            self.copy(0, self.z - i).wait_recv()
            self.push(self.z - i, (0,))

        @pl.when(self.z + i <= self.nz - 1)
        def _():
            self.copy(1, self.z + i).wait_recv()
            self.push(self.z + i, (1,))

    def drain(self):
        for piece in range(self.nz):

            @pl.when((self.z >= piece) & (self.z < self.nz - 1))
            def _():
                self.copy(0, piece).wait_send()

            @pl.when((self.z <= piece) & (self.z > 0))
            def _():
                self.copy(1, piece).wait_send()


class LineSum:
    def __init__(self, z, nz, e, send_buf, recv_buf, send, recv):
        self.z, self.nz, self.e = z, nz, e
        self.send_buf, self.recv_buf, self.send, self.recv = send_buf, recv_buf, send, recv

    def copy(self, way, target):
        to = self.z + 1 if way == 0 else self.z - 1
        return remote(
            self.send_buf.at[way, target],
            self.recv_buf.at[way, target],
            self.send.at[way, target],
            self.recv.at[way, target],
            (self.e, to),
        )

    def hop(self, i, own_of):
        for way, target in ((0, self.nz - 1 - i), (1, i)):
            passes = self.z < target if way == 0 else self.z > target
            first = self.z == 0 if way == 0 else self.z == self.nz - 1
            inner = self.z > 0 if way == 0 else self.z < self.nz - 1

            @pl.when(passes & first)
            def _():
                self.send_buf[way, target] = own_of(target).astype(bf16)
                self.copy(way, target).start()

            @pl.when(passes & inner)
            def _():
                self.copy(way, target).wait_recv()
                self.send_buf[way, target] = (
                    own_of(target) + self.recv_buf[way, target].astype(f32)
                ).astype(bf16)
                self.copy(way, target).start()

    def total(self, ref, own_of):
        ref[...] = own_of(self.z)

        @pl.when(self.z > 0)
        def _():
            self.copy(0, self.z).wait_recv()
            ref[...] += self.recv_buf[0, self.z].astype(f32)

        @pl.when(self.z < self.nz - 1)
        def _():
            self.copy(1, self.z).wait_recv()
            ref[...] += self.recv_buf[1, self.z].astype(f32)

    def drain(self):
        for target in range(self.nz):

            @pl.when(self.z < target)
            def _():
                self.copy(0, target).wait_send()

            @pl.when(self.z > target)
            def _():
                self.copy(1, target).wait_send()


def return_layer(
    n, nz, gmid, mid, glog, ggrad, xn, x, gain, wq, wk, wv, wo, cos, sin, q, kv, lrow, att, lens, mixed
):
    tok, width = x.shape
    rows = tok // nz
    qw, kw = wq.shape[1], wk.shape[1]
    seqs = lens.shape[0]
    span = tok // seqs
    half = n // 2
    stacked = (qw // kw) * span
    pairs = seqs * (kw // HD)
    experts = glog.shape[0]
    small_rows = experts + 16
    dma = pltpu.SemaphoreType.DMA
    vmem = pl.BlockSpec(memory_space=pltpu.VMEM)
    sds = jax.ShapeDtypeStruct
    zdma = dma((nz - 1,))
    line = dma((2, nz))
    hdma = dma((half,))
    fdma = dma((half - 1,))
    def plane_bufs(cols):
        return [
            pltpu.VMEM((n, width // n, cols), bf16),
            pltpu.VMEM((half, width // n, cols), bf16),
            pltpu.VMEM((half - 1, width // n, cols), bf16),
            pltpu.VMEM((half - 1, width // n, cols), bf16),
        ]

    line_buf = pltpu.VMEM((2, nz, rows, width), bf16)
    return pl.pallas_call(
        functools.partial(return_kernel, n, nz),
        out_shape=[
            sds((tok, width), bf16),
            sds((tok, width), bf16),
            sds((n, width // n, 2 * qw), bf16),
            sds((n, width // n, 2 * kw), bf16),
            sds((small_rows, width), f32),
        ],
        in_specs=[vmem] * 17
        + [pl.BlockSpec(memory_space=pltpu.SMEM), pl.BlockSpec(memory_space=pl.ANY)],
        out_specs=[vmem] * 5,
        scratch_shapes=[
            pltpu.VMEM((width, qw + 2 * kw), bf16),
            pltpu.VMEM((tok, width), bf16),
            pltpu.VMEM((tok, qw), bf16),
            pltpu.VMEM((tok, qw), f32),
            pltpu.VMEM((pairs, stacked, HD), bf16),
            pltpu.VMEM((pairs, stacked, HD), bf16),
            pltpu.VMEM((pairs, stacked, HD), f32),
            pltpu.VMEM((seqs, n * span, 2 * kw), f32),
            pltpu.VMEM((half, seqs, span, 2 * kw), bf16),
            pltpu.VMEM((half, seqs, span, 2 * kw), bf16),
            pltpu.VMEM((half - 1, seqs, span, 2 * kw), bf16),
            pltpu.VMEM((half - 1, seqs, span, 2 * kw), bf16),
            pltpu.VMEM((tok, width), f32),
            pltpu.VMEM((rows, width), f32),
            line_buf,
            line_buf,
            pltpu.VMEM((nz - 1, rows, width), bf16),
            pltpu.VMEM((nz - 1, rows, width), bf16),
            plane_bufs(2 * qw),
            plane_bufs(2 * kw),
            pltpu.VMEM((nz, experts, 128), bf16),
            pltpu.VMEM((nz, 16, width), bf16),
            pltpu.VMEM((small_rows, width), bf16),
            pltpu.VMEM((small_rows, width), bf16),
            pltpu.VMEM((half, small_rows, width), bf16),
            pltpu.VMEM((half, nz, rows, width), bf16),
        ]
        + [line] * 8
        + [zdma] * 6
        + [hdma, hdma, fdma, fdma]
        + [[hdma] * 8, [hdma] * 8]
        + [dma, dma, fdma, fdma]
        + [dma((6 if half == 4 else half - 1,))] * 2
        + [dma((3,)), pltpu.VMEM((nz, rows, width), bf16)],
        compiler_params=pltpu.CompilerParams(
            collective_id=3, has_side_effects=True, vmem_limit_bytes=58 << 20
        ),
        name="attend_back",
    )(
        gmid,
        mid,
        glog,
        ggrad,
        xn,
        x,
        gain[None],
        wq,
        wk,
        wv,
        wo,
        cos,
        sin,
        q,
        kv,
        lrow,
        att,
        lens,
        mixed,
    )


def finish_kernel(
    out_low,
    igrad_low,
    wall,
    wall2,
    small,
    load,
    dgate_in,
    dup_in,
    ddown_in,
    out_ref,
    igrad_ref,
    q_ref,
    k_ref,
    v_ref,
    o_ref,
    router_ref,
    again_ref,
    egain_ref,
    loss_ref,
    load_ref,
    dgate,
    dup,
    ddown,
    dgate_s,
    dup_s,
    ddown_s,
    sems,
):
    pairs = ((dgate_in, dgate_s, dgate), (dup_in, dup_s, dup), (ddown_in, ddown_s, ddown))
    reads = [pltpu.make_async_copy(p[0], p[1], sems.at[0, i]) for i, p in enumerate(pairs)]
    writes = [pltpu.make_async_copy(p[1], p[2], sems.at[1, i]) for i, p in enumerate(pairs)]
    for copy in reads:
        copy.start()
    qw, kw = q_ref.shape[1], k_ref.shape[1]
    experts = load.shape[1]
    out_ref[...] = out_low[...].astype(f32)
    for read, write in zip(reads, writes):
        read.wait()
        write.start()
    igrad_ref[...] = igrad_low[...].astype(f32)
    chunks, dn, _ = wall.shape
    flat = wall[...].reshape(chunks * dn, 2 * qw).astype(f32)
    q_ref[...] = flat[:, :qw]
    o_ref[...] = flat[:, qw:].T
    flat = wall2[...].reshape(chunks * dn, 2 * kw).astype(f32)
    k_ref[...] = flat[:, :kw]
    v_ref[...] = flat[:, kw:]
    router_ref[...] = small[0:experts, :]
    again_ref[...] = small[experts : experts + 1, :]
    egain_ref[...] = small[experts + 1 : experts + 2, :]
    load_ref[...] = load[...]
    loss_ref[...] = jnp.mean(load[...], -1, keepdims=True)
    for copy in writes:
        copy.wait()


def finish_layer(out_low, igrad_low, wall, wall2, small, load, dgate, dup, ddown, qw, kw):
    tok, width = out_low.shape
    experts = load.shape[1]
    vmem = pl.BlockSpec(memory_space=pltpu.VMEM)
    hbm = pl.BlockSpec(memory_space=pl.ANY)
    sds = jax.ShapeDtypeStruct
    return pl.pallas_call(
        finish_kernel,
        out_shape=[
            sds((tok, width), f32),
            sds((tok, width), f32),
            sds((width, qw), f32),
            sds((width, kw), f32),
            sds((width, kw), f32),
            sds((qw, width), f32),
            sds((experts, width), f32),
            sds((1, width), f32),
            sds((1, width), f32),
            sds((1, 1), f32),
            sds((1, experts), f32),
            sds(dgate.shape, f32),
            sds(dup.shape, f32),
            sds(ddown.shape, f32),
        ],
        in_specs=[vmem] * 6 + [hbm] * 3,
        out_specs=[vmem] * 11 + [hbm] * 3,
        scratch_shapes=[
            pltpu.VMEM(dgate.shape, f32),
            pltpu.VMEM(dup.shape, f32),
            pltpu.VMEM(ddown.shape, f32),
            pltpu.SemaphoreType.DMA((2, 3)),
        ],
        compiler_params=pltpu.CompilerParams(vmem_limit_bytes=60 << 20),
        name="finish",
    )(out_low, igrad_low, wall, wall2, small, load, dgate, dup, ddown)


def shards(
    inputs,
    attention_gain,
    query_weight,
    key_weight,
    value_weight,
    out_weight,
    expert_gain,
    router_weight,
    gate_weight,
    up_weight,
    down_weight,
    routes,
    seq_lens,
    cotangent,
):
    n = lax.axis_size("expert")
    nz = lax.axis_size("tensor")
    tok_rows = inputs.shape[0]
    seq_count = seq_lens.shape[0]
    span_rows = tok_rows // seq_count
    row = lax.broadcasted_iota(jnp.int32, (tok_rows, 128), 0) % span_rows
    lane = lax.broadcasted_iota(jnp.int32, (tok_rows, 128), 1) % (HD // 2)
    frequency = THETA ** (-2.0 * lane.astype(f32) / HD)
    angles = (lax.axis_index("expert") * span_rows + row).astype(f32) * frequency
    cosines = jnp.cos(angles)
    sines = jnp.sin(angles)
    cot_all = lax.all_gather(cotangent.astype(bf16), "expert", axis=0, tiled=True)
    weights = (query_weight, key_weight, value_weight, out_weight, cosines, sines)
    middle, queries, pairs, logs, attended = attend_layer(
        n, nz, inputs, attention_gain, *weights, seq_lens
    )
    (
        grad_middle,
        logit_grads,
        expert_gain_part,
        expert_load,
        gate_grad,
        up_grad,
        down_grad,
        mixed,
        normed2,
    ) = expert_layer(
        n,
        nz,
        middle,
        expert_gain,
        router_weight,
        routes,
        gate_weight,
        up_weight,
        down_weight,
        cotangent,
        cot_all,
    )
    out_low, igrad_low, packed, packed2, small = return_layer(
        n,
        nz,
        grad_middle,
        middle,
        logit_grads,
        expert_gain_part,
        normed2,
        inputs,
        attention_gain,
        *weights,
        queries,
        pairs,
        logs,
        attended,
        seq_lens,
        mixed,
    )
    (
        output,
        input_grad,
        query_grad,
        key_grad,
        value_grad,
        out_weight_grad,
        router_grad,
        attention_gain_grad,
        expert_gain_grad,
        balance_loss,
        expert_load,
        gate_grad,
        up_grad,
        down_grad,
    ) = finish_layer(
        out_low,
        igrad_low,
        packed,
        packed2,
        small,
        expert_load,
        gate_grad,
        up_grad,
        down_grad,
        query_weight.shape[1],
        key_weight.shape[1],
    )
    return (
        output,
        input_grad,
        balance_loss[0, 0],
        expert_load[0],
        attention_gain_grad[0],
        query_grad,
        key_grad,
        value_grad,
        out_weight_grad,
        expert_gain_grad[0],
        router_grad.T,
        gate_grad,
        up_grad,
        down_grad.reshape(down_weight.shape),
    )


def solution(mesh):
    placed = (
        P("expert", None),
        P(),
        P(None, "tensor"),
        P(None, "tensor"),
        P(None, "tensor"),
        P("tensor", None),
        P(),
        P(),
        P("expert", None, "tensor"),
        P("expert", None, "tensor"),
        P("expert", "tensor", None),
        P("expert", None),
        P(),
        P("expert", None),
    )
    return jax.shard_map(
        shards,
        mesh=mesh,
        in_specs=placed,
        out_specs=(
            P("expert", None),
            P("expert", None),
            P(),
            P(),
            P(),
            P(None, "tensor"),
            P(None, "tensor"),
            P(None, "tensor"),
            P("tensor", None),
            P(),
            P(),
            P("expert", None, "tensor"),
            P("expert", None, "tensor"),
            P("expert", "tensor", None),
        ),
        check_vma=False,
    )
```

```python
import functools

import jax
import jax.numpy as jnp
from jax import lax
from jax.experimental import pallas as pl
from jax.experimental.pallas import tpu as pltpu
from jax.sharding import PartitionSpec as P

HD = 64
EPS = 1e-06
THETA = 10000.0
MESH = pl.DeviceIdType.MESH
f32 = jnp.float32
bf16 = jnp.bfloat16


def dot_nn(left, right):
    return lax.dot_general(left, right, (((1,), (0,)), ((), ())), preferred_element_type=f32)


def dot_nt(left, right):
    return lax.dot_general(left, right, (((1,), (1,)), ((), ())), preferred_element_type=f32)


def dot_tn(left, right):
    return lax.dot_general(left, right, (((0,), (0,)), ((), ())), preferred_element_type=f32)


def remote(src, dst, send_sem, recv_sem, device):
    return pltpu.make_async_remote_copy(
        src_ref=src,
        dst_ref=dst,
        send_sem=send_sem,
        recv_sem=recv_sem,
        device_id=device,
        device_id_type=MESH,
    )


def turn(values, cos, sin, last, forward):
    lane = lax.broadcasted_iota(jnp.int32, (values.shape[0], 128), 1)
    first_half = lax.rem(lane, HD) < HD // 2
    parts = []
    for g in range(values.shape[1] // 128):
        v = values[:, g * 128 : (g + 1) * 128]
        if g * 128 >= last:
            parts.append(v)
            continue
        turned = jnp.where(
            first_half, -pltpu.roll(v, 128 - HD // 2, 1), pltpu.roll(v, HD // 2, 1)
        )
        new = v * cos + turned * sin if forward else v * cos - turned * sin
        if (g + 1) * 128 > last:
            new = jnp.where(lane + g * 128 < last, new, v)
        parts.append(new)
    return jnp.concatenate(parts, 1) if len(parts) > 1 else parts[0]


def greet(n, nz, e, z, sib):
    barrier = pltpu.get_barrier_semaphore()
    pl.semaphore_signal(barrier, inc=1, device_id=(sib, z), device_id_type=MESH)
    for s in range(1, n // 2):
        pl.semaphore_signal(
            barrier, inc=1, device_id=(lax.rem(e + 2 * s, n), z), device_id_type=MESH
        )
    for k in range(1, nz):
        pl.semaphore_signal(barrier, inc=1, device_id=(e, lax.rem(z + k, nz)), device_id_type=MESH)
    return barrier


def expert_kernel(
    n,
    nz,
    big,
    mid_ref,
    gain_ref,
    router_ref,
    routes_ref,
    cot_ref,
    gate_hbm,
    up_hbm,
    down_hbm,
    cot_all,
    *rest,
):
    outs, rest = rest[:9], rest[9:]
    gmid_ref, glog_ref, ggrad_ref, load_ref = outs[:4]
    dgate_hbm, dup_hbm, ddown_hbm, mixed_hbm, normed_hbm = outs[4:]
    xbuf, rest = rest[0], rest[1:]
    if big:
        xstage, rest = rest[0], rest[1:]
    (
        wbuf,
        xn_s,
        wg,
        wu,
        down_ref,
        dgate,
        dup,
        ddown,
        cbuf,
        dg_s,
        du_s,
        wi_s,
        hold,
        osend,
        sin,
        hold_o,
        osend_o,
        sin_o,
        hold_g,
        osend_g,
        sin_g,
        own_s,
        own_g,
        fsend,
        fin,
        fsend_g,
        fin_g,
        zsend,
        zin,
        zsend_g,
        zin_g,
        wsem,
        gsem,
        csem,
        msem,
        lsem,
        zs,
        zr,
        zws,
        zwr,
        xs,
        xr,
        ws,
        wr,
        fs,
        fr,
        wfs,
        wfr,
        gs,
        gr,
        oss,
        osr,
        ggs,
        ggr,
        ps,
        pr,
        pgs,
        pgr,
        zgs,
        zgr,
        zggs,
        zggr,
        picks_s,
    ) = rest
    e = lax.axis_index("expert")
    z = lax.axis_index("tensor")
    core = lax.rem(e, 2)
    other = 1 - core
    me = e // 2
    sib = e + 1 - 2 * core
    half = n // 2
    rows, width = mid_ref.shape
    tok = rows * nz
    experts = router_ref.shape[0]
    local_experts, _, hid = gate_hbm.shape
    inner_w = local_experts * hid
    fc = min(inner_w, 256)
    fslots = fsend.shape[0]
    square = half == 4
    chip_x = me + 1 - 2 * lax.rem(me, 2)
    chip_y = lax.rem(me + 2, 4)
    chip_d = 3 - me
    mid_row = rows // 2

    loads = []
    for el in range(local_experts):
        cols = pl.ds(el * hid, hid)
        loads.append(pltpu.make_async_copy(gate_hbm.at[el], wg.at[:, cols], wsem.at[0, el]))
        loads.append(pltpu.make_async_copy(up_hbm.at[el], wu.at[:, cols], wsem.at[1, el]))
    loads.append(pltpu.make_async_copy(down_hbm, down_ref, wsem.at[2, 0]))
    for copy in loads:
        copy.start()

    def piece_of(g):
        return lax.rem(z + nz - g, nz)

    def cot_start(g, parity, slot):
        zz = piece_of(g)
        for h in range(half):
            start = (2 * h + parity) * tok + zz * rows
            pltpu.make_async_copy(
                cot_all.at[pl.ds(pl.multiple_of(start, 16), rows)],
                cbuf.at[slot, pl.ds(h * rows, rows)],
                csem.at[slot],
            ).start()

    def cot_wait(slot):
        pltpu.make_async_copy(
            cot_all.at[pl.ds(0, half * rows)], cbuf.at[slot], csem.at[slot]
        ).wait()

    cot_start(0, core, 0)
    barrier = greet(n, nz, e, z, sib)

    own_rows = pl.ds(pl.multiple_of(z * rows, 16), rows)
    my_rows = pl.ds(pl.multiple_of(me * rows, 16), rows)
    mid = mid_ref[...]
    scale2 = lax.rsqrt(jnp.mean(mid * mid, -1, keepdims=True) + EPS)
    xn = (mid * scale2 * gain_ref[...]).astype(bf16)
    xn_s[...] = xn
    logits = dot_nt(xn, router_ref[...])
    choices = routes_ref[...].astype(f32)
    top_count = choices.shape[0]
    picks_s[...] = jnp.concatenate([choices, jnp.zeros((128 - top_count, tok), f32)], 0).T
    picks = picks_s[own_rows, 0:top_count].astype(jnp.int32)
    lanes = lax.broadcasted_iota(jnp.int32, (rows, experts), 1)
    chosen = jnp.zeros((rows, experts), f32)
    for k in range(picks.shape[1]):
        chosen = jnp.where(picks[:, k : k + 1] == lanes, 1.0, chosen)
    top = jnp.max(logits, -1, keepdims=True)
    powers = jnp.exp(logits - top)
    probs = powers / jnp.sum(powers, -1, keepdims=True)
    low_logits = jnp.where(chosen > 0.0, logits, -1e30)
    ctop = jnp.max(low_logits, -1, keepdims=True)
    cpow = jnp.exp(low_logits - ctop)
    comb = cpow / jnp.sum(cpow, -1, keepdims=True)
    padded = jnp.concatenate([comb, jnp.zeros((rows, 128 - experts), f32)], 1)
    if rows < 128:
        padded = jnp.concatenate([padded, jnp.zeros((128 - rows, 128), f32)], 0)
    piece = padded.T[:experts]
    lane_pad = jnp.zeros((1, 128 - experts), f32)
    cnt = jnp.concatenate([jnp.sum(chosen, 0, keepdims=True), lane_pad], 1)
    psum = jnp.concatenate([jnp.sum(probs, 0, keepdims=True), lane_pad], 1)
    psum_hi = psum.astype(bf16).astype(f32)
    stats = jnp.concatenate([cnt, psum_hi, psum - psum_hi, jnp.zeros((13, 128), f32)], 0)
    wbuf[z, core, me] = jnp.concatenate([piece, stats], 0).astype(bf16)
    if big:
        copy = pltpu.make_async_copy(xn_s, xbuf.at[z, core, my_rows], lsem)
        copy.start()
        copy.wait()
    else:
        xbuf[z, core, my_rows] = xn
    pl.semaphore_wait(barrier, half + nz - 1)

    def z_row(zz, k, to):
        ref = xbuf.at[zz, core, my_rows]
        return remote(ref, ref, zs.at[k - 1], zr.at[k - 1], (e, to))

    def z_small(zz, k, to):
        ref = wbuf.at[zz, core, me]
        return remote(ref, ref, zws.at[k - 1], zwr.at[k - 1], (e, to))

    def x_row(zz, h, g, s, to):
        ref = xbuf.at[zz, core, pl.ds(pl.multiple_of(h * rows, 16), rows)]
        return remote(ref, ref, xs.at[g, s], xr.at[g, s], (to, z))

    def x_small(zz, h, g, s, to):
        ref = wbuf.at[zz, core, h]
        return remote(ref, ref, ws.at[g, s], wr.at[g, s], (to, z))

    def x_part(zz, h, first, count, g, i, to):
        start = pl.multiple_of(h * rows + first, 16)
        ref = xbuf.at[zz, core, pl.ds(start, count)]
        return remote(ref, ref, xs.at[g, i], xr.at[g, i], (2 * to + core, z))

    def push_piece(g):
        zz = piece_of(g)
        if square:
            x_part(zz, me, 0, rows, g, 0, chip_x).start()
            x_part(zz, me, 0, rows, g, 1, chip_y).start()
        for s in range(1, half):
            to = lax.rem(e + 2 * s, n)
            if not square:
                x_row(zz, me, g, s, to).start()
            x_small(zz, me, g, s, to).start()

    def relays(g):
        zz = piece_of(g)
        return (
            x_part(zz, chip_x, 0, mid_row, g, 2, chip_y),
            x_part(zz, chip_y, mid_row, rows - mid_row, g, 3, chip_x),
        )

    def relay_pieces(g):
        zz = piece_of(g)
        low, high = relays(g)
        x_part(zz, chip_x, 0, rows, g, 0, chip_x).wait_recv()
        low.start()
        x_part(zz, chip_y, 0, rows, g, 1, chip_y).wait_recv()
        high.start()

    push_piece(jnp.int32(0))
    def z_push(k):
        z_row(z, k, lax.rem(z + k, nz)).start()
        z_small(z, k, lax.rem(z + k, nz)).start()

    for k in range(1, min(nz, 2) if square else nz):
        z_push(k)

    if square:
        relay_pieces(jnp.int32(0))
        if nz > 2:
            z_push(2)

    dgate[...] = jnp.zeros_like(dgate)
    dup[...] = jnp.zeros_like(dup)
    ddown[...] = jnp.zeros_like(ddown)
    for copy in loads:
        copy.wait()

    sel_row = lax.broadcasted_iota(jnp.int32, (experts, fc), 0)
    sel_col = lax.broadcasted_iota(jnp.int32, (experts, fc), 1)

    def block(zz, parity, slot, dst, dst_o, dst_g, dslot):
        if big:
            copy = pltpu.make_async_copy(xbuf.at[zz, parity], xstage, lsem)
            copy.start()
            copy.wait()
            x_ref = xstage
        else:
            x_ref = xbuf.at[zz, parity]
        c_ref = cbuf.at[slot]
        sums = [jnp.zeros((experts, rows), f32) for _ in range(half)]
        for q in range(inner_w // fc):
            cols = slice(q * fc, (q + 1) * fc)
            x = x_ref[...]
            gate_val = dot_nn(x, wg[:, cols])
            up_val = dot_nn(x, wu[:, cols])
            back = dot_nt(c_ref[...], down_ref[cols, :])
            select = jnp.where(
                sel_row == e * local_experts + (q * fc + sel_col) // hid, 1.0, 0.0
            ).astype(bf16)
            wide = jnp.concatenate(
                [dot_tn(wbuf[zz, parity, h, :experts, :], select)[:rows] for h in range(half)], 0
            )
            sig = 1.0 / (1.0 + jnp.exp(-gate_val))
            silu = gate_val * sig
            inner = silu * up_val
            wi_s[:, cols] = (inner * wide).astype(bf16)
            scaled = back * wide
            dg_s[:, cols] = (scaled * up_val * (sig * (1.0 + gate_val * (1.0 - sig)))).astype(bf16)
            du_s[:, cols] = (scaled * silu).astype(bf16)
            both = (inner * back).astype(bf16)
            for h in range(half):
                sums[h] = sums[h] + dot_nt(select, both[h * rows : (h + 1) * rows])
        for h in range(half):
            gap = jnp.zeros((experts, 128 - rows), f32)
            dst_g[dslot, h] = jnp.concatenate([sums[h], gap], 1).astype(bf16)
        for h in range(width // 256):
            cols = slice(h * 256, (h + 1) * 256)
            dst[dslot, :, cols] = (
                dot_nt(dg_s[...], wg[cols, :]) + dot_nt(du_s[...], wu[cols, :])
            ).astype(bf16)
            dst_o[dslot, :, cols] = dot_nn(wi_s[...], down_ref[:, cols]).astype(bf16)
        for h in range(width // 256):
            cols = slice(h * 256, (h + 1) * 256)
            x_part = x_ref[:, cols]
            gate_part = dot_tn(x_part, dg_s[...])
            up_part = dot_tn(x_part, du_s[...])
            for el in range(local_experts):
                dgate[el, cols, :] += gate_part[:, el * hid : (el + 1) * hid]
                dup[el, cols, :] += up_part[:, el * hid : (el + 1) * hid]
            ddown[:, cols] += dot_tn(wi_s[...], c_ref[:, cols])

    def gives(slot):
        return [
            remote(osend.at[slot], sin.at[slot], gs.at[slot], gr.at[slot], (sib, z)),
            remote(osend_g.at[slot], sin_g.at[slot], ggs.at[slot], ggr.at[slot], (sib, z)),
            remote(osend_o.at[slot], sin_o.at[slot], oss.at[slot], osr.at[slot], (sib, z)),
        ]

    def finals(g, s, to):
        at = lax.rem(g, fslots)
        rows_copy = []
        if not square:
            rows_copy = [
                remote(
                    fsend.at[at, s - 1], fin.at[g, s - 1], ps.at[g, s - 1], pr.at[g, s - 1], (to, z)
                )
            ]
        return rows_copy + [
            remote(
                fsend_g.at[at, s - 1],
                fin_g.at[g, s - 1],
                pgs.at[g, s - 1],
                pgr.at[g, s - 1],
                (to, z),
            ),
        ]

    def half_copy(g, buf, upper, i, chip):
        first, count = (mid_row, rows - mid_row) if upper else (0, mid_row)
        return remote(
            fsend.at[g, buf, pl.ds(first, count)],
            fin.at[g, buf, pl.ds(first, count)],
            ps.at[g, i],
            pr.at[g, i],
            (2 * chip + core, z),
        )

    def half_copies(g):
        return [
            half_copy(g, 2, False, 0, chip_x),
            half_copy(g, 2, True, 1, chip_y),
            half_copy(g, 0, False, 2, chip_x),
            half_copy(g, 1, True, 3, chip_y),
            half_copy(g, 1, False, 4, chip_y),
            half_copy(g, 0, True, 5, chip_x),
        ]

    def chip_sum(slot, chip, upper):
        first, count = (mid_row, rows - mid_row) if upper else (0, mid_row)
        at = pl.ds(pl.multiple_of(chip * rows + first, 16), count)
        return hold[slot, at, :].astype(f32) + sin[slot, at, :].astype(f32)

    def direct_stage(g):
        slot = lax.rem(g, 2)
        copies = half_copies(g)
        fsend[g, 2, :mid_row] = chip_sum(slot, chip_d, False).astype(bf16)
        copies[0].start()
        fsend[g, 2, mid_row:] = chip_sum(slot, chip_d, True).astype(bf16)
        copies[1].start()
        fsend[g, 0, :mid_row] = chip_sum(slot, chip_x, False).astype(bf16)
        copies[2].start()
        fsend[g, 1, mid_row:] = chip_sum(slot, chip_y, True).astype(bf16)
        copies[3].start()

    def relay_stage(g):
        slot = lax.rem(g, 2)
        copies = half_copies(g)
        copies[0].wait_recv()
        passed = chip_sum(slot, chip_y, False) + fin[g, 2, :mid_row].astype(f32)
        fsend[g, 1, :mid_row] = passed.astype(bf16)
        copies[4].start()
        copies[1].wait_recv()
        passed = chip_sum(slot, chip_x, True) + fin[g, 2, mid_row:].astype(f32)
        fsend[g, 0, mid_row:] = passed.astype(bf16)
        copies[5].start()

    def lasts(k, to):
        return [
            remote(zsend.at[k - 1], zin.at[k - 1], zgs.at[k - 1], zgr.at[k - 1], (e, to)),
            remote(zsend_g.at[k - 1], zin_g.at[k - 1], zggs.at[k - 1], zggr.at[k - 1], (e, to)),
        ]

    def mixed_copy(g, slot):
        return pltpu.make_async_copy(hold_o.at[slot], mixed_hbm.at[piece_of(g)], msem.at[slot])

    def plane_stage(g):
        slot = lax.rem(g, 2)
        for copy in gives(slot)[:2]:
            copy.wait_recv()
        if fslots < nz:

            @pl.when(g >= fslots)
            def _():
                for s in range(1, half):
                    for copy in finals(g - fslots, s, sib):
                        copy.wait_send()

        spot = lax.rem(g, fslots)
        if square:
            direct_stage(g)
        for s in range(1, half):
            h = lax.rem(me + half - s, half)
            at = pl.ds(pl.multiple_of(h * rows, 16), rows)
            if not square:
                fsend[spot, s - 1] = (
                    hold[slot, at, :].astype(f32) + sin[slot, at, :].astype(f32)
                ).astype(bf16)
            fsend_g[spot, s - 1] = (hold_g[slot, h].astype(f32) + sin_g[slot, h].astype(f32)).astype(
                bf16
            )
            for copy in finals(g, s, lax.rem(e - 2 * s + n, n)):
                copy.start()
        own_s[g] = hold[slot, my_rows, :].astype(f32) + sin[slot, my_rows, :].astype(f32)
        own_g[g] = hold_g[slot, me].astype(f32) + sin_g[slot, me].astype(f32)

    def mixed_stage(g):
        slot = lax.rem(g, 2)
        gives(slot)[2].wait_recv()
        hold_o[slot] = (hold_o[slot].astype(f32) + sin_o[slot].astype(f32)).astype(bf16)
        mixed_copy(g, slot).start()

    def tensor_stage(g):
        total = own_s[g]
        total_g = own_g[g]
        for s in range(1, half):
            for copy in finals(g, s, sib):
                copy.wait_recv()
            if not square:
                total = total + fin[g, s - 1].astype(f32)
            total_g = total_g + fin_g[g, s - 1].astype(f32)

        if square:
            for copy in half_copies(g)[2:]:
                copy.wait_recv()
            total = total + fin[g, 0].astype(f32) + fin[g, 1].astype(f32)

        @pl.when(g == 0)
        def _():
            own_s[0] = total
            own_g[0] = total_g

        @pl.when(g > 0)
        def _():
            zsend[g - 1] = total.astype(bf16)
            zsend_g[g - 1] = total_g.astype(bf16)
            for copy in lasts(g, piece_of(g)):
                copy.start()

    def step(g, carry):
        zz = piece_of(g)
        slot = lax.rem(g, 2)

        @pl.when(g < nz - 1)
        def _():
            coming = piece_of(g + 1)
            z_row(coming, g + 1, coming).wait_recv()
            z_small(coming, g + 1, coming).wait_recv()
            push_piece(g + 1)

        if square:
            x_part(zz, chip_d, 0, mid_row, g, 2, chip_y).wait_recv()
            x_part(zz, chip_d, mid_row, rows - mid_row, g, 3, chip_x).wait_recv()

        for s in range(1, half):
            h = lax.rem(me + half - s, half)
            src = 2 * h + core
            if not square:
                x_row(zz, h, g, s, src).wait_recv()
            x_small(zz, h, g, s, src).wait_recv()
        for copy in forward(zz, core, g):
            copy.start()
        cot_start(g, other, 1)
        cot_wait(0)

        @pl.when(g >= 2)
        def _():
            mixed_copy(g - 2, slot).wait()

        block(zz, core, 0, hold, hold_o, hold_g, slot)
        if square:

            @pl.when(g == 0)
            def _():
                for k in range(3, nz):
                    z_push(k)

            @pl.when(g < nz - 1)
            def _():
                relay_pieces(g + 1)


        @pl.when(g < nz - 1)
        def _():
            cot_start(g + 1, core, 0)

        @pl.when(g >= 2)
        def _():
            tensor_stage(g - 2)

        @pl.when(g >= 1)
        def _():
            plane_stage(g - 1)
            mixed_stage(g - 1)

        @pl.when(g >= 2)
        def _():
            for copy in gives(slot):
                copy.wait_send()

        for copy in forward(zz, other, g):
            copy.wait_recv()
        cot_wait(1)
        block(zz, other, 1, osend, osend_o, osend_g, slot)
        for copy in gives(slot):
            copy.start()
        if square:

            @pl.when(g >= 1)
            def _():
                relay_stage(g - 1)

        return carry

    def forward(zz, parity, g):
        ref = xbuf.at[zz, parity]
        small = wbuf.at[zz, parity]
        return (
            remote(ref, ref, fs.at[g], fr.at[g], (sib, z)),
            remote(small, small, wfs.at[g], wfr.at[g], (sib, z)),
        )

    lax.fori_loop(0, nz, step, 0)
    grads = [
        pltpu.make_async_copy(dgate, dgate_hbm, gsem.at[0]),
        pltpu.make_async_copy(dup, dup_hbm, gsem.at[1]),
        pltpu.make_async_copy(ddown, ddown_hbm, gsem.at[2]),
        pltpu.make_async_copy(xbuf.at[:, core, my_rows, :], normed_hbm, gsem.at[3]),
    ]
    plane_stage(jnp.int32(nz - 1))
    for copy in grads:
        copy.start()
    if nz >= 2:
        tensor_stage(jnp.int32(nz - 2))
    if square:
        relay_stage(jnp.int32(nz - 1))

    def total_stats(j, carry):
        for zz in range(nz):
            for parity in range(2):
                carry = carry + wbuf[zz, parity, j, experts:, :].astype(f32)
        return carry

    stats = lax.fori_loop(0, half, total_stats, jnp.zeros((16, 128), f32))
    total_rows = n * tok
    share = stats[0:1, :experts] / (total_rows * top_count)
    load_ref[...] = (
        experts * experts * share * ((stats[1:2, :experts] + stats[2:3, :experts]) / total_rows)
    )
    loss_w = experts * share / total_rows
    mixed_stage(jnp.int32(nz - 1))
    tensor_stage(jnp.int32(nz - 1))

    gate_sums = own_g[0]
    grad_rows = own_s[0]
    for k in range(1, nz):
        for copy in lasts(k, z):
            copy.wait_recv()
        gate_sums = gate_sums + zin_g[k - 1].astype(f32)
        grad_rows = grad_rows + zin[k - 1].astype(f32)
    grow = jnp.concatenate([gate_sums, jnp.zeros((128 - experts, 128), f32)], 0).T
    grad_gates = grow[:rows, :experts]
    grad_logits = comb * (grad_gates - jnp.sum(grad_gates * comb, -1, keepdims=True))
    grad_logits = grad_logits + probs * (loss_w - jnp.sum(loss_w * probs, -1, keepdims=True))
    low_grad = grad_logits.astype(bf16)
    wide_grad = jnp.concatenate([grad_logits, jnp.zeros((rows, 128 - experts), f32)], 1)
    if rows < 128:
        wide_grad = jnp.concatenate([wide_grad, jnp.zeros((128 - rows, 128), f32)], 0)
    glog_ref[...] = wide_grad.T[:experts].astype(bf16)
    grad_rows = grad_rows + dot_nn(low_grad, router_ref[...])
    mid = mid_ref[...]
    ggrad_ref[...] = jnp.sum(grad_rows * mid * scale2, 0, keepdims=True)
    gained = grad_rows * gain_ref[...]
    gmid_ref[...] = (
        cot_ref[own_rows, :]
        + scale2 * gained
        - mid * (scale2 * scale2 * scale2) * jnp.mean(gained * mid, -1, keepdims=True)
    )

    for copy in grads:
        copy.wait()
    for k in range(1, nz):
        z_row(z, k, z).wait_send()
        z_small(z, k, z).wait_send()
        for copy in lasts(k, z):
            copy.wait_send()
    for g in range(max(0, nz - 2), nz):
        mixed_copy(jnp.int32(g), g % 2).wait()
        for copy in gives(g % 2):
            copy.wait_send()

    def drained(g, carry):
        if square:
            x_part(z, me, 0, rows, g, 0, chip_x).wait_send()
            x_part(z, me, 0, rows, g, 1, chip_y).wait_send()
            for copy in relays(g) + tuple(half_copies(g)):
                copy.wait_send()
        for s in range(1, half):
            if not square:
                x_row(z, me, g, s, sib).wait_send()
            x_small(z, me, g, s, sib).wait_send()
        for copy in forward(z, core, g):
            copy.wait_send()
        return carry

    lax.fori_loop(0, nz, drained, 0)

    def sums_sent(g, carry):
        for s in range(1, half):
            for copy in finals(g, s, sib):
                copy.wait_send()
        return carry

    lax.fori_loop(nz - fslots, nz, sums_sent, 0)


def expert_layer(n, nz, mid, gain, router, routes, gate, up, down, cot, cot_all):
    rows, width = mid.shape
    experts = router.shape[1]
    local_experts, _, hid = gate.shape
    inner_w = local_experts * hid
    half = n // 2
    batch = half * rows
    big = n > 8
    fslots = 2 if big else nz
    dma = pltpu.SemaphoreType.DMA
    vmem = pl.BlockSpec(memory_space=pltpu.VMEM)
    hbm = pl.BlockSpec(memory_space=pl.ANY)
    sds = jax.ShapeDtypeStruct
    out_shape = [
        sds((rows, width), f32),
        sds((experts, 128), bf16),
        sds((1, width), f32),
        sds((1, experts), f32),
        sds((local_experts, width, hid), f32),
        sds((local_experts, width, hid), f32),
        sds((inner_w, width), f32),
        sds((nz, batch, width), bf16),
        sds((nz, rows, width), bf16),
    ]
    out_specs = [vmem] * 4 + [hbm] * 5
    scratch = []
    if big:
        out_shape.append(sds((nz, 2, batch, width), bf16))
        out_specs.append(hbm)
        scratch.append(pltpu.VMEM((batch, width), bf16))
    else:
        scratch.append(pltpu.VMEM((nz, 2, batch, width), bf16))
    pair = pltpu.VMEM((2, batch, width), bf16)
    small = pltpu.VMEM((2, half, experts, 128), bf16)
    scratch += [
        pltpu.VMEM((nz, 2, half, experts + 16, 128), bf16),
        pltpu.VMEM((rows, width), bf16),
        pltpu.VMEM((width, inner_w), bf16),
        pltpu.VMEM((width, inner_w), bf16),
        pltpu.VMEM((inner_w, width), bf16),
        pltpu.VMEM((local_experts, width, hid), f32),
        pltpu.VMEM((local_experts, width, hid), f32),
        pltpu.VMEM((inner_w, width), f32),
        pair,
        pltpu.VMEM((batch, inner_w), bf16),
        pltpu.VMEM((batch, inner_w), bf16),
        pltpu.VMEM((batch, inner_w), bf16),
        pair,
        pair,
        pair,
        pair,
        pair,
        pair,
        small,
        small,
        small,
        pltpu.VMEM((nz, rows, width), f32),
        pltpu.VMEM((nz, experts, 128), f32),
        pltpu.VMEM((fslots, half - 1, rows, width), bf16),
        pltpu.VMEM((nz, half - 1, rows, width), bf16),
        pltpu.VMEM((fslots, half - 1, experts, 128), bf16),
        pltpu.VMEM((nz, half - 1, experts, 128), bf16),
        pltpu.VMEM((nz - 1, rows, width), bf16),
        pltpu.VMEM((nz - 1, rows, width), bf16),
        pltpu.VMEM((nz - 1, experts, 128), bf16),
        pltpu.VMEM((nz - 1, experts, 128), bf16),
        dma((3, local_experts)),
        dma((4,)),
        dma((2,)),
        dma((2,)),
        dma,
    ]
    scratch += [dma((nz - 1,))] * 4
    scratch += [dma((nz, half))] * 4
    scratch += [dma((nz,))] * 4
    scratch += [dma((2,))] * 6
    scratch += [dma((nz, 6 if half == 4 else half - 1))] * 2
    scratch += [dma((nz, half - 1))] * 2
    scratch += [dma((nz - 1,))] * 4 + [pltpu.VMEM((nz * rows, 128), f32)]
    return pl.pallas_call(
        functools.partial(expert_kernel, n, nz, big),
        out_shape=out_shape,
        in_specs=[vmem] * 5 + [hbm] * 4,
        out_specs=out_specs,
        scratch_shapes=scratch,
        compiler_params=pltpu.CompilerParams(
            collective_id=1, has_side_effects=True, vmem_limit_bytes=60 << 20
        ),
        name="experts",
    )(mid, gain[None], router.T, routes.T, cot, gate, up, down.reshape(inner_w, width), cot_all)[:9]


def attend_kernel(
    n,
    nz,
    x_ref,
    gain_ref,
    wq_ref,
    wk_ref,
    wv_ref,
    wo_ref,
    cos_ref,
    sin_ref,
    cot_ref,
    lens_ref,
    mid_ref,
    q_ref,
    kv_ref,
    lrow_ref,
    att_ref,
    cot_hbm,
    wqkv,
    wfull,
    qst_s,
    m_s,
    l_s,
    o_s,
    att_low,
    acol,
    ks,
    kr,
    kfs,
    kfr,
    zgs,
    zgr,
    gos,
    gor,
    gps,
    gpr,
    cot_low,
    cs,
    cr,
    cps,
    cpr,
    csem,
):
    e = lax.axis_index("expert")
    z = lax.axis_index("tensor")
    core = lax.rem(e, 2)
    sib = e + 1 - 2 * core
    half = n // 2
    me = e // 2
    tok, width = x_ref.shape
    rows = tok // nz
    qw = wq_ref.shape[1]
    kw = wk_ref.shape[1]
    seqs = kv_ref.shape[0]
    span = tok // seqs
    heads = kw // HD
    groups = qw // kw
    barrier = greet(n, nz, e, z, sib)

    wqkv[:, 0:qw] = wq_ref[...]
    wqkv[:, qw : qw + kw] = wk_ref[...]
    wqkv[:, qw + kw :] = wv_ref[...]
    x = x_ref[...].astype(f32)
    scale1 = lax.rsqrt(jnp.mean(x * x, -1, keepdims=True) + EPS)
    normed = (x * scale1 * gain_ref[...]).astype(bf16)
    lin = dot_nn(normed, wqkv[...])
    turned = turn(lin, cos_ref[...], sin_ref[...], qw + kw, True).astype(bf16)
    q_ref[...] = turned[:, :qw]
    for s in range(seqs):
        kv_ref[s, pl.ds(pl.multiple_of(e * span, 16), span)] = turned[
            s * span : (s + 1) * span, qw:
        ]
    cot_low[...] = cot_ref[...].astype(bf16)
    cot_local = pltpu.make_async_copy(
        cot_low, cot_hbm.at[pl.ds(pl.multiple_of(e * tok, 16), tok)], csem
    )
    cot_local.start()
    pl.semaphore_wait(barrier, half + nz - 1)

    def rows_of(j, s):
        return kv_ref.at[s, pl.ds(pl.multiple_of(j * span, 16), span)]

    half_rows = qw // 2
    my_half = pl.ds(pl.multiple_of(core * half_rows, 16), half_rows)

    def weight_send(k):
        to = (e, lax.rem(z + k, nz))
        return remote(
            wo_ref.at[my_half], wfull.at[z, my_half], gos.at[k - 1], gor.at[k - 1], to
        )

    def weight_copy(zz, k, to):
        ref = wfull.at[zz, my_half]
        return remote(ref, ref, gos.at[k - 1], gor.at[k - 1], (e, to))

    def weight_pass(zz, which, k):
        at = pl.ds(pl.multiple_of(which * half_rows, 16), half_rows)
        ref = wfull.at[zz, at]
        return remote(ref, ref, gps.at[k - 1], gpr.at[k - 1], (sib, z))

    for t in range(1, half):
        to = (lax.rem(e + 2 * t, n), z)
        for s in range(seqs):
            remote(rows_of(e, s), rows_of(e, s), ks.at[t, s], kr.at[t, s], to).start()
    for s in range(seqs):
        remote(rows_of(e, s), rows_of(e, s), kfs.at[0, s], kfr.at[0, s], (sib, z)).start()
    for k in range(1, nz):
        weight_send(k).start()

    square = half == 4
    chip_x = me + 1 - 2 * lax.rem(me, 2)
    chip_y = lax.rem(me + 2, 4)
    chip_d = 3 - me
    low_rows = tok // 2

    def cot_at(chip, first=0, count=tok):
        start = (2 * chip + core) * tok + first
        return cot_hbm.at[pl.ds(pl.multiple_of(start, 16), count)]

    def cot_send(i, chip):
        return remote(cot_low, cot_at(me), cs.at[i], cr.at[i], (2 * chip + core, z))

    def cot_recv(i, chip):
        return remote(cot_at(chip), cot_at(chip), cs.at[i], cr.at[i], (2 * chip + core, z))

    def cot_relay(i, chip, to):
        ref = cot_at(chip, 0, low_rows) if i == 2 else cot_at(chip, low_rows, tok - low_rows)
        return remote(ref, ref, cs.at[i], cr.at[i], (2 * to + core, z))

    def cot_pass(t, chip, parity):
        start = (2 * chip + parity) * tok
        ref = cot_hbm.at[pl.ds(pl.multiple_of(start, 16), tok)]
        return remote(ref, ref, cps.at[t], cpr.at[t], (sib, z))

    if square:
        cot_pushes = [cot_send(0, chip_x), cot_send(1, chip_y)]
        cot_chips = [me, chip_x, chip_y, chip_d]
    else:
        cot_pushes = [cot_send(t - 1, lax.rem(me + t, half)) for t in range(1, half)]
        cot_chips = [lax.rem(me + half - t, half) for t in range(half)]
    for copy in cot_pushes:
        copy.start()
    cot_local.wait()
    cot_pass(0, me, core).start()
    wfull[z] = wo_ref[...]

    def forward(t, carry):
        src = lax.rem(e - 2 * t + n, n)
        for s in range(seqs):
            remote(rows_of(src, s), rows_of(src, s), ks.at[t, s], kr.at[t, s], (src, z)).wait_recv()
            remote(rows_of(src, s), rows_of(src, s), kfs.at[t, s], kfr.at[t, s], (sib, z)).start()
        return carry

    lax.fori_loop(1, half, forward, 0)

    def arrive(t, carry):
        src = lax.rem(sib - 2 * t + n, n)
        for s in range(seqs):
            remote(
                rows_of(src, s), rows_of(src, s), kfs.at[t, s], kfr.at[t, s], (sib, z)
            ).wait_recv()
        return carry

    lax.fori_loop(0, half, arrive, 0)

    ck = 2 * span
    last = (e * span + span - 1) // ck
    stacked = groups * span
    qpos = lax.broadcasted_iota(jnp.int32, (stacked, ck), 0)
    qpos = e * span + lax.rem(qpos, span)
    kiota = lax.broadcasted_iota(jnp.int32, (stacked, ck), 1)
    klane = lax.broadcasted_iota(jnp.int32, (1, ck), 1)
    m_s[...] = jnp.full_like(m_s, -1e30)
    l_s[...] = jnp.zeros_like(l_s)
    o_s[...] = jnp.zeros_like(o_s)
    for s in range(seqs):
        for h in range(heads):
            qst_s[s * heads + h] = jnp.concatenate(
                [
                    q_ref[
                        s * span : (s + 1) * span,
                        (h * groups + g) * HD : (h * groups + g + 1) * HD,
                    ]
                    for g in range(groups)
                ],
                0,
            ) * jnp.array(HD ** (-0.5), bf16)

    def chunk(c, diagonal):
        at = pl.ds(pl.multiple_of(c * ck, 16), ck)
        for s in range(seqs):
            for h in range(heads):
                i = s * heads + h
                keys = kv_ref[s, at, h * HD : (h + 1) * HD]
                vals = kv_ref[s, at, kw + h * HD : kw + (h + 1) * HD]
                scores = dot_nt(qst_s[i], keys)
                if diagonal:
                    kpos = kiota + c * ck
                    scores = jnp.where((kpos <= qpos) & (kpos < lens_ref[s]), scores, -1e30)
                else:
                    scores = scores + jnp.where(klane + c * ck < lens_ref[s], 0.0, -1e30)
                old = m_s[i, :, 0:1]
                new = jnp.maximum(old, jnp.max(scores, -1, keepdims=True))
                weights = jnp.exp(scores - new)
                shrink = jnp.exp(old - new)
                m_s[i] = jnp.broadcast_to(new, (stacked, 128))
                l_s[i] = l_s[i] * shrink + jnp.sum(weights, -1, keepdims=True)
                o_s[i] = o_s[i] * shrink + dot_nn(weights.astype(bf16), vals)

    def whole_chunk(c, carry):
        chunk(c, False)
        return carry

    lax.fori_loop(0, last, whole_chunk, 0)
    chunk(last, True)
    for s in range(seqs):
        for h in range(heads):
            i = s * heads + h
            result = o_s[i] / l_s[i, :, 0:HD]
            for g in range(groups):
                cols = slice((h * groups + g) * HD, (h * groups + g + 1) * HD)
                att_ref[s * span : (s + 1) * span, cols] = result[g * span : (g + 1) * span]
            logs = m_s[i] + jnp.log(l_s[i])
            lrow_ref[i] = logs.T[0:8]

    att_low[...] = att_ref[...].astype(bf16)
    own_rows = pl.ds(pl.multiple_of(z * rows, 16), rows)

    def row_copy(k, to):
        src = att_low.at[pl.ds(pl.multiple_of(to * rows, 16), rows)]
        return remote(src, acol.at[z], zgs.at[k - 1], zgr.at[k - 1], (e, to))

    for k in range(1, nz):
        row_copy(k, lax.rem(z + k, nz)).start()
    acol[z] = att_low[own_rows, :]
    for k in range(1, nz):
        zz = lax.rem(z + nz - k, nz)
        weight_copy(zz, k, zz).wait_recv()
        weight_pass(zz, core, k).start()
    if square:
        cot_recv(0, chip_x).wait_recv()
        cot_relay(2, chip_x, chip_y).start()
        cot_pass(1, chip_x, core).start()
        cot_recv(1, chip_y).wait_recv()
        cot_relay(3, chip_y, chip_x).start()
        cot_pass(2, chip_y, core).start()
    else:
        for t in range(1, half):
            cot_recv(t - 1, cot_chips[t]).wait_recv()
            cot_pass(t, cot_chips[t], core).start()
    for k in range(1, nz):
        row_copy(k, lax.rem(z + nz - k, nz)).wait_recv()
        weight_pass(lax.rem(z + nz - k, nz), 1 - core, k).wait_recv()
    mid = x_ref[own_rows, :].astype(f32)
    for zz in range(nz):
        mid = mid + dot_nn(acol[zz], wfull[zz])
    mid_ref[...] = mid
    if square:
        cot_relay(2, chip_d, chip_y).wait_recv()
        cot_relay(3, chip_d, chip_x).wait_recv()
        cot_pass(3, chip_d, core).start()
        cot_relay(2, chip_x, chip_y).wait_send()
        cot_relay(3, chip_y, chip_x).wait_send()
    for copy in cot_pushes:
        copy.wait_send()
    for t in range(half):
        cot_pass(t, cot_chips[t], 1 - core).wait_recv()
        cot_pass(t, cot_chips[t], core).wait_send()
    for k in range(1, nz):
        row_copy(k, lax.rem(z + k, nz)).wait_send()
        weight_send(k).wait_send()
        weight_pass(lax.rem(z + nz - k, nz), core, k).wait_send()

    def sent(t, carry):
        for s in range(seqs):

            @pl.when(t > 0)
            def _():
                remote(
                    rows_of(e, s), rows_of(e, s), ks.at[t, s], kr.at[t, s], (sib, z)
                ).wait_send()

            remote(rows_of(e, s), rows_of(e, s), kfs.at[t, s], kfr.at[t, s], (sib, z)).wait_send()
        return carry

    lax.fori_loop(0, half, sent, 0)


def attend_layer(n, nz, x, gain, wq, wk, wv, wo, cos, sin, cot, lens):
    tok, width = x.shape
    rows = tok // nz
    qw, kw = wq.shape[1], wk.shape[1]
    seqs = lens.shape[0]
    span = tok // seqs
    half = n // 2
    stacked = (qw // kw) * span
    pairs = seqs * (kw // HD)
    dma = pltpu.SemaphoreType.DMA
    vmem = pl.BlockSpec(memory_space=pltpu.VMEM)
    sds = jax.ShapeDtypeStruct
    return pl.pallas_call(
        functools.partial(attend_kernel, n, nz),
        out_shape=[
            sds((rows, width), f32),
            sds((tok, qw), bf16),
            sds((seqs, n * span, 2 * kw), bf16),
            sds((seqs * (kw // HD), 8, stacked), f32),
            sds((tok, qw), f32),
            sds((n * tok, width), bf16),
        ],
        in_specs=[vmem] * 9 + [pl.BlockSpec(memory_space=pltpu.SMEM)],
        out_specs=[vmem] * 5 + [pl.BlockSpec(memory_space=pl.ANY)],
        scratch_shapes=[
            pltpu.VMEM((width, qw + 2 * kw), bf16),
            pltpu.VMEM((nz, qw, width), bf16),
            pltpu.VMEM((pairs, stacked, HD), bf16),
            pltpu.VMEM((pairs, stacked, 128), f32),
            pltpu.VMEM((pairs, stacked, 128), f32),
            pltpu.VMEM((pairs, stacked, HD), f32),
            pltpu.VMEM((tok, qw), bf16),
            pltpu.VMEM((nz, rows, qw), bf16),
        ]
        + [dma((half, seqs))] * 4
        + [dma((nz - 1,))] * 6
        + [pltpu.VMEM((tok, width), bf16)]
        + [dma((max(half, 4),))] * 4
        + [dma],
        compiler_params=pltpu.CompilerParams(
            collective_id=2, has_side_effects=True, vmem_limit_bytes=60 << 20
        ),
        name="attend",
    )(x, gain[None], wq, wk, wv, wo, cos, sin, cot, lens)


def return_kernel(
    n,
    nz,
    gmid_ref,
    mid_ref,
    glog_ref,
    ggrad_ref,
    xn_ref,
    x_ref,
    gain_ref,
    wq_ref,
    wk_ref,
    wv_ref,
    wo_ref,
    cos_ref,
    sin_ref,
    q_ref,
    kv_ref,
    lrow_ref,
    att_ref,
    lens_ref,
    mixed_hbm,
    obuf,
    igbuf,
    wall,
    wall2,
    small_ref,
    wqkv,
    gat,
    datt,
    dq_s,
    qst_s,
    dst_s,
    acc_q,
    dkv,
    kvo,
    kvi,
    kvf,
    kvr,
    part,
    sums,
    csend,
    crecv,
    osend,
    orecv,
    wbufs,
    wbufs2,
    sz1,
    sz2,
    sown,
    ssib,
    schip,
    ofin,
    zas,
    zar,
    zos,
    zor,
    zis,
    zir,
    zps,
    zpr,
    zqs,
    zqr,
    z1s,
    z1r,
    z2s,
    z2r,
    kos,
    kor,
    kfs,
    kfr,
    wsems,
    wsems2,
    sbs,
    sbr,
    scs,
    scr,
    ofs,
    ofr,
    olsem,
    obase,
):
    e = lax.axis_index("expert")
    z = lax.axis_index("tensor")
    core = lax.rem(e, 2)
    me = e // 2
    sib = e + 1 - 2 * core
    half = n // 2
    rows, width = gmid_ref.shape
    tok = rows * nz
    qw = wq_ref.shape[1]
    kw = wk_ref.shape[1]
    seqs = kv_ref.shape[0]
    span = tok // seqs
    heads = kw // HD
    groups = qw // kw
    dn = width // n
    experts = glog_ref.shape[0]
    own_rows = pl.ds(pl.multiple_of(z * rows, 16), rows)
    barrier = greet(n, nz, e, z, sib)
    w1 = PlaneSum(n, e, z, sib, wall, *wbufs, *wsems)
    w2 = PlaneSum(n, e, z, sib, wall2, *wbufs2, *wsems2)

    gat[own_rows, :] = gmid_ref[...].astype(bf16)
    sz1[z] = glog_ref[...]
    pl.semaphore_wait(barrier, half + nz - 1)

    def part_of(ref):
        return lambda zz: ref.at[pl.ds(pl.multiple_of(zz * rows, 16), rows)]

    def slot_of(ref):
        return lambda zz: ref.at[zz]

    gat_line = Line(z, nz, e, part_of(gat), zas, zar)
    out_line = Line(z, nz, e, part_of(obuf), zos, zor)
    igrad_line = Line(z, nz, e, part_of(igbuf), zis, zir)
    normed_sum = LineSum(z, nz, e, csend, crecv, zps, zpr)

    def z_copies(buf_of, send, recv):
        return [
            remote(
                buf_of(z), buf_of(z), send.at[k - 1], recv.at[k - 1], (e, lax.rem(z + k, nz))
            )
            for k in range(1, nz)
        ]

    def z_arrivals(buf_of, send, recv):
        return [
            remote(
                buf_of(lax.rem(z + nz - k, nz)),
                buf_of(lax.rem(z + nz - k, nz)),
                send.at[k - 1],
                recv.at[k - 1],
                (e, lax.rem(z + nz - k, nz)),
            )
            for k in range(1, nz)
        ]

    gat_line.start()
    for copy in z_copies(slot_of(sz1), z1s, z1r):
        copy.start()

    square = half == 4
    chip_x = me + 1 - 2 * lax.rem(me, 2)
    chip_y = lax.rem(me + 2, 4)
    chip_d = 3 - me
    low, high = pl.ds(0, nz // 2), pl.ds(nz // 2, nz - nz // 2)

    def mixed_at(chip, which=slice(None)):
        return mixed_hbm.at[which, pl.ds(pl.multiple_of(chip * rows, 16), rows), :]

    def mixed_copy(src, dst, i, chip):
        return remote(src, dst, ofs.at[i], ofr.at[i], (2 * chip + core, z))

    def mixed_sends():
        if not square:
            return [
                mixed_copy(
                    mixed_at(lax.rem(me + half - t, half)),
                    ofin.at[t],
                    t - 1,
                    lax.rem(me + half - t, half),
                )
                for t in range(1, half)
            ]
        return [
            mixed_copy(mixed_at(chip_d, low), ofin.at[3, low], 0, chip_x),
            mixed_copy(mixed_at(chip_d, high), ofin.at[3, high], 1, chip_y),
            mixed_copy(mixed_at(chip_x, low), ofin.at[1, low], 2, chip_x),
            mixed_copy(mixed_at(chip_y, high), ofin.at[2, high], 3, chip_y),
        ]

    def mixed_relays():
        return [
            mixed_copy(obase.at[low], ofin.at[2, low], 4, chip_y),
            mixed_copy(obase.at[high], ofin.at[1, high], 5, chip_x),
        ]

    for copy in mixed_sends():
        copy.start()
    mixed_own = [pltpu.make_async_copy(mixed_at(me), ofin.at[0], olsem.at[0])]
    if square:
        mixed_own += [
            pltpu.make_async_copy(mixed_at(chip_y, low), obase.at[low], olsem.at[1]),
            pltpu.make_async_copy(mixed_at(chip_x, high), obase.at[high], olsem.at[2]),
        ]
    for copy in mixed_own:
        copy.start()

    def mixed_relay():
        waits = mixed_sends()
        for copy, part, i in zip(mixed_relays(), (low, high), (0, 1)):
            waits[i].wait_recv()
            obase[part] = (obase[part].astype(f32) + ofin[3, part].astype(f32)).astype(bf16)
            copy.start()

    mixed_count = 3 if square else half

    def mixed_sum(zz):
        total = ofin[0, zz].astype(f32)
        for t in range(1, mixed_count):
            total = total + ofin[t, zz].astype(f32)
        return total

    wqkv[:, 0:qw] = wq_ref[...]
    wqkv[:, qw : qw + kw] = wk_ref[...]
    wqkv[:, qw + kw :] = wv_ref[...]
    x = x_ref[...].astype(f32)
    scale1 = lax.rsqrt(jnp.mean(x * x, -1, keepdims=True) + EPS)
    normed = (x * scale1 * gain_ref[...]).astype(bf16)
    dkv[...] = jnp.zeros_like(dkv)

    for hop in range(1, nz):
        gat_line.hop(hop)
    datt[...] = dot_nt(gat[...], wo_ref[...]).astype(bf16)

    ck = 2 * span
    last = (e * span + span - 1) // ck
    stacked = groups * span
    kiota = lax.broadcasted_iota(jnp.int32, (ck, stacked), 0)
    krow = lax.broadcasted_iota(jnp.int32, (ck, 1), 0)
    qpos = e * span + lax.rem(lax.broadcasted_iota(jnp.int32, (ck, stacked), 1), span)
    drows = []
    for s in range(seqs):
        for h in range(heads):

            def gather(ref):
                return jnp.concatenate(
                    [
                        ref[
                            s * span : (s + 1) * span,
                            (h * groups + g) * HD : (h * groups + g + 1) * HD,
                        ]
                        for g in range(groups)
                    ],
                    0,
                )

            i = s * heads + h
            qst_s[i] = gather(q_ref) * jnp.array(HD ** (-0.5), bf16)
            dst = gather(datt)
            dst_s[i] = dst
            delta = jnp.sum(dst.astype(f32) * gather(att_ref), -1, keepdims=True)
            drows.append(jnp.broadcast_to(delta, (stacked, 128)).T[0:1])
    acc_q[...] = jnp.zeros_like(acc_q)
    for copy in mixed_own:
        copy.wait()
    if square:
        mixed_relay()

    def chunk(c, diagonal):
        at = pl.ds(pl.multiple_of(c * ck, 16), ck)
        for s in range(seqs):
            for h in range(heads):
                i = s * heads + h
                keys = kv_ref[s, at, h * HD : (h + 1) * HD]
                vals = kv_ref[s, at, kw + h * HD : kw + (h + 1) * HD]
                scores = dot_nt(keys, qst_s[i]) - lrow_ref[i, 0:1, :]
                if diagonal:
                    kpos = kiota + c * ck
                    allowed = (kpos <= qpos) & (kpos < lens_ref[s])
                    soft = jnp.where(allowed, jnp.exp(scores), 0.0)
                else:
                    soft = jnp.exp(scores + jnp.where(krow + c * ck < lens_ref[s], 0.0, -1e30))
                grad_probs = dot_nt(vals, dst_s[i])
                grad_scores = (soft * (grad_probs - drows[i])).astype(bf16)
                dkv[s, at, h * HD : (h + 1) * HD] = dot_nn(grad_scores, qst_s[i])
                dkv[s, at, kw + h * HD : kw + (h + 1) * HD] = dot_nn(soft.astype(bf16), dst_s[i])
                acc_q[i] += dot_tn(grad_scores, keys)

    def whole_chunk(c, carry):
        chunk(c, False)
        return carry

    lax.fori_loop(0, last, whole_chunk, 0)
    chunk(last, True)
    for s in range(seqs):
        for h in range(heads):
            result = acc_q[s * heads + h] * HD ** (-0.5)
            for g in range(groups):
                cols = slice((h * groups + g) * HD, (h * groups + g + 1) * HD)
                dq_s[s * span : (s + 1) * span, cols] = result[g * span : (g + 1) * span]

    def key_rows(j, s):
        return dkv[s, pl.ds(pl.multiple_of(j * span, 16), span), :]

    def key_send(t):
        return remote(kvo.at[t], kvi.at[t], kos.at[t], kor.at[t], (sib, z))

    def key_final(t):
        to = (lax.rem(e - 2 * t + n, n), z)
        return remote(kvf.at[t - 1], kvr.at[t - 1], kfs.at[t - 1], kfr.at[t - 1], to)

    def key_give(i, carry):
        t = half - 1 - i
        oth = lax.rem(sib - 2 * t + n, n)
        for s in range(seqs):
            kvo[t, s] = key_rows(oth, s).astype(bf16)
        key_send(t).start()
        return carry

    lax.fori_loop(0, half, key_give, 0)

    def key_pass(i, carry):
        t = half - 1 - i
        key_send(t).wait_recv()
        own = lax.rem(e - 2 * t + n, n)
        for s in range(seqs):
            kvf[t - 1, s] = (key_rows(own, s) + kvi[t, s].astype(f32)).astype(bf16)
        key_final(t).start()
        return carry

    cos, sin = cos_ref[...], sin_ref[...]
    gq = turn(dq_s[...], cos, sin, qw, False).astype(bf16)
    query_part = dot_tn(normed, gq)
    out_part = dot_tn(gat[...], att_ref[...].astype(bf16))
    for j in range(n):
        w1.pack[j, :, :qw] = query_part[j * dn : (j + 1) * dn].astype(bf16)
        w1.pack[j, :, qw:] = out_part[j * dn : (j + 1) * dn].astype(bf16)
    lax.fori_loop(0, half - 1, key_pass, 0)
    w1.give()

    def mixed_last(k, to):
        return remote(osend.at[k - 1], orecv.at[k - 1], zqs.at[k - 1], zqr.at[k - 1], (e, to))

    for copy in mixed_sends()[2:] + mixed_relays() if square else mixed_sends():
        copy.wait_recv()
    for k in range(1, nz):
        zz = lax.rem(z + k, nz)
        osend[k - 1] = mixed_sum(zz).astype(bf16)
        mixed_last(k, zz).start()
    own_mixed = mid_ref[...] + mixed_sum(z)
    w1.spread()
    for copy in z_arrivals(slot_of(sz1), z1s, z1r):
        copy.wait_recv()
    rgrad = dot_nn(sz1[0][:, :rows], xn_ref[0])
    for zz in range(1, nz):
        rgrad = rgrad + dot_nn(sz1[zz][:, :rows], xn_ref[zz])
    sown[0:experts, :] = rgrad.astype(bf16)

    key_send(0).wait_recv()
    own_kv = [key_rows(e, s) + kvi[0, s].astype(f32) for s in range(seqs)]
    for t in range(1, half):
        key_final(t).wait_recv()
        for s in range(seqs):
            own_kv[s] = own_kv[s] + kvr[t - 1, s].astype(f32)
    gkv = turn(jnp.concatenate(own_kv, 0), cos, sin, kw, False).astype(bf16)
    part[...] = dot_nt(gq, wqkv[:, :qw]) + dot_nt(gkv, wqkv[:, qw:])

    def normed_part(zz):
        return part[pl.ds(pl.multiple_of(zz * rows, 16), rows), :]

    for hop in range(nz - 1):
        normed_sum.hop(hop, normed_part)
        if hop > 0:
            out_line.hop(hop)
        if hop == 0:
            for k in range(1, nz):
                mixed_last(k, z).wait_recv()
                own_mixed = own_mixed + orecv[k - 1].astype(f32)
            obuf[own_rows, :] = own_mixed.astype(bf16)
            out_line.start()
            again = jnp.sum(part[...] * x * scale1, 0, keepdims=True)
            sz2[z] = jnp.concatenate([again, ggrad_ref[...], jnp.zeros((14, width), f32)], 0).astype(
                bf16
            )
            for copy in z_copies(slot_of(sz2), z2s, z2r):
                copy.start()
            pair_part = dot_tn(normed, gkv)
            for j in range(n):
                w2.pack[j] = pair_part[j * dn : (j + 1) * dn].astype(bf16)
            w2.give()
            w1.total()
    w2.spread()
    normed_sum.total(sums, normed_part)

    own_x = x_ref[own_rows, :].astype(f32)
    own_scale = lax.rsqrt(jnp.mean(own_x * own_x, -1, keepdims=True) + EPS)
    grad_normed = sums[...]
    gained = grad_normed * gain_ref[...]
    igrad = (
        gmid_ref[...]
        + own_scale * gained
        - own_x
        * (own_scale * own_scale * own_scale)
        * jnp.mean(gained * own_x, -1, keepdims=True)
    )
    igbuf[own_rows, :] = igrad.astype(bf16)
    igrad_line.start()
    out_line.hop(nz - 1)

    w1.forward()
    for copy in z_arrivals(slot_of(sz2), z2s, z2r):
        copy.wait_recv()
    second = sz2[0].astype(f32)
    for zz in range(1, nz):
        second = second + sz2[zz].astype(f32)
    sown[experts:, :] = second.astype(bf16)
    small_sib = remote(sown, ssib, sbs, sbr, (sib, z))
    small_sib.start()
    if nz > 2:
        igrad_line.hop(1)
    small_sib.wait_recv()
    schip[me] = (sown[...].astype(f32) + ssib[...].astype(f32)).astype(bf16)

    def small_send(t):
        to = (lax.rem(e + 2 * t, n), z)
        return remote(schip.at[me], schip.at[me], scs.at[t - 1], scr.at[t - 1], to)

    for t in range(1, half):
        small_send(t).start()

    w2.total()
    for hop in range(2, nz - 1):
        igrad_line.hop(hop)
    igrad_line.hop(nz - 1)

    w2.forward()
    for t in range(1, half):
        src = lax.rem(me + half - t, half)
        remote(
            schip.at[src], schip.at[src], scs.at[t - 1], scr.at[t - 1], (sib, z)
        ).wait_recv()
    small = schip[0].astype(f32)
    for t in range(1, half):
        small = small + schip[t].astype(f32)
    small_ref[...] = small

    w1.arrive()
    w2.arrive()
    for k in range(1, nz):
        mixed_last(k, z).wait_send()
    for line in (gat_line, out_line, igrad_line, normed_sum, w1, w2):
        line.drain()
    for copy in z_copies(slot_of(sz1), z1s, z1r) + z_copies(slot_of(sz2), z2s, z2r):
        copy.wait_send()
    small_sib.wait_send()
    for copy in mixed_sends() + (mixed_relays() if square else []):
        copy.wait_send()

    def drained(t, carry):
        key_send(t).wait_send()

        @pl.when(t > 0)
        def _():
            key_final(t).wait_send()
            small_send(t).wait_send()

        return carry

    lax.fori_loop(0, half, drained, 0)


class PlaneSum:
    def __init__(self, n, e, z, sib, wall, pack, near, send, recv, *sems):
        self.n, self.e, self.z, self.sib, self.half = n, e, z, sib, n // 2
        self.wall, self.pack, self.near, self.send, self.recv = wall, pack, near, send, recv
        self.sems = sems

    def peer(self, base, t):
        return lax.rem(base - 2 * t + self.n, self.n)

    def near_copy(self, t):
        src = self.pack.at[self.peer(self.sib, t)]
        return remote(
            src, self.near.at[t], self.sems[0].at[t], self.sems[1].at[t], (self.sib, self.z)
        )

    def far_copy(self, t):
        return remote(
            self.send.at[t - 1],
            self.recv.at[t - 1],
            self.sems[2].at[t],
            self.sems[3].at[t],
            (self.peer(self.e, t), self.z),
        )

    def all_copy(self, src, t, to):
        ref = self.wall.at[src]
        return remote(ref, ref, self.sems[4].at[t], self.sems[5].at[t], (to, self.z))

    def pass_copy(self, src, t):
        ref = self.wall.at[src]
        return remote(ref, ref, self.sems[6].at[t], self.sems[7].at[t], (self.sib, self.z))

    def give(self):
        def one(i, carry):
            self.near_copy(self.half - 1 - i).start()
            return carry

        lax.fori_loop(0, self.half, one, 0)

    def spread(self):
        def one(i, carry):
            t = self.half - 1 - i
            self.near_copy(t).wait_recv()
            own = self.pack[self.peer(self.e, t)].astype(f32)
            self.send[t - 1] = (own + self.near[t].astype(f32)).astype(bf16)
            self.far_copy(t).start()
            return carry

        lax.fori_loop(0, self.half - 1, one, 0)

    def total(self):
        self.near_copy(0).wait_recv()
        total = self.pack[self.e].astype(f32) + self.near[0].astype(f32)
        for t in range(1, self.half):
            self.far_copy(t).wait_recv()
            total = total + self.recv[t - 1].astype(f32)
        self.wall[self.e] = total.astype(bf16)
        for t in range(1, self.half):
            self.all_copy(self.e, t, lax.rem(self.e + 2 * t, self.n)).start()
        self.pass_copy(self.e, 0).start()

    def forward(self):
        def one(t, carry):
            src = self.peer(self.e, t)
            self.all_copy(src, t, src).wait_recv()
            self.pass_copy(src, t).start()
            return carry

        lax.fori_loop(1, self.half, one, 0)

    def arrive(self):
        def one(t, carry):
            self.pass_copy(self.peer(self.sib, t), t).wait_recv()
            return carry

        lax.fori_loop(0, self.half, one, 0)

    def drain(self):
        def one(t, carry):
            self.near_copy(t).wait_send()
            self.pass_copy(self.e, t).wait_send()

            @pl.when(t > 0)
            def _():
                self.far_copy(t).wait_send()
                self.all_copy(self.e, t, self.sib).wait_send()

            return carry

        lax.fori_loop(0, self.half, one, 0)


class Line:
    def __init__(self, z, nz, e, buf_of, send, recv):
        self.z, self.nz, self.e = z, nz, e
        self.buf_of, self.send, self.recv = buf_of, send, recv

    def copy(self, way, piece):
        to = self.z + 1 if way == 0 else self.z - 1
        ref = self.buf_of(piece)
        return remote(ref, ref, self.send.at[way, piece], self.recv.at[way, piece], (self.e, to))

    def push(self, piece, ways=(0, 1)):
        for way in ways:

            @pl.when(self.z < self.nz - 1 if way == 0 else self.z > 0)
            def _():
                self.copy(way, piece).start()

    def start(self):
        self.push(self.z)

    def hop(self, i):
        @pl.when(self.z >= i)
        def _():
            self.copy(0, self.z - i).wait_recv()
            self.push(self.z - i, (0,))

        @pl.when(self.z + i <= self.nz - 1)
        def _():
            self.copy(1, self.z + i).wait_recv()
            self.push(self.z + i, (1,))

    def drain(self):
        for piece in range(self.nz):

            @pl.when((self.z >= piece) & (self.z < self.nz - 1))
            def _():
                self.copy(0, piece).wait_send()

            @pl.when((self.z <= piece) & (self.z > 0))
            def _():
                self.copy(1, piece).wait_send()


class LineSum:
    def __init__(self, z, nz, e, send_buf, recv_buf, send, recv):
        self.z, self.nz, self.e = z, nz, e
        self.send_buf, self.recv_buf, self.send, self.recv = send_buf, recv_buf, send, recv

    def copy(self, way, target):
        to = self.z + 1 if way == 0 else self.z - 1
        return remote(
            self.send_buf.at[way, target],
            self.recv_buf.at[way, target],
            self.send.at[way, target],
            self.recv.at[way, target],
            (self.e, to),
        )

    def hop(self, i, own_of):
        for way, target in ((0, self.nz - 1 - i), (1, i)):
            passes = self.z < target if way == 0 else self.z > target
            first = self.z == 0 if way == 0 else self.z == self.nz - 1
            inner = self.z > 0 if way == 0 else self.z < self.nz - 1

            @pl.when(passes & first)
            def _():
                self.send_buf[way, target] = own_of(target).astype(bf16)
                self.copy(way, target).start()

            @pl.when(passes & inner)
            def _():
                self.copy(way, target).wait_recv()
                self.send_buf[way, target] = (
                    own_of(target) + self.recv_buf[way, target].astype(f32)
                ).astype(bf16)
                self.copy(way, target).start()

    def total(self, ref, own_of):
        ref[...] = own_of(self.z)

        @pl.when(self.z > 0)
        def _():
            self.copy(0, self.z).wait_recv()
            ref[...] += self.recv_buf[0, self.z].astype(f32)

        @pl.when(self.z < self.nz - 1)
        def _():
            self.copy(1, self.z).wait_recv()
            ref[...] += self.recv_buf[1, self.z].astype(f32)

    def drain(self):
        for target in range(self.nz):

            @pl.when(self.z < target)
            def _():
                self.copy(0, target).wait_send()

            @pl.when(self.z > target)
            def _():
                self.copy(1, target).wait_send()


def return_layer(
    n, nz, gmid, mid, glog, ggrad, xn, x, gain, wq, wk, wv, wo, cos, sin, q, kv, lrow, att, lens, mixed
):
    tok, width = x.shape
    rows = tok // nz
    qw, kw = wq.shape[1], wk.shape[1]
    seqs = lens.shape[0]
    span = tok // seqs
    half = n // 2
    stacked = (qw // kw) * span
    pairs = seqs * (kw // HD)
    experts = glog.shape[0]
    small_rows = experts + 16
    dma = pltpu.SemaphoreType.DMA
    vmem = pl.BlockSpec(memory_space=pltpu.VMEM)
    sds = jax.ShapeDtypeStruct
    zdma = dma((nz - 1,))
    line = dma((2, nz))
    hdma = dma((half,))
    fdma = dma((half - 1,))
    def plane_bufs(cols):
        return [
            pltpu.VMEM((n, width // n, cols), bf16),
            pltpu.VMEM((half, width // n, cols), bf16),
            pltpu.VMEM((half - 1, width // n, cols), bf16),
            pltpu.VMEM((half - 1, width // n, cols), bf16),
        ]

    line_buf = pltpu.VMEM((2, nz, rows, width), bf16)
    return pl.pallas_call(
        functools.partial(return_kernel, n, nz),
        out_shape=[
            sds((tok, width), bf16),
            sds((tok, width), bf16),
            sds((n, width // n, 2 * qw), bf16),
            sds((n, width // n, 2 * kw), bf16),
            sds((small_rows, width), f32),
        ],
        in_specs=[vmem] * 17
        + [pl.BlockSpec(memory_space=pltpu.SMEM), pl.BlockSpec(memory_space=pl.ANY)],
        out_specs=[vmem] * 5,
        scratch_shapes=[
            pltpu.VMEM((width, qw + 2 * kw), bf16),
            pltpu.VMEM((tok, width), bf16),
            pltpu.VMEM((tok, qw), bf16),
            pltpu.VMEM((tok, qw), f32),
            pltpu.VMEM((pairs, stacked, HD), bf16),
            pltpu.VMEM((pairs, stacked, HD), bf16),
            pltpu.VMEM((pairs, stacked, HD), f32),
            pltpu.VMEM((seqs, n * span, 2 * kw), f32),
            pltpu.VMEM((half, seqs, span, 2 * kw), bf16),
            pltpu.VMEM((half, seqs, span, 2 * kw), bf16),
            pltpu.VMEM((half - 1, seqs, span, 2 * kw), bf16),
            pltpu.VMEM((half - 1, seqs, span, 2 * kw), bf16),
            pltpu.VMEM((tok, width), f32),
            pltpu.VMEM((rows, width), f32),
            line_buf,
            line_buf,
            pltpu.VMEM((nz - 1, rows, width), bf16),
            pltpu.VMEM((nz - 1, rows, width), bf16),
            plane_bufs(2 * qw),
            plane_bufs(2 * kw),
            pltpu.VMEM((nz, experts, 128), bf16),
            pltpu.VMEM((nz, 16, width), bf16),
            pltpu.VMEM((small_rows, width), bf16),
            pltpu.VMEM((small_rows, width), bf16),
            pltpu.VMEM((half, small_rows, width), bf16),
            pltpu.VMEM((half, nz, rows, width), bf16),
        ]
        + [line] * 8
        + [zdma] * 6
        + [hdma, hdma, fdma, fdma]
        + [[hdma] * 8, [hdma] * 8]
        + [dma, dma, fdma, fdma]
        + [dma((6 if half == 4 else half - 1,))] * 2
        + [dma((3,)), pltpu.VMEM((nz, rows, width), bf16)],
        compiler_params=pltpu.CompilerParams(
            collective_id=3, has_side_effects=True, vmem_limit_bytes=58 << 20
        ),
        name="attend_back",
    )(
        gmid,
        mid,
        glog,
        ggrad,
        xn,
        x,
        gain[None],
        wq,
        wk,
        wv,
        wo,
        cos,
        sin,
        q,
        kv,
        lrow,
        att,
        lens,
        mixed,
    )


def finish_kernel(
    out_low,
    igrad_low,
    wall,
    wall2,
    small,
    load,
    dgate_in,
    dup_in,
    ddown_in,
    out_ref,
    igrad_ref,
    q_ref,
    k_ref,
    v_ref,
    o_ref,
    router_ref,
    again_ref,
    egain_ref,
    loss_ref,
    load_ref,
    dgate,
    dup,
    ddown,
    dgate_s,
    dup_s,
    ddown_s,
    sems,
):
    pairs = ((dgate_in, dgate_s, dgate), (dup_in, dup_s, dup), (ddown_in, ddown_s, ddown))
    reads = [pltpu.make_async_copy(p[0], p[1], sems.at[0, i]) for i, p in enumerate(pairs)]
    writes = [pltpu.make_async_copy(p[1], p[2], sems.at[1, i]) for i, p in enumerate(pairs)]
    for copy in reads:
        copy.start()
    qw, kw = q_ref.shape[1], k_ref.shape[1]
    experts = load.shape[1]
    out_ref[...] = out_low[...].astype(f32)
    for read, write in zip(reads, writes):
        read.wait()
        write.start()
    igrad_ref[...] = igrad_low[...].astype(f32)
    chunks, dn, _ = wall.shape
    flat = wall[...].reshape(chunks * dn, 2 * qw).astype(f32)
    q_ref[...] = flat[:, :qw]
    o_ref[...] = flat[:, qw:].T
    flat = wall2[...].reshape(chunks * dn, 2 * kw).astype(f32)
    k_ref[...] = flat[:, :kw]
    v_ref[...] = flat[:, kw:]
    router_ref[...] = small[0:experts, :]
    again_ref[...] = small[experts : experts + 1, :]
    egain_ref[...] = small[experts + 1 : experts + 2, :]
    load_ref[...] = load[...]
    loss_ref[...] = jnp.mean(load[...], -1, keepdims=True)
    for copy in writes:
        copy.wait()


def finish_layer(out_low, igrad_low, wall, wall2, small, load, dgate, dup, ddown, qw, kw):
    tok, width = out_low.shape
    experts = load.shape[1]
    vmem = pl.BlockSpec(memory_space=pltpu.VMEM)
    hbm = pl.BlockSpec(memory_space=pl.ANY)
    sds = jax.ShapeDtypeStruct
    return pl.pallas_call(
        finish_kernel,
        out_shape=[
            sds((tok, width), f32),
            sds((tok, width), f32),
            sds((width, qw), f32),
            sds((width, kw), f32),
            sds((width, kw), f32),
            sds((qw, width), f32),
            sds((experts, width), f32),
            sds((1, width), f32),
            sds((1, width), f32),
            sds((1, 1), f32),
            sds((1, experts), f32),
            sds(dgate.shape, f32),
            sds(dup.shape, f32),
            sds(ddown.shape, f32),
        ],
        in_specs=[vmem] * 6 + [hbm] * 3,
        out_specs=[vmem] * 11 + [hbm] * 3,
        scratch_shapes=[
            pltpu.VMEM(dgate.shape, f32),
            pltpu.VMEM(dup.shape, f32),
            pltpu.VMEM(ddown.shape, f32),
            pltpu.SemaphoreType.DMA((2, 3)),
        ],
        compiler_params=pltpu.CompilerParams(vmem_limit_bytes=60 << 20),
        name="finish",
    )(out_low, igrad_low, wall, wall2, small, load, dgate, dup, ddown)


def shards(
    inputs,
    attention_gain,
    query_weight,
    key_weight,
    value_weight,
    out_weight,
    expert_gain,
    router_weight,
    gate_weight,
    up_weight,
    down_weight,
    routes,
    seq_lens,
    cotangent,
):
    n = lax.axis_size("expert")
    nz = lax.axis_size("tensor")
    tok_rows = inputs.shape[0]
    seq_count = seq_lens.shape[0]
    span_rows = tok_rows // seq_count
    row = lax.broadcasted_iota(jnp.int32, (tok_rows, 128), 0) % span_rows
    lane = lax.broadcasted_iota(jnp.int32, (tok_rows, 128), 1) % (HD // 2)
    frequency = THETA ** (-2.0 * lane.astype(f32) / HD)
    angles = (lax.axis_index("expert") * span_rows + row).astype(f32) * frequency
    cosines = jnp.cos(angles)
    sines = jnp.sin(angles)
    weights = (query_weight, key_weight, value_weight, out_weight, cosines, sines)
    middle, queries, pairs, logs, attended, cot_all = attend_layer(
        n, nz, inputs, attention_gain, *weights, cotangent, seq_lens
    )
    (
        grad_middle,
        logit_grads,
        expert_gain_part,
        expert_load,
        gate_grad,
        up_grad,
        down_grad,
        mixed,
        normed2,
    ) = expert_layer(
        n,
        nz,
        middle,
        expert_gain,
        router_weight,
        routes,
        gate_weight,
        up_weight,
        down_weight,
        cotangent,
        cot_all,
    )
    out_low, igrad_low, packed, packed2, small = return_layer(
        n,
        nz,
        grad_middle,
        middle,
        logit_grads,
        expert_gain_part,
        normed2,
        inputs,
        attention_gain,
        *weights,
        queries,
        pairs,
        logs,
        attended,
        seq_lens,
        mixed,
    )
    (
        output,
        input_grad,
        query_grad,
        key_grad,
        value_grad,
        out_weight_grad,
        router_grad,
        attention_gain_grad,
        expert_gain_grad,
        balance_loss,
        expert_load,
        gate_grad,
        up_grad,
        down_grad,
    ) = finish_layer(
        out_low,
        igrad_low,
        packed,
        packed2,
        small,
        expert_load,
        gate_grad,
        up_grad,
        down_grad,
        query_weight.shape[1],
        key_weight.shape[1],
    )
    return (
        output,
        input_grad,
        balance_loss[0, 0],
        expert_load[0],
        attention_gain_grad[0],
        query_grad,
        key_grad,
        value_grad,
        out_weight_grad,
        expert_gain_grad[0],
        router_grad.T,
        gate_grad,
        up_grad,
        down_grad.reshape(down_weight.shape),
    )


def solution(mesh):
    placed = (
        P("expert", None),
        P(),
        P(None, "tensor"),
        P(None, "tensor"),
        P(None, "tensor"),
        P("tensor", None),
        P(),
        P(),
        P("expert", None, "tensor"),
        P("expert", None, "tensor"),
        P("expert", "tensor", None),
        P("expert", None),
        P(),
        P("expert", None),
    )
    return jax.shard_map(
        shards,
        mesh=mesh,
        in_specs=placed,
        out_specs=(
            P("expert", None),
            P("expert", None),
            P(),
            P(),
            P(),
            P(None, "tensor"),
            P(None, "tensor"),
            P(None, "tensor"),
            P("tensor", None),
            P(),
            P(),
            P("expert", None, "tensor"),
            P("expert", None, "tensor"),
            P("expert", "tensor", None),
        ),
        check_vma=False,
    )
```

```python
import functools

import jax
import jax.numpy as jnp
from jax import lax
from jax.experimental import pallas as pl
from jax.experimental.pallas import tpu as pltpu
from jax.sharding import PartitionSpec as P

HD = 64
EPS = 1e-06
THETA = 10000.0
MESH = pl.DeviceIdType.MESH
f32 = jnp.float32
bf16 = jnp.bfloat16


def dot_nn(left, right):
    return lax.dot_general(left, right, (((1,), (0,)), ((), ())), preferred_element_type=f32)


def dot_nt(left, right):
    return lax.dot_general(left, right, (((1,), (1,)), ((), ())), preferred_element_type=f32)


def dot_tn(left, right):
    return lax.dot_general(left, right, (((0,), (0,)), ((), ())), preferred_element_type=f32)


def remote(src, dst, send_sem, recv_sem, device):
    return pltpu.make_async_remote_copy(
        src_ref=src,
        dst_ref=dst,
        send_sem=send_sem,
        recv_sem=recv_sem,
        device_id=device,
        device_id_type=MESH,
    )


def turn(values, cos, sin, last, forward):
    lane = lax.broadcasted_iota(jnp.int32, (values.shape[0], 128), 1)
    first_half = lax.rem(lane, HD) < HD // 2
    parts = []
    for g in range(values.shape[1] // 128):
        v = values[:, g * 128 : (g + 1) * 128]
        if g * 128 >= last:
            parts.append(v)
            continue
        turned = jnp.where(
            first_half, -pltpu.roll(v, 128 - HD // 2, 1), pltpu.roll(v, HD // 2, 1)
        )
        new = v * cos + turned * sin if forward else v * cos - turned * sin
        if (g + 1) * 128 > last:
            new = jnp.where(lane + g * 128 < last, new, v)
        parts.append(new)
    return jnp.concatenate(parts, 1) if len(parts) > 1 else parts[0]


def greet(n, nz, e, z, sib):
    barrier = pltpu.get_barrier_semaphore()
    pl.semaphore_signal(barrier, inc=1, device_id=(sib, z), device_id_type=MESH)
    for s in range(1, n // 2):
        pl.semaphore_signal(
            barrier, inc=1, device_id=(lax.rem(e + 2 * s, n), z), device_id_type=MESH
        )
    for k in range(1, nz):
        pl.semaphore_signal(barrier, inc=1, device_id=(e, lax.rem(z + k, nz)), device_id_type=MESH)
    return barrier


def expert_kernel(
    n,
    nz,
    big,
    mid_ref,
    gain_ref,
    router_ref,
    routes_ref,
    cot_ref,
    gate_hbm,
    up_hbm,
    down_hbm,
    cot_all,
    *rest,
):
    outs, rest = rest[:9], rest[9:]
    gmid_ref, glog_ref, ggrad_ref, load_ref = outs[:4]
    dgate_hbm, dup_hbm, ddown_hbm, mixed_hbm, normed_hbm = outs[4:]
    xbuf, rest = rest[0], rest[1:]
    if big:
        xstage, rest = rest[0], rest[1:]
    (
        wbuf,
        xn_s,
        wg,
        wu,
        down_ref,
        dgate,
        dup,
        ddown,
        cbuf,
        dg_s,
        du_s,
        wi_s,
        hold,
        osend,
        sin,
        hold_o,
        osend_o,
        sin_o,
        hold_g,
        osend_g,
        sin_g,
        own_s,
        own_g,
        fsend,
        fin,
        fsend_g,
        fin_g,
        zsend,
        zin,
        zsend_g,
        zin_g,
        wsem,
        gsem,
        csem,
        msem,
        lsem,
        zs,
        zr,
        zws,
        zwr,
        xs,
        xr,
        ws,
        wr,
        fs,
        fr,
        wfs,
        wfr,
        gs,
        gr,
        oss,
        osr,
        ggs,
        ggr,
        ps,
        pr,
        pgs,
        pgr,
        zgs,
        zgr,
        zggs,
        zggr,
        picks_s,
    ) = rest
    e = lax.axis_index("expert")
    z = lax.axis_index("tensor")
    core = lax.rem(e, 2)
    other = 1 - core
    me = e // 2
    sib = e + 1 - 2 * core
    half = n // 2
    rows, width = mid_ref.shape
    tok = rows * nz
    experts = router_ref.shape[0]
    local_experts, _, hid = gate_hbm.shape
    inner_w = local_experts * hid
    fc = min(inner_w, 256)
    fslots = fsend.shape[0]
    square = half == 4
    chip_x = me + 1 - 2 * lax.rem(me, 2)
    chip_y = lax.rem(me + 2, 4)
    chip_d = 3 - me
    mid_row = rows // 2

    loads = []
    for el in range(local_experts):
        cols = pl.ds(el * hid, hid)
        loads.append(pltpu.make_async_copy(gate_hbm.at[el], wg.at[:, cols], wsem.at[0, el]))
        loads.append(pltpu.make_async_copy(up_hbm.at[el], wu.at[:, cols], wsem.at[1, el]))
    loads.append(pltpu.make_async_copy(down_hbm, down_ref, wsem.at[2, 0]))
    for copy in loads:
        copy.start()

    def piece_of(g):
        return lax.rem(z + nz - g, nz)

    def cot_start(g, parity, slot):
        zz = piece_of(g)
        for h in range(half):
            start = (2 * h + parity) * tok + zz * rows
            pltpu.make_async_copy(
                cot_all.at[pl.ds(pl.multiple_of(start, 16), rows)],
                cbuf.at[slot, pl.ds(h * rows, rows)],
                csem.at[slot],
            ).start()

    def cot_wait(slot):
        pltpu.make_async_copy(
            cot_all.at[pl.ds(0, half * rows)], cbuf.at[slot], csem.at[slot]
        ).wait()

    cot_start(0, core, 0)
    barrier = greet(n, nz, e, z, sib)

    own_rows = pl.ds(pl.multiple_of(z * rows, 16), rows)
    my_rows = pl.ds(pl.multiple_of(me * rows, 16), rows)
    mid = mid_ref[...]
    scale2 = lax.rsqrt(jnp.mean(mid * mid, -1, keepdims=True) + EPS)
    xn = (mid * scale2 * gain_ref[...]).astype(bf16)
    xn_s[...] = xn
    logits = dot_nt(xn, router_ref[...])
    choices = routes_ref[...].astype(f32)
    top_count = choices.shape[0]
    picks_s[...] = jnp.concatenate([choices, jnp.zeros((128 - top_count, tok), f32)], 0).T
    picks = picks_s[own_rows, 0:top_count].astype(jnp.int32)
    lanes = lax.broadcasted_iota(jnp.int32, (rows, experts), 1)
    chosen = jnp.zeros((rows, experts), f32)
    for k in range(picks.shape[1]):
        chosen = jnp.where(picks[:, k : k + 1] == lanes, 1.0, chosen)
    top = jnp.max(logits, -1, keepdims=True)
    powers = jnp.exp(logits - top)
    probs = powers / jnp.sum(powers, -1, keepdims=True)
    low_logits = jnp.where(chosen > 0.0, logits, -1e30)
    ctop = jnp.max(low_logits, -1, keepdims=True)
    cpow = jnp.exp(low_logits - ctop)
    comb = cpow / jnp.sum(cpow, -1, keepdims=True)
    padded = jnp.concatenate([comb, jnp.zeros((rows, 128 - experts), f32)], 1)
    if rows < 128:
        padded = jnp.concatenate([padded, jnp.zeros((128 - rows, 128), f32)], 0)
    piece = padded.T[:experts]
    lane_pad = jnp.zeros((1, 128 - experts), f32)
    cnt = jnp.concatenate([jnp.sum(chosen, 0, keepdims=True), lane_pad], 1)
    psum = jnp.concatenate([jnp.sum(probs, 0, keepdims=True), lane_pad], 1)
    psum_hi = psum.astype(bf16).astype(f32)
    stats = jnp.concatenate([cnt, psum_hi, psum - psum_hi, jnp.zeros((13, 128), f32)], 0)
    wbuf[z, core, me] = jnp.concatenate([piece, stats], 0).astype(bf16)
    if big:
        copy = pltpu.make_async_copy(xn_s, xbuf.at[z, core, my_rows], lsem)
        copy.start()
        copy.wait()
    else:
        xbuf[z, core, my_rows] = xn
    pl.semaphore_wait(barrier, half + nz - 1)

    def z_row(zz, k, to):
        ref = xbuf.at[zz, core, my_rows]
        return remote(ref, ref, zs.at[k - 1], zr.at[k - 1], (e, to))

    def z_small(zz, k, to):
        ref = wbuf.at[zz, core, me]
        return remote(ref, ref, zws.at[k - 1], zwr.at[k - 1], (e, to))

    def x_row(zz, h, g, s, to):
        ref = xbuf.at[zz, core, pl.ds(pl.multiple_of(h * rows, 16), rows)]
        return remote(ref, ref, xs.at[g, s], xr.at[g, s], (to, z))

    def x_small(zz, h, g, s, to):
        ref = wbuf.at[zz, core, h]
        return remote(ref, ref, ws.at[g, s], wr.at[g, s], (to, z))

    def x_part(zz, h, first, count, g, i, to):
        start = pl.multiple_of(h * rows + first, 16)
        ref = xbuf.at[zz, core, pl.ds(start, count)]
        return remote(ref, ref, xs.at[g, i], xr.at[g, i], (2 * to + core, z))

    def push_piece(g):
        zz = piece_of(g)
        if square:
            x_part(zz, me, 0, rows, g, 0, chip_x).start()
            x_part(zz, me, 0, rows, g, 1, chip_y).start()
        for s in range(1, half):
            to = lax.rem(e + 2 * s, n)
            if not square:
                x_row(zz, me, g, s, to).start()
            x_small(zz, me, g, s, to).start()

    def relays(g):
        zz = piece_of(g)
        return (
            x_part(zz, chip_x, 0, mid_row, g, 2, chip_y),
            x_part(zz, chip_y, mid_row, rows - mid_row, g, 3, chip_x),
        )

    def relay_pieces(g):
        zz = piece_of(g)
        low, high = relays(g)
        x_part(zz, chip_x, 0, rows, g, 0, chip_x).wait_recv()
        low.start()
        x_part(zz, chip_y, 0, rows, g, 1, chip_y).wait_recv()
        high.start()

    push_piece(jnp.int32(0))
    def z_push(k):
        z_row(z, k, lax.rem(z + k, nz)).start()
        z_small(z, k, lax.rem(z + k, nz)).start()

    for k in range(1, min(nz, 2) if square else nz):
        z_push(k)

    if square:
        relay_pieces(jnp.int32(0))
        if nz > 2:
            z_push(2)

    dgate[...] = jnp.zeros_like(dgate)
    dup[...] = jnp.zeros_like(dup)
    ddown[...] = jnp.zeros_like(ddown)
    for copy in loads:
        copy.wait()

    sel_row = lax.broadcasted_iota(jnp.int32, (experts, fc), 0)
    sel_col = lax.broadcasted_iota(jnp.int32, (experts, fc), 1)

    def block(zz, parity, slot, dst, dst_o, dst_g, dslot):
        if big:
            copy = pltpu.make_async_copy(xbuf.at[zz, parity], xstage, lsem)
            copy.start()
            copy.wait()
            x_ref = xstage
        else:
            x_ref = xbuf.at[zz, parity]
        c_ref = cbuf.at[slot]
        sums = [jnp.zeros((experts, rows), f32) for _ in range(half)]
        for q in range(inner_w // fc):
            cols = slice(q * fc, (q + 1) * fc)
            x = x_ref[...]
            gate_val = dot_nn(x, wg[:, cols])
            up_val = dot_nn(x, wu[:, cols])
            back = dot_nt(c_ref[...], down_ref[cols, :])
            select = jnp.where(
                sel_row == e * local_experts + (q * fc + sel_col) // hid, 1.0, 0.0
            ).astype(bf16)
            wide = jnp.concatenate(
                [dot_tn(wbuf[zz, parity, h, :experts, :], select)[:rows] for h in range(half)], 0
            )
            sig = 1.0 / (1.0 + jnp.exp(-gate_val))
            silu = gate_val * sig
            inner = silu * up_val
            wi_s[:, cols] = (inner * wide).astype(bf16)
            scaled = back * wide
            dg_s[:, cols] = (scaled * up_val * (sig * (1.0 + gate_val * (1.0 - sig)))).astype(bf16)
            du_s[:, cols] = (scaled * silu).astype(bf16)
            both = (inner * back).astype(bf16)
            for h in range(half):
                sums[h] = sums[h] + dot_nt(select, both[h * rows : (h + 1) * rows])
        for h in range(half):
            gap = jnp.zeros((experts, 128 - rows), f32)
            dst_g[dslot, h] = jnp.concatenate([sums[h], gap], 1).astype(bf16)
        for h in range(width // 256):
            cols = slice(h * 256, (h + 1) * 256)
            dst[dslot, :, cols] = (
                dot_nt(dg_s[...], wg[cols, :]) + dot_nt(du_s[...], wu[cols, :])
            ).astype(bf16)
            dst_o[dslot, :, cols] = dot_nn(wi_s[...], down_ref[:, cols]).astype(bf16)
        for h in range(width // 256):
            cols = slice(h * 256, (h + 1) * 256)
            x_part = x_ref[:, cols]
            gate_part = dot_tn(x_part, dg_s[...])
            up_part = dot_tn(x_part, du_s[...])
            for el in range(local_experts):
                dgate[el, cols, :] += gate_part[:, el * hid : (el + 1) * hid]
                dup[el, cols, :] += up_part[:, el * hid : (el + 1) * hid]
            ddown[:, cols] += dot_tn(wi_s[...], c_ref[:, cols])

    def gives(slot):
        return [
            remote(osend.at[slot], sin.at[slot], gs.at[slot], gr.at[slot], (sib, z)),
            remote(osend_g.at[slot], sin_g.at[slot], ggs.at[slot], ggr.at[slot], (sib, z)),
            remote(osend_o.at[slot], sin_o.at[slot], oss.at[slot], osr.at[slot], (sib, z)),
        ]

    def finals(g, s, to):
        at = lax.rem(g, fslots)
        rows_copy = []
        if not square:
            rows_copy = [
                remote(
                    fsend.at[at, s - 1], fin.at[g, s - 1], ps.at[g, s - 1], pr.at[g, s - 1], (to, z)
                )
            ]
        return rows_copy + [
            remote(
                fsend_g.at[at, s - 1],
                fin_g.at[g, s - 1],
                pgs.at[g, s - 1],
                pgr.at[g, s - 1],
                (to, z),
            ),
        ]

    def half_copy(g, buf, upper, i, chip):
        first, count = (mid_row, rows - mid_row) if upper else (0, mid_row)
        return remote(
            fsend.at[g, buf, pl.ds(first, count)],
            fin.at[g, buf, pl.ds(first, count)],
            ps.at[g, i],
            pr.at[g, i],
            (2 * chip + core, z),
        )

    def half_copies(g):
        return [
            half_copy(g, 2, False, 0, chip_x),
            half_copy(g, 2, True, 1, chip_y),
            half_copy(g, 0, False, 2, chip_x),
            half_copy(g, 1, True, 3, chip_y),
            half_copy(g, 1, False, 4, chip_y),
            half_copy(g, 0, True, 5, chip_x),
        ]

    def chip_sum(slot, chip, upper):
        first, count = (mid_row, rows - mid_row) if upper else (0, mid_row)
        at = pl.ds(pl.multiple_of(chip * rows + first, 16), count)
        return hold[slot, at, :].astype(f32) + sin[slot, at, :].astype(f32)

    def direct_stage(g):
        slot = lax.rem(g, 2)
        copies = half_copies(g)
        fsend[g, 2, :mid_row] = chip_sum(slot, chip_d, False).astype(bf16)
        copies[0].start()
        fsend[g, 2, mid_row:] = chip_sum(slot, chip_d, True).astype(bf16)
        copies[1].start()
        fsend[g, 0, :mid_row] = chip_sum(slot, chip_x, False).astype(bf16)
        copies[2].start()
        fsend[g, 1, mid_row:] = chip_sum(slot, chip_y, True).astype(bf16)
        copies[3].start()

    def relay_stage(g):
        slot = lax.rem(g, 2)
        copies = half_copies(g)
        copies[0].wait_recv()
        passed = chip_sum(slot, chip_y, False) + fin[g, 2, :mid_row].astype(f32)
        fsend[g, 1, :mid_row] = passed.astype(bf16)
        copies[4].start()
        copies[1].wait_recv()
        passed = chip_sum(slot, chip_x, True) + fin[g, 2, mid_row:].astype(f32)
        fsend[g, 0, mid_row:] = passed.astype(bf16)
        copies[5].start()

    def lasts(k, to):
        return [
            remote(zsend.at[k - 1], zin.at[k - 1], zgs.at[k - 1], zgr.at[k - 1], (e, to)),
            remote(zsend_g.at[k - 1], zin_g.at[k - 1], zggs.at[k - 1], zggr.at[k - 1], (e, to)),
        ]

    def mixed_copy(g, slot):
        return pltpu.make_async_copy(hold_o.at[slot], mixed_hbm.at[piece_of(g)], msem.at[slot])

    def plane_stage(g):
        slot = lax.rem(g, 2)
        for copy in gives(slot)[:2]:
            copy.wait_recv()
        if fslots < nz:

            @pl.when(g >= fslots)
            def _():
                for s in range(1, half):
                    for copy in finals(g - fslots, s, sib):
                        copy.wait_send()

        spot = lax.rem(g, fslots)
        if square:
            direct_stage(g)
        for s in range(1, half):
            h = lax.rem(me + half - s, half)
            at = pl.ds(pl.multiple_of(h * rows, 16), rows)
            if not square:
                fsend[spot, s - 1] = (
                    hold[slot, at, :].astype(f32) + sin[slot, at, :].astype(f32)
                ).astype(bf16)
            fsend_g[spot, s - 1] = (hold_g[slot, h].astype(f32) + sin_g[slot, h].astype(f32)).astype(
                bf16
            )
            for copy in finals(g, s, lax.rem(e - 2 * s + n, n)):
                copy.start()
        own_s[g] = hold[slot, my_rows, :].astype(f32) + sin[slot, my_rows, :].astype(f32)
        own_g[g] = hold_g[slot, me].astype(f32) + sin_g[slot, me].astype(f32)

    def mixed_stage(g):
        slot = lax.rem(g, 2)
        gives(slot)[2].wait_recv()
        hold_o[slot] = (hold_o[slot].astype(f32) + sin_o[slot].astype(f32)).astype(bf16)
        mixed_copy(g, slot).start()

    def tensor_stage(g):
        total = own_s[g]
        total_g = own_g[g]
        for s in range(1, half):
            for copy in finals(g, s, sib):
                copy.wait_recv()
            if not square:
                total = total + fin[g, s - 1].astype(f32)
            total_g = total_g + fin_g[g, s - 1].astype(f32)

        if square:
            for copy in half_copies(g)[2:]:
                copy.wait_recv()
            total = total + fin[g, 0].astype(f32) + fin[g, 1].astype(f32)

        @pl.when(g == 0)
        def _():
            own_s[0] = total
            own_g[0] = total_g

        @pl.when(g > 0)
        def _():
            zsend[g - 1] = total.astype(bf16)
            zsend_g[g - 1] = total_g.astype(bf16)
            for copy in lasts(g, piece_of(g)):
                copy.start()

    def step(g, carry):
        zz = piece_of(g)
        slot = lax.rem(g, 2)

        @pl.when(g < nz - 1)
        def _():
            coming = piece_of(g + 1)
            z_row(coming, g + 1, coming).wait_recv()
            z_small(coming, g + 1, coming).wait_recv()
            push_piece(g + 1)

        if square:
            x_part(zz, chip_d, 0, mid_row, g, 2, chip_y).wait_recv()
            x_part(zz, chip_d, mid_row, rows - mid_row, g, 3, chip_x).wait_recv()

        for s in range(1, half):
            h = lax.rem(me + half - s, half)
            src = 2 * h + core
            if not square:
                x_row(zz, h, g, s, src).wait_recv()
            x_small(zz, h, g, s, src).wait_recv()
        for copy in forward(zz, core, g):
            copy.start()
        cot_start(g, other, 1)
        cot_wait(0)

        @pl.when(g >= 2)
        def _():
            mixed_copy(g - 2, slot).wait()

        block(zz, core, 0, hold, hold_o, hold_g, slot)
        if square:

            @pl.when(g == 0)
            def _():
                for k in range(3, nz):
                    z_push(k)

            @pl.when(g < nz - 1)
            def _():
                relay_pieces(g + 1)


        @pl.when(g < nz - 1)
        def _():
            cot_start(g + 1, core, 0)

        @pl.when(g >= 2)
        def _():
            tensor_stage(g - 2)

        @pl.when(g >= 1)
        def _():
            plane_stage(g - 1)
            mixed_stage(g - 1)

        @pl.when(g >= 2)
        def _():
            for copy in gives(slot):
                copy.wait_send()

        for copy in forward(zz, other, g):
            copy.wait_recv()
        cot_wait(1)
        block(zz, other, 1, osend, osend_o, osend_g, slot)
        for copy in gives(slot):
            copy.start()
        if square:

            @pl.when(g >= 1)
            def _():
                relay_stage(g - 1)

        return carry

    def forward(zz, parity, g):
        ref = xbuf.at[zz, parity]
        small = wbuf.at[zz, parity]
        return (
            remote(ref, ref, fs.at[g], fr.at[g], (sib, z)),
            remote(small, small, wfs.at[g], wfr.at[g], (sib, z)),
        )

    lax.fori_loop(0, nz, step, 0)
    grads = [
        pltpu.make_async_copy(dgate, dgate_hbm, gsem.at[0]),
        pltpu.make_async_copy(dup, dup_hbm, gsem.at[1]),
        pltpu.make_async_copy(ddown, ddown_hbm, gsem.at[2]),
        pltpu.make_async_copy(xbuf.at[:, core, my_rows, :], normed_hbm, gsem.at[3]),
    ]
    plane_stage(jnp.int32(nz - 1))
    for copy in grads:
        copy.start()
    if nz >= 2:
        tensor_stage(jnp.int32(nz - 2))
    if square:
        relay_stage(jnp.int32(nz - 1))

    def total_stats(j, carry):
        for zz in range(nz):
            for parity in range(2):
                carry = carry + wbuf[zz, parity, j, experts:, :].astype(f32)
        return carry

    stats = lax.fori_loop(0, half, total_stats, jnp.zeros((16, 128), f32))
    total_rows = n * tok
    share = stats[0:1, :experts] / (total_rows * top_count)
    load_ref[...] = (
        experts * experts * share * ((stats[1:2, :experts] + stats[2:3, :experts]) / total_rows)
    )
    loss_w = experts * share / total_rows
    mixed_stage(jnp.int32(nz - 1))
    tensor_stage(jnp.int32(nz - 1))

    gate_sums = own_g[0]
    grad_rows = own_s[0]
    for k in range(1, nz):
        for copy in lasts(k, z):
            copy.wait_recv()
        gate_sums = gate_sums + zin_g[k - 1].astype(f32)
        grad_rows = grad_rows + zin[k - 1].astype(f32)
    grow = jnp.concatenate([gate_sums, jnp.zeros((128 - experts, 128), f32)], 0).T
    grad_gates = grow[:rows, :experts]
    grad_logits = comb * (grad_gates - jnp.sum(grad_gates * comb, -1, keepdims=True))
    grad_logits = grad_logits + probs * (loss_w - jnp.sum(loss_w * probs, -1, keepdims=True))
    low_grad = grad_logits.astype(bf16)
    wide_grad = jnp.concatenate([grad_logits, jnp.zeros((rows, 128 - experts), f32)], 1)
    if rows < 128:
        wide_grad = jnp.concatenate([wide_grad, jnp.zeros((128 - rows, 128), f32)], 0)
    glog_ref[...] = wide_grad.T[:experts].astype(bf16)
    grad_rows = grad_rows + dot_nn(low_grad, router_ref[...])
    mid = mid_ref[...]
    ggrad_ref[...] = jnp.sum(grad_rows * mid * scale2, 0, keepdims=True)
    gained = grad_rows * gain_ref[...]
    gmid_ref[...] = (
        cot_ref[own_rows, :]
        + scale2 * gained
        - mid * (scale2 * scale2 * scale2) * jnp.mean(gained * mid, -1, keepdims=True)
    )

    for copy in grads:
        copy.wait()
    for k in range(1, nz):
        z_row(z, k, z).wait_send()
        z_small(z, k, z).wait_send()
        for copy in lasts(k, z):
            copy.wait_send()
    for g in range(max(0, nz - 2), nz):
        mixed_copy(jnp.int32(g), g % 2).wait()
        for copy in gives(g % 2):
            copy.wait_send()

    def drained(g, carry):
        if square:
            x_part(z, me, 0, rows, g, 0, chip_x).wait_send()
            x_part(z, me, 0, rows, g, 1, chip_y).wait_send()
            for copy in relays(g) + tuple(half_copies(g)):
                copy.wait_send()
        for s in range(1, half):
            if not square:
                x_row(z, me, g, s, sib).wait_send()
            x_small(z, me, g, s, sib).wait_send()
        for copy in forward(z, core, g):
            copy.wait_send()
        return carry

    lax.fori_loop(0, nz, drained, 0)

    def sums_sent(g, carry):
        for s in range(1, half):
            for copy in finals(g, s, sib):
                copy.wait_send()
        return carry

    lax.fori_loop(nz - fslots, nz, sums_sent, 0)


def expert_layer(n, nz, mid, gain, router, routes, gate, up, down, cot, cot_all):
    rows, width = mid.shape
    experts = router.shape[1]
    local_experts, _, hid = gate.shape
    inner_w = local_experts * hid
    half = n // 2
    batch = half * rows
    big = n > 8
    fslots = 2 if big else nz
    dma = pltpu.SemaphoreType.DMA
    vmem = pl.BlockSpec(memory_space=pltpu.VMEM)
    hbm = pl.BlockSpec(memory_space=pl.ANY)
    sds = jax.ShapeDtypeStruct
    out_shape = [
        sds((rows, width), f32),
        sds((experts, 128), bf16),
        sds((1, width), f32),
        sds((1, experts), f32),
        sds((local_experts, width, hid), f32),
        sds((local_experts, width, hid), f32),
        sds((inner_w, width), f32),
        sds((nz, batch, width), bf16),
        sds((nz, rows, width), bf16),
    ]
    out_specs = [vmem] * 4 + [hbm] * 5
    scratch = []
    if big:
        out_shape.append(sds((nz, 2, batch, width), bf16))
        out_specs.append(hbm)
        scratch.append(pltpu.VMEM((batch, width), bf16))
    else:
        scratch.append(pltpu.VMEM((nz, 2, batch, width), bf16))
    pair = pltpu.VMEM((2, batch, width), bf16)
    small = pltpu.VMEM((2, half, experts, 128), bf16)
    scratch += [
        pltpu.VMEM((nz, 2, half, experts + 16, 128), bf16),
        pltpu.VMEM((rows, width), bf16),
        pltpu.VMEM((width, inner_w), bf16),
        pltpu.VMEM((width, inner_w), bf16),
        pltpu.VMEM((inner_w, width), bf16),
        pltpu.VMEM((local_experts, width, hid), f32),
        pltpu.VMEM((local_experts, width, hid), f32),
        pltpu.VMEM((inner_w, width), f32),
        pair,
        pltpu.VMEM((batch, inner_w), bf16),
        pltpu.VMEM((batch, inner_w), bf16),
        pltpu.VMEM((batch, inner_w), bf16),
        pair,
        pair,
        pair,
        pair,
        pair,
        pair,
        small,
        small,
        small,
        pltpu.VMEM((nz, rows, width), f32),
        pltpu.VMEM((nz, experts, 128), f32),
        pltpu.VMEM((fslots, half - 1, rows, width), bf16),
        pltpu.VMEM((nz, half - 1, rows, width), bf16),
        pltpu.VMEM((fslots, half - 1, experts, 128), bf16),
        pltpu.VMEM((nz, half - 1, experts, 128), bf16),
        pltpu.VMEM((nz - 1, rows, width), bf16),
        pltpu.VMEM((nz - 1, rows, width), bf16),
        pltpu.VMEM((nz - 1, experts, 128), bf16),
        pltpu.VMEM((nz - 1, experts, 128), bf16),
        dma((3, local_experts)),
        dma((4,)),
        dma((2,)),
        dma((2,)),
        dma,
    ]
    scratch += [dma((nz - 1,))] * 4
    scratch += [dma((nz, half))] * 4
    scratch += [dma((nz,))] * 4
    scratch += [dma((2,))] * 6
    scratch += [dma((nz, 6 if half == 4 else half - 1))] * 2
    scratch += [dma((nz, half - 1))] * 2
    scratch += [dma((nz - 1,))] * 4 + [pltpu.VMEM((nz * rows, 128), f32)]
    return pl.pallas_call(
        functools.partial(expert_kernel, n, nz, big),
        out_shape=out_shape,
        in_specs=[vmem] * 5 + [hbm] * 4,
        out_specs=out_specs,
        scratch_shapes=scratch,
        compiler_params=pltpu.CompilerParams(
            collective_id=1, has_side_effects=True, vmem_limit_bytes=60 << 20
        ),
        name="experts",
    )(mid, gain[None], router.T, routes.T, cot, gate, up, down.reshape(inner_w, width), cot_all)[:9]


def attend_kernel(
    n,
    nz,
    x_ref,
    gain_ref,
    wq_ref,
    wk_ref,
    wv_ref,
    wo_ref,
    cos_ref,
    sin_ref,
    cot_ref,
    lens_ref,
    mid_ref,
    q_ref,
    kv_ref,
    lrow_ref,
    att_ref,
    cot_hbm,
    wqkv,
    wfull,
    qst_s,
    m_s,
    l_s,
    o_s,
    att_low,
    acol,
    ks,
    kr,
    kfs,
    kfr,
    zgs,
    zgr,
    gos,
    gor,
    gps,
    gpr,
    cot_low,
    cs,
    cr,
    cps,
    cpr,
    csem,
):
    e = lax.axis_index("expert")
    z = lax.axis_index("tensor")
    core = lax.rem(e, 2)
    sib = e + 1 - 2 * core
    half = n // 2
    me = e // 2
    tok, width = x_ref.shape
    rows = tok // nz
    qw = wq_ref.shape[1]
    kw = wk_ref.shape[1]
    seqs = kv_ref.shape[0]
    span = tok // seqs
    heads = kw // HD
    groups = qw // kw
    barrier = greet(n, nz, e, z, sib)

    wqkv[:, 0:qw] = wq_ref[...]
    wqkv[:, qw : qw + kw] = wk_ref[...]
    wqkv[:, qw + kw :] = wv_ref[...]
    x = x_ref[...].astype(f32)
    scale1 = lax.rsqrt(jnp.mean(x * x, -1, keepdims=True) + EPS)
    normed = (x * scale1 * gain_ref[...]).astype(bf16)
    lin = dot_nn(normed, wqkv[...])
    turned = turn(lin, cos_ref[...], sin_ref[...], qw + kw, True).astype(bf16)
    q_ref[...] = turned[:, :qw]
    for s in range(seqs):
        kv_ref[s, pl.ds(pl.multiple_of(e * span, 16), span)] = turned[
            s * span : (s + 1) * span, qw:
        ]
    cot_low[...] = cot_ref[...].astype(bf16)
    cot_local = pltpu.make_async_copy(
        cot_low, cot_hbm.at[pl.ds(pl.multiple_of(e * tok, 16), tok)], csem
    )
    cot_local.start()
    pl.semaphore_wait(barrier, half + nz - 1)

    def rows_of(j, s):
        return kv_ref.at[s, pl.ds(pl.multiple_of(j * span, 16), span)]

    half_rows = qw // 2
    my_half = pl.ds(pl.multiple_of(core * half_rows, 16), half_rows)

    def weight_send(k):
        to = (e, lax.rem(z + k, nz))
        return remote(
            wo_ref.at[my_half], wfull.at[z, my_half], gos.at[k - 1], gor.at[k - 1], to
        )

    def weight_copy(zz, k, to):
        ref = wfull.at[zz, my_half]
        return remote(ref, ref, gos.at[k - 1], gor.at[k - 1], (e, to))

    def weight_pass(zz, which, k):
        at = pl.ds(pl.multiple_of(which * half_rows, 16), half_rows)
        ref = wfull.at[zz, at]
        return remote(ref, ref, gps.at[k - 1], gpr.at[k - 1], (sib, z))

    for t in range(1, half):
        to = (lax.rem(e + 2 * t, n), z)
        for s in range(seqs):
            remote(rows_of(e, s), rows_of(e, s), ks.at[t, s], kr.at[t, s], to).start()
    for s in range(seqs):
        remote(rows_of(e, s), rows_of(e, s), kfs.at[0, s], kfr.at[0, s], (sib, z)).start()
    for k in range(1, nz):
        weight_send(k).start()

    square = half == 4
    chip_x = me + 1 - 2 * lax.rem(me, 2)
    chip_y = lax.rem(me + 2, 4)
    chip_d = 3 - me
    low_rows = tok // 2

    def cot_at(chip, first=0, count=tok):
        start = (2 * chip + core) * tok + first
        return cot_hbm.at[pl.ds(pl.multiple_of(start, 16), count)]

    def cot_send(i, chip):
        return remote(cot_low, cot_at(me), cs.at[i], cr.at[i], (2 * chip + core, z))

    def cot_recv(i, chip):
        return remote(cot_at(chip), cot_at(chip), cs.at[i], cr.at[i], (2 * chip + core, z))

    def cot_relay(i, chip, to):
        ref = cot_at(chip, 0, low_rows) if i == 2 else cot_at(chip, low_rows, tok - low_rows)
        return remote(ref, ref, cs.at[i], cr.at[i], (2 * to + core, z))

    def cot_pass(t, chip, parity):
        start = (2 * chip + parity) * tok
        ref = cot_hbm.at[pl.ds(pl.multiple_of(start, 16), tok)]
        return remote(ref, ref, cps.at[t], cpr.at[t], (sib, z))

    if square:
        cot_pushes = [cot_send(0, chip_x), cot_send(1, chip_y)]
        cot_chips = [me, chip_x, chip_y, chip_d]
    else:
        cot_pushes = [cot_send(t - 1, lax.rem(me + t, half)) for t in range(1, half)]
        cot_chips = [lax.rem(me + half - t, half) for t in range(half)]
    for copy in cot_pushes:
        copy.start()
    cot_local.wait()
    cot_pass(0, me, core).start()
    wfull[z] = wo_ref[...]

    def forward(t, carry):
        src = lax.rem(e - 2 * t + n, n)
        for s in range(seqs):
            remote(rows_of(src, s), rows_of(src, s), ks.at[t, s], kr.at[t, s], (src, z)).wait_recv()
            remote(rows_of(src, s), rows_of(src, s), kfs.at[t, s], kfr.at[t, s], (sib, z)).start()
        return carry

    lax.fori_loop(1, half, forward, 0)

    def arrive(t, carry):
        src = lax.rem(sib - 2 * t + n, n)
        for s in range(seqs):
            remote(
                rows_of(src, s), rows_of(src, s), kfs.at[t, s], kfr.at[t, s], (sib, z)
            ).wait_recv()
        return carry

    lax.fori_loop(0, half, arrive, 0)

    ck = 2 * span
    last = (e * span + span - 1) // ck
    stacked = groups * span
    qpos = lax.broadcasted_iota(jnp.int32, (stacked, ck), 0)
    qpos = e * span + lax.rem(qpos, span)
    kiota = lax.broadcasted_iota(jnp.int32, (stacked, ck), 1)
    klane = lax.broadcasted_iota(jnp.int32, (1, ck), 1)
    m_s[...] = jnp.full_like(m_s, -1e30)
    l_s[...] = jnp.zeros_like(l_s)
    o_s[...] = jnp.zeros_like(o_s)
    for s in range(seqs):
        for h in range(heads):
            qst_s[s * heads + h] = jnp.concatenate(
                [
                    q_ref[
                        s * span : (s + 1) * span,
                        (h * groups + g) * HD : (h * groups + g + 1) * HD,
                    ]
                    for g in range(groups)
                ],
                0,
            ) * jnp.array(HD ** (-0.5), bf16)

    def chunk(c, diagonal):
        at = pl.ds(pl.multiple_of(c * ck, 16), ck)
        for s in range(seqs):
            for h in range(heads):
                i = s * heads + h
                keys = kv_ref[s, at, h * HD : (h + 1) * HD]
                vals = kv_ref[s, at, kw + h * HD : kw + (h + 1) * HD]
                scores = dot_nt(qst_s[i], keys)
                if diagonal:
                    kpos = kiota + c * ck
                    scores = jnp.where((kpos <= qpos) & (kpos < lens_ref[s]), scores, -1e30)
                else:
                    scores = scores + jnp.where(klane + c * ck < lens_ref[s], 0.0, -1e30)
                old = m_s[i, :, 0:1]
                new = jnp.maximum(old, jnp.max(scores, -1, keepdims=True))
                weights = jnp.exp(scores - new)
                shrink = jnp.exp(old - new)
                m_s[i] = jnp.broadcast_to(new, (stacked, 128))
                l_s[i] = l_s[i] * shrink + jnp.sum(weights, -1, keepdims=True)
                o_s[i] = o_s[i] * shrink + dot_nn(weights.astype(bf16), vals)

    def whole_chunk(c, carry):
        chunk(c, False)
        return carry

    lax.fori_loop(0, last, whole_chunk, 0)
    chunk(last, True)
    for s in range(seqs):
        for h in range(heads):
            i = s * heads + h
            result = o_s[i] / l_s[i, :, 0:HD]
            for g in range(groups):
                cols = slice((h * groups + g) * HD, (h * groups + g + 1) * HD)
                att_ref[s * span : (s + 1) * span, cols] = result[g * span : (g + 1) * span]
            logs = m_s[i] + jnp.log(l_s[i])
            lrow_ref[i] = logs.T[0:8]

    att_low[...] = att_ref[...].astype(bf16)
    own_rows = pl.ds(pl.multiple_of(z * rows, 16), rows)

    def row_copy(k, to):
        src = att_low.at[pl.ds(pl.multiple_of(to * rows, 16), rows)]
        return remote(src, acol.at[z], zgs.at[k - 1], zgr.at[k - 1], (e, to))

    for k in range(1, nz):
        row_copy(k, lax.rem(z + k, nz)).start()
    acol[z] = att_low[own_rows, :]
    for k in range(1, nz):
        zz = lax.rem(z + nz - k, nz)
        weight_copy(zz, k, zz).wait_recv()
        weight_pass(zz, core, k).start()
    if square:
        cot_recv(0, chip_x).wait_recv()
        cot_relay(2, chip_x, chip_y).start()
        cot_pass(1, chip_x, core).start()
        cot_recv(1, chip_y).wait_recv()
        cot_relay(3, chip_y, chip_x).start()
        cot_pass(2, chip_y, core).start()
    else:
        for t in range(1, half):
            cot_recv(t - 1, cot_chips[t]).wait_recv()
            cot_pass(t, cot_chips[t], core).start()
    for k in range(1, nz):
        row_copy(k, lax.rem(z + nz - k, nz)).wait_recv()
        weight_pass(lax.rem(z + nz - k, nz), 1 - core, k).wait_recv()
    mid = x_ref[own_rows, :].astype(f32)
    for zz in range(nz):
        mid = mid + dot_nn(acol[zz], wfull[zz])
    mid_ref[...] = mid
    if square:
        cot_relay(2, chip_d, chip_y).wait_recv()
        cot_relay(3, chip_d, chip_x).wait_recv()
        cot_pass(3, chip_d, core).start()
        cot_relay(2, chip_x, chip_y).wait_send()
        cot_relay(3, chip_y, chip_x).wait_send()
    for copy in cot_pushes:
        copy.wait_send()
    for t in range(half):
        cot_pass(t, cot_chips[t], 1 - core).wait_recv()
        cot_pass(t, cot_chips[t], core).wait_send()
    for k in range(1, nz):
        row_copy(k, lax.rem(z + k, nz)).wait_send()
        weight_send(k).wait_send()
        weight_pass(lax.rem(z + nz - k, nz), core, k).wait_send()

    def sent(t, carry):
        for s in range(seqs):

            @pl.when(t > 0)
            def _():
                remote(
                    rows_of(e, s), rows_of(e, s), ks.at[t, s], kr.at[t, s], (sib, z)
                ).wait_send()

            remote(rows_of(e, s), rows_of(e, s), kfs.at[t, s], kfr.at[t, s], (sib, z)).wait_send()
        return carry

    lax.fori_loop(0, half, sent, 0)


def attend_layer(n, nz, x, gain, wq, wk, wv, wo, cos, sin, cot, lens):
    tok, width = x.shape
    rows = tok // nz
    qw, kw = wq.shape[1], wk.shape[1]
    seqs = lens.shape[0]
    span = tok // seqs
    half = n // 2
    stacked = (qw // kw) * span
    pairs = seqs * (kw // HD)
    dma = pltpu.SemaphoreType.DMA
    vmem = pl.BlockSpec(memory_space=pltpu.VMEM)
    sds = jax.ShapeDtypeStruct
    return pl.pallas_call(
        functools.partial(attend_kernel, n, nz),
        out_shape=[
            sds((rows, width), f32),
            sds((tok, qw), bf16),
            sds((seqs, n * span, 2 * kw), bf16),
            sds((seqs * (kw // HD), 8, stacked), f32),
            sds((tok, qw), f32),
            sds((n * tok, width), bf16),
        ],
        in_specs=[vmem] * 9 + [pl.BlockSpec(memory_space=pltpu.SMEM)],
        out_specs=[vmem] * 5 + [pl.BlockSpec(memory_space=pl.ANY)],
        scratch_shapes=[
            pltpu.VMEM((width, qw + 2 * kw), bf16),
            pltpu.VMEM((nz, qw, width), bf16),
            pltpu.VMEM((pairs, stacked, HD), bf16),
            pltpu.VMEM((pairs, stacked, 128), f32),
            pltpu.VMEM((pairs, stacked, 128), f32),
            pltpu.VMEM((pairs, stacked, HD), f32),
            pltpu.VMEM((tok, qw), bf16),
            pltpu.VMEM((nz, rows, qw), bf16),
        ]
        + [dma((half, seqs))] * 4
        + [dma((nz - 1,))] * 6
        + [pltpu.VMEM((tok, width), bf16)]
        + [dma((max(half, 4),))] * 4
        + [dma],
        compiler_params=pltpu.CompilerParams(
            collective_id=2, has_side_effects=True, vmem_limit_bytes=60 << 20
        ),
        name="attend",
    )(x, gain[None], wq, wk, wv, wo, cos, sin, cot, lens)


def return_kernel(
    n,
    nz,
    gmid_ref,
    mid_ref,
    glog_ref,
    ggrad_ref,
    xn_ref,
    x_ref,
    gain_ref,
    wq_ref,
    wk_ref,
    wv_ref,
    wo_ref,
    cos_ref,
    sin_ref,
    q_ref,
    kv_ref,
    lrow_ref,
    att_ref,
    lens_ref,
    mixed_hbm,
    obuf,
    igbuf,
    wall,
    wall2,
    small_ref,
    wqkv,
    gat,
    datt,
    dq_s,
    qst_s,
    dst_s,
    acc_q,
    dkv,
    kvo,
    kvi,
    kvf,
    kvr,
    part,
    sums,
    csend,
    crecv,
    osend,
    orecv,
    wbufs,
    wbufs2,
    sz1,
    sz2,
    sown,
    ssib,
    schip,
    ofin,
    zas,
    zar,
    zos,
    zor,
    zis,
    zir,
    zps,
    zpr,
    zqs,
    zqr,
    z1s,
    z1r,
    z2s,
    z2r,
    kos,
    kor,
    kfs,
    kfr,
    wsems,
    wsems2,
    sbs,
    sbr,
    scs,
    scr,
    ofs,
    ofr,
    olsem,
    obase,
):
    e = lax.axis_index("expert")
    z = lax.axis_index("tensor")
    core = lax.rem(e, 2)
    me = e // 2
    sib = e + 1 - 2 * core
    half = n // 2
    rows, width = gmid_ref.shape
    tok = rows * nz
    qw = wq_ref.shape[1]
    kw = wk_ref.shape[1]
    seqs = kv_ref.shape[0]
    span = tok // seqs
    heads = kw // HD
    groups = qw // kw
    dn = width // n
    experts = glog_ref.shape[0]
    own_rows = pl.ds(pl.multiple_of(z * rows, 16), rows)
    barrier = greet(n, nz, e, z, sib)
    w1 = PlaneSum(n, e, z, sib, wall, *wbufs, *wsems)
    w2 = PlaneSum(n, e, z, sib, wall2, *wbufs2, *wsems2)

    gat[own_rows, :] = gmid_ref[...].astype(bf16)
    sz1[z] = glog_ref[...]
    pl.semaphore_wait(barrier, half + nz - 1)

    def part_of(ref):
        return lambda zz: ref.at[pl.ds(pl.multiple_of(zz * rows, 16), rows)]

    def slot_of(ref):
        return lambda zz: ref.at[zz]

    gat_line = Line(z, nz, e, part_of(gat), zas, zar)
    out_line = Line(z, nz, e, part_of(obuf), zos, zor)
    igrad_line = Line(z, nz, e, part_of(igbuf), zis, zir)
    normed_sum = LineSum(z, nz, e, csend, crecv, zps, zpr)

    def z_copies(buf_of, send, recv):
        return [
            remote(
                buf_of(z), buf_of(z), send.at[k - 1], recv.at[k - 1], (e, lax.rem(z + k, nz))
            )
            for k in range(1, nz)
        ]

    def z_arrivals(buf_of, send, recv):
        return [
            remote(
                buf_of(lax.rem(z + nz - k, nz)),
                buf_of(lax.rem(z + nz - k, nz)),
                send.at[k - 1],
                recv.at[k - 1],
                (e, lax.rem(z + nz - k, nz)),
            )
            for k in range(1, nz)
        ]

    gat_line.start()
    for copy in z_copies(slot_of(sz1), z1s, z1r):
        copy.start()

    square = half == 4
    chip_x = me + 1 - 2 * lax.rem(me, 2)
    chip_y = lax.rem(me + 2, 4)
    chip_d = 3 - me
    low, high = pl.ds(0, nz // 2), pl.ds(nz // 2, nz - nz // 2)

    def mixed_at(chip, which=slice(None)):
        return mixed_hbm.at[which, pl.ds(pl.multiple_of(chip * rows, 16), rows), :]

    def mixed_copy(src, dst, i, chip):
        return remote(src, dst, ofs.at[i], ofr.at[i], (2 * chip + core, z))

    def mixed_sends():
        if not square:
            return [
                mixed_copy(
                    mixed_at(lax.rem(me + half - t, half)),
                    ofin.at[t],
                    t - 1,
                    lax.rem(me + half - t, half),
                )
                for t in range(1, half)
            ]
        return [
            mixed_copy(mixed_at(chip_d, low), ofin.at[3, low], 0, chip_x),
            mixed_copy(mixed_at(chip_d, high), ofin.at[3, high], 1, chip_y),
            mixed_copy(mixed_at(chip_x, low), ofin.at[1, low], 2, chip_x),
            mixed_copy(mixed_at(chip_y, high), ofin.at[2, high], 3, chip_y),
        ]

    def mixed_relays():
        return [
            mixed_copy(obase.at[low], ofin.at[2, low], 4, chip_y),
            mixed_copy(obase.at[high], ofin.at[1, high], 5, chip_x),
        ]

    for copy in mixed_sends():
        copy.start()
    mixed_own = [pltpu.make_async_copy(mixed_at(me), ofin.at[0], olsem.at[0])]
    if square:
        mixed_own += [
            pltpu.make_async_copy(mixed_at(chip_y, low), obase.at[low], olsem.at[1]),
            pltpu.make_async_copy(mixed_at(chip_x, high), obase.at[high], olsem.at[2]),
        ]
    for copy in mixed_own:
        copy.start()

    def mixed_relay():
        waits = mixed_sends()
        for copy, part, i in zip(mixed_relays(), (low, high), (0, 1)):
            waits[i].wait_recv()
            obase[part] = (obase[part].astype(f32) + ofin[3, part].astype(f32)).astype(bf16)
            copy.start()

    mixed_count = 3 if square else half

    def mixed_sum(zz):
        total = ofin[0, zz].astype(f32)
        for t in range(1, mixed_count):
            total = total + ofin[t, zz].astype(f32)
        return total

    wqkv[:, 0:qw] = wq_ref[...]
    wqkv[:, qw : qw + kw] = wk_ref[...]
    wqkv[:, qw + kw :] = wv_ref[...]
    x = x_ref[...].astype(f32)
    scale1 = lax.rsqrt(jnp.mean(x * x, -1, keepdims=True) + EPS)
    normed = (x * scale1 * gain_ref[...]).astype(bf16)
    dkv[...] = jnp.zeros_like(dkv)

    for hop in range(1, nz):
        gat_line.hop(hop)
    datt[...] = dot_nt(gat[...], wo_ref[...]).astype(bf16)

    ck = 2 * span
    last = (e * span + span - 1) // ck
    stacked = groups * span
    kiota = lax.broadcasted_iota(jnp.int32, (ck, stacked), 0)
    krow = lax.broadcasted_iota(jnp.int32, (ck, 1), 0)
    qpos = e * span + lax.rem(lax.broadcasted_iota(jnp.int32, (ck, stacked), 1), span)
    drows = []
    for s in range(seqs):
        for h in range(heads):

            def gather(ref):
                return jnp.concatenate(
                    [
                        ref[
                            s * span : (s + 1) * span,
                            (h * groups + g) * HD : (h * groups + g + 1) * HD,
                        ]
                        for g in range(groups)
                    ],
                    0,
                )

            i = s * heads + h
            qst_s[i] = gather(q_ref) * jnp.array(HD ** (-0.5), bf16)
            dst = gather(datt)
            dst_s[i] = dst
            delta = jnp.sum(dst.astype(f32) * gather(att_ref), -1, keepdims=True)
            drows.append(jnp.broadcast_to(delta, (stacked, 128)).T[0:1])
    acc_q[...] = jnp.zeros_like(acc_q)
    for copy in mixed_own:
        copy.wait()
    if square:
        mixed_relay()

    def chunk(c, diagonal):
        at = pl.ds(pl.multiple_of(c * ck, 16), ck)
        for s in range(seqs):
            for h in range(heads):
                i = s * heads + h
                keys = kv_ref[s, at, h * HD : (h + 1) * HD]
                vals = kv_ref[s, at, kw + h * HD : kw + (h + 1) * HD]
                scores = dot_nt(keys, qst_s[i]) - lrow_ref[i, 0:1, :]
                if diagonal:
                    kpos = kiota + c * ck
                    allowed = (kpos <= qpos) & (kpos < lens_ref[s])
                    soft = jnp.where(allowed, jnp.exp(scores), 0.0)
                else:
                    soft = jnp.exp(scores + jnp.where(krow + c * ck < lens_ref[s], 0.0, -1e30))
                grad_probs = dot_nt(vals, dst_s[i])
                grad_scores = (soft * (grad_probs - drows[i])).astype(bf16)
                dkv[s, at, h * HD : (h + 1) * HD] = dot_nn(grad_scores, qst_s[i])
                dkv[s, at, kw + h * HD : kw + (h + 1) * HD] = dot_nn(soft.astype(bf16), dst_s[i])
                acc_q[i] += dot_tn(grad_scores, keys)

    def whole_chunk(c, carry):
        chunk(c, False)
        return carry

    lax.fori_loop(0, last, whole_chunk, 0)
    chunk(last, True)
    for s in range(seqs):
        for h in range(heads):
            result = acc_q[s * heads + h] * HD ** (-0.5)
            for g in range(groups):
                cols = slice((h * groups + g) * HD, (h * groups + g + 1) * HD)
                dq_s[s * span : (s + 1) * span, cols] = result[g * span : (g + 1) * span]

    def key_rows(j, s):
        return dkv[s, pl.ds(pl.multiple_of(j * span, 16), span), :]

    def key_send(t):
        return remote(kvo.at[t], kvi.at[t], kos.at[t], kor.at[t], (sib, z))

    def key_final(t):
        to = (lax.rem(e - 2 * t + n, n), z)
        return remote(kvf.at[t - 1], kvr.at[t - 1], kfs.at[t - 1], kfr.at[t - 1], to)

    def key_give(i, carry):
        t = half - 1 - i
        oth = lax.rem(sib - 2 * t + n, n)
        for s in range(seqs):
            kvo[t, s] = key_rows(oth, s).astype(bf16)
        key_send(t).start()
        return carry

    lax.fori_loop(0, half, key_give, 0)

    def key_pass(i, carry):
        t = half - 1 - i
        key_send(t).wait_recv()
        own = lax.rem(e - 2 * t + n, n)
        for s in range(seqs):
            kvf[t - 1, s] = (key_rows(own, s) + kvi[t, s].astype(f32)).astype(bf16)
        key_final(t).start()
        return carry

    cos, sin = cos_ref[...], sin_ref[...]
    gq = turn(dq_s[...], cos, sin, qw, False).astype(bf16)
    query_part = dot_tn(normed, gq)
    out_part = dot_tn(gat[...], att_ref[...].astype(bf16))
    for j in range(n):
        w1.pack[j, :, :qw] = query_part[j * dn : (j + 1) * dn].astype(bf16)
        w1.pack[j, :, qw:] = out_part[j * dn : (j + 1) * dn].astype(bf16)
    lax.fori_loop(0, half - 1, key_pass, 0)
    w1.give()

    def mixed_last(k, to):
        return remote(osend.at[k - 1], orecv.at[k - 1], zqs.at[k - 1], zqr.at[k - 1], (e, to))

    for copy in mixed_sends()[2:] + mixed_relays() if square else mixed_sends():
        copy.wait_recv()
    for k in range(1, nz):
        zz = lax.rem(z + k, nz)
        osend[k - 1] = mixed_sum(zz).astype(bf16)
        mixed_last(k, zz).start()
    own_mixed = mid_ref[...] + mixed_sum(z)
    w1.spread()
    for copy in z_arrivals(slot_of(sz1), z1s, z1r):
        copy.wait_recv()
    rgrad = dot_nn(sz1[0][:, :rows], xn_ref[0])
    for zz in range(1, nz):
        rgrad = rgrad + dot_nn(sz1[zz][:, :rows], xn_ref[zz])
    sown[0:experts, :] = rgrad.astype(bf16)

    key_send(0).wait_recv()
    own_kv = [key_rows(e, s) + kvi[0, s].astype(f32) for s in range(seqs)]
    for t in range(1, half):
        key_final(t).wait_recv()
        for s in range(seqs):
            own_kv[s] = own_kv[s] + kvr[t - 1, s].astype(f32)
    gkv = turn(jnp.concatenate(own_kv, 0), cos, sin, kw, False).astype(bf16)
    part[...] = dot_nt(gq, wqkv[:, :qw]) + dot_nt(gkv, wqkv[:, qw:])

    def normed_part(zz):
        return part[pl.ds(pl.multiple_of(zz * rows, 16), rows), :]

    for hop in range(nz - 1):
        normed_sum.hop(hop, normed_part)
        if hop > 0:
            out_line.hop(hop)
        if hop == 0:
            for k in range(1, nz):
                mixed_last(k, z).wait_recv()
                own_mixed = own_mixed + orecv[k - 1].astype(f32)
            obuf[own_rows, :] = own_mixed.astype(bf16)
            out_line.start()
            again = jnp.sum(part[...] * x * scale1, 0, keepdims=True)
            sz2[z] = jnp.concatenate([again, ggrad_ref[...], jnp.zeros((14, width), f32)], 0).astype(
                bf16
            )
            for copy in z_copies(slot_of(sz2), z2s, z2r):
                copy.start()
            pair_part = dot_tn(normed, gkv)
            for j in range(n):
                w2.pack[j] = pair_part[j * dn : (j + 1) * dn].astype(bf16)
            w2.give()
            w1.total()
        if hop == 1:
            w2.spread()
    if nz == 2:
        w2.spread()
    normed_sum.total(sums, normed_part)

    own_x = x_ref[own_rows, :].astype(f32)
    own_scale = lax.rsqrt(jnp.mean(own_x * own_x, -1, keepdims=True) + EPS)
    grad_normed = sums[...]
    gained = grad_normed * gain_ref[...]
    igrad = (
        gmid_ref[...]
        + own_scale * gained
        - own_x
        * (own_scale * own_scale * own_scale)
        * jnp.mean(gained * own_x, -1, keepdims=True)
    )
    igbuf[own_rows, :] = igrad.astype(bf16)
    igrad_line.start()
    out_line.hop(nz - 1)

    w2.total()
    w1.forward()
    for copy in z_arrivals(slot_of(sz2), z2s, z2r):
        copy.wait_recv()
    second = sz2[0].astype(f32)
    for zz in range(1, nz):
        second = second + sz2[zz].astype(f32)
    sown[experts:, :] = second.astype(bf16)
    small_sib = remote(sown, ssib, sbs, sbr, (sib, z))
    small_sib.start()
    if nz > 2:
        igrad_line.hop(1)
    small_sib.wait_recv()
    schip[me] = (sown[...].astype(f32) + ssib[...].astype(f32)).astype(bf16)

    def small_send(t):
        to = (lax.rem(e + 2 * t, n), z)
        return remote(schip.at[me], schip.at[me], scs.at[t - 1], scr.at[t - 1], to)

    for t in range(1, half):
        small_send(t).start()

    for hop in range(2, nz - 1):
        igrad_line.hop(hop)
    w2.forward()
    igrad_line.hop(nz - 1)
    for t in range(1, half):
        src = lax.rem(me + half - t, half)
        remote(
            schip.at[src], schip.at[src], scs.at[t - 1], scr.at[t - 1], (sib, z)
        ).wait_recv()
    small = schip[0].astype(f32)
    for t in range(1, half):
        small = small + schip[t].astype(f32)
    small_ref[...] = small

    w1.arrive()
    w2.arrive()
    for k in range(1, nz):
        mixed_last(k, z).wait_send()
    for line in (gat_line, out_line, igrad_line, normed_sum, w1, w2):
        line.drain()
    for copy in z_copies(slot_of(sz1), z1s, z1r) + z_copies(slot_of(sz2), z2s, z2r):
        copy.wait_send()
    small_sib.wait_send()
    for copy in mixed_sends() + (mixed_relays() if square else []):
        copy.wait_send()

    def drained(t, carry):
        key_send(t).wait_send()

        @pl.when(t > 0)
        def _():
            key_final(t).wait_send()
            small_send(t).wait_send()

        return carry

    lax.fori_loop(0, half, drained, 0)


class PlaneSum:
    def __init__(self, n, e, z, sib, wall, pack, near, send, recv, *sems):
        self.n, self.e, self.z, self.sib, self.half = n, e, z, sib, n // 2
        self.wall, self.pack, self.near, self.send, self.recv = wall, pack, near, send, recv
        self.sems = sems

    def peer(self, base, t):
        return lax.rem(base - 2 * t + self.n, self.n)

    def near_copy(self, t):
        src = self.pack.at[self.peer(self.sib, t)]
        return remote(
            src, self.near.at[t], self.sems[0].at[t], self.sems[1].at[t], (self.sib, self.z)
        )

    def far_copy(self, t):
        return remote(
            self.send.at[t - 1],
            self.recv.at[t - 1],
            self.sems[2].at[t],
            self.sems[3].at[t],
            (self.peer(self.e, t), self.z),
        )

    def all_copy(self, src, t, to):
        ref = self.wall.at[src]
        return remote(ref, ref, self.sems[4].at[t], self.sems[5].at[t], (to, self.z))

    def pass_copy(self, src, t):
        ref = self.wall.at[src]
        return remote(ref, ref, self.sems[6].at[t], self.sems[7].at[t], (self.sib, self.z))

    def give(self):
        def one(i, carry):
            self.near_copy(self.half - 1 - i).start()
            return carry

        lax.fori_loop(0, self.half, one, 0)

    def spread(self):
        def one(i, carry):
            t = self.half - 1 - i
            self.near_copy(t).wait_recv()
            own = self.pack[self.peer(self.e, t)].astype(f32)
            self.send[t - 1] = (own + self.near[t].astype(f32)).astype(bf16)
            self.far_copy(t).start()
            return carry

        lax.fori_loop(0, self.half - 1, one, 0)

    def total(self):
        self.near_copy(0).wait_recv()
        total = self.pack[self.e].astype(f32) + self.near[0].astype(f32)
        for t in range(1, self.half):
            self.far_copy(t).wait_recv()
            total = total + self.recv[t - 1].astype(f32)
        self.wall[self.e] = total.astype(bf16)
        for t in range(1, self.half):
            self.all_copy(self.e, t, lax.rem(self.e + 2 * t, self.n)).start()
        self.pass_copy(self.e, 0).start()

    def forward(self):
        def one(t, carry):
            src = self.peer(self.e, t)
            self.all_copy(src, t, src).wait_recv()
            self.pass_copy(src, t).start()
            return carry

        lax.fori_loop(1, self.half, one, 0)

    def arrive(self):
        def one(t, carry):
            self.pass_copy(self.peer(self.sib, t), t).wait_recv()
            return carry

        lax.fori_loop(0, self.half, one, 0)

    def drain(self):
        def one(t, carry):
            self.near_copy(t).wait_send()
            self.pass_copy(self.e, t).wait_send()

            @pl.when(t > 0)
            def _():
                self.far_copy(t).wait_send()
                self.all_copy(self.e, t, self.sib).wait_send()

            return carry

        lax.fori_loop(0, self.half, one, 0)


class Line:
    def __init__(self, z, nz, e, buf_of, send, recv):
        self.z, self.nz, self.e = z, nz, e
        self.buf_of, self.send, self.recv = buf_of, send, recv

    def copy(self, way, piece):
        to = self.z + 1 if way == 0 else self.z - 1
        ref = self.buf_of(piece)
        return remote(ref, ref, self.send.at[way, piece], self.recv.at[way, piece], (self.e, to))

    def push(self, piece, ways=(0, 1)):
        for way in ways:

            @pl.when(self.z < self.nz - 1 if way == 0 else self.z > 0)
            def _():
                self.copy(way, piece).start()

    def start(self):
        self.push(self.z)

    def hop(self, i):
        @pl.when(self.z >= i)
        def _():
            self.copy(0, self.z - i).wait_recv()
            self.push(self.z - i, (0,))

        @pl.when(self.z + i <= self.nz - 1)
        def _():
            self.copy(1, self.z + i).wait_recv()
            self.push(self.z + i, (1,))

    def drain(self):
        for piece in range(self.nz):

            @pl.when((self.z >= piece) & (self.z < self.nz - 1))
            def _():
                self.copy(0, piece).wait_send()

            @pl.when((self.z <= piece) & (self.z > 0))
            def _():
                self.copy(1, piece).wait_send()


class LineSum:
    def __init__(self, z, nz, e, send_buf, recv_buf, send, recv):
        self.z, self.nz, self.e = z, nz, e
        self.send_buf, self.recv_buf, self.send, self.recv = send_buf, recv_buf, send, recv

    def copy(self, way, target):
        to = self.z + 1 if way == 0 else self.z - 1
        return remote(
            self.send_buf.at[way, target],
            self.recv_buf.at[way, target],
            self.send.at[way, target],
            self.recv.at[way, target],
            (self.e, to),
        )

    def hop(self, i, own_of):
        for way, target in ((0, self.nz - 1 - i), (1, i)):
            passes = self.z < target if way == 0 else self.z > target
            first = self.z == 0 if way == 0 else self.z == self.nz - 1
            inner = self.z > 0 if way == 0 else self.z < self.nz - 1

            @pl.when(passes & first)
            def _():
                self.send_buf[way, target] = own_of(target).astype(bf16)
                self.copy(way, target).start()

            @pl.when(passes & inner)
            def _():
                self.copy(way, target).wait_recv()
                self.send_buf[way, target] = (
                    own_of(target) + self.recv_buf[way, target].astype(f32)
                ).astype(bf16)
                self.copy(way, target).start()

    def total(self, ref, own_of):
        ref[...] = own_of(self.z)

        @pl.when(self.z > 0)
        def _():
            self.copy(0, self.z).wait_recv()
            ref[...] += self.recv_buf[0, self.z].astype(f32)

        @pl.when(self.z < self.nz - 1)
        def _():
            self.copy(1, self.z).wait_recv()
            ref[...] += self.recv_buf[1, self.z].astype(f32)

    def drain(self):
        for target in range(self.nz):

            @pl.when(self.z < target)
            def _():
                self.copy(0, target).wait_send()

            @pl.when(self.z > target)
            def _():
                self.copy(1, target).wait_send()


def return_layer(
    n, nz, gmid, mid, glog, ggrad, xn, x, gain, wq, wk, wv, wo, cos, sin, q, kv, lrow, att, lens, mixed
):
    tok, width = x.shape
    rows = tok // nz
    qw, kw = wq.shape[1], wk.shape[1]
    seqs = lens.shape[0]
    span = tok // seqs
    half = n // 2
    stacked = (qw // kw) * span
    pairs = seqs * (kw // HD)
    experts = glog.shape[0]
    small_rows = experts + 16
    dma = pltpu.SemaphoreType.DMA
    vmem = pl.BlockSpec(memory_space=pltpu.VMEM)
    sds = jax.ShapeDtypeStruct
    zdma = dma((nz - 1,))
    line = dma((2, nz))
    hdma = dma((half,))
    fdma = dma((half - 1,))
    def plane_bufs(cols):
        return [
            pltpu.VMEM((n, width // n, cols), bf16),
            pltpu.VMEM((half, width // n, cols), bf16),
            pltpu.VMEM((half - 1, width // n, cols), bf16),
            pltpu.VMEM((half - 1, width // n, cols), bf16),
        ]

    line_buf = pltpu.VMEM((2, nz, rows, width), bf16)
    return pl.pallas_call(
        functools.partial(return_kernel, n, nz),
        out_shape=[
            sds((tok, width), bf16),
            sds((tok, width), bf16),
            sds((n, width // n, 2 * qw), bf16),
            sds((n, width // n, 2 * kw), bf16),
            sds((small_rows, width), f32),
        ],
        in_specs=[vmem] * 17
        + [pl.BlockSpec(memory_space=pltpu.SMEM), pl.BlockSpec(memory_space=pl.ANY)],
        out_specs=[vmem] * 5,
        scratch_shapes=[
            pltpu.VMEM((width, qw + 2 * kw), bf16),
            pltpu.VMEM((tok, width), bf16),
            pltpu.VMEM((tok, qw), bf16),
            pltpu.VMEM((tok, qw), f32),
            pltpu.VMEM((pairs, stacked, HD), bf16),
            pltpu.VMEM((pairs, stacked, HD), bf16),
            pltpu.VMEM((pairs, stacked, HD), f32),
            pltpu.VMEM((seqs, n * span, 2 * kw), f32),
            pltpu.VMEM((half, seqs, span, 2 * kw), bf16),
            pltpu.VMEM((half, seqs, span, 2 * kw), bf16),
            pltpu.VMEM((half - 1, seqs, span, 2 * kw), bf16),
            pltpu.VMEM((half - 1, seqs, span, 2 * kw), bf16),
            pltpu.VMEM((tok, width), f32),
            pltpu.VMEM((rows, width), f32),
            line_buf,
            line_buf,
            pltpu.VMEM((nz - 1, rows, width), bf16),
            pltpu.VMEM((nz - 1, rows, width), bf16),
            plane_bufs(2 * qw),
            plane_bufs(2 * kw),
            pltpu.VMEM((nz, experts, 128), bf16),
            pltpu.VMEM((nz, 16, width), bf16),
            pltpu.VMEM((small_rows, width), bf16),
            pltpu.VMEM((small_rows, width), bf16),
            pltpu.VMEM((half, small_rows, width), bf16),
            pltpu.VMEM((half, nz, rows, width), bf16),
        ]
        + [line] * 8
        + [zdma] * 6
        + [hdma, hdma, fdma, fdma]
        + [[hdma] * 8, [hdma] * 8]
        + [dma, dma, fdma, fdma]
        + [dma((6 if half == 4 else half - 1,))] * 2
        + [dma((3,)), pltpu.VMEM((nz, rows, width), bf16)],
        compiler_params=pltpu.CompilerParams(
            collective_id=3, has_side_effects=True, vmem_limit_bytes=58 << 20
        ),
        name="attend_back",
    )(
        gmid,
        mid,
        glog,
        ggrad,
        xn,
        x,
        gain[None],
        wq,
        wk,
        wv,
        wo,
        cos,
        sin,
        q,
        kv,
        lrow,
        att,
        lens,
        mixed,
    )


def finish_kernel(
    out_low,
    igrad_low,
    wall,
    wall2,
    small,
    load,
    dgate_in,
    dup_in,
    ddown_in,
    out_ref,
    igrad_ref,
    q_ref,
    k_ref,
    v_ref,
    o_ref,
    router_ref,
    again_ref,
    egain_ref,
    loss_ref,
    load_ref,
    dgate,
    dup,
    ddown,
    dgate_s,
    dup_s,
    ddown_s,
    sems,
):
    pairs = ((dgate_in, dgate_s, dgate), (dup_in, dup_s, dup), (ddown_in, ddown_s, ddown))
    reads = [pltpu.make_async_copy(p[0], p[1], sems.at[0, i]) for i, p in enumerate(pairs)]
    writes = [pltpu.make_async_copy(p[1], p[2], sems.at[1, i]) for i, p in enumerate(pairs)]
    for copy in reads:
        copy.start()
    qw, kw = q_ref.shape[1], k_ref.shape[1]
    experts = load.shape[1]
    out_ref[...] = out_low[...].astype(f32)
    for read, write in zip(reads, writes):
        read.wait()
        write.start()
    igrad_ref[...] = igrad_low[...].astype(f32)
    chunks, dn, _ = wall.shape
    flat = wall[...].reshape(chunks * dn, 2 * qw).astype(f32)
    q_ref[...] = flat[:, :qw]
    o_ref[...] = flat[:, qw:].T
    flat = wall2[...].reshape(chunks * dn, 2 * kw).astype(f32)
    k_ref[...] = flat[:, :kw]
    v_ref[...] = flat[:, kw:]
    router_ref[...] = small[0:experts, :]
    again_ref[...] = small[experts : experts + 1, :]
    egain_ref[...] = small[experts + 1 : experts + 2, :]
    load_ref[...] = load[...]
    loss_ref[...] = jnp.mean(load[...], -1, keepdims=True)
    for copy in writes:
        copy.wait()


def finish_layer(out_low, igrad_low, wall, wall2, small, load, dgate, dup, ddown, qw, kw):
    tok, width = out_low.shape
    experts = load.shape[1]
    vmem = pl.BlockSpec(memory_space=pltpu.VMEM)
    hbm = pl.BlockSpec(memory_space=pl.ANY)
    sds = jax.ShapeDtypeStruct
    return pl.pallas_call(
        finish_kernel,
        out_shape=[
            sds((tok, width), f32),
            sds((tok, width), f32),
            sds((width, qw), f32),
            sds((width, kw), f32),
            sds((width, kw), f32),
            sds((qw, width), f32),
            sds((experts, width), f32),
            sds((1, width), f32),
            sds((1, width), f32),
            sds((1, 1), f32),
            sds((1, experts), f32),
            sds(dgate.shape, f32),
            sds(dup.shape, f32),
            sds(ddown.shape, f32),
        ],
        in_specs=[vmem] * 6 + [hbm] * 3,
        out_specs=[vmem] * 11 + [hbm] * 3,
        scratch_shapes=[
            pltpu.VMEM(dgate.shape, f32),
            pltpu.VMEM(dup.shape, f32),
            pltpu.VMEM(ddown.shape, f32),
            pltpu.SemaphoreType.DMA((2, 3)),
        ],
        compiler_params=pltpu.CompilerParams(vmem_limit_bytes=60 << 20),
        name="finish",
    )(out_low, igrad_low, wall, wall2, small, load, dgate, dup, ddown)


def shards(
    inputs,
    attention_gain,
    query_weight,
    key_weight,
    value_weight,
    out_weight,
    expert_gain,
    router_weight,
    gate_weight,
    up_weight,
    down_weight,
    routes,
    seq_lens,
    cotangent,
):
    n = lax.axis_size("expert")
    nz = lax.axis_size("tensor")
    tok_rows = inputs.shape[0]
    seq_count = seq_lens.shape[0]
    span_rows = tok_rows // seq_count
    row = lax.broadcasted_iota(jnp.int32, (tok_rows, 128), 0) % span_rows
    lane = lax.broadcasted_iota(jnp.int32, (tok_rows, 128), 1) % (HD // 2)
    frequency = THETA ** (-2.0 * lane.astype(f32) / HD)
    angles = (lax.axis_index("expert") * span_rows + row).astype(f32) * frequency
    cosines = jnp.cos(angles)
    sines = jnp.sin(angles)
    weights = (query_weight, key_weight, value_weight, out_weight, cosines, sines)
    middle, queries, pairs, logs, attended, cot_all = attend_layer(
        n, nz, inputs, attention_gain, *weights, cotangent, seq_lens
    )
    (
        grad_middle,
        logit_grads,
        expert_gain_part,
        expert_load,
        gate_grad,
        up_grad,
        down_grad,
        mixed,
        normed2,
    ) = expert_layer(
        n,
        nz,
        middle,
        expert_gain,
        router_weight,
        routes,
        gate_weight,
        up_weight,
        down_weight,
        cotangent,
        cot_all,
    )
    out_low, igrad_low, packed, packed2, small = return_layer(
        n,
        nz,
        grad_middle,
        middle,
        logit_grads,
        expert_gain_part,
        normed2,
        inputs,
        attention_gain,
        *weights,
        queries,
        pairs,
        logs,
        attended,
        seq_lens,
        mixed,
    )
    (
        output,
        input_grad,
        query_grad,
        key_grad,
        value_grad,
        out_weight_grad,
        router_grad,
        attention_gain_grad,
        expert_gain_grad,
        balance_loss,
        expert_load,
        gate_grad,
        up_grad,
        down_grad,
    ) = finish_layer(
        out_low,
        igrad_low,
        packed,
        packed2,
        small,
        expert_load,
        gate_grad,
        up_grad,
        down_grad,
        query_weight.shape[1],
        key_weight.shape[1],
    )
    return (
        output,
        input_grad,
        balance_loss[0, 0],
        expert_load[0],
        attention_gain_grad[0],
        query_grad,
        key_grad,
        value_grad,
        out_weight_grad,
        expert_gain_grad[0],
        router_grad.T,
        gate_grad,
        up_grad,
        down_grad.reshape(down_weight.shape),
    )


def solution(mesh):
    placed = (
        P("expert", None),
        P(),
        P(None, "tensor"),
        P(None, "tensor"),
        P(None, "tensor"),
        P("tensor", None),
        P(),
        P(),
        P("expert", None, "tensor"),
        P("expert", None, "tensor"),
        P("expert", "tensor", None),
        P("expert", None),
        P(),
        P("expert", None),
    )
    return jax.shard_map(
        shards,
        mesh=mesh,
        in_specs=placed,
        out_specs=(
            P("expert", None),
            P("expert", None),
            P(),
            P(),
            P(),
            P(None, "tensor"),
            P(None, "tensor"),
            P(None, "tensor"),
            P("tensor", None),
            P(),
            P(),
            P("expert", None, "tensor"),
            P("expert", None, "tensor"),
            P("expert", "tensor", None),
        ),
        check_vma=False,
    )
```

```python
import functools

import jax
import jax.numpy as jnp
from jax import lax
from jax.experimental import pallas as pl
from jax.experimental.pallas import tpu as pltpu
from jax.sharding import PartitionSpec as P

HD = 64
EPS = 1e-06
THETA = 10000.0
MESH = pl.DeviceIdType.MESH
f32 = jnp.float32
bf16 = jnp.bfloat16


def dot_nn(left, right):
    return lax.dot_general(left, right, (((1,), (0,)), ((), ())), preferred_element_type=f32)


def dot_nt(left, right):
    return lax.dot_general(left, right, (((1,), (1,)), ((), ())), preferred_element_type=f32)


def dot_tn(left, right):
    return lax.dot_general(left, right, (((0,), (0,)), ((), ())), preferred_element_type=f32)


def remote(src, dst, send_sem, recv_sem, device):
    return pltpu.make_async_remote_copy(
        src_ref=src,
        dst_ref=dst,
        send_sem=send_sem,
        recv_sem=recv_sem,
        device_id=device,
        device_id_type=MESH,
    )


def turn(values, cos, sin, last, forward):
    lane = lax.broadcasted_iota(jnp.int32, (values.shape[0], 128), 1)
    first_half = lax.rem(lane, HD) < HD // 2
    parts = []
    for g in range(values.shape[1] // 128):
        v = values[:, g * 128 : (g + 1) * 128]
        if g * 128 >= last:
            parts.append(v)
            continue
        turned = jnp.where(
            first_half, -pltpu.roll(v, 128 - HD // 2, 1), pltpu.roll(v, HD // 2, 1)
        )
        new = v * cos + turned * sin if forward else v * cos - turned * sin
        if (g + 1) * 128 > last:
            new = jnp.where(lane + g * 128 < last, new, v)
        parts.append(new)
    return jnp.concatenate(parts, 1) if len(parts) > 1 else parts[0]


def greet(n, nz, e, z, sib):
    barrier = pltpu.get_barrier_semaphore()
    pl.semaphore_signal(barrier, inc=1, device_id=(sib, z), device_id_type=MESH)
    for s in range(1, n // 2):
        pl.semaphore_signal(
            barrier, inc=1, device_id=(lax.rem(e + 2 * s, n), z), device_id_type=MESH
        )
    for k in range(1, nz):
        pl.semaphore_signal(barrier, inc=1, device_id=(e, lax.rem(z + k, nz)), device_id_type=MESH)
    return barrier


def expert_kernel(
    n,
    nz,
    big,
    mid_ref,
    gain_ref,
    router_ref,
    routes_ref,
    cot_ref,
    gate_hbm,
    up_hbm,
    down_hbm,
    cot_all,
    *rest,
):
    outs, rest = rest[:9], rest[9:]
    gmid_ref, glog_ref, ggrad_ref, load_ref = outs[:4]
    dgate_hbm, dup_hbm, ddown_hbm, mixed_hbm, normed_hbm = outs[4:]
    xbuf, rest = rest[0], rest[1:]
    if big:
        xstage, rest = rest[0], rest[1:]
    (
        wbuf,
        xn_s,
        wg,
        wu,
        down_ref,
        dgate,
        dup,
        ddown,
        cbuf,
        dg_s,
        du_s,
        wi_s,
        hold,
        osend,
        sin,
        hold_o,
        osend_o,
        sin_o,
        hold_g,
        osend_g,
        sin_g,
        own_s,
        own_g,
        fsend,
        fin,
        fsend_g,
        fin_g,
        zsend,
        zin,
        zsend_g,
        zin_g,
        wsem,
        gsem,
        csem,
        msem,
        lsem,
        zs,
        zr,
        zws,
        zwr,
        xs,
        xr,
        ws,
        wr,
        fs,
        fr,
        wfs,
        wfr,
        gs,
        gr,
        oss,
        osr,
        ggs,
        ggr,
        ps,
        pr,
        pgs,
        pgr,
        zgs,
        zgr,
        zggs,
        zggr,
        picks_s,
    ) = rest
    e = lax.axis_index("expert")
    z = lax.axis_index("tensor")
    core = lax.rem(e, 2)
    other = 1 - core
    me = e // 2
    sib = e + 1 - 2 * core
    half = n // 2
    rows, width = mid_ref.shape
    tok = rows * nz
    experts = router_ref.shape[0]
    local_experts, _, hid = gate_hbm.shape
    inner_w = local_experts * hid
    fc = min(inner_w, 256)
    fslots = fsend.shape[0]
    square = half == 4
    chip_x = me + 1 - 2 * lax.rem(me, 2)
    chip_y = lax.rem(me + 2, 4)
    chip_d = 3 - me
    mid_row = rows // 2

    loads = []
    for el in range(local_experts):
        cols = pl.ds(el * hid, hid)
        loads.append(pltpu.make_async_copy(gate_hbm.at[el], wg.at[:, cols], wsem.at[0, el]))
        loads.append(pltpu.make_async_copy(up_hbm.at[el], wu.at[:, cols], wsem.at[1, el]))
    loads.append(pltpu.make_async_copy(down_hbm, down_ref, wsem.at[2, 0]))
    for copy in loads:
        copy.start()

    def piece_of(g):
        return lax.rem(z + nz - g, nz)

    def cot_start(g, parity, slot):
        zz = piece_of(g)
        for h in range(half):
            start = (2 * h + parity) * tok + zz * rows
            pltpu.make_async_copy(
                cot_all.at[pl.ds(pl.multiple_of(start, 16), rows)],
                cbuf.at[slot, pl.ds(h * rows, rows)],
                csem.at[slot],
            ).start()

    def cot_wait(slot):
        pltpu.make_async_copy(
            cot_all.at[pl.ds(0, half * rows)], cbuf.at[slot], csem.at[slot]
        ).wait()

    cot_start(0, core, 0)
    barrier = greet(n, nz, e, z, sib)

    own_rows = pl.ds(pl.multiple_of(z * rows, 16), rows)
    my_rows = pl.ds(pl.multiple_of(me * rows, 16), rows)
    mid = mid_ref[...]
    scale2 = lax.rsqrt(jnp.mean(mid * mid, -1, keepdims=True) + EPS)
    xn = (mid * scale2 * gain_ref[...]).astype(bf16)
    xn_s[...] = xn
    logits = dot_nt(xn, router_ref[...])
    choices = routes_ref[...].astype(f32)
    top_count = choices.shape[0]
    picks_s[...] = jnp.concatenate([choices, jnp.zeros((128 - top_count, tok), f32)], 0).T
    picks = picks_s[own_rows, 0:top_count].astype(jnp.int32)
    lanes = lax.broadcasted_iota(jnp.int32, (rows, experts), 1)
    chosen = jnp.zeros((rows, experts), f32)
    for k in range(picks.shape[1]):
        chosen = jnp.where(picks[:, k : k + 1] == lanes, 1.0, chosen)
    top = jnp.max(logits, -1, keepdims=True)
    powers = jnp.exp(logits - top)
    probs = powers / jnp.sum(powers, -1, keepdims=True)
    low_logits = jnp.where(chosen > 0.0, logits, -1e30)
    ctop = jnp.max(low_logits, -1, keepdims=True)
    cpow = jnp.exp(low_logits - ctop)
    comb = cpow / jnp.sum(cpow, -1, keepdims=True)
    padded = jnp.concatenate([comb, jnp.zeros((rows, 128 - experts), f32)], 1)
    if rows < 128:
        padded = jnp.concatenate([padded, jnp.zeros((128 - rows, 128), f32)], 0)
    piece = padded.T[:experts]
    lane_pad = jnp.zeros((1, 128 - experts), f32)
    cnt = jnp.concatenate([jnp.sum(chosen, 0, keepdims=True), lane_pad], 1)
    psum = jnp.concatenate([jnp.sum(probs, 0, keepdims=True), lane_pad], 1)
    psum_hi = psum.astype(bf16).astype(f32)
    stats = jnp.concatenate([cnt, psum_hi, psum - psum_hi, jnp.zeros((13, 128), f32)], 0)
    wbuf[z, core, me] = jnp.concatenate([piece, stats], 0).astype(bf16)
    if big:
        copy = pltpu.make_async_copy(xn_s, xbuf.at[z, core, my_rows], lsem)
        copy.start()
        copy.wait()
    else:
        xbuf[z, core, my_rows] = xn
    pl.semaphore_wait(barrier, half + nz - 1)

    def z_row(zz, k, to):
        ref = xbuf.at[zz, core, my_rows]
        return remote(ref, ref, zs.at[k - 1], zr.at[k - 1], (e, to))

    def z_small(zz, k, to):
        ref = wbuf.at[zz, core, me]
        return remote(ref, ref, zws.at[k - 1], zwr.at[k - 1], (e, to))

    def x_row(zz, h, g, s, to):
        ref = xbuf.at[zz, core, pl.ds(pl.multiple_of(h * rows, 16), rows)]
        return remote(ref, ref, xs.at[g, s], xr.at[g, s], (to, z))

    def x_small(zz, h, g, s, to):
        ref = wbuf.at[zz, core, h]
        return remote(ref, ref, ws.at[g, s], wr.at[g, s], (to, z))

    def x_part(zz, h, first, count, g, i, to):
        start = pl.multiple_of(h * rows + first, 16)
        ref = xbuf.at[zz, core, pl.ds(start, count)]
        return remote(ref, ref, xs.at[g, i], xr.at[g, i], (2 * to + core, z))

    def push_piece(g):
        zz = piece_of(g)
        if square:
            x_part(zz, me, 0, rows, g, 0, chip_x).start()
            x_part(zz, me, 0, rows, g, 1, chip_y).start()
        for s in range(1, half):
            to = lax.rem(e + 2 * s, n)
            if not square:
                x_row(zz, me, g, s, to).start()
            x_small(zz, me, g, s, to).start()

    def relays(g):
        zz = piece_of(g)
        return (
            x_part(zz, chip_x, 0, mid_row, g, 2, chip_y),
            x_part(zz, chip_y, mid_row, rows - mid_row, g, 3, chip_x),
        )

    def relay_pieces(g):
        zz = piece_of(g)
        low, high = relays(g)
        x_part(zz, chip_x, 0, rows, g, 0, chip_x).wait_recv()
        low.start()
        x_part(zz, chip_y, 0, rows, g, 1, chip_y).wait_recv()
        high.start()

    push_piece(jnp.int32(0))
    def z_push(k):
        z_row(z, k, lax.rem(z + k, nz)).start()
        z_small(z, k, lax.rem(z + k, nz)).start()

    for k in range(1, min(nz, 2) if square else nz):
        z_push(k)

    if square:
        relay_pieces(jnp.int32(0))
        if nz > 2:
            z_push(2)

    dgate[...] = jnp.zeros_like(dgate)
    dup[...] = jnp.zeros_like(dup)
    ddown[...] = jnp.zeros_like(ddown)
    for copy in loads:
        copy.wait()

    sel_row = lax.broadcasted_iota(jnp.int32, (experts, fc), 0)
    sel_col = lax.broadcasted_iota(jnp.int32, (experts, fc), 1)

    def block(zz, parity, slot, dst, dst_o, dst_g, dslot):
        if big:
            copy = pltpu.make_async_copy(xbuf.at[zz, parity], xstage, lsem)
            copy.start()
            copy.wait()
            x_ref = xstage
        else:
            x_ref = xbuf.at[zz, parity]
        c_ref = cbuf.at[slot]
        sums = [jnp.zeros((experts, rows), f32) for _ in range(half)]
        for q in range(inner_w // fc):
            cols = slice(q * fc, (q + 1) * fc)
            x = x_ref[...]
            gate_val = dot_nn(x, wg[:, cols])
            up_val = dot_nn(x, wu[:, cols])
            back = dot_nt(c_ref[...], down_ref[cols, :])
            select = jnp.where(
                sel_row == e * local_experts + (q * fc + sel_col) // hid, 1.0, 0.0
            ).astype(bf16)
            wide = jnp.concatenate(
                [dot_tn(wbuf[zz, parity, h, :experts, :], select)[:rows] for h in range(half)], 0
            )
            sig = 1.0 / (1.0 + jnp.exp(-gate_val))
            silu = gate_val * sig
            inner = silu * up_val
            wi_s[:, cols] = (inner * wide).astype(bf16)
            scaled = back * wide
            dg_s[:, cols] = (scaled * up_val * (sig * (1.0 + gate_val * (1.0 - sig)))).astype(bf16)
            du_s[:, cols] = (scaled * silu).astype(bf16)
            both = (inner * back).astype(bf16)
            for h in range(half):
                sums[h] = sums[h] + dot_nt(select, both[h * rows : (h + 1) * rows])
        for h in range(half):
            gap = jnp.zeros((experts, 128 - rows), f32)
            dst_g[dslot, h] = jnp.concatenate([sums[h], gap], 1).astype(bf16)
        for h in range(width // 256):
            cols = slice(h * 256, (h + 1) * 256)
            dst[dslot, :, cols] = (
                dot_nt(dg_s[...], wg[cols, :]) + dot_nt(du_s[...], wu[cols, :])
            ).astype(bf16)
            dst_o[dslot, :, cols] = dot_nn(wi_s[...], down_ref[:, cols]).astype(bf16)
        for h in range(width // 256):
            cols = slice(h * 256, (h + 1) * 256)
            x_part = x_ref[:, cols]
            gate_part = dot_tn(x_part, dg_s[...])
            up_part = dot_tn(x_part, du_s[...])
            for el in range(local_experts):
                dgate[el, cols, :] += gate_part[:, el * hid : (el + 1) * hid]
                dup[el, cols, :] += up_part[:, el * hid : (el + 1) * hid]
            ddown[:, cols] += dot_tn(wi_s[...], c_ref[:, cols])

    def gives(slot):
        return [
            remote(osend.at[slot], sin.at[slot], gs.at[slot], gr.at[slot], (sib, z)),
            remote(osend_g.at[slot], sin_g.at[slot], ggs.at[slot], ggr.at[slot], (sib, z)),
            remote(osend_o.at[slot], sin_o.at[slot], oss.at[slot], osr.at[slot], (sib, z)),
        ]

    def finals(g, s, to):
        at = lax.rem(g, fslots)
        rows_copy = []
        if not square:
            rows_copy = [
                remote(
                    fsend.at[at, s - 1], fin.at[g, s - 1], ps.at[g, s - 1], pr.at[g, s - 1], (to, z)
                )
            ]
        return rows_copy + [
            remote(
                fsend_g.at[at, s - 1],
                fin_g.at[g, s - 1],
                pgs.at[g, s - 1],
                pgr.at[g, s - 1],
                (to, z),
            ),
        ]

    def half_copy(g, buf, upper, i, chip):
        first, count = (mid_row, rows - mid_row) if upper else (0, mid_row)
        return remote(
            fsend.at[g, buf, pl.ds(first, count)],
            fin.at[g, buf, pl.ds(first, count)],
            ps.at[g, i],
            pr.at[g, i],
            (2 * chip + core, z),
        )

    def half_copies(g):
        return [
            half_copy(g, 2, False, 0, chip_x),
            half_copy(g, 2, True, 1, chip_y),
            half_copy(g, 0, False, 2, chip_x),
            half_copy(g, 1, True, 3, chip_y),
            half_copy(g, 1, False, 4, chip_y),
            half_copy(g, 0, True, 5, chip_x),
        ]

    def chip_sum(slot, chip, upper):
        first, count = (mid_row, rows - mid_row) if upper else (0, mid_row)
        at = pl.ds(pl.multiple_of(chip * rows + first, 16), count)
        return hold[slot, at, :].astype(f32) + sin[slot, at, :].astype(f32)

    def direct_stage(g):
        slot = lax.rem(g, 2)
        copies = half_copies(g)
        fsend[g, 2, :mid_row] = chip_sum(slot, chip_d, False).astype(bf16)
        copies[0].start()
        fsend[g, 2, mid_row:] = chip_sum(slot, chip_d, True).astype(bf16)
        copies[1].start()
        fsend[g, 0, :mid_row] = chip_sum(slot, chip_x, False).astype(bf16)
        copies[2].start()
        fsend[g, 1, mid_row:] = chip_sum(slot, chip_y, True).astype(bf16)
        copies[3].start()

    def relay_stage(g):
        slot = lax.rem(g, 2)
        copies = half_copies(g)
        copies[0].wait_recv()
        passed = chip_sum(slot, chip_y, False) + fin[g, 2, :mid_row].astype(f32)
        fsend[g, 1, :mid_row] = passed.astype(bf16)
        copies[4].start()
        copies[1].wait_recv()
        passed = chip_sum(slot, chip_x, True) + fin[g, 2, mid_row:].astype(f32)
        fsend[g, 0, mid_row:] = passed.astype(bf16)
        copies[5].start()

    def lasts(k, to):
        return [
            remote(zsend.at[k - 1], zin.at[k - 1], zgs.at[k - 1], zgr.at[k - 1], (e, to)),
            remote(zsend_g.at[k - 1], zin_g.at[k - 1], zggs.at[k - 1], zggr.at[k - 1], (e, to)),
        ]

    def mixed_copy(g, slot):
        return pltpu.make_async_copy(hold_o.at[slot], mixed_hbm.at[piece_of(g)], msem.at[slot])

    def plane_stage(g):
        slot = lax.rem(g, 2)
        for copy in gives(slot)[:2]:
            copy.wait_recv()
        if fslots < nz:

            @pl.when(g >= fslots)
            def _():
                for s in range(1, half):
                    for copy in finals(g - fslots, s, sib):
                        copy.wait_send()

        spot = lax.rem(g, fslots)
        if square:
            direct_stage(g)
        for s in range(1, half):
            h = lax.rem(me + half - s, half)
            at = pl.ds(pl.multiple_of(h * rows, 16), rows)
            if not square:
                fsend[spot, s - 1] = (
                    hold[slot, at, :].astype(f32) + sin[slot, at, :].astype(f32)
                ).astype(bf16)
            fsend_g[spot, s - 1] = (hold_g[slot, h].astype(f32) + sin_g[slot, h].astype(f32)).astype(
                bf16
            )
            for copy in finals(g, s, lax.rem(e - 2 * s + n, n)):
                copy.start()
        own_s[g] = hold[slot, my_rows, :].astype(f32) + sin[slot, my_rows, :].astype(f32)
        own_g[g] = hold_g[slot, me].astype(f32) + sin_g[slot, me].astype(f32)

    def mixed_stage(g):
        slot = lax.rem(g, 2)
        gives(slot)[2].wait_recv()
        hold_o[slot] = (hold_o[slot].astype(f32) + sin_o[slot].astype(f32)).astype(bf16)
        mixed_copy(g, slot).start()

    def tensor_stage(g):
        total = own_s[g]
        total_g = own_g[g]
        for s in range(1, half):
            for copy in finals(g, s, sib):
                copy.wait_recv()
            if not square:
                total = total + fin[g, s - 1].astype(f32)
            total_g = total_g + fin_g[g, s - 1].astype(f32)

        if square:
            for copy in half_copies(g)[2:]:
                copy.wait_recv()
            total = total + fin[g, 0].astype(f32) + fin[g, 1].astype(f32)

        @pl.when(g == 0)
        def _():
            own_s[0] = total
            own_g[0] = total_g

        @pl.when(g > 0)
        def _():
            zsend[g - 1] = total.astype(bf16)
            zsend_g[g - 1] = total_g.astype(bf16)
            for copy in lasts(g, piece_of(g)):
                copy.start()

    def step(g, carry):
        zz = piece_of(g)
        slot = lax.rem(g, 2)

        @pl.when(g < nz - 1)
        def _():
            coming = piece_of(g + 1)
            z_row(coming, g + 1, coming).wait_recv()
            z_small(coming, g + 1, coming).wait_recv()
            push_piece(g + 1)

        if square:
            x_part(zz, chip_d, 0, mid_row, g, 2, chip_y).wait_recv()
            x_part(zz, chip_d, mid_row, rows - mid_row, g, 3, chip_x).wait_recv()

        for s in range(1, half):
            h = lax.rem(me + half - s, half)
            src = 2 * h + core
            if not square:
                x_row(zz, h, g, s, src).wait_recv()
            x_small(zz, h, g, s, src).wait_recv()
        for copy in forward(zz, core, g):
            copy.start()
        cot_start(g, other, 1)
        cot_wait(0)

        @pl.when(g >= 2)
        def _():
            mixed_copy(g - 2, slot).wait()

        block(zz, core, 0, hold, hold_o, hold_g, slot)
        if square:

            @pl.when(g == 0)
            def _():
                for k in range(3, nz):
                    z_push(k)

            @pl.when(g < nz - 1)
            def _():
                relay_pieces(g + 1)


        @pl.when(g < nz - 1)
        def _():
            cot_start(g + 1, core, 0)

        @pl.when(g >= 2)
        def _():
            tensor_stage(g - 2)

        @pl.when(g >= 1)
        def _():
            plane_stage(g - 1)
            mixed_stage(g - 1)

        @pl.when(g >= 2)
        def _():
            for copy in gives(slot):
                copy.wait_send()

        for copy in forward(zz, other, g):
            copy.wait_recv()
        cot_wait(1)
        block(zz, other, 1, osend, osend_o, osend_g, slot)
        for copy in gives(slot):
            copy.start()
        if square:

            @pl.when(g >= 1)
            def _():
                relay_stage(g - 1)

        return carry

    def forward(zz, parity, g):
        ref = xbuf.at[zz, parity]
        small = wbuf.at[zz, parity]
        return (
            remote(ref, ref, fs.at[g], fr.at[g], (sib, z)),
            remote(small, small, wfs.at[g], wfr.at[g], (sib, z)),
        )

    lax.fori_loop(0, nz, step, 0)
    grads = [
        pltpu.make_async_copy(dgate, dgate_hbm, gsem.at[0]),
        pltpu.make_async_copy(dup, dup_hbm, gsem.at[1]),
        pltpu.make_async_copy(ddown, ddown_hbm, gsem.at[2]),
        pltpu.make_async_copy(xbuf.at[:, core, my_rows, :], normed_hbm, gsem.at[3]),
    ]
    plane_stage(jnp.int32(nz - 1))
    for copy in grads:
        copy.start()
    if nz >= 2:
        tensor_stage(jnp.int32(nz - 2))
    if square:
        relay_stage(jnp.int32(nz - 1))

    def total_stats(j, carry):
        for zz in range(nz):
            for parity in range(2):
                carry = carry + wbuf[zz, parity, j, experts:, :].astype(f32)
        return carry

    stats = lax.fori_loop(0, half, total_stats, jnp.zeros((16, 128), f32))
    total_rows = n * tok
    share = stats[0:1, :experts] / (total_rows * top_count)
    load_ref[...] = (
        experts * experts * share * ((stats[1:2, :experts] + stats[2:3, :experts]) / total_rows)
    )
    loss_w = experts * share / total_rows
    mixed_stage(jnp.int32(nz - 1))
    tensor_stage(jnp.int32(nz - 1))

    gate_sums = own_g[0]
    grad_rows = own_s[0]
    for k in range(1, nz):
        for copy in lasts(k, z):
            copy.wait_recv()
        gate_sums = gate_sums + zin_g[k - 1].astype(f32)
        grad_rows = grad_rows + zin[k - 1].astype(f32)
    grow = jnp.concatenate([gate_sums, jnp.zeros((128 - experts, 128), f32)], 0).T
    grad_gates = grow[:rows, :experts]
    grad_logits = comb * (grad_gates - jnp.sum(grad_gates * comb, -1, keepdims=True))
    grad_logits = grad_logits + probs * (loss_w - jnp.sum(loss_w * probs, -1, keepdims=True))
    low_grad = grad_logits.astype(bf16)
    wide_grad = jnp.concatenate([grad_logits, jnp.zeros((rows, 128 - experts), f32)], 1)
    if rows < 128:
        wide_grad = jnp.concatenate([wide_grad, jnp.zeros((128 - rows, 128), f32)], 0)
    glog_ref[...] = wide_grad.T[:experts].astype(bf16)
    grad_rows = grad_rows + dot_nn(low_grad, router_ref[...])
    mid = mid_ref[...]
    ggrad_ref[...] = jnp.sum(grad_rows * mid * scale2, 0, keepdims=True)
    gained = grad_rows * gain_ref[...]
    gmid_ref[...] = (
        cot_ref[own_rows, :]
        + scale2 * gained
        - mid * (scale2 * scale2 * scale2) * jnp.mean(gained * mid, -1, keepdims=True)
    )

    for copy in grads:
        copy.wait()
    for k in range(1, nz):
        z_row(z, k, z).wait_send()
        z_small(z, k, z).wait_send()
        for copy in lasts(k, z):
            copy.wait_send()
    for g in range(max(0, nz - 2), nz):
        mixed_copy(jnp.int32(g), g % 2).wait()
        for copy in gives(g % 2):
            copy.wait_send()

    def drained(g, carry):
        if square:
            x_part(z, me, 0, rows, g, 0, chip_x).wait_send()
            x_part(z, me, 0, rows, g, 1, chip_y).wait_send()
            for copy in relays(g) + tuple(half_copies(g)):
                copy.wait_send()
        for s in range(1, half):
            if not square:
                x_row(z, me, g, s, sib).wait_send()
            x_small(z, me, g, s, sib).wait_send()
        for copy in forward(z, core, g):
            copy.wait_send()
        return carry

    lax.fori_loop(0, nz, drained, 0)

    def sums_sent(g, carry):
        for s in range(1, half):
            for copy in finals(g, s, sib):
                copy.wait_send()
        return carry

    lax.fori_loop(nz - fslots, nz, sums_sent, 0)


def expert_layer(n, nz, mid, gain, router, routes, gate, up, down, cot, cot_all):
    rows, width = mid.shape
    experts = router.shape[1]
    local_experts, _, hid = gate.shape
    inner_w = local_experts * hid
    half = n // 2
    batch = half * rows
    big = n > 8
    fslots = 2 if big else nz
    dma = pltpu.SemaphoreType.DMA
    vmem = pl.BlockSpec(memory_space=pltpu.VMEM)
    hbm = pl.BlockSpec(memory_space=pl.ANY)
    sds = jax.ShapeDtypeStruct
    out_shape = [
        sds((rows, width), f32),
        sds((experts, 128), bf16),
        sds((1, width), f32),
        sds((1, experts), f32),
        sds((local_experts, width, hid), f32),
        sds((local_experts, width, hid), f32),
        sds((inner_w, width), f32),
        sds((nz, batch, width), bf16),
        sds((nz, rows, width), bf16),
    ]
    out_specs = [vmem] * 4 + [hbm] * 5
    scratch = []
    if big:
        out_shape.append(sds((nz, 2, batch, width), bf16))
        out_specs.append(hbm)
        scratch.append(pltpu.VMEM((batch, width), bf16))
    else:
        scratch.append(pltpu.VMEM((nz, 2, batch, width), bf16))
    pair = pltpu.VMEM((2, batch, width), bf16)
    small = pltpu.VMEM((2, half, experts, 128), bf16)
    scratch += [
        pltpu.VMEM((nz, 2, half, experts + 16, 128), bf16),
        pltpu.VMEM((rows, width), bf16),
        pltpu.VMEM((width, inner_w), bf16),
        pltpu.VMEM((width, inner_w), bf16),
        pltpu.VMEM((inner_w, width), bf16),
        pltpu.VMEM((local_experts, width, hid), f32),
        pltpu.VMEM((local_experts, width, hid), f32),
        pltpu.VMEM((inner_w, width), f32),
        pair,
        pltpu.VMEM((batch, inner_w), bf16),
        pltpu.VMEM((batch, inner_w), bf16),
        pltpu.VMEM((batch, inner_w), bf16),
        pair,
        pair,
        pair,
        pair,
        pair,
        pair,
        small,
        small,
        small,
        pltpu.VMEM((nz, rows, width), f32),
        pltpu.VMEM((nz, experts, 128), f32),
        pltpu.VMEM((fslots, half - 1, rows, width), bf16),
        pltpu.VMEM((nz, half - 1, rows, width), bf16),
        pltpu.VMEM((fslots, half - 1, experts, 128), bf16),
        pltpu.VMEM((nz, half - 1, experts, 128), bf16),
        pltpu.VMEM((nz - 1, rows, width), bf16),
        pltpu.VMEM((nz - 1, rows, width), bf16),
        pltpu.VMEM((nz - 1, experts, 128), bf16),
        pltpu.VMEM((nz - 1, experts, 128), bf16),
        dma((3, local_experts)),
        dma((4,)),
        dma((2,)),
        dma((2,)),
        dma,
    ]
    scratch += [dma((nz - 1,))] * 4
    scratch += [dma((nz, half))] * 4
    scratch += [dma((nz,))] * 4
    scratch += [dma((2,))] * 6
    scratch += [dma((nz, 6 if half == 4 else half - 1))] * 2
    scratch += [dma((nz, half - 1))] * 2
    scratch += [dma((nz - 1,))] * 4 + [pltpu.VMEM((nz * rows, 128), f32)]
    return pl.pallas_call(
        functools.partial(expert_kernel, n, nz, big),
        out_shape=out_shape,
        in_specs=[vmem] * 5 + [hbm] * 4,
        out_specs=out_specs,
        scratch_shapes=scratch,
        compiler_params=pltpu.CompilerParams(
            collective_id=1, has_side_effects=True, vmem_limit_bytes=60 << 20
        ),
        name="experts",
    )(mid, gain[None], router.T, routes.T, cot, gate, up, down.reshape(inner_w, width), cot_all)[:9]


def attend_kernel(
    n,
    nz,
    x_ref,
    gain_ref,
    wq_ref,
    wk_ref,
    wv_ref,
    wo_ref,
    cos_ref,
    sin_ref,
    cot_ref,
    lens_ref,
    mid_ref,
    q_ref,
    kv_ref,
    lrow_ref,
    att_ref,
    cot_hbm,
    wqkv,
    wfull,
    qst_s,
    m_s,
    l_s,
    o_s,
    att_low,
    acol,
    ks,
    kr,
    kfs,
    kfr,
    zgs,
    zgr,
    gos,
    gor,
    gps,
    gpr,
    cot_low,
    cs,
    cr,
    cps,
    cpr,
    csem,
):
    e = lax.axis_index("expert")
    z = lax.axis_index("tensor")
    core = lax.rem(e, 2)
    sib = e + 1 - 2 * core
    half = n // 2
    me = e // 2
    tok, width = x_ref.shape
    rows = tok // nz
    qw = wq_ref.shape[1]
    kw = wk_ref.shape[1]
    seqs = kv_ref.shape[0]
    span = tok // seqs
    heads = kw // HD
    groups = qw // kw
    barrier = greet(n, nz, e, z, sib)

    wqkv[:, 0:qw] = wq_ref[...]
    wqkv[:, qw : qw + kw] = wk_ref[...]
    wqkv[:, qw + kw :] = wv_ref[...]
    x = x_ref[...].astype(f32)
    scale1 = lax.rsqrt(jnp.mean(x * x, -1, keepdims=True) + EPS)
    normed = (x * scale1 * gain_ref[...]).astype(bf16)
    lin = dot_nn(normed, wqkv[...])
    turned = turn(lin, cos_ref[...], sin_ref[...], qw + kw, True).astype(bf16)
    q_ref[...] = turned[:, :qw]
    for s in range(seqs):
        kv_ref[s, pl.ds(pl.multiple_of(e * span, 16), span)] = turned[
            s * span : (s + 1) * span, qw:
        ]
    cot_low[...] = cot_ref[...].astype(bf16)
    cot_local = pltpu.make_async_copy(
        cot_low, cot_hbm.at[pl.ds(pl.multiple_of(e * tok, 16), tok)], csem
    )
    cot_local.start()
    pl.semaphore_wait(barrier, half + nz - 1)

    def rows_of(j, s):
        return kv_ref.at[s, pl.ds(pl.multiple_of(j * span, 16), span)]

    half_rows = qw // 2
    my_half = pl.ds(pl.multiple_of(core * half_rows, 16), half_rows)

    def weight_send(k):
        to = (e, lax.rem(z + k, nz))
        return remote(
            wo_ref.at[my_half], wfull.at[z, my_half], gos.at[k - 1], gor.at[k - 1], to
        )

    def weight_copy(zz, k, to):
        ref = wfull.at[zz, my_half]
        return remote(ref, ref, gos.at[k - 1], gor.at[k - 1], (e, to))

    def weight_pass(zz, which, k):
        at = pl.ds(pl.multiple_of(which * half_rows, 16), half_rows)
        ref = wfull.at[zz, at]
        return remote(ref, ref, gps.at[k - 1], gpr.at[k - 1], (sib, z))

    for t in range(1, half):
        to = (lax.rem(e + 2 * t, n), z)
        for s in range(seqs):
            remote(rows_of(e, s), rows_of(e, s), ks.at[t, s], kr.at[t, s], to).start()
    for s in range(seqs):
        remote(rows_of(e, s), rows_of(e, s), kfs.at[0, s], kfr.at[0, s], (sib, z)).start()
    for k in range(1, nz):
        weight_send(k).start()

    square = half == 4
    chip_x = me + 1 - 2 * lax.rem(me, 2)
    chip_y = lax.rem(me + 2, 4)
    chip_d = 3 - me
    low_rows = tok // 2

    def cot_at(chip, first=0, count=tok):
        start = (2 * chip + core) * tok + first
        return cot_hbm.at[pl.ds(pl.multiple_of(start, 16), count)]

    def cot_send(i, chip):
        return remote(cot_low, cot_at(me), cs.at[i], cr.at[i], (2 * chip + core, z))

    def cot_recv(i, chip):
        return remote(cot_at(chip), cot_at(chip), cs.at[i], cr.at[i], (2 * chip + core, z))

    def cot_relay(i, chip, to):
        ref = cot_at(chip, 0, low_rows) if i == 2 else cot_at(chip, low_rows, tok - low_rows)
        return remote(ref, ref, cs.at[i], cr.at[i], (2 * to + core, z))

    def cot_pass(t, chip, parity):
        start = (2 * chip + parity) * tok
        ref = cot_hbm.at[pl.ds(pl.multiple_of(start, 16), tok)]
        return remote(ref, ref, cps.at[t], cpr.at[t], (sib, z))

    if square:
        cot_pushes = [cot_send(0, chip_x), cot_send(1, chip_y)]
        cot_chips = [me, chip_x, chip_y, chip_d]
    else:
        cot_pushes = [cot_send(t - 1, lax.rem(me + t, half)) for t in range(1, half)]
        cot_chips = [lax.rem(me + half - t, half) for t in range(half)]
    for copy in cot_pushes:
        copy.start()
    cot_local.wait()
    cot_pass(0, me, core).start()
    wfull[z] = wo_ref[...]

    def forward(t, carry):
        src = lax.rem(e - 2 * t + n, n)
        for s in range(seqs):
            remote(rows_of(src, s), rows_of(src, s), ks.at[t, s], kr.at[t, s], (src, z)).wait_recv()
            remote(rows_of(src, s), rows_of(src, s), kfs.at[t, s], kfr.at[t, s], (sib, z)).start()
        return carry

    lax.fori_loop(1, half, forward, 0)

    def arrive(t, carry):
        src = lax.rem(sib - 2 * t + n, n)
        for s in range(seqs):
            remote(
                rows_of(src, s), rows_of(src, s), kfs.at[t, s], kfr.at[t, s], (sib, z)
            ).wait_recv()
        return carry

    lax.fori_loop(0, half, arrive, 0)

    ck = 2 * span
    last = (e * span + span - 1) // ck
    stacked = groups * span
    qpos = lax.broadcasted_iota(jnp.int32, (stacked, ck), 0)
    qpos = e * span + lax.rem(qpos, span)
    kiota = lax.broadcasted_iota(jnp.int32, (stacked, ck), 1)
    klane = lax.broadcasted_iota(jnp.int32, (1, ck), 1)
    m_s[...] = jnp.full_like(m_s, -1e30)
    l_s[...] = jnp.zeros_like(l_s)
    o_s[...] = jnp.zeros_like(o_s)
    for s in range(seqs):
        for h in range(heads):
            qst_s[s * heads + h] = jnp.concatenate(
                [
                    q_ref[
                        s * span : (s + 1) * span,
                        (h * groups + g) * HD : (h * groups + g + 1) * HD,
                    ]
                    for g in range(groups)
                ],
                0,
            ) * jnp.array(HD ** (-0.5), bf16)

    def chunk(c, diagonal):
        at = pl.ds(pl.multiple_of(c * ck, 16), ck)
        for s in range(seqs):
            for h in range(heads):
                i = s * heads + h
                keys = kv_ref[s, at, h * HD : (h + 1) * HD]
                vals = kv_ref[s, at, kw + h * HD : kw + (h + 1) * HD]
                scores = dot_nt(qst_s[i], keys)
                if diagonal:
                    kpos = kiota + c * ck
                    scores = jnp.where((kpos <= qpos) & (kpos < lens_ref[s]), scores, -1e30)
                else:
                    scores = scores + jnp.where(klane + c * ck < lens_ref[s], 0.0, -1e30)
                old = m_s[i, :, 0:1]
                new = jnp.maximum(old, jnp.max(scores, -1, keepdims=True))
                weights = jnp.exp(scores - new)
                shrink = jnp.exp(old - new)
                m_s[i] = jnp.broadcast_to(new, (stacked, 128))
                l_s[i] = l_s[i] * shrink + jnp.sum(weights, -1, keepdims=True)
                o_s[i] = o_s[i] * shrink + dot_nn(weights.astype(bf16), vals)

    def whole_chunk(c, carry):
        chunk(c, False)
        return carry

    lax.fori_loop(0, last, whole_chunk, 0)
    chunk(last, True)
    for s in range(seqs):
        for h in range(heads):
            i = s * heads + h
            result = o_s[i] / l_s[i, :, 0:HD]
            for g in range(groups):
                cols = slice((h * groups + g) * HD, (h * groups + g + 1) * HD)
                att_ref[s * span : (s + 1) * span, cols] = result[g * span : (g + 1) * span]
            logs = m_s[i] + jnp.log(l_s[i])
            lrow_ref[i] = logs.T[0:8]

    att_low[...] = att_ref[...].astype(bf16)
    own_rows = pl.ds(pl.multiple_of(z * rows, 16), rows)

    def row_copy(k, to):
        src = att_low.at[pl.ds(pl.multiple_of(to * rows, 16), rows)]
        return remote(src, acol.at[z], zgs.at[k - 1], zgr.at[k - 1], (e, to))

    for k in range(1, nz):
        row_copy(k, lax.rem(z + k, nz)).start()
    acol[z] = att_low[own_rows, :]
    for k in range(1, nz):
        zz = lax.rem(z + nz - k, nz)
        weight_copy(zz, k, zz).wait_recv()
        weight_pass(zz, core, k).start()
    if square:
        cot_recv(0, chip_x).wait_recv()
        cot_relay(2, chip_x, chip_y).start()
        cot_pass(1, chip_x, core).start()
        cot_recv(1, chip_y).wait_recv()
        cot_relay(3, chip_y, chip_x).start()
        cot_pass(2, chip_y, core).start()
    else:
        for t in range(1, half):
            cot_recv(t - 1, cot_chips[t]).wait_recv()
            cot_pass(t, cot_chips[t], core).start()
    for k in range(1, nz):
        row_copy(k, lax.rem(z + nz - k, nz)).wait_recv()
        weight_pass(lax.rem(z + nz - k, nz), 1 - core, k).wait_recv()
    mid = x_ref[own_rows, :].astype(f32)
    for zz in range(nz):
        mid = mid + dot_nn(acol[zz], wfull[zz])
    mid_ref[...] = mid
    if square:
        cot_relay(2, chip_d, chip_y).wait_recv()
        cot_relay(3, chip_d, chip_x).wait_recv()
        cot_pass(3, chip_d, core).start()
        cot_relay(2, chip_x, chip_y).wait_send()
        cot_relay(3, chip_y, chip_x).wait_send()
    for copy in cot_pushes:
        copy.wait_send()
    for t in range(half):
        cot_pass(t, cot_chips[t], 1 - core).wait_recv()
        cot_pass(t, cot_chips[t], core).wait_send()
    for k in range(1, nz):
        row_copy(k, lax.rem(z + k, nz)).wait_send()
        weight_send(k).wait_send()
        weight_pass(lax.rem(z + nz - k, nz), core, k).wait_send()

    def sent(t, carry):
        for s in range(seqs):

            @pl.when(t > 0)
            def _():
                remote(
                    rows_of(e, s), rows_of(e, s), ks.at[t, s], kr.at[t, s], (sib, z)
                ).wait_send()

            remote(rows_of(e, s), rows_of(e, s), kfs.at[t, s], kfr.at[t, s], (sib, z)).wait_send()
        return carry

    lax.fori_loop(0, half, sent, 0)


def attend_layer(n, nz, x, gain, wq, wk, wv, wo, cos, sin, cot, lens):
    tok, width = x.shape
    rows = tok // nz
    qw, kw = wq.shape[1], wk.shape[1]
    seqs = lens.shape[0]
    span = tok // seqs
    half = n // 2
    stacked = (qw // kw) * span
    pairs = seqs * (kw // HD)
    dma = pltpu.SemaphoreType.DMA
    vmem = pl.BlockSpec(memory_space=pltpu.VMEM)
    sds = jax.ShapeDtypeStruct
    return pl.pallas_call(
        functools.partial(attend_kernel, n, nz),
        out_shape=[
            sds((rows, width), f32),
            sds((tok, qw), bf16),
            sds((seqs, n * span, 2 * kw), bf16),
            sds((seqs * (kw // HD), 8, stacked), f32),
            sds((tok, qw), f32),
            sds((n * tok, width), bf16),
        ],
        in_specs=[vmem] * 9 + [pl.BlockSpec(memory_space=pltpu.SMEM)],
        out_specs=[vmem] * 5 + [pl.BlockSpec(memory_space=pl.ANY)],
        scratch_shapes=[
            pltpu.VMEM((width, qw + 2 * kw), bf16),
            pltpu.VMEM((nz, qw, width), bf16),
            pltpu.VMEM((pairs, stacked, HD), bf16),
            pltpu.VMEM((pairs, stacked, 128), f32),
            pltpu.VMEM((pairs, stacked, 128), f32),
            pltpu.VMEM((pairs, stacked, HD), f32),
            pltpu.VMEM((tok, qw), bf16),
            pltpu.VMEM((nz, rows, qw), bf16),
        ]
        + [dma((half, seqs))] * 4
        + [dma((nz - 1,))] * 6
        + [pltpu.VMEM((tok, width), bf16)]
        + [dma((max(half, 4),))] * 4
        + [dma],
        compiler_params=pltpu.CompilerParams(
            collective_id=2, has_side_effects=True, vmem_limit_bytes=60 << 20
        ),
        name="attend",
    )(x, gain[None], wq, wk, wv, wo, cos, sin, cot, lens)


def return_kernel(
    n,
    nz,
    gmid_ref,
    mid_ref,
    glog_ref,
    ggrad_ref,
    xn_ref,
    x_ref,
    gain_ref,
    wq_ref,
    wk_ref,
    wv_ref,
    wo_ref,
    cos_ref,
    sin_ref,
    q_ref,
    kv_ref,
    lrow_ref,
    att_ref,
    lens_ref,
    mixed_hbm,
    obuf,
    igbuf,
    wall,
    wall2,
    small_ref,
    wqkv,
    gat,
    datt,
    dq_s,
    qst_s,
    dst_s,
    acc_q,
    dkv,
    kvo,
    kvi,
    kvf,
    kvr,
    part,
    sums,
    csend,
    crecv,
    osend,
    orecv,
    wbufs,
    wbufs2,
    sz1,
    sz2,
    sown,
    ssib,
    schip,
    ofin,
    zas,
    zar,
    zos,
    zor,
    zis,
    zir,
    zps,
    zpr,
    zqs,
    zqr,
    z1s,
    z1r,
    z2s,
    z2r,
    kos,
    kor,
    kfs,
    kfr,
    wsems,
    wsems2,
    sbs,
    sbr,
    scs,
    scr,
    ofs,
    ofr,
    olsem,
    obase,
):
    e = lax.axis_index("expert")
    z = lax.axis_index("tensor")
    core = lax.rem(e, 2)
    me = e // 2
    sib = e + 1 - 2 * core
    half = n // 2
    rows, width = gmid_ref.shape
    tok = rows * nz
    qw = wq_ref.shape[1]
    kw = wk_ref.shape[1]
    seqs = kv_ref.shape[0]
    span = tok // seqs
    heads = kw // HD
    groups = qw // kw
    dn = width // n
    experts = glog_ref.shape[0]
    own_rows = pl.ds(pl.multiple_of(z * rows, 16), rows)
    barrier = greet(n, nz, e, z, sib)
    w1 = PlaneSum(n, e, z, sib, wall, *wbufs, *wsems)
    w2 = PlaneSum(n, e, z, sib, wall2, *wbufs2, *wsems2)

    gat[own_rows, :] = gmid_ref[...].astype(bf16)
    sz1[z] = glog_ref[...]
    pl.semaphore_wait(barrier, half + nz - 1)

    def part_of(ref):
        return lambda zz: ref.at[pl.ds(pl.multiple_of(zz * rows, 16), rows)]

    def slot_of(ref):
        return lambda zz: ref.at[zz]

    gat_line = Line(z, nz, e, part_of(gat), zas, zar)
    out_line = Line(z, nz, e, part_of(obuf), zos, zor)
    igrad_line = Line(z, nz, e, part_of(igbuf), zis, zir)
    normed_sum = LineSum(z, nz, e, csend, crecv, zps, zpr)

    def z_copies(buf_of, send, recv):
        return [
            remote(
                buf_of(z), buf_of(z), send.at[k - 1], recv.at[k - 1], (e, lax.rem(z + k, nz))
            )
            for k in range(1, nz)
        ]

    def z_arrivals(buf_of, send, recv):
        return [
            remote(
                buf_of(lax.rem(z + nz - k, nz)),
                buf_of(lax.rem(z + nz - k, nz)),
                send.at[k - 1],
                recv.at[k - 1],
                (e, lax.rem(z + nz - k, nz)),
            )
            for k in range(1, nz)
        ]

    gat_line.start()
    for copy in z_copies(slot_of(sz1), z1s, z1r):
        copy.start()

    square = half == 4
    chip_x = me + 1 - 2 * lax.rem(me, 2)
    chip_y = lax.rem(me + 2, 4)
    chip_d = 3 - me
    low, high = pl.ds(0, nz // 2), pl.ds(nz // 2, nz - nz // 2)

    def mixed_at(chip, which=slice(None)):
        return mixed_hbm.at[which, pl.ds(pl.multiple_of(chip * rows, 16), rows), :]

    def mixed_copy(src, dst, i, chip):
        return remote(src, dst, ofs.at[i], ofr.at[i], (2 * chip + core, z))

    def mixed_sends():
        if not square:
            return [
                mixed_copy(
                    mixed_at(lax.rem(me + half - t, half)),
                    ofin.at[t],
                    t - 1,
                    lax.rem(me + half - t, half),
                )
                for t in range(1, half)
            ]
        return [
            mixed_copy(mixed_at(chip_d, low), ofin.at[3, low], 0, chip_x),
            mixed_copy(mixed_at(chip_d, high), ofin.at[3, high], 1, chip_y),
            mixed_copy(mixed_at(chip_x, low), ofin.at[1, low], 2, chip_x),
            mixed_copy(mixed_at(chip_y, high), ofin.at[2, high], 3, chip_y),
        ]

    def mixed_relays():
        return [
            mixed_copy(obase.at[low], ofin.at[2, low], 4, chip_y),
            mixed_copy(obase.at[high], ofin.at[1, high], 5, chip_x),
        ]

    for copy in mixed_sends():
        copy.start()
    mixed_own = [pltpu.make_async_copy(mixed_at(me), ofin.at[0], olsem.at[0])]
    if square:
        mixed_own += [
            pltpu.make_async_copy(mixed_at(chip_y, low), obase.at[low], olsem.at[1]),
            pltpu.make_async_copy(mixed_at(chip_x, high), obase.at[high], olsem.at[2]),
        ]
    for copy in mixed_own:
        copy.start()

    def mixed_relay():
        waits = mixed_sends()
        for copy, part, i in zip(mixed_relays(), (low, high), (0, 1)):
            waits[i].wait_recv()
            obase[part] = (obase[part].astype(f32) + ofin[3, part].astype(f32)).astype(bf16)
            copy.start()

    mixed_count = 3 if square else half

    def mixed_sum(zz):
        total = ofin[0, zz].astype(f32)
        for t in range(1, mixed_count):
            total = total + ofin[t, zz].astype(f32)
        return total

    wqkv[:, 0:qw] = wq_ref[...]
    wqkv[:, qw : qw + kw] = wk_ref[...]
    wqkv[:, qw + kw :] = wv_ref[...]
    x = x_ref[...].astype(f32)
    scale1 = lax.rsqrt(jnp.mean(x * x, -1, keepdims=True) + EPS)
    normed = (x * scale1 * gain_ref[...]).astype(bf16)
    dkv[...] = jnp.zeros_like(dkv)

    for hop in range(1, nz):
        gat_line.hop(hop)
    datt[...] = dot_nt(gat[...], wo_ref[...]).astype(bf16)

    ck = 2 * span
    last = (e * span + span - 1) // ck
    stacked = groups * span
    kiota = lax.broadcasted_iota(jnp.int32, (ck, stacked), 0)
    krow = lax.broadcasted_iota(jnp.int32, (ck, 1), 0)
    qpos = e * span + lax.rem(lax.broadcasted_iota(jnp.int32, (ck, stacked), 1), span)
    drows = []
    for s in range(seqs):
        for h in range(heads):

            def gather(ref):
                return jnp.concatenate(
                    [
                        ref[
                            s * span : (s + 1) * span,
                            (h * groups + g) * HD : (h * groups + g + 1) * HD,
                        ]
                        for g in range(groups)
                    ],
                    0,
                )

            i = s * heads + h
            qst_s[i] = gather(q_ref) * jnp.array(HD ** (-0.5), bf16)
            dst = gather(datt)
            dst_s[i] = dst
            delta = jnp.sum(dst.astype(f32) * gather(att_ref), -1, keepdims=True)
            drows.append(jnp.broadcast_to(delta, (stacked, 128)).T[0:1])
    acc_q[...] = jnp.zeros_like(acc_q)
    for copy in mixed_own:
        copy.wait()
    if square:
        mixed_relay()

    def chunk(c, diagonal):
        at = pl.ds(pl.multiple_of(c * ck, 16), ck)
        for s in range(seqs):
            for h in range(heads):
                i = s * heads + h
                keys = kv_ref[s, at, h * HD : (h + 1) * HD]
                vals = kv_ref[s, at, kw + h * HD : kw + (h + 1) * HD]
                scores = dot_nt(keys, qst_s[i]) - lrow_ref[i, 0:1, :]
                if diagonal:
                    kpos = kiota + c * ck
                    allowed = (kpos <= qpos) & (kpos < lens_ref[s])
                    soft = jnp.where(allowed, jnp.exp(scores), 0.0)
                else:
                    soft = jnp.exp(scores + jnp.where(krow + c * ck < lens_ref[s], 0.0, -1e30))
                grad_probs = dot_nt(vals, dst_s[i])
                grad_scores = (soft * (grad_probs - drows[i])).astype(bf16)
                dkv[s, at, h * HD : (h + 1) * HD] = dot_nn(grad_scores, qst_s[i])
                dkv[s, at, kw + h * HD : kw + (h + 1) * HD] = dot_nn(soft.astype(bf16), dst_s[i])
                acc_q[i] += dot_tn(grad_scores, keys)

    def whole_chunk(c, carry):
        chunk(c, False)
        return carry

    lax.fori_loop(0, last, whole_chunk, 0)
    chunk(last, True)
    for s in range(seqs):
        for h in range(heads):
            result = acc_q[s * heads + h] * HD ** (-0.5)
            for g in range(groups):
                cols = slice((h * groups + g) * HD, (h * groups + g + 1) * HD)
                dq_s[s * span : (s + 1) * span, cols] = result[g * span : (g + 1) * span]

    def key_rows(j, s):
        return dkv[s, pl.ds(pl.multiple_of(j * span, 16), span), :]

    def key_send(t):
        return remote(kvo.at[t], kvi.at[t], kos.at[t], kor.at[t], (sib, z))

    def key_final(t):
        to = (lax.rem(e - 2 * t + n, n), z)
        return remote(kvf.at[t - 1], kvr.at[t - 1], kfs.at[t - 1], kfr.at[t - 1], to)

    def key_give(i, carry):
        t = half - 1 - i
        oth = lax.rem(sib - 2 * t + n, n)
        for s in range(seqs):
            kvo[t, s] = key_rows(oth, s).astype(bf16)
        key_send(t).start()
        return carry

    lax.fori_loop(0, half, key_give, 0)

    def key_pass(i, carry):
        t = half - 1 - i
        key_send(t).wait_recv()
        own = lax.rem(e - 2 * t + n, n)
        for s in range(seqs):
            kvf[t - 1, s] = (key_rows(own, s) + kvi[t, s].astype(f32)).astype(bf16)
        key_final(t).start()
        return carry

    cos, sin = cos_ref[...], sin_ref[...]
    gq = turn(dq_s[...], cos, sin, qw, False).astype(bf16)
    query_part = dot_tn(normed, gq)
    out_part = dot_tn(gat[...], att_ref[...].astype(bf16))
    for j in range(n):
        w1.pack[j, :, :qw] = query_part[j * dn : (j + 1) * dn].astype(bf16)
        w1.pack[j, :, qw:] = out_part[j * dn : (j + 1) * dn].astype(bf16)
    lax.fori_loop(0, half - 1, key_pass, 0)
    w1.give()

    def mixed_last(k, to):
        return remote(osend.at[k - 1], orecv.at[k - 1], zqs.at[k - 1], zqr.at[k - 1], (e, to))

    for copy in mixed_sends()[2:] + mixed_relays() if square else mixed_sends():
        copy.wait_recv()
    for k in range(1, nz):
        zz = lax.rem(z + k, nz)
        osend[k - 1] = mixed_sum(zz).astype(bf16)
        mixed_last(k, zz).start()
    own_mixed = mid_ref[...] + mixed_sum(z)
    w1.spread()
    for copy in z_arrivals(slot_of(sz1), z1s, z1r):
        copy.wait_recv()
    rgrad = dot_nn(sz1[0][:, :rows], xn_ref[0])
    for zz in range(1, nz):
        rgrad = rgrad + dot_nn(sz1[zz][:, :rows], xn_ref[zz])
    sown[0:experts, :] = rgrad.astype(bf16)

    key_send(0).wait_recv()
    own_kv = [key_rows(e, s) + kvi[0, s].astype(f32) for s in range(seqs)]
    for t in range(1, half):
        key_final(t).wait_recv()
        for s in range(seqs):
            own_kv[s] = own_kv[s] + kvr[t - 1, s].astype(f32)
    gkv = turn(jnp.concatenate(own_kv, 0), cos, sin, kw, False).astype(bf16)
    part[...] = dot_nt(gq, wqkv[:, :qw]) + dot_nt(gkv, wqkv[:, qw:])

    def normed_part(zz):
        return part[pl.ds(pl.multiple_of(zz * rows, 16), rows), :]

    for hop in range(nz - 1):
        normed_sum.hop(hop, normed_part)
        if hop > 0:
            out_line.hop(hop)
        if hop == 0:
            for k in range(1, nz):
                mixed_last(k, z).wait_recv()
                own_mixed = own_mixed + orecv[k - 1].astype(f32)
            obuf[own_rows, :] = own_mixed.astype(bf16)
            out_line.start()
            again = jnp.sum(part[...] * x * scale1, 0, keepdims=True)
            sz2[z] = jnp.concatenate([again, ggrad_ref[...], jnp.zeros((14, width), f32)], 0).astype(
                bf16
            )
            for copy in z_copies(slot_of(sz2), z2s, z2r):
                copy.start()
            pair_part = dot_tn(normed, gkv)
            for j in range(n):
                w2.pack[j] = pair_part[j * dn : (j + 1) * dn].astype(bf16)
            w2.give()
            w1.total()
        if hop == 1:
            w2.spread()
    if nz == 2:
        w2.spread()
    w1.forward()
    for copy in z_arrivals(slot_of(sz2), z2s, z2r):
        copy.wait_recv()
    second = sz2[0].astype(f32)
    for zz in range(1, nz):
        second = second + sz2[zz].astype(f32)
    sown[experts:, :] = second.astype(bf16)
    small_sib = remote(sown, ssib, sbs, sbr, (sib, z))
    small_sib.start()
    normed_sum.total(sums, normed_part)

    own_x = x_ref[own_rows, :].astype(f32)
    own_scale = lax.rsqrt(jnp.mean(own_x * own_x, -1, keepdims=True) + EPS)
    grad_normed = sums[...]
    gained = grad_normed * gain_ref[...]
    igrad = (
        gmid_ref[...]
        + own_scale * gained
        - own_x
        * (own_scale * own_scale * own_scale)
        * jnp.mean(gained * own_x, -1, keepdims=True)
    )
    igbuf[own_rows, :] = igrad.astype(bf16)
    igrad_line.start()
    out_line.hop(nz - 1)

    w2.total()
    small_sib.wait_recv()
    schip[me] = (sown[...].astype(f32) + ssib[...].astype(f32)).astype(bf16)

    def small_send(t):
        to = (lax.rem(e + 2 * t, n), z)
        return remote(schip.at[me], schip.at[me], scs.at[t - 1], scr.at[t - 1], to)

    for t in range(1, half):
        small_send(t).start()

    for hop in range(1, nz - 1):
        igrad_line.hop(hop)
    w2.forward()
    igrad_line.hop(nz - 1)
    for t in range(1, half):
        src = lax.rem(me + half - t, half)
        remote(
            schip.at[src], schip.at[src], scs.at[t - 1], scr.at[t - 1], (sib, z)
        ).wait_recv()
    small = schip[0].astype(f32)
    for t in range(1, half):
        small = small + schip[t].astype(f32)
    small_ref[...] = small

    w1.arrive()
    w2.arrive()
    for k in range(1, nz):
        mixed_last(k, z).wait_send()
    for line in (gat_line, out_line, igrad_line, normed_sum, w1, w2):
        line.drain()
    for copy in z_copies(slot_of(sz1), z1s, z1r) + z_copies(slot_of(sz2), z2s, z2r):
        copy.wait_send()
    small_sib.wait_send()
    for copy in mixed_sends() + (mixed_relays() if square else []):
        copy.wait_send()

    def drained(t, carry):
        key_send(t).wait_send()

        @pl.when(t > 0)
        def _():
            key_final(t).wait_send()
            small_send(t).wait_send()

        return carry

    lax.fori_loop(0, half, drained, 0)


class PlaneSum:
    def __init__(self, n, e, z, sib, wall, pack, near, send, recv, *sems):
        self.n, self.e, self.z, self.sib, self.half = n, e, z, sib, n // 2
        self.wall, self.pack, self.near, self.send, self.recv = wall, pack, near, send, recv
        self.sems = sems

    def peer(self, base, t):
        return lax.rem(base - 2 * t + self.n, self.n)

    def near_copy(self, t):
        src = self.pack.at[self.peer(self.sib, t)]
        return remote(
            src, self.near.at[t], self.sems[0].at[t], self.sems[1].at[t], (self.sib, self.z)
        )

    def far_copy(self, t):
        return remote(
            self.send.at[t - 1],
            self.recv.at[t - 1],
            self.sems[2].at[t],
            self.sems[3].at[t],
            (self.peer(self.e, t), self.z),
        )

    def all_copy(self, src, t, to):
        ref = self.wall.at[src]
        return remote(ref, ref, self.sems[4].at[t], self.sems[5].at[t], (to, self.z))

    def pass_copy(self, src, t):
        ref = self.wall.at[src]
        return remote(ref, ref, self.sems[6].at[t], self.sems[7].at[t], (self.sib, self.z))

    def give(self):
        def one(i, carry):
            self.near_copy(self.half - 1 - i).start()
            return carry

        lax.fori_loop(0, self.half, one, 0)

    def spread(self):
        def one(i, carry):
            t = self.half - 1 - i
            self.near_copy(t).wait_recv()
            own = self.pack[self.peer(self.e, t)].astype(f32)
            self.send[t - 1] = (own + self.near[t].astype(f32)).astype(bf16)
            self.far_copy(t).start()
            return carry

        lax.fori_loop(0, self.half - 1, one, 0)

    def total(self):
        self.near_copy(0).wait_recv()
        total = self.pack[self.e].astype(f32) + self.near[0].astype(f32)
        for t in range(1, self.half):
            self.far_copy(t).wait_recv()
            total = total + self.recv[t - 1].astype(f32)
        self.wall[self.e] = total.astype(bf16)
        for t in range(1, self.half):
            self.all_copy(self.e, t, lax.rem(self.e + 2 * t, self.n)).start()
        self.pass_copy(self.e, 0).start()

    def forward(self):
        def one(t, carry):
            src = self.peer(self.e, t)
            self.all_copy(src, t, src).wait_recv()
            self.pass_copy(src, t).start()
            return carry

        lax.fori_loop(1, self.half, one, 0)

    def arrive(self):
        def one(t, carry):
            self.pass_copy(self.peer(self.sib, t), t).wait_recv()
            return carry

        lax.fori_loop(0, self.half, one, 0)

    def drain(self):
        def one(t, carry):
            self.near_copy(t).wait_send()
            self.pass_copy(self.e, t).wait_send()

            @pl.when(t > 0)
            def _():
                self.far_copy(t).wait_send()
                self.all_copy(self.e, t, self.sib).wait_send()

            return carry

        lax.fori_loop(0, self.half, one, 0)


class Line:
    def __init__(self, z, nz, e, buf_of, send, recv):
        self.z, self.nz, self.e = z, nz, e
        self.buf_of, self.send, self.recv = buf_of, send, recv

    def copy(self, way, piece):
        to = self.z + 1 if way == 0 else self.z - 1
        ref = self.buf_of(piece)
        return remote(ref, ref, self.send.at[way, piece], self.recv.at[way, piece], (self.e, to))

    def push(self, piece, ways=(0, 1)):
        for way in ways:

            @pl.when(self.z < self.nz - 1 if way == 0 else self.z > 0)
            def _():
                self.copy(way, piece).start()

    def start(self):
        self.push(self.z)

    def hop(self, i):
        @pl.when(self.z >= i)
        def _():
            self.copy(0, self.z - i).wait_recv()
            self.push(self.z - i, (0,))

        @pl.when(self.z + i <= self.nz - 1)
        def _():
            self.copy(1, self.z + i).wait_recv()
            self.push(self.z + i, (1,))

    def drain(self):
        for piece in range(self.nz):

            @pl.when((self.z >= piece) & (self.z < self.nz - 1))
            def _():
                self.copy(0, piece).wait_send()

            @pl.when((self.z <= piece) & (self.z > 0))
            def _():
                self.copy(1, piece).wait_send()


class LineSum:
    def __init__(self, z, nz, e, send_buf, recv_buf, send, recv):
        self.z, self.nz, self.e = z, nz, e
        self.send_buf, self.recv_buf, self.send, self.recv = send_buf, recv_buf, send, recv

    def copy(self, way, target):
        to = self.z + 1 if way == 0 else self.z - 1
        return remote(
            self.send_buf.at[way, target],
            self.recv_buf.at[way, target],
            self.send.at[way, target],
            self.recv.at[way, target],
            (self.e, to),
        )

    def hop(self, i, own_of):
        for way, target in ((0, self.nz - 1 - i), (1, i)):
            passes = self.z < target if way == 0 else self.z > target
            first = self.z == 0 if way == 0 else self.z == self.nz - 1
            inner = self.z > 0 if way == 0 else self.z < self.nz - 1

            @pl.when(passes & first)
            def _():
                self.send_buf[way, target] = own_of(target).astype(bf16)
                self.copy(way, target).start()

            @pl.when(passes & inner)
            def _():
                self.copy(way, target).wait_recv()
                self.send_buf[way, target] = (
                    own_of(target) + self.recv_buf[way, target].astype(f32)
                ).astype(bf16)
                self.copy(way, target).start()

    def total(self, ref, own_of):
        ref[...] = own_of(self.z)

        @pl.when(self.z > 0)
        def _():
            self.copy(0, self.z).wait_recv()
            ref[...] += self.recv_buf[0, self.z].astype(f32)

        @pl.when(self.z < self.nz - 1)
        def _():
            self.copy(1, self.z).wait_recv()
            ref[...] += self.recv_buf[1, self.z].astype(f32)

    def drain(self):
        for target in range(self.nz):

            @pl.when(self.z < target)
            def _():
                self.copy(0, target).wait_send()

            @pl.when(self.z > target)
            def _():
                self.copy(1, target).wait_send()


def return_layer(
    n, nz, gmid, mid, glog, ggrad, xn, x, gain, wq, wk, wv, wo, cos, sin, q, kv, lrow, att, lens, mixed
):
    tok, width = x.shape
    rows = tok // nz
    qw, kw = wq.shape[1], wk.shape[1]
    seqs = lens.shape[0]
    span = tok // seqs
    half = n // 2
    stacked = (qw // kw) * span
    pairs = seqs * (kw // HD)
    experts = glog.shape[0]
    small_rows = experts + 16
    dma = pltpu.SemaphoreType.DMA
    vmem = pl.BlockSpec(memory_space=pltpu.VMEM)
    sds = jax.ShapeDtypeStruct
    zdma = dma((nz - 1,))
    line = dma((2, nz))
    hdma = dma((half,))
    fdma = dma((half - 1,))
    def plane_bufs(cols):
        return [
            pltpu.VMEM((n, width // n, cols), bf16),
            pltpu.VMEM((half, width // n, cols), bf16),
            pltpu.VMEM((half - 1, width // n, cols), bf16),
            pltpu.VMEM((half - 1, width // n, cols), bf16),
        ]

    line_buf = pltpu.VMEM((2, nz, rows, width), bf16)
    return pl.pallas_call(
        functools.partial(return_kernel, n, nz),
        out_shape=[
            sds((tok, width), bf16),
            sds((tok, width), bf16),
            sds((n, width // n, 2 * qw), bf16),
            sds((n, width // n, 2 * kw), bf16),
            sds((small_rows, width), f32),
        ],
        in_specs=[vmem] * 17
        + [pl.BlockSpec(memory_space=pltpu.SMEM), pl.BlockSpec(memory_space=pl.ANY)],
        out_specs=[vmem] * 5,
        scratch_shapes=[
            pltpu.VMEM((width, qw + 2 * kw), bf16),
            pltpu.VMEM((tok, width), bf16),
            pltpu.VMEM((tok, qw), bf16),
            pltpu.VMEM((tok, qw), f32),
            pltpu.VMEM((pairs, stacked, HD), bf16),
            pltpu.VMEM((pairs, stacked, HD), bf16),
            pltpu.VMEM((pairs, stacked, HD), f32),
            pltpu.VMEM((seqs, n * span, 2 * kw), f32),
            pltpu.VMEM((half, seqs, span, 2 * kw), bf16),
            pltpu.VMEM((half, seqs, span, 2 * kw), bf16),
            pltpu.VMEM((half - 1, seqs, span, 2 * kw), bf16),
            pltpu.VMEM((half - 1, seqs, span, 2 * kw), bf16),
            pltpu.VMEM((tok, width), f32),
            pltpu.VMEM((rows, width), f32),
            line_buf,
            line_buf,
            pltpu.VMEM((nz - 1, rows, width), bf16),
            pltpu.VMEM((nz - 1, rows, width), bf16),
            plane_bufs(2 * qw),
            plane_bufs(2 * kw),
            pltpu.VMEM((nz, experts, 128), bf16),
            pltpu.VMEM((nz, 16, width), bf16),
            pltpu.VMEM((small_rows, width), bf16),
            pltpu.VMEM((small_rows, width), bf16),
            pltpu.VMEM((half, small_rows, width), bf16),
            pltpu.VMEM((half, nz, rows, width), bf16),
        ]
        + [line] * 8
        + [zdma] * 6
        + [hdma, hdma, fdma, fdma]
        + [[hdma] * 8, [hdma] * 8]
        + [dma, dma, fdma, fdma]
        + [dma((6 if half == 4 else half - 1,))] * 2
        + [dma((3,)), pltpu.VMEM((nz, rows, width), bf16)],
        compiler_params=pltpu.CompilerParams(
            collective_id=3, has_side_effects=True, vmem_limit_bytes=58 << 20
        ),
        name="attend_back",
    )(
        gmid,
        mid,
        glog,
        ggrad,
        xn,
        x,
        gain[None],
        wq,
        wk,
        wv,
        wo,
        cos,
        sin,
        q,
        kv,
        lrow,
        att,
        lens,
        mixed,
    )


def finish_kernel(
    out_low,
    igrad_low,
    wall,
    wall2,
    small,
    load,
    dgate_in,
    dup_in,
    ddown_in,
    out_ref,
    igrad_ref,
    q_ref,
    k_ref,
    v_ref,
    o_ref,
    router_ref,
    again_ref,
    egain_ref,
    loss_ref,
    load_ref,
    dgate,
    dup,
    ddown,
    dgate_s,
    dup_s,
    ddown_s,
    sems,
):
    pairs = ((dgate_in, dgate_s, dgate), (dup_in, dup_s, dup), (ddown_in, ddown_s, ddown))
    reads = [pltpu.make_async_copy(p[0], p[1], sems.at[0, i]) for i, p in enumerate(pairs)]
    writes = [pltpu.make_async_copy(p[1], p[2], sems.at[1, i]) for i, p in enumerate(pairs)]
    for copy in reads:
        copy.start()
    qw, kw = q_ref.shape[1], k_ref.shape[1]
    experts = load.shape[1]
    out_ref[...] = out_low[...].astype(f32)
    for read, write in zip(reads, writes):
        read.wait()
        write.start()
    igrad_ref[...] = igrad_low[...].astype(f32)
    chunks, dn, _ = wall.shape
    flat = wall[...].reshape(chunks * dn, 2 * qw).astype(f32)
    q_ref[...] = flat[:, :qw]
    o_ref[...] = flat[:, qw:].T
    flat = wall2[...].reshape(chunks * dn, 2 * kw).astype(f32)
    k_ref[...] = flat[:, :kw]
    v_ref[...] = flat[:, kw:]
    router_ref[...] = small[0:experts, :]
    again_ref[...] = small[experts : experts + 1, :]
    egain_ref[...] = small[experts + 1 : experts + 2, :]
    load_ref[...] = load[...]
    loss_ref[...] = jnp.mean(load[...], -1, keepdims=True)
    for copy in writes:
        copy.wait()


def finish_layer(out_low, igrad_low, wall, wall2, small, load, dgate, dup, ddown, qw, kw):
    tok, width = out_low.shape
    experts = load.shape[1]
    vmem = pl.BlockSpec(memory_space=pltpu.VMEM)
    hbm = pl.BlockSpec(memory_space=pl.ANY)
    sds = jax.ShapeDtypeStruct
    return pl.pallas_call(
        finish_kernel,
        out_shape=[
            sds((tok, width), f32),
            sds((tok, width), f32),
            sds((width, qw), f32),
            sds((width, kw), f32),
            sds((width, kw), f32),
            sds((qw, width), f32),
            sds((experts, width), f32),
            sds((1, width), f32),
            sds((1, width), f32),
            sds((1, 1), f32),
            sds((1, experts), f32),
            sds(dgate.shape, f32),
            sds(dup.shape, f32),
            sds(ddown.shape, f32),
        ],
        in_specs=[vmem] * 6 + [hbm] * 3,
        out_specs=[vmem] * 11 + [hbm] * 3,
        scratch_shapes=[
            pltpu.VMEM(dgate.shape, f32),
            pltpu.VMEM(dup.shape, f32),
            pltpu.VMEM(ddown.shape, f32),
            pltpu.SemaphoreType.DMA((2, 3)),
        ],
        compiler_params=pltpu.CompilerParams(vmem_limit_bytes=60 << 20),
        name="finish",
    )(out_low, igrad_low, wall, wall2, small, load, dgate, dup, ddown)


def shards(
    inputs,
    attention_gain,
    query_weight,
    key_weight,
    value_weight,
    out_weight,
    expert_gain,
    router_weight,
    gate_weight,
    up_weight,
    down_weight,
    routes,
    seq_lens,
    cotangent,
):
    n = lax.axis_size("expert")
    nz = lax.axis_size("tensor")
    tok_rows = inputs.shape[0]
    seq_count = seq_lens.shape[0]
    span_rows = tok_rows // seq_count
    row = lax.broadcasted_iota(jnp.int32, (tok_rows, 128), 0) % span_rows
    lane = lax.broadcasted_iota(jnp.int32, (tok_rows, 128), 1) % (HD // 2)
    frequency = THETA ** (-2.0 * lane.astype(f32) / HD)
    angles = (lax.axis_index("expert") * span_rows + row).astype(f32) * frequency
    cosines = jnp.cos(angles)
    sines = jnp.sin(angles)
    weights = (query_weight, key_weight, value_weight, out_weight, cosines, sines)
    middle, queries, pairs, logs, attended, cot_all = attend_layer(
        n, nz, inputs, attention_gain, *weights, cotangent, seq_lens
    )
    (
        grad_middle,
        logit_grads,
        expert_gain_part,
        expert_load,
        gate_grad,
        up_grad,
        down_grad,
        mixed,
        normed2,
    ) = expert_layer(
        n,
        nz,
        middle,
        expert_gain,
        router_weight,
        routes,
        gate_weight,
        up_weight,
        down_weight,
        cotangent,
        cot_all,
    )
    out_low, igrad_low, packed, packed2, small = return_layer(
        n,
        nz,
        grad_middle,
        middle,
        logit_grads,
        expert_gain_part,
        normed2,
        inputs,
        attention_gain,
        *weights,
        queries,
        pairs,
        logs,
        attended,
        seq_lens,
        mixed,
    )
    (
        output,
        input_grad,
        query_grad,
        key_grad,
        value_grad,
        out_weight_grad,
        router_grad,
        attention_gain_grad,
        expert_gain_grad,
        balance_loss,
        expert_load,
        gate_grad,
        up_grad,
        down_grad,
    ) = finish_layer(
        out_low,
        igrad_low,
        packed,
        packed2,
        small,
        expert_load,
        gate_grad,
        up_grad,
        down_grad,
        query_weight.shape[1],
        key_weight.shape[1],
    )
    return (
        output,
        input_grad,
        balance_loss[0, 0],
        expert_load[0],
        attention_gain_grad[0],
        query_grad,
        key_grad,
        value_grad,
        out_weight_grad,
        expert_gain_grad[0],
        router_grad.T,
        gate_grad,
        up_grad,
        down_grad.reshape(down_weight.shape),
    )


def solution(mesh):
    placed = (
        P("expert", None),
        P(),
        P(None, "tensor"),
        P(None, "tensor"),
        P(None, "tensor"),
        P("tensor", None),
        P(),
        P(),
        P("expert", None, "tensor"),
        P("expert", None, "tensor"),
        P("expert", "tensor", None),
        P("expert", None),
        P(),
        P("expert", None),
    )
    return jax.shard_map(
        shards,
        mesh=mesh,
        in_specs=placed,
        out_specs=(
            P("expert", None),
            P("expert", None),
            P(),
            P(),
            P(),
            P(None, "tensor"),
            P(None, "tensor"),
            P(None, "tensor"),
            P("tensor", None),
            P(),
            P(),
            P("expert", None, "tensor"),
            P("expert", None, "tensor"),
            P("expert", "tensor", None),
        ),
        check_vma=False,
    )
```
